32 devices in a mesh: pipe: 2 (over x), dp: 4 (over z), tensor: 4 (over y, core).
Axes of the slice: x: 2, y: 2, z: 4, core: 2. Of those that a mesh axis runs over, the one named last changes fastest.
Arguments:
- embeds: bfloat16 [2, 8, 1024, 512], P('pipe', 'dp', 'tensor'), may hold values from -6 to 6
- segments: int32 [2, 8, 1024], P(None, 'dp'), may hold values from -1 to 23, as said below
- cotangent: bfloat16 [8, 1024, 512], P('dp', 'tensor'), may hold values from -6 to 6
- norm_gains: float32 [2, 3, 512], P('pipe'), may hold values from 0.5 to 1.5
- attn_in: bfloat16 [2, 512, 3, 512], P('pipe', None, None, 'tensor'), may hold values from -0.25 to 0.25
- attn_out: bfloat16 [2, 512, 512], P('pipe', 'tensor'), may hold values from -1.75 to 1.75
- cross_proj: bfloat16 [2, 512, 2, 512], P('pipe', None, None, 'tensor'), may hold values from -1 to 1
- ffn_in: bfloat16 [2, 512, 2048], P('pipe', None, 'tensor'), may hold values from -0.25 to 0.25
- ffn_out: bfloat16 [2, 2048, 512], P('pipe', 'tensor'), may hold values from -1 to 1
Outputs:
- section_out: bfloat16 [2, 8, 1024, 512], P('pipe', 'dp', 'tensor')
- embeds_grad: bfloat16 [2, 8, 1024, 512], P('pipe', 'dp', 'tensor')
- norm_gains_grad: float32 [2, 3, 512], P('pipe', None, 'dp')
- attn_in_grad: float32 [2, 512, 3, 512], P('pipe', 'dp', None, 'tensor')
- attn_out_grad: float32 [2, 512, 512], P('pipe', 'tensor', 'dp')
- cross_proj_grad: float32 [2, 512, 2, 512], P('pipe', 'dp', None, 'tensor')
- ffn_in_grad: float32 [2, 512, 2048], P('pipe', 'dp', 'tensor')
- ffn_out_grad: float32 [2, 2048, 512], P('pipe', 'tensor', 'dp')
The draws below stay inside these ranges and needn't reach their ends.
Inputs may be any that keep to these rules, and one draw needn't show every extreme that they name: In every packed row the 24 sentence pairs take the numbers 0 to 23 in order on both sides, segments[0] for the source and segments[1] for the target; each pair is a run of 34 to 42 consecutive slots on each side, and the slots after the last pair, at least one on each side, are padding numbered -1.
All inputs are finite; a program needn't handle non-finite values.
Results may differ from the reference program's by a relative error of at most 0.028.
Values may be sent and summed in bfloat16 or wider, within the bound.
A program may use at most 128 MiB of HBM per device.

```python
import jax
import jax.numpy as jnp
from jax import lax

D = 512
HEADS = 8
DH = 64
FF = 2048
SLOTS = 1024
DOCS = 24
ROWS_ALL = 8


def draw_segments(key, part):
    key = jax.random.fold_in(key, 11)
    shortest = 4 * SLOTS // (5 * DOCS)
    upper_bound = (SLOTS - 1) // DOCS + 1
    lengths = jax.random.randint(key, (2, ROWS_ALL, DOCS), shortest, upper_bound)
    bounds = jnp.cumsum(lengths, axis=-1)
    places = jnp.arange(SLOTS, dtype=jnp.int32)
    passed = jnp.sum((places[None, None, :, None] >= bounds[:, :, None, :]).astype(jnp.int32), axis=-1)
    return jnp.where(passed >= DOCS, -1, passed).astype(jnp.int32)


def draw_cross_proj(key, part):
    key = jax.random.fold_in(key, 23)
    base = jax.random.normal(key, (2, D, 2, D), jnp.float32)
    section_ids = jnp.arange(2)[:, None, None, None]
    map_ids = jnp.arange(2)[None, None, :, None]
    wide_scale = (D * DOCS // SLOTS) ** (-0.5)
    narrow_scale = D ** (-0.5)
    factor = jnp.where((section_ids == 1) & (map_ids == 1), wide_scale, narrow_scale)
    return jnp.clip(base * factor, -1.0, 1.0).astype(jnp.bfloat16)


def draw_ffn_out(key, part):
    key = jax.random.fold_in(key, 37)
    base = jax.random.normal(key, (2, FF, D), jnp.float32)
    section_ids = jnp.arange(2)[:, None, None]
    factor = jnp.where(section_ids == 1, (FF // 4) ** (-0.5), FF ** (-0.5))
    return jnp.clip(base * factor, -1.0, 1.0).astype(jnp.bfloat16)


def strengthened(entries, key, source, target, shards_of, factor):
    owner, partner = [(jnp.arange(entries.shape[dim]) // (entries.shape[dim] // shards_of)).reshape([-1 if axis == dim else 1 for axis in range(entries.ndim)]) for dim in (source, target)]
    chosen = jax.random.permutation(key, shards_of)[partner]
    strong = (owner == chosen) | (owner == (partner + shards_of // 2) % shards_of)
    return jnp.where(strong, factor * entries, entries)


def block_levels(own_key, dims, pieces, low, top_value):
    loudness = 1.0
    for axis_at, shards_of in pieces:
        draws = jax.random.uniform(jax.random.fold_in(jax.random.fold_in(own_key, 6), axis_at), (shards_of,), jnp.float32, low / len(pieces), top_value / len(pieces))
        loudness = loudness * jnp.repeat(jnp.exp(draws), dims[axis_at] // shards_of).reshape((-1,) + (1,) * (len(dims) - 1 - axis_at))
    return loudness


def centred(stream_key, shape, scale, bound, cuts=(), kind=jnp.bfloat16):
    level = block_levels(stream_key, shape, cuts, -0.22, 0.18) if cuts else 1.0
    entries = jax.random.normal(stream_key, shape, jnp.float32) * scale * level
    return jnp.minimum(jnp.maximum(entries, -bound), bound).astype(kind)


def bell_draw_with(stream_key, shape, scale, limit, cuts, heavy, kind=jnp.bfloat16):
    result = scale * jax.random.normal(stream_key, shape, jnp.float32)
    if cuts:
        result = result * block_levels(stream_key, shape, cuts, -0.22, 0.18)
    return jnp.clip(strengthened(result, jax.random.fold_in(stream_key, 3), *heavy), -limit, limit).astype(kind)


def setup_inputs(seed: int = 0) -> dict:
    key_of = jax.random.split(jax.random.key(seed), 10)
    embeds = centred(key_of[0], (2, ROWS_ALL, SLOTS, D), 1.0, 6.0, ((0, 2), (1, 4), (2, 4)))
    segments = draw_segments(jax.random.fold_in(key_of[9], 71), 0)
    cotangent = bell_draw_with(key_of[2], (ROWS_ALL, SLOTS, D), 1.0, 6.0, ((0, 4), (1, 4)), (0, 2, 4, 2.0))
    norm_gains = jnp.clip(1.0 + 0.1 * jax.random.normal(key_of[3], (2, 3, D), jnp.float32), 0.5, 1.5)
    attn_in = centred(key_of[4], (2, D, 3, D), D ** -0.5, 0.25, ((0, 2), (3, 4)))
    attn_out = centred(key_of[5], (2, D, D), (D * DOCS // SLOTS) ** -0.5, 1.75, ((0, 2), (1, 4)))
    cross_proj = draw_cross_proj(jax.random.fold_in(key_of[9], 71), 0)
    ffn_in = centred(key_of[7], (2, D, FF), D ** -0.5, 0.25, ((0, 2), (2, 4)))
    ffn_out = draw_ffn_out(jax.random.fold_in(key_of[9], 71), 0)
    return dict(embeds=embeds, segments=segments, cotangent=cotangent, norm_gains=norm_gains, attn_in=attn_in, attn_out=attn_out, cross_proj=cross_proj, ffn_in=ffn_in, ffn_out=ffn_out)


norm_eps = 1e-05
masked_score = -1000000000.0
highest = lax.Precision.HIGHEST

@jax.custom_vjp
def low(v):
    return lax.optimization_barrier(v.astype(jnp.bfloat16)).astype(jnp.float32)

@jax.custom_vjp
def low_back(v):
    return v

def low_keep(v):
    return (low(v), None)

def low_pass(kept, grad):
    return (grad,)

def back_keep(v):
    return (v, None)

def back_low(kept, grad):
    return (low(grad),)
low.defvjp(low_keep, low_pass)
low_back.defvjp(back_keep, back_low)

def layer_norm(values, gain_row):
    centered = values - lax.optimization_barrier(jnp.mean(values, axis=-1, keepdims=True))
    spread = lax.optimization_barrier(jnp.mean(centered * centered, axis=-1, keepdims=True))
    return centered * lax.rsqrt(spread + norm_eps) * gain_row

def both_rounded(values):
    return low(low_back(values))

def attend(query, key_rows, value_rows, allowed):
    head_query = query.reshape(query.shape[0], HEADS, DH)
    head_keys = key_rows.reshape(key_rows.shape[0], HEADS, DH)
    head_values = value_rows.reshape(value_rows.shape[0], HEADS, DH)
    scores = jnp.einsum('qhd,khd->hqk', head_query, head_keys, precision=highest) * DH ** (-0.5)
    scores = low_back(jnp.where(allowed[None], scores, masked_score))
    probabilities = low(jax.nn.softmax(scores, axis=-1))
    mixed_heads = jnp.einsum('hqk,khd->qhd', probabilities, head_values, precision=highest)
    return both_rounded(mixed_heads.reshape(mixed_heads.shape[0], D))

def self_block(values, gain_row, in_map, out_map, allowed):
    normed = low(layer_norm(values, gain_row))
    packed = both_rounded(jnp.einsum('ld,dcj->lcj', normed, in_map, precision=highest))
    mixed_rows = attend(packed[:, 0], packed[:, 1], packed[:, 2], allowed)
    return low_back(jnp.dot(mixed_rows, out_map, precision=highest))

def ffn_block(values, gain_row, up_map, down_map):
    normed = low(layer_norm(values, gain_row))
    hidden = low_back(jnp.dot(normed, up_map, precision=highest))
    active = low(jax.nn.gelu(hidden))
    return low_back(jnp.dot(active, down_map, precision=highest))

def cross_block(values, gain_row, cross_maps, memory_kv, allowed):
    normed = low(layer_norm(values, gain_row))
    query = both_rounded(jnp.dot(normed, cross_maps[:, 0], precision=highest))
    mixed_rows = attend(query, memory_kv[:, 0], memory_kv[:, 1], allowed)
    return low_back(jnp.einsum('lj,dj->ld', mixed_rows, cross_maps[:, 1], precision=highest))

def row_forward(params, packed_row):
    norm_gains, attn_in, attn_out, cross_proj, ffn_in, ffn_out = params
    source, target, seg_source, seg_target = packed_row
    places = jnp.arange(SLOTS)
    enc_allowed = seg_source[:, None] == seg_source[None, :]
    dec_allowed = (seg_target[:, None] == seg_target[None, :]) & (places[None, :] <= places[:, None])
    cross_allowed = seg_target[:, None] == seg_source[None, :]
    enc_first = source + self_block(source, norm_gains[0, 0], attn_in[0], attn_out[0], enc_allowed)
    enc_second = enc_first + ffn_block(enc_first, norm_gains[0, 1], ffn_in[0], ffn_out[0])
    memory = low(layer_norm(enc_second, norm_gains[0, 2]))
    memory_kv = both_rounded(jnp.einsum('ld,dcj->lcj', memory, cross_proj[0], precision=highest))
    dec_first = target + self_block(target, norm_gains[1, 0], attn_in[1], attn_out[1], dec_allowed)
    dec_second = dec_first + cross_block(dec_first, norm_gains[1, 1], cross_proj[1], memory_kv, cross_allowed)
    decoded = dec_second + ffn_block(dec_second, norm_gains[1, 2], ffn_in[1], ffn_out[1])
    return (memory, decoded)

def reference(embeds, segments, cotangent, norm_gains, attn_in, attn_out, cross_proj, ffn_in, ffn_out):
    params = (norm_gains.astype(jnp.float32), attn_in.astype(jnp.float32), attn_out.astype(jnp.float32), cross_proj.astype(jnp.float32), ffn_in.astype(jnp.float32), ffn_out.astype(jnp.float32))
    inputs = embeds.astype(jnp.float32)
    row_step = jax.checkpoint(row_forward)

    def forward(weights, values):
        return lax.map(lambda packed_row: row_step(weights, packed_row), (values[0], values[1], segments[0], segments[1]))
    (memory, decoded), pullback = jax.vjp(forward, params, inputs)
    weight_grads, input_grads = pullback((jnp.zeros_like(memory), cotangent.astype(jnp.float32)))
    section_out = jnp.stack([memory, decoded]).astype(jnp.bfloat16)
    return (section_out, input_grads.astype(jnp.bfloat16), weight_grads[0], weight_grads[1], weight_grads[2], weight_grads[3], weight_grads[4], weight_grads[5])
```

```python
import functools

import jax
import jax.numpy as jnp
from jax import lax
from jax.experimental import pallas as pl
from jax.experimental.pallas import tpu as pltpu
from jax.sharding import PartitionSpec as P

EPS = 1e-05
MASKED = -1000000000.0
DH = 64
HALO = 64
F32 = jnp.float32
BF16 = jnp.bfloat16
GELU_C = 0.7978845608028654
GELU_A = 0.044715
VMEM = pl.BlockSpec(memory_space=pltpu.VMEM)
SMEM = pl.BlockSpec(memory_space=pltpu.SMEM)


def mm(a, b):
    return lax.dot_general(a, b, (((1,), (0,)), ((), ())), preferred_element_type=F32)


def mm_nt(a, b):
    return lax.dot_general(a, b, (((1,), (1,)), ((), ())), preferred_element_type=F32)


def mm_tn(a, b):
    return lax.dot_general(a, b, (((0,), (0,)), ((), ())), preferred_element_type=F32)


def norm_parts(v):
    c = v - jnp.mean(v, axis=-1, keepdims=True)
    r = lax.rsqrt(jnp.mean(c * c, axis=-1, keepdims=True) + EPS)
    return c * r, r


def norm(v, gain):
    xhat, _ = norm_parts(v)
    return xhat * gain


def norm_back(v, gain, dn):
    xhat, r = norm_parts(v)
    dxh = dn * gain
    m1 = jnp.mean(dxh, axis=-1, keepdims=True)
    m2 = jnp.mean(dxh * xhat, axis=-1, keepdims=True)
    return r * (dxh - m1 - xhat * m2), jnp.sum(dn * xhat, axis=0, keepdims=True)


def lane_low(shape):
    return lax.broadcasted_iota(jnp.int32, shape, 1) < DH


def head_pick(rows, h):
    low = lane_low(rows.shape)
    return jnp.where(low if h == 0 else jnp.logical_not(low), rows, jnp.zeros_like(rows))


def pair_join(a, b):
    return jnp.where(lane_low(a.shape), a, b)


def attend(q2, k2, v2, bias, keep):
    outs = []
    for h in range(2):
        s = mm_nt(head_pick(q2, h), k2) + bias
        e = jnp.exp(s - jnp.max(s, axis=-1, keepdims=True))
        p = e * (1.0 / jnp.sum(e, axis=-1, keepdims=True))
        pb = p.astype(BF16)
        keep(h, pb)
        outs.append(mm(pb, v2))
    return pair_join(*outs)


def attend_back(q2, k2, v2, do2, pbs):
    dq, dk, dv = [], [], []
    for h in range(2):
        pb = pbs(h)
        dp = mm_nt(head_pick(do2, h), v2)
        dv.append(mm_tn(pb, do2))
        p = pb.astype(F32)
        ds = (p * (dp - jnp.sum(dp * p, axis=-1, keepdims=True))).astype(BF16)
        dq.append(mm(ds, k2))
        dk.append(mm_tn(ds, q2))
    return pair_join(*dq) * (DH**-0.5), pair_join(*dk), pair_join(*dv)


def gelu_parts(h):
    th = jnp.tanh(GELU_C * (h + GELU_A * (h * h * h)))
    half = 0.5 * (1.0 + th)
    u = h * half
    slope = half + (0.5 * GELU_C) * h * (1.0 - th * th) * (1.0 + (3.0 * GELU_A) * (h * h))
    return u, slope


def self_forward(is_enc_ref, xw_ref, sq_ref, sk_ref, gain_ref, wa_ref, wo_ref, nw_ref, q_ref, k_ref, v_ref, p_ref, o_ref, e1_ref, bias_ref):
    rows, win, width = xw_ref.shape
    own = sq_ref.shape[1]
    is_enc = is_enc_ref[0] > 0
    for r in range(rows):
        xr = xw_ref[r].astype(F32)
        nw_ref[pl.ds(r * win, win), :] = norm(xr, gain_ref[pl.ds(0, 1), :]).astype(BF16)
        same = sq_ref[r] == sk_ref[r]
        qpos = lax.broadcasted_iota(jnp.int32, (own, win), 0)
        kpos = lax.broadcasted_iota(jnp.int32, (own, win), 1) - HALO
        before = kpos - qpos <= jnp.where(is_enc, 4 * win, 0)
        bias_ref[r] = jnp.where(same & before, 0.0, MASKED)

    def project(t, _):
        packed = mm(nw_ref[...], wa_ref[t])
        hw = q_ref.shape[-1]
        for r in range(rows):
            q = packed[r * win + HALO : r * win + HALO + own, :hw].astype(BF16)
            q_ref[t, r] = q * jnp.asarray(DH**-0.5, BF16)
            k_ref[t, r] = packed[r * win : (r + 1) * win, hw : 2 * hw].astype(BF16)
            v_ref[t, r] = packed[r * win : (r + 1) * win, 2 * hw :].astype(BF16)
        return 0

    lax.fori_loop(0, wa_ref.shape[0], project, 0)

    def one(i, _):
        t, r = i // rows, i % rows

        def keep(h, pb):
            p_ref[t, r, h] = pb

        o2 = attend(q_ref[t, r], k_ref[t, r], v_ref[t, r], bias_ref[r], keep)
        hw = o2.shape[1]
        o_ref[pl.ds(pl.multiple_of(r * own, own), own), pl.ds(pl.multiple_of(t * hw, hw), hw)] = o2.astype(BF16)
        return 0

    lax.fori_loop(0, wa_ref.shape[0] * rows, one, 0)
    e1 = mm(o_ref[...], wo_ref[...])
    for r in range(rows):
        e1_ref[pl.ds(r * own, own), :] = xw_ref[r, pl.ds(HALO, own), :].astype(F32) + e1[r * own : (r + 1) * own]


def enc_feed(is_enc_ref, e1_ref, gain_ref, w1_ref, w2_ref, n2_ref, u_ref, gp_ref, e2_ref, mem_ref):
    @pl.when(is_enc_ref[0] > 0)
    def _():
        n2_ref[...] = norm(e1_ref[...], gain_ref[pl.ds(1, 1), :]).astype(BF16)
        e2_ref[...] = e1_ref[...]

        def one(t, _):
            u, gp = gelu_parts(mm(n2_ref[...], w1_ref[t]))
            u = u.astype(BF16)
            u_ref[t] = u
            gp_ref[t] = gp.astype(BF16)
            e2_ref[...] += mm(u, w2_ref[t])
            return 0

        lax.fori_loop(0, w1_ref.shape[0], one, 0)
        mem_ref[...] = norm(e2_ref[...], gain_ref[pl.ds(2, 1), :]).astype(BF16)


def dec_middle(
    is_enc_ref, memw_ref, sq_ref, sk_ref, d1_ref, gain_ref, cot_ref, c0_ref, c1_ref, w1_ref, w2_ref,
    out_ref, dw1_ref, dw2_ref, dc0_ref, dc1_ref, dmem_ref, g1_ref, dgain_ref,
    c_ref, q_ref, k_ref, v_ref, p_ref, oc_ref, d2_ref, n3_ref, dn_ref, do_ref, dkv_ref, bias_ref,
):
    @pl.when(is_enc_ref[0] == 0)
    def _():
        rows, win, width = memw_ref.shape
        own = sq_ref.shape[1]
        pairs = c0_ref.shape[0]
        hw = q_ref.shape[-1]
        for r in range(rows):
            bias_ref[r] = jnp.where(sq_ref[r] == sk_ref[r], 0.0, MASKED)
        c_ref[...] = norm(d1_ref[...], gain_ref[pl.ds(1, 1), :]).astype(BF16)

        def project(t, _):
            q = mm(c_ref[...], c1_ref[t, :, :hw]).astype(BF16) * jnp.asarray(DH**-0.5, BF16)
            for r in range(rows):
                q_ref[t, r] = q[r * own : (r + 1) * own]
                kv = mm(memw_ref[r], c0_ref[t])
                k_ref[t, r] = kv[:, :hw].astype(BF16)
                v_ref[t, r] = kv[:, hw:].astype(BF16)
            return 0

        lax.fori_loop(0, pairs, project, 0)
        d2_ref[...] = d1_ref[...]

        def at(t, r):
            return pl.ds(pl.multiple_of(r * own, own), own), pl.ds(pl.multiple_of(t * hw, hw), hw)

        def one(i, _):
            t, r = i // rows, i % rows

            def keep(h, pb):
                p_ref[t, r, h] = pb

            o2 = attend(q_ref[t, r], k_ref[t, r], v_ref[t, r], bias_ref[r], keep).astype(BF16)
            oc_ref[at(t, r)] = o2
            rs = pl.ds(pl.multiple_of(r * own, own), own)
            d2_ref[rs, :] += mm_nt(o2, c1_ref[t, :, hw:])
            return 0

        lax.fori_loop(0, pairs * rows, one, 0)
        n3_ref[...] = norm(d2_ref[...], gain_ref[pl.ds(2, 1), :]).astype(BF16)
        out_ref[...] = d2_ref[...]
        dn_ref[...] = jnp.zeros_like(dn_ref)

        def feed(t, _):
            u, gp = gelu_parts(mm(n3_ref[...], w1_ref[t]))
            u = u.astype(BF16)
            out_ref[...] += mm(u, w2_ref[t])
            dh = (mm_nt(cot_ref[...], w2_ref[t]) * gp).astype(BF16)
            dw2_ref[t] = mm_tn(u, cot_ref[...]).astype(BF16)
            dw1_ref[t] = mm_tn(n3_ref[...], dh).astype(BF16)
            dn_ref[...] += mm_nt(dh, w1_ref[t])
            return 0

        lax.fori_loop(0, w1_ref.shape[0], feed, 0)
        dx, dg = norm_back(d2_ref[...], gain_ref[pl.ds(2, 1), :], dn_ref[...])
        dgain_ref[pl.ds(2, 1), :] = dg
        g2 = cot_ref[...].astype(F32) + dx
        g1_ref[...] = g2
        gb = g2.astype(BF16)
        do_ref[...] = jnp.zeros_like(do_ref)
        dn_ref[...] = jnp.zeros_like(dn_ref)

        def out_back(t, _):
            lanes = pl.ds(pl.multiple_of(t * hw, hw), hw)
            dc1_ref[t, :, hw:] = mm_tn(gb, oc_ref[:, lanes]).astype(BF16)
            do_ref[:, lanes] = mm(gb, c1_ref[t, :, hw:]).astype(BF16)
            return 0

        lax.fori_loop(0, pairs, out_back, 0)

        def back(i, _):
            t, r = i // rows, i % rows
            dq, dk, dv = attend_back(q_ref[t, r], k_ref[t, r], v_ref[t, r], do_ref[at(t, r)], lambda h: p_ref[t, r, h])
            q_ref[t, r] = dq.astype(BF16)
            rs = pl.ds(pl.multiple_of(r * win, win), win)
            dkv_ref[t, rs, :hw] = dk.astype(BF16)
            dkv_ref[t, rs, hw:] = dv.astype(BF16)
            return 0

        lax.fori_loop(0, pairs * rows, back, 0)
        dmem_ref[...] = jnp.zeros_like(dmem_ref)
        memw = memw_ref[...].reshape(rows * win, width)

        def maps_back(t, _):
            dq = q_ref[t].reshape(rows * own, hw)
            dc1_ref[t, :, :hw] = mm_tn(c_ref[...], dq).astype(BF16)
            dn_ref[...] += mm_nt(dq, c1_ref[t, :, :hw])
            dc0_ref[t] = mm_tn(memw, dkv_ref[t]).astype(BF16)
            dmem_ref[...] += mm_nt(dkv_ref[t], c0_ref[t])
            return 0

        lax.fori_loop(0, pairs, maps_back, 0)
        dx, dg = norm_back(d1_ref[...], gain_ref[pl.ds(1, 1), :], dn_ref[...])
        dgain_ref[pl.ds(1, 1), :] = dg
        dgain_ref[pl.ds(0, 1), :] = jnp.zeros_like(dg)
        g1_ref[...] += dx


def enc_feed_back(is_enc_ref, dmem_ref, e2_ref, e1_ref, n2_ref, u_ref, gp_ref, gain_ref, w1_ref, w2_ref, dw1_ref, dw2_ref, g_ref, dgain_ref, dn_ref):
    @pl.when(is_enc_ref[0] > 0)
    def _():
        dx, dg = norm_back(e2_ref[...], gain_ref[pl.ds(2, 1), :], dmem_ref[...].astype(F32))
        dgain_ref[pl.ds(2, 1), :] = dg
        g_ref[...] = dx
        gb = dx.astype(BF16)
        dn_ref[...] = jnp.zeros_like(dn_ref)

        def feed(t, _):
            dh = (mm_nt(gb, w2_ref[t]) * gp_ref[t].astype(F32)).astype(BF16)
            dw2_ref[t] = mm_tn(u_ref[t], gb).astype(BF16)
            dw1_ref[t] = mm_tn(n2_ref[...], dh).astype(BF16)
            dn_ref[...] += mm_nt(dh, w1_ref[t])
            return 0

        lax.fori_loop(0, w1_ref.shape[0], feed, 0)
        dx, dg = norm_back(e1_ref[...], gain_ref[pl.ds(1, 1), :], dn_ref[...])
        dgain_ref[pl.ds(1, 1), :] = dg
        dgain_ref[pl.ds(0, 1), :] = jnp.zeros_like(dg)
        g_ref[...] += dx


def self_backward(g_ref, nw_ref, q_ref, k_ref, v_ref, p_ref, o_ref, wa_ref, wo_ref, da_ref, do_out_ref, dnw_ref, do_ref, dqkv_ref):
    pairs, rows, own, hw = q_ref.shape
    win = k_ref.shape[2]
    gb = g_ref[...].astype(BF16)
    do_out_ref[...] = mm_tn(o_ref[...], gb).astype(BF16)
    do_ref[...] = mm_nt(gb, wo_ref[...]).astype(BF16)
    dnw_ref[...] = jnp.zeros_like(dnw_ref)

    def back(i, _):
        t, r = i // rows, i % rows
        do2 = do_ref[pl.ds(pl.multiple_of(r * own, own), own), pl.ds(pl.multiple_of(t * hw, hw), hw)]
        dq, dk, dv = attend_back(q_ref[t, r], k_ref[t, r], v_ref[t, r], do2, lambda h: p_ref[t, r, h])
        base = pl.multiple_of(r * win, HALO)
        dqkv_ref[t, pl.ds(base, HALO), :hw] = jnp.zeros((HALO, hw), BF16)
        dqkv_ref[t, pl.ds(base + HALO + own, HALO), :hw] = jnp.zeros((HALO, hw), BF16)
        dqkv_ref[t, pl.ds(base + HALO, own), :hw] = dq.astype(BF16)
        dqkv_ref[t, pl.ds(base, win), hw : 2 * hw] = dk.astype(BF16)
        dqkv_ref[t, pl.ds(base, win), 2 * hw :] = dv.astype(BF16)
        return 0

    lax.fori_loop(0, pairs * rows, back, 0)

    def maps_back(t, _):
        da_ref[t] = mm_tn(nw_ref[...], dqkv_ref[t]).astype(BF16)
        dnw_ref[...] += mm_nt(dqkv_ref[t], wa_ref[t])
        return 0

    lax.fori_loop(0, pairs, maps_back, 0)


def call(kernel, name, outs, scratch, args, scalars=1):
    return pl.pallas_call(
        kernel,
        name=name,
        out_shape=[jax.ShapeDtypeStruct(*o) for o in outs],
        in_specs=[SMEM] * scalars + [VMEM] * (len(args) - scalars),
        out_specs=[VMEM] * len(outs),
        scratch_shapes=[pltpu.VMEM(*s) for s in scratch],
        compiler_params=pltpu.CompilerParams(vmem_limit_bytes=60 << 20),
    )(*args)


def shifted(rows, by):
    n = lax.axis_size("tensor")
    return lax.ppermute(rows, "tensor", [(i, i + by) for i in range(n) if 0 <= i + by < n])


def body(embeds, segments, cotangent, norm_gains, attn_in, attn_out, cross_proj, ffn_in, ffn_out):
    pipe = lax.axis_index("pipe")
    me = lax.axis_index("tensor")
    shards = lax.axis_size("tensor")
    is_enc = pipe == 0
    enc_flag = jnp.where(is_enc, 1, 0).astype(jnp.int32).reshape(1)
    rows, own, width = embeds.shape[1:]
    slots = segments.shape[2]
    hw = attn_in.shape[3]
    fw = ffn_in.shape[2]
    win = own + 2 * HALO
    cwin = 2 * own + 2 * HALO
    tokens = rows * own

    gather = functools.partial(lax.all_gather, axis_name="tensor", axis=0)
    wa = gather(attn_in[0].reshape(width, 3 * hw))
    wo = gather(attn_out[0], tiled=True)
    w1 = gather(ffn_in[0])
    w2 = gather(ffn_out[0])
    cx = cross_proj[0].reshape(width, 2 * hw)
    c1 = gather(cx)
    c0 = gather(lax.ppermute(cx, "pipe", [(0, 1), (1, 0)]))
    gains = norm_gains[0]

    x = embeds[0]
    xw = jnp.concatenate([shifted(x[:, own - HALO :], 1), x, shifted(x[:, :HALO], -1)], axis=1)
    seg_self = jnp.where(is_enc, segments[0], segments[1])
    padded = jnp.pad(seg_self, ((0, 0), (HALO, HALO)), constant_values=-2)
    start = me * own
    sq = lax.dynamic_slice(seg_self, (0, start), (rows, own))[:, :, None]
    sk = lax.dynamic_slice(padded, (0, start), (rows, win))[:, None, :]

    nw, q, k, v, p, o, e1 = call(
        self_forward,
        "self_forward",
        [
            ((rows * win, width), BF16),
            ((shards, rows, own, hw), BF16),
            ((shards, rows, win, hw), BF16),
            ((shards, rows, win, hw), BF16),
            ((shards, rows, 2, own, win), BF16),
            ((tokens, width), BF16),
            ((tokens, width), F32),
        ],
        [((rows, own, win), F32)],
        (enc_flag, xw, sq, sk, gains, wa, wo),
    )
    n2, u, gp, e2, mem = call(
        enc_feed,
        "enc_feed",
        [
            ((tokens, width), BF16),
            ((shards, tokens, fw), BF16),
            ((shards, tokens, fw), BF16),
            ((tokens, width), F32),
            ((tokens, width), BF16),
        ],
        [],
        (enc_flag, e1, gains, w1, w2),
    )
    mem = mem.reshape(rows, own, width)
    moved = lax.ppermute(mem, "pipe", [(0, 1), (1, 0)])
    all_mem = lax.all_gather(moved, "tensor", axis=1, tiled=True)
    cstart = jnp.minimum(me * (own - HALO), slots - cwin)
    memw = lax.dynamic_slice(all_mem, (0, cstart, 0), (rows, cwin, width))
    csk = lax.dynamic_slice(segments[0], (0, cstart), (rows, cwin))[:, None, :]
    csq = lax.dynamic_slice(segments[1], (0, start), (rows, own))[:, :, None]
    dec_out, dw1d, dw2d, dc0, dc1, dmemw, g1, dgain_d = call(
        dec_middle,
        "dec_middle",
        [
            ((tokens, width), F32),
            ((shards, width, fw), BF16),
            ((shards, fw, width), BF16),
            ((shards, width, 2 * hw), BF16),
            ((shards, width, 2 * hw), BF16),
            ((rows * cwin, width), F32),
            ((tokens, width), F32),
            ((3, width), F32),
        ],
        [
            ((tokens, width), BF16),
            ((shards, rows, own, hw), BF16),
            ((shards, rows, cwin, hw), BF16),
            ((shards, rows, cwin, hw), BF16),
            ((shards, rows, 2, own, cwin), BF16),
            ((tokens, width), BF16),
            ((tokens, width), F32),
            ((tokens, width), BF16),
            ((tokens, width), F32),
            ((tokens, width), BF16),
            ((shards, rows * cwin, 2 * hw), BF16),
            ((rows, own, cwin), F32),
        ],
        (enc_flag, memw, csq, csk, e1, gains, cotangent.reshape(tokens, width), c0, c1, w1, w2),
    )
    dmem = jnp.zeros((rows, slots, width), BF16)
    dmem = lax.dynamic_update_slice(dmem, dmemw.reshape(rows, cwin, width).astype(BF16), (0, cstart, 0))
    dmem = lax.psum_scatter(dmem, "tensor", scatter_dimension=1, tiled=True)
    dmem = lax.ppermute(dmem, "pipe", [(0, 1), (1, 0)]).reshape(tokens, width)
    dw1e, dw2e, ge, dgain_e = call(
        enc_feed_back,
        "enc_feed_back",
        [
            ((shards, width, fw), BF16),
            ((shards, fw, width), BF16),
            ((tokens, width), F32),
            ((3, width), F32),
        ],
        [((tokens, width), F32)],
        (enc_flag, dmem, e2, e1, n2, u, gp, gains, w1, w2),
    )
    g = jnp.where(is_enc, ge, g1)
    dw1 = jnp.where(is_enc, dw1e, dw1d)
    dw2 = jnp.where(is_enc, dw2e, dw2d)
    dgain = jnp.where(is_enc, dgain_e, dgain_d)
    da, dwo, dnw = call(
        self_backward,
        "self_backward",
        [
            ((shards, width, 3 * hw), BF16),
            ((width, width), BF16),
            ((rows * win, width), F32),
        ],
        [
            ((tokens, width), BF16),
            ((shards, rows * win, 3 * hw), BF16),
        ],
        (g, nw, q, k, v, p, o, wa, wo),
        scalars=0,
    )
    dnw = dnw.reshape(rows, win, width)
    from_right = shifted(dnw[:, :HALO].astype(BF16), -1).astype(F32)
    from_left = shifted(dnw[:, own + HALO :].astype(BF16), 1).astype(F32)
    dn = dnw[:, HALO : HALO + own]
    dn = dn.at[:, own - HALO :].add(from_right).at[:, :HALO].add(from_left).reshape(tokens, width)
    dx, dg0 = norm_back(x.reshape(tokens, width).astype(F32), gains[0:1], dn)
    grad_x = (g + dx).astype(BF16).reshape(rows, own, width)
    dgain = dgain.at[0:1].add(dg0)
    dgain = lax.psum(dgain, ("tensor", "dp"))
    share = width // lax.axis_size("dp")
    dgain = lax.dynamic_slice(dgain, (0, lax.axis_index("dp") * share), (3, share))

    section = jnp.where(is_enc, mem, dec_out.reshape(rows, own, width).astype(BF16))

    def scattered(v, dim):
        v = lax.psum_scatter(v, "tensor", scatter_dimension=0, tiled=False)
        return lax.psum_scatter(v, "dp", scatter_dimension=dim, tiled=True).astype(F32)

    da = scattered(da, 0).reshape(-1, 3, hw)
    dwo = scattered(dwo.reshape(shards, hw, width), 1)
    dw1 = scattered(dw1, 0)
    dw2 = scattered(dw2, 1)
    dc0 = scattered(dc0, 0)
    dc1 = scattered(dc1, 0)
    dc0 = lax.ppermute(dc0, "pipe", [(0, 1), (1, 0)])
    dc = jnp.where(is_enc, dc0, dc1).reshape(-1, 2, hw)
    return (section[None], grad_x[None], dgain[None], da[None], dwo[None], dc[None], dw1[None], dw2[None])


def solution(mesh):
    return jax.shard_map(
        body,
        mesh=mesh,
        in_specs=(
            P("pipe", "dp", "tensor", None),
            P(None, "dp", None),
            P("dp", "tensor", None),
            P("pipe", None, None),
            P("pipe", None, None, "tensor"),
            P("pipe", "tensor", None),
            P("pipe", None, None, "tensor"),
            P("pipe", None, "tensor"),
            P("pipe", "tensor", None),
        ),
        out_specs=(
            P("pipe", "dp", "tensor", None),
            P("pipe", "dp", "tensor", None),
            P("pipe", None, "dp"),
            P("pipe", "dp", None, "tensor"),
            P("pipe", "tensor", "dp"),
            P("pipe", "dp", None, "tensor"),
            P("pipe", "dp", "tensor"),
            P("pipe", "tensor", "dp"),
        ),
        check_vma=False,
    )
```

```python
import functools

import jax
import jax.numpy as jnp
from jax import lax
from jax.experimental import pallas as pl
from jax.experimental.pallas import tpu as pltpu
from jax.sharding import PartitionSpec as P

EPS = 1e-05
MASKED = -1000000000.0
DH = 64
HALO = 64
F32 = jnp.float32
BF16 = jnp.bfloat16
GELU_C = 0.7978845608028654
GELU_A = 0.044715
MESH = pl.DeviceIdType.MESH
VMEM_LIMIT = 63 << 20


def mm(a, b):
    return lax.dot_general(a, b, (((1,), (0,)), ((), ())), preferred_element_type=F32)


def mm_nt(a, b):
    return lax.dot_general(a, b, (((1,), (1,)), ((), ())), preferred_element_type=F32)


def mm_tn(a, b):
    return lax.dot_general(a, b, (((0,), (0,)), ((), ())), preferred_element_type=F32)


def norm_parts(v):
    c = v - jnp.mean(v, axis=-1, keepdims=True)
    r = lax.rsqrt(jnp.mean(c * c, axis=-1, keepdims=True) + EPS)
    return c * r, r


def norm(v, gain):
    xhat, _ = norm_parts(v)
    return xhat * gain


def norm_back(v, gain, dn):
    xhat, r = norm_parts(v)
    dxh = dn * gain
    m1 = jnp.mean(dxh, axis=-1, keepdims=True)
    m2 = jnp.mean(dxh * xhat, axis=-1, keepdims=True)
    return r * (dxh - m1 - xhat * m2), jnp.sum(dn * xhat, axis=0, keepdims=True)


def lane_low(shape):
    return lax.broadcasted_iota(jnp.int32, shape, 1) < DH


def head_pick(rows, h):
    low = lane_low(rows.shape)
    return jnp.where(low if h == 0 else jnp.logical_not(low), rows, jnp.zeros_like(rows))


def pair_join(a, b):
    return jnp.where(lane_low(a.shape), a, b)


def attend(q2, k2, v2, bias, keep):
    outs = []
    for h in range(2):
        s = mm_nt(head_pick(q2, h), k2) + bias
        e = jnp.exp(s - jnp.max(s, axis=-1, keepdims=True))
        p = e * (1.0 / jnp.sum(e, axis=-1, keepdims=True))
        pb = p.astype(BF16)
        keep(h, pb)
        outs.append(mm(pb, v2))
    return pair_join(*outs)


def attend_back(q2, k2, v2, do2, pbs):
    dq, dk, dv = [], [], []
    for h in range(2):
        pb = pbs(h)
        dp = mm_nt(head_pick(do2, h), v2)
        dv.append(mm_tn(pb, do2))
        p = pb.astype(F32)
        ds = (p * (dp - jnp.sum(dp * p, axis=-1, keepdims=True))).astype(BF16)
        dq.append(mm(ds, k2))
        dk.append(mm_tn(ds, q2))
    return pair_join(*dq) * (DH**-0.5), pair_join(*dk), pair_join(*dv)


def gelu_parts(h):
    th = jnp.tanh(GELU_C * (h + GELU_A * (h * h * h)))
    half = 0.5 * (1.0 + th)
    u = h * half
    slope = half + (0.5 * GELU_C) * h * (1.0 - th * th) * (1.0 + (3.0 * GELU_A) * (h * h))
    return u, slope


def flip(i, bit):
    return i + bit - 2 * bit * lax.rem(lax.div(i, bit), 2)


def bit_of(i, bit):
    return lax.rem(lax.div(i, bit), 2)


def reversed_bits(i, count):
    out, bit = 0, 1
    while bit < count:
        out = 2 * out + (i // bit) % 2
        bit *= 2
    return out


class Links:
    def __init__(self, send, recv, local):
        self.send, self.recv, self.local = send, recv, local
        self.n = self.m = 0
        self.sent = []

    def take(self, count=1):
        self.n += count
        return self.n - count

    def remote(self, src, dst, device, at=None):
        at = self.take() if at is None else at
        return pltpu.make_async_remote_copy(
            src_ref=src, dst_ref=dst, send_sem=self.send.at[at], recv_sem=self.recv.at[at],
            device_id=device, device_id_type=MESH,
        )

    def here(self, src, dst):
        self.m += 1
        return pltpu.make_async_copy(src, dst, self.local.at[self.m - 1])


class Gather:
    def __init__(self, links, src, full, at, inner):
        t, t2 = at["t"], at["t2"]
        half = full.shape[1] // 2
        mine = pl.ds(pl.multiple_of(at["b"] * half, half), half)
        other = pl.ds(pl.multiple_of((1 - at["b"]) * half, half), half)
        self.own = None if inner else links.here(src, full.at[t])
        self.core = links.remote(src, full.at[t], at["C"])
        self.over_y = links.remote(src.at[mine], full.at[t, mine], at["Y"])
        self.over_z = links.remote(full.at[t2, mine], full.at[t2, mine], at["Z"][0])
        self.core_a = links.remote(full.at[t2, mine], full.at[t2, mine], at["C"])
        self.core_b = links.remote(full.at[t2, other], full.at[t2, other], at["C"])

    def start_near(self):
        if self.own is not None:
            self.own.start()
        self.core.start()

    def start_y(self):
        self.over_y.start()

    def step1(self):
        self.over_y.wait_recv()
        self.over_z.start()
        self.core_a.start()

    def step2(self):
        self.over_z.wait_recv()
        self.core_b.start()

    def ready(self, i):
        if i == 0 and self.own is not None:
            self.own.wait()
        if i == 1:
            self.core.wait_recv()
        if i == 3:
            self.core_a.wait_recv()
            self.core_b.wait_recv()

    def finish(self):
        for c in (self.core, self.over_y, self.over_z, self.core_a, self.core_b):
            c.wait_send()


class Reduce:
    def __init__(self, links, part, rc, ry, zb, zr, at):
        self.part, self.at = part, at
        self.rc, self.ry, self.zb, self.zr = rc, ry, zb, zr
        self.dp = zb.shape[0]
        self.core = [links.remote(part(at[f]), rc.at[j], at["C"]) for j, f in enumerate(("t1", "t3"))]
        self.over_y = links.remote(part(at["t2"]), ry, at["Y"])
        self.over_z = []
        off, m, bit, k = 0, self.dp, 1, 0
        self.kept = []
        while m > 1:
            m //= 2
            b = bit_of(at["d"], bit)
            keep, give = off + b * m, off + (1 - b) * m
            self.over_z.append(links.remote(zb.at[pl.ds(give, m)], zr[k], at["Z"][k]))
            self.kept.append((keep, m))
            off, bit, k = keep, 2 * bit, k + 1

    def core_send(self, j):
        self.core[j].start()

    def core_done(self):
        self.core[0].wait_recv()
        self.core[1].wait_recv()
        far, near = self.part(self.at["t2"]), self.part(self.at["t"])
        far[...] = (far[...].astype(F32) + self.rc[1].astype(F32)).astype(BF16)
        self.over_y.start()
        near[...] = (near[...].astype(F32) + self.rc[0].astype(F32)).astype(BF16)

    def y_done(self):
        self.over_y.wait_recv()
        near = self.part(self.at["t"])
        rows = self.zb.shape[1]
        for i in range(self.dp):
            where = pl.ds(i * rows, rows)
            total = near[where].astype(F32) + self.ry[where].astype(F32)
            self.zb[reversed_bits(i, self.dp)] = total.astype(BF16)
        self.over_z[0].start()

    def z_done(self, k, out=None):
        self.over_z[k].wait_recv()
        keep, m = self.kept[k]
        if k == len(self.over_z) - 1:
            out[...] = self.zb[keep].astype(F32) + self.zr[k][0].astype(F32)
        else:
            live = self.zb.at[pl.ds(keep, m)]
            live[...] = (live[...].astype(F32) + self.zr[k][...].astype(F32)).astype(BF16)
            self.over_z[k + 1].start()

    def rest_z(self, k, out):
        for j in range(k, len(self.over_z)):
            self.z_done(j, out)

    def finish(self):
        for c in self.core + [self.over_y] + self.over_z:
            c.wait_send()


def layers(names, *refs):
    ref = dict(zip(names, refs))
    R = lambda name: ref[name]
    p, d, t = lax.axis_index("pipe"), lax.axis_index("dp"), lax.axis_index("tensor")
    is_enc, is_dec = p == 0, p == 1
    dp = lax.axis_size("dp")
    t1, t2, t3 = flip(t, 1), flip(t, 2), 3 - t
    zbits = []
    while 2 ** len(zbits) < dp:
        zbits.append((p, flip(d, 2 ** len(zbits)), t))
    at = dict(t=t, t1=t1, t2=t2, t3=t3, d=d, b=bit_of(d, 1), C=(p, d, t1), Y=(p, d, t2), T=(p, d, t3), X=(1 - p, d, t), Z=zbits)
    rows, own, width = R("x").shape
    win, cwin = own + 2 * HALO, 2 * own + 2 * HALO
    slots = 4 * own
    tokens = rows * own
    hw = R("wa").shape[2] // 3
    inner = t % 3 != 0
    scale = jnp.asarray(DH**-0.5, BF16)
    gain_ref, x_ref = R("gains"), R("x")
    side = 3 * own // 4

    def rowsl(r, n=own):
        return pl.ds(pl.multiple_of(r * n, n), n)

    def lanes(s, n=hw):
        return pl.ds(pl.multiple_of(s * n, n), n)

    def near_first(i):
        return 2 * lax.rem(lax.div(t, 2) + lax.div(i, 2), 2) + lax.rem(lax.rem(t, 2) + lax.rem(i, 2), 2)

    def far_first(i):
        return 2 * lax.rem(lax.div(t, 2) + lax.rem(lax.div(i + 1, 2), 2), 2) + lax.rem(lax.rem(t, 2) + 1 - lax.div(i, 2), 2)

    links = Links(R("send"), R("recv"), R("local"))
    g_wa = Gather(links, R("wa_h"), R("wa"), at, False)
    g_wo = Gather(links, R("wo_h"), R("wo"), at, False)
    g_w1 = Gather(links, R("w1_h"), R("w1"), at, False)
    g_w2 = Gather(links, R("w2_h"), R("w2"), at, False)
    g_c1 = Gather(links, R("cx_h"), R("c1"), at, False)
    c0_x = links.remote(R("cx_h"), R("c0").at[t], at["X"])
    g_c0 = Gather(links, R("c0").at[t], R("c0"), at, True)
    x_right = links.remote(x_ref.at[:, pl.ds(own - HALO, HALO)], R("xh").at[0], (p, d, lax.rem(t + 1, 4)))
    x_left = links.remote(x_ref.at[:, pl.ds(0, HALO)], R("xh").at[1], (p, d, lax.rem(t + 3, 4)))
    base_mem, base_memc, base_memt = links.take(rows), links.take(rows), links.take(rows)
    base_dmc, base_dmt, base_dmx = links.take(rows), links.take(rows), links.take(rows)
    block = pl.ds(pl.multiple_of(t * own, own), own)
    block1 = pl.ds(pl.multiple_of(t1 * own, own), own)
    edge_out = pl.ds(pl.multiple_of(lax.rem(own // 2 + side * t, slots), HALO), side)
    edge_in = pl.ds(pl.multiple_of(lax.rem(own // 2 + side * t3, slots), HALO), side)

    def mem_x(r):
        return links.remote(R("sec").at[rowsl(r)], R("memf").at[r, block], at["X"], base_mem + r)

    def mem_c(r):
        return links.remote(R("memf").at[r, block], R("memf").at[r, block], at["C"], base_memc + r)

    def mem_t(r):
        return links.remote(R("memf").at[r, edge_out], R("memf").at[r, edge_out], at["T"], base_memt + r)

    def in_row(r, span):
        return pl.ds(pl.multiple_of(r * slots + span.start, HALO), span.size)

    def dm_rows(r, span):
        return R("dmf").at[in_row(r, span)]

    def dm_c(r):
        return links.remote(dm_rows(r, block1), R("rcc").at[r], at["C"], base_dmc + r)

    def dm_t(r):
        return links.remote(dm_rows(r, edge_in), R("rct").at[r], at["T"], base_dmt + r)

    def dm_x(r):
        return links.remote(R("dmt").at[r], R("dmr").at[r], at["X"], base_dmx + r)

    def parts_of(buf, n_rows, n_cols, skip=0):
        def part(s):
            return buf.at[pl.ds(pl.multiple_of(skip + s * n_rows, n_rows), n_rows), pl.ds(0, n_cols)]

        return part

    def reduce_of(name, buf, skip=0):
        rc, ry, zb = R("rc_" + name), R("ry_" + name), R("zb_" + name)
        zr = [R(f"zr{k}_{name}") for k in range(len(zbits))]
        return Reduce(links, parts_of(buf, ry.shape[0], ry.shape[1], skip), rc, ry, zb, zr, at)

    r_w2 = reduce_of("w2", R("dw2"))
    r_w1 = reduce_of("w1", R("dmf"))
    r_wo = reduce_of("wo", R("dwo"))
    r_wa = reduce_of("wa", R("cp"))
    r_c0 = reduce_of("c0", R("kv"))
    r_c1 = reduce_of("c1", R("kv"), 4 * width)
    c0_back = links.remote(R("dc0"), R("dc0r"), at["X"])
    dn_right = links.remote(R("dhs").at[1], R("dhr").at[0], (p, d, lax.rem(t + 1, 4)))
    dn_left = links.remote(R("dhs").at[0], R("dhr").at[1], (p, d, lax.rem(t + 3, 4)))
    gain_links = [links.remote(R("dgs").at[k], R("dgr").at[k], dev) for k, dev in enumerate([at["C"], at["Y"]] + zbits)]

    @pl.when(is_dec)
    def _():
        for at_t, start in ((0, 2 * own), (1, 2 * own + side), (3, 2 * own - 2 * HALO)):
            @pl.when(t == at_t)
            def _():
                for r in range(rows):
                    R("memf")[r, pl.ds(start, 2 * HALO), :] = jnp.zeros((2 * HALO, width), BF16)

    barrier = pltpu.get_barrier_semaphore()
    partners = [at["C"], at["Y"], at["T"], at["X"]] + zbits
    for dev in partners:
        pl.semaphore_signal(barrier, inc=1, device_id=dev, device_id_type=MESH)
    pl.semaphore_wait(barrier, len(partners))

    pl.when(t < 3)(x_right.start)
    pl.when(t > 0)(x_left.start)
    g_wa.start_near()
    g_wa.start_y()
    g_wo.start_near()
    g_wo.start_y()

    @pl.when(is_enc)
    def _():
        c0_x.start()
        g_w1.start_near()
        g_w2.start_near()

    @pl.when(is_dec)
    def _():
        g_c1.start_near()
        g_w2.start_near()
        g_w1.start_near()

    nw_ref, bias_ref = R("nw"), R("bias")
    gain0 = gain_ref[pl.ds(0, 1), :]
    for r in range(rows):
        nw_ref[pl.ds(r * win + HALO, own), :] = norm(x_ref[r].astype(F32), gain0).astype(BF16)
        same = R("sq")[r] == R("sk")[r]
        qpos = lax.broadcasted_iota(jnp.int32, (own, win), 0)
        kpos = lax.broadcasted_iota(jnp.int32, (own, win), 1) - HALO
        before = kpos - qpos <= jnp.where(is_enc, 4 * win, 0)
        bias_ref[r] = jnp.where(same & before, 0.0, MASKED)

    @pl.when(t == 0)
    def _():
        R("xh")[0] = jnp.zeros((rows, HALO, width), BF16)

    @pl.when(t == 3)
    def _():
        R("xh")[1] = jnp.zeros((rows, HALO, width), BF16)

    pl.when(t > 0)(x_right.wait_recv)
    pl.when(t < 3)(x_left.wait_recv)
    for r in range(rows):
        nw_ref[pl.ds(r * win, HALO), :] = norm(R("xh")[0, r].astype(F32), gain0).astype(BF16)
        nw_ref[pl.ds(r * win + HALO + own, HALO), :] = norm(R("xh")[1, r].astype(F32), gain0).astype(BF16)

    def after_pair(i):
        @pl.when(i == 0)
        def _():
            g_wa.step1()
            pl.when(is_enc)(g_w1.start_y)
            pl.when(is_dec)(g_c1.start_y)

        @pl.when(i == 1)
        def _():
            g_wa.step2()
            g_wo.step1()
            pl.when(is_enc)(g_w2.start_y)

            @pl.when(is_dec)
            def _():
                c0_x.wait_recv()
                g_c0.start_near()
                g_c0.start_y()
                g_w2.start_y()

        @pl.when(i == 2)
        def _():
            g_wo.step2()
            pl.when(is_enc)(g_w1.step1)

            @pl.when(is_dec)
            def _():
                g_c1.step1()
                g_w1.start_y()

        @pl.when(i == 3)
        def _():
            pl.when(is_enc)(g_w1.step2)

            @pl.when(is_dec)
            def _():
                g_c1.step2()
                g_c0.step1()

    def wait_ready(i, *weights):
        for k in range(4):
            @pl.when(i == k)
            def _():
                for w in weights:
                    w.ready(k)

    q_ref, k_ref, v_ref, p_ref, o_ref = R("q"), R("k"), R("v"), R("p"), R("o")

    def self_pair(i, _):
        s = near_first(i)
        wait_ready(i, g_wa)
        packed = mm(nw_ref[...], R("wa")[s])
        for r in range(rows):
            q_ref[s, r] = packed[r * win + HALO : r * win + HALO + own, :hw].astype(BF16) * scale
            k_ref[s, r] = packed[r * win : (r + 1) * win, hw : 2 * hw].astype(BF16)
            v_ref[s, r] = packed[r * win : (r + 1) * win, 2 * hw :].astype(BF16)

        def one(r, _):
            def keep(h, pb):
                p_ref[s, r, h] = pb

            o2 = attend(q_ref[s, r], k_ref[s, r], v_ref[s, r], bias_ref[r], keep)
            o_ref[rowsl(r), lanes(s)] = o2.astype(BF16)
            return 0

        lax.fori_loop(0, rows, one, 0)
        after_pair(i)
        return 0

    lax.fori_loop(0, 4, self_pair, 0)
    for k in range(4):
        g_wo.ready(k)
    r1_ref, r2_ref, n2_ref, n3_ref = R("r1"), R("r2"), R("n2"), R("n3")
    u_ref, gp_ref, sec_ref = R("u"), R("gp"), R("sec")
    acc_ref, g_ref, gb_ref = R("acc"), R("g"), R("gb")
    first = mm(o_ref[...], R("wo")[...].reshape(4 * hw, width))
    for r in range(rows):
        r1_ref[pl.ds(r * own, own), :] = x_ref[r].astype(F32) + first[r * own : (r + 1) * own]
    n2_ref[...] = norm(r1_ref[...], gain_ref[pl.ds(1, 1), :]).astype(BF16)

    @pl.when(is_enc)
    def _():
        def row(r, _):
            rs = rowsl(r)
            r2_ref[rs, :] = r1_ref[rs, :]

            def one(i, _):
                s = near_first(i)

                @pl.when(r == 0)
                def _():
                    wait_ready(i, g_w1, g_w2)

                u, gp = gelu_parts(mm(n2_ref[rs, :], R("w1")[s]))
                u = u.astype(BF16)
                u_ref[s, rs, :] = u
                gp_ref[s, rs, :] = gp.astype(BF16)
                r2_ref[rs, :] += mm(u, R("w2")[s])
                pl.when((r == 0) & (i == 0))(g_w2.step1)
                pl.when((r == 0) & (i == 1))(g_w2.step2)
                return 0

            lax.fori_loop(0, 4, one, 0)
            sec_ref[rs, :] = norm(r2_ref[rs, :], gain_ref[pl.ds(2, 1), :]).astype(BF16)
            mem_x(r).start()
            return 0

        lax.fori_loop(0, rows, row, 0)

    cstart = pl.multiple_of(jnp.minimum(t * (own - HALO), slots - cwin), HALO)
    cwindow = pl.ds(cstart, cwin)
    kv_ref, cq_ref, cp_ref, dkv_ref, cbias_ref = R("kv"), R("cq"), R("cp"), R("dkv"), R("cbias")
    c0_ref, c1_ref, oc_ref, cot_ref = R("c0"), R("c1"), R("oc"), R("cot")

    @pl.when(is_dec)
    def _():
        g_c0.step2()
        g_w2.step1()
        kv_ref[...] = jnp.zeros_like(kv_ref)
        R("dmf")[...] = jnp.zeros_like(R("dmf"))
        for k in range(4):
            g_c1.ready(k)

        def queries(s, _):
            q = mm(n2_ref[...], c1_ref[s, :, :hw]).astype(BF16) * scale
            for r in range(rows):
                cq_ref[s, r] = q[r * own : (r + 1) * own]
            return 0

        lax.fori_loop(0, 4, queries, 0)
        g_w2.step2()
        g_w1.step1()
        for k in range(4):
            g_w2.ready(k)

        def early(s, _):
            gp_ref[s] = mm_nt(cot_ref[...], R("w2")[s]).astype(BF16)
            return 0

        lax.fori_loop(0, 4, early, 0)
        g_w1.step2()
        for k in range(4):
            g_w1.ready(k)
            g_c0.ready(k)

        def row(r, _):
            rs = rowsl(r)
            cbias_ref[...] = jnp.where(R("csq")[r] == R("csk")[r], 0.0, MASKED)

            def keys(span, n):
                def one(s, _):
                    kv = mm(R("memf")[r, span, :], c0_ref[s])
                    kv_ref[pl.ds(pl.multiple_of(s * slots + span.start, HALO), n), :] = kv.astype(BF16)
                    return 0

                lax.fori_loop(0, 4, one, 0)

            mem_x(r).wait_recv()
            mem_c(r).start()
            pl.when(inner)(mem_t(r).start)
            keys(block, own)
            mem_c(r).wait_recv()
            keys(block1, own)

            @pl.when(inner)
            def _():
                mem_t(r).wait_recv()
                keys(edge_in, side)

            r2_ref[rs, :] = r1_ref[rs, :]

            def window(s):
                return pl.ds(pl.multiple_of(s * slots + cstart, HALO), cwin)

            def cross(s, _):
                def keep(h, pb):
                    cp_ref[rowsl(2 * s + h), :] = pb

                o2 = attend(cq_ref[s, r], kv_ref[window(s), :hw], kv_ref[window(s), hw:], cbias_ref[...], keep).astype(BF16)
                oc_ref[rs, lanes(s)] = o2
                r2_ref[rs, :] += mm_nt(o2, c1_ref[s, :, hw:])
                return 0

            lax.fori_loop(0, 4, cross, 0)
            n3_ref[rs, :] = norm(r2_ref[rs, :], gain_ref[pl.ds(2, 1), :]).astype(BF16)
            dn = pl.ds(0, own)
            acc_ref[dn, :] = jnp.zeros((own, width), F32)
            g_ref[rs, :] = r2_ref[rs, :]

            def feed(s, _):
                u, gp = gelu_parts(mm(n3_ref[rs, :], R("w1")[s]))
                u = u.astype(BF16)
                u_ref[s, rs, :] = u
                g_ref[rs, :] += mm(u, R("w2")[s])
                dh = (gp_ref[s, rs, :].astype(F32) * gp).astype(BF16)
                gp_ref[s, rs, :] = dh
                acc_ref[dn, :] += mm_nt(dh, R("w1")[s])
                return 0

            lax.fori_loop(0, 4, feed, 0)
            sec_ref[rs, :] = g_ref[rs, :].astype(BF16)
            dx, dg = norm_back(r2_ref[rs, :], gain_ref[pl.ds(2, 1), :], acc_ref[dn, :])
            R("dg")[r, pl.ds(2, 1), :] = dg
            g2 = cot_ref[rs, :].astype(F32) + dx
            g_ref[rs, :] = g2
            gb_ref[rs, :] = g2.astype(BF16)
            acc_ref[pl.ds(0, cwin), :] = jnp.zeros((cwin, width), F32)
            ws = pl.ds(pl.multiple_of(r * cwin, HALO), cwin)

            def back(s, _):
                do2 = mm(gb_ref[rs, :], c1_ref[s, :, hw:]).astype(BF16)
                dq, dk, dv = attend_back(
                    cq_ref[s, r], kv_ref[window(s), :hw], kv_ref[window(s), hw:], do2, lambda h: cp_ref[rowsl(2 * s + h), :]
                )
                cq_ref[s, r] = dq.astype(BF16)
                dkv_ref[s, ws, :hw] = dk.astype(BF16)
                dkv_ref[s, ws, hw:] = dv.astype(BF16)
                acc_ref[pl.ds(0, cwin), :] += mm_nt(dkv_ref[s, ws, :], c0_ref[s])
                return 0

            lax.fori_loop(0, 4, back, 0)
            R("dmf")[in_row(r, cwindow), :] = acc_ref[pl.ds(0, cwin), :].astype(BF16)
            dm_c(r).start()
            pl.when(inner)(dm_t(r).start)
            acc_ref[dn, :] = jnp.zeros((own, width), F32)

            def to_normed(s, _):
                acc_ref[dn, :] += mm_nt(cq_ref[s, r], c1_ref[s, :, :hw])
                return 0

            lax.fori_loop(0, 4, to_normed, 0)
            dx, dg = norm_back(r1_ref[rs, :], gain_ref[pl.ds(1, 1), :], acc_ref[dn, :])
            R("dg")[r, pl.ds(1, 1), :] = dg
            dm_c(r).wait_recv()
            acc_ref[dn, :] = R("dmf")[in_row(r, block), :].astype(F32) + R("rcc")[r].astype(F32)

            @pl.when(inner)
            def _():
                dm_t(r).wait_recv()
                place = pl.ds(pl.multiple_of((2 - t) * (own - side), HALO), side)
                acc_ref[place, :] += R("rct")[r].astype(F32)

            R("dmt")[r] = acc_ref[dn, :].astype(BF16)
            dm_x(r).start()
            g_ref[rs, :] += dx
            return 0

        lax.fori_loop(0, rows, row, 0)
        for r in range(rows):
            dm_c(r).wait_send()
            pl.when(inner)(dm_t(r).wait_send)

        def c0_grad(i, _):
            s = far_first(i)
            dst = r_c0.part(s)
            total = mm_tn(R("memf")[0, cwindow, :], dkv_ref[s, pl.ds(0, cwin), :])
            for r in range(1, rows):
                total += mm_tn(R("memf")[r, cwindow, :], dkv_ref[s, pl.ds(r * cwin, cwin), :])
            dst[...] = total.astype(BF16)
            pl.when(i == 0)(lambda: r_c0.core_send(0))
            pl.when(i == 1)(lambda: r_c0.core_send(1))
            return 0

        lax.fori_loop(0, 4, c0_grad, 0)

        def c1_grad(i, _):
            s = far_first(i)
            dst = r_c1.part(s)
            dst[:, :hw] = mm_tn(n2_ref[...], cq_ref[s].reshape(tokens, hw)).astype(BF16)
            dst[:, hw:] = mm_tn(gb_ref[...], oc_ref[:, lanes(s)]).astype(BF16)
            pl.when(i == 0)(lambda: r_c1.core_send(0))
            pl.when(i == 1)(lambda: r_c1.core_send(1))
            return 0

        lax.fori_loop(0, 4, c1_grad, 0)
        r_c0.core_done()

        def w2_grad(i, _):
            s = far_first(i)
            r_w2.part(s)[...] = mm_tn(cot_ref[...], u_ref[s]).astype(BF16)
            pl.when(i == 0)(lambda: r_w2.core_send(0))
            pl.when(i == 1)(lambda: r_w2.core_send(1))
            return 0

        lax.fori_loop(0, 4, w2_grad, 0)
        r_c1.core_done()

        def w1_grad(i, _):
            s = far_first(i)
            r_w1.part(s)[...] = mm_tn(n3_ref[...], gp_ref[s]).astype(BF16)
            pl.when(i == 0)(lambda: r_w1.core_send(0))
            pl.when(i == 1)(lambda: r_w1.core_send(1))
            return 0

        lax.fori_loop(0, 4, w1_grad, 0)

    @pl.when(is_enc)
    def _():
        def row(r, _):
            rs = rowsl(r)
            dm_x(r).wait_recv()
            dx, dg = norm_back(r2_ref[rs, :], gain_ref[pl.ds(2, 1), :], R("dmr")[r].astype(F32))
            R("dg")[r, pl.ds(2, 1), :] = dg
            g_ref[rs, :] = dx
            gb_ref[rs, :] = dx.astype(BF16)
            return 0

        lax.fori_loop(0, rows, row, 0)

        def w2_grad(i, _):
            s = far_first(i)
            r_w2.part(s)[...] = mm_tn(gb_ref[...], u_ref[s]).astype(BF16)
            pl.when(i == 0)(lambda: r_w2.core_send(0))
            pl.when(i == 1)(lambda: r_w2.core_send(1))
            return 0

        lax.fori_loop(0, 4, w2_grad, 0)
        dn = pl.ds(0, tokens)
        acc_ref[dn, :] = jnp.zeros((tokens, width), F32)

        def w1_grad(i, _):
            s = far_first(i)
            dh = (mm_nt(gb_ref[...], R("w2")[s]) * gp_ref[s].astype(F32)).astype(BF16)
            r_w1.part(s)[...] = mm_tn(n2_ref[...], dh).astype(BF16)
            pl.when(i == 0)(lambda: r_w1.core_send(0))
            pl.when(i == 1)(lambda: r_w1.core_send(1))
            acc_ref[dn, :] += mm_nt(dh, R("w1")[s])
            return 0

        lax.fori_loop(0, 4, w1_grad, 0)
        dx, dg = norm_back(r1_ref[...], gain_ref[pl.ds(1, 1), :], acc_ref[dn, :])
        R("dg")[0, pl.ds(1, 1), :] = dg
        for r in range(1, rows):
            R("dg")[r, pl.ds(1, 1), :] = jnp.zeros_like(dg)
        g_ref[...] += dx

    r_w2.core_done()
    gb_ref[...] = g_ref[...].astype(BF16)

    def wo_grad(i, _):
        s = far_first(i)
        r_wo.part(s)[...] = mm_tn(gb_ref[...], o_ref[:, lanes(s)]).astype(BF16)
        pl.when(i == 0)(lambda: r_wo.core_send(0))
        pl.when(i == 1)(lambda: r_wo.core_send(1))
        return 0

    lax.fori_loop(0, 4, wo_grad, 0)
    acc_ref[...] = jnp.zeros_like(acc_ref)
    dqkv_ref = R("dqkv")
    for r in range(rows):
        dqkv_ref[pl.ds(r * win, HALO), :hw] = jnp.zeros((HALO, hw), BF16)
        dqkv_ref[pl.ds(r * win + HALO + own, HALO), :hw] = jnp.zeros((HALO, hw), BF16)

    def self_back(i, _):
        s = far_first(i)
        do = mm_nt(gb_ref[...], R("wo")[s]).astype(BF16)
        R("do")[...] = do

        def one(r, _):
            dq, dk, dv = attend_back(q_ref[s, r], k_ref[s, r], v_ref[s, r], R("do")[rowsl(r), :], lambda h: p_ref[s, r, h])
            base = pl.multiple_of(r * win, HALO)
            dqkv_ref[pl.ds(base + HALO, own), :hw] = dq.astype(BF16)
            dqkv_ref[pl.ds(base, win), hw : 2 * hw] = dk.astype(BF16)
            dqkv_ref[pl.ds(base, win), 2 * hw :] = dv.astype(BF16)
            return 0

        lax.fori_loop(0, rows, one, 0)
        r_wa.part(s)[...] = mm_tn(nw_ref[...], dqkv_ref[...]).astype(BF16)
        acc_ref[...] += mm_nt(dqkv_ref[...], R("wa")[s])

        @pl.when(i == 0)
        def _():
            r_wa.core_send(0)
            r_w1.core_done()

        @pl.when(i == 1)
        def _():
            r_wa.core_send(1)
            r_wo.core_done()
            pl.when(is_dec)(r_c0.y_done)

        @pl.when(i == 2)
        def _():
            pl.when(is_dec)(r_c1.y_done)
            pl.when(is_dec)(lambda: r_c0.z_done(0))

        return 0

    lax.fori_loop(0, 4, self_back, 0)
    for r in range(rows):
        R("dhs")[0, r] = acc_ref[pl.ds(r * win, HALO), :].astype(BF16)
        R("dhs")[1, r] = acc_ref[pl.ds(r * win + HALO + own, HALO), :].astype(BF16)
    pl.when(t < 3)(dn_right.start)
    pl.when(t > 0)(dn_left.start)
    r_wa.core_done()

    @pl.when(t == 0)
    def _():
        R("dhr")[0] = jnp.zeros((rows, HALO, width), BF16)

    @pl.when(t == 3)
    def _():
        R("dhr")[1] = jnp.zeros((rows, HALO, width), BF16)

    pl.when(t > 0)(dn_right.wait_recv)
    pl.when(t < 3)(dn_left.wait_recv)
    for r in range(rows):
        lo, hi = pl.ds(r * win + HALO, HALO), pl.ds(r * win + own, HALO)
        acc_ref[lo, :] += R("dhr")[0, r].astype(F32)
        acc_ref[hi, :] += R("dhr")[1, r].astype(F32)
    total = jnp.zeros((1, width), F32)
    for r in range(rows):
        rs = pl.ds(r * own, own)
        dx, dg = norm_back(x_ref[r].astype(F32), gain0, acc_ref[pl.ds(r * win + HALO, own), :])
        R("gx")[rs, :] = (g_ref[rs, :] + dx).astype(BF16)
        total += dg
    R("dgs")[0] = jnp.zeros((8, width), F32)
    R("dgs")[0, pl.ds(0, 1), :] = total
    R("dgs")[0, pl.ds(1, 2), :] = sum(R("dg")[r, pl.ds(1, 2), :] for r in range(rows))
    gain_links[0].start()

    r_w2.y_done()

    def gain_step(k):
        gain_links[k].wait_recv()
        if k + 1 < len(gain_links):
            R("dgs")[k + 1] = R("dgs")[k] + R("dgr")[k]
            gain_links[k + 1].start()
        else:
            R("dgain")[...] = R("dgs")[k] + R("dgr")[k]

    gain_step(0)

    @pl.when(is_dec)
    def _():
        r_c0.rest_z(1, R("dc0"))
        c0_back.start()
        r_c1.rest_z(0, R("dc"))

    r_w1.y_done()
    gain_step(1)
    r_w2.z_done(0, R("dw2_o"))
    r_wo.y_done()
    gain_step(2)
    r_wa.y_done()
    r_w1.z_done(0, R("dw1_o"))
    for k in range(3, len(gain_links)):
        gain_step(k)
    r_w2.rest_z(1, R("dw2_o"))
    r_wo.z_done(0, R("dwo_o"))
    r_wa.z_done(0, R("da_o"))
    r_w1.rest_z(1, R("dw1_o"))
    r_wo.rest_z(1, R("dwo_o"))
    r_wa.rest_z(1, R("da_o"))

    for g in (g_wa, g_wo, g_w1, g_w2):
        g.finish()
    for g in (r_w2, r_w1, r_wo, r_wa):
        g.finish()
    for c in gain_links:
        c.wait_send()
    pl.when(t < 3)(x_right.wait_send)
    pl.when(t > 0)(x_left.wait_send)
    pl.when(t < 3)(dn_right.wait_send)
    pl.when(t > 0)(dn_left.wait_send)

    @pl.when(is_enc)
    def _():
        c0_x.wait_send()
        for r in range(rows):
            mem_x(r).wait_send()
        c0_back.wait_recv()
        R("dc")[...] = R("dc0r")[...]

    @pl.when(is_dec)
    def _():
        for g in (g_c1, g_c0, r_c0, r_c1):
            g.finish()
        for r in range(rows):
            mem_c(r).wait_send()
            pl.when(inner)(mem_t(r).wait_send)
            dm_x(r).wait_send()
        c0_back.wait_send()


def body(embeds, segments, cotangent, norm_gains, attn_in, attn_out, cross_proj, ffn_in, ffn_out):
    me = lax.axis_index("tensor")
    is_enc = lax.axis_index("pipe") == 0
    dp = lax.axis_size("dp")
    rows, own, width = embeds.shape[1:]
    slots = segments.shape[2]
    hw = attn_in.shape[3]
    fw = ffn_in.shape[2]
    win = own + 2 * HALO
    cwin = 2 * own + 2 * HALO
    tokens = rows * own
    side = 3 * own // 4
    zsteps = (dp - 1).bit_length()

    start = me * own
    seg_self = jnp.where(is_enc, segments[0], segments[1])
    padded = jnp.pad(seg_self, ((0, 0), (HALO, HALO)), constant_values=-2)
    cstart = jnp.minimum(me * (own - HALO), slots - cwin)
    sq = lax.dynamic_slice(seg_self, (0, start), (rows, own))[:, :, None]
    sk = lax.dynamic_slice(padded, (0, start), (rows, win))[:, None, :]
    csq = lax.dynamic_slice(segments[1], (0, start), (rows, own))[:, :, None]
    csk = lax.dynamic_slice(segments[0], (0, cstart), (rows, cwin))[:, None, :]

    ins = dict(
        x=embeds[0], sq=sq, sk=sk, csq=csq, csk=csk, gains=norm_gains[0], cot=cotangent.reshape(tokens, width),
        wa_h=attn_in[0].reshape(width, 3 * hw), wo_h=attn_out[0], w1_h=ffn_in[0], w2_h=ffn_out[0],
        cx_h=cross_proj[0].reshape(width, 2 * hw),
    )
    outs = dict(
        sec=((tokens, width), BF16), gx=((tokens, width), BF16), dgain=((8, width), F32),
        da_o=((width // dp, 3 * hw), F32), dwo_o=((width // dp, hw), F32), dc=((width // dp, 2 * hw), F32),
        dw1_o=((width // dp, fw), F32), dw2_o=((width // dp, fw), F32),
    )
    vm = dict(
        wa=((4, width, 3 * hw), BF16), wo=((4, hw, width), BF16), w1=((4, width, fw), BF16), w2=((4, fw, width), BF16),
        c0=((4, width, 2 * hw), BF16), c1=((4, width, 2 * hw), BF16),
        xh=((2, rows, HALO, width), BF16), nw=((rows * win, width), BF16),
        q=((4, rows, own, hw), BF16), k=((4, rows, win, hw), BF16), v=((4, rows, win, hw), BF16),
        p=((4, rows, 2, own, win), BF16), o=((tokens, width), BF16), bias=((rows, own, win), F32),
        r1=((tokens, width), F32), r2=((tokens, width), F32), n2=((tokens, width), BF16), n3=((tokens, width), BF16),
        u=((4, tokens, fw), BF16), gp=((4, tokens, fw), BF16),
        acc=((rows * win, width), F32), g=((tokens, width), F32), gb=((tokens, width), BF16),
        memf=((rows, slots, width), BF16), kv=((4 * slots, 2 * hw), BF16), cq=((4, rows, own, hw), BF16),
        cp=((8 * own, cwin), BF16), cbias=((own, cwin), F32), oc=((tokens, width), BF16),
        dkv=((4, rows * cwin, 2 * hw), BF16), dmf=((max(rows * slots, 4 * width), max(width, fw)), BF16),
        rcc=((rows, own, width), BF16), rct=((rows, side, width), BF16), dmt=((rows, own, width), BF16),
        dmr=((rows, own, width), BF16), dg=((rows, 8, width), F32), do=((tokens, hw), BF16),
        dqkv=((rows * win, 3 * hw), BF16), dhs=((2, rows, HALO, width), BF16), dhr=((2, rows, HALO, width), BF16),
        dgs=((2 + zsteps, 8, width), F32), dgr=((2 + zsteps, 8, width), F32),
        dw2=((4 * width, fw), BF16), dwo=((4 * width, hw), BF16),
        dc0=((width // dp, 2 * hw), F32), dc0r=((width // dp, 2 * hw), F32),
    )
    grads = dict(
        w2=fw, w1=fw, wo=hw, wa=3 * hw, c0=2 * hw, c1=2 * hw
    )
    for name, m in grads.items():
        vm["rc_" + name] = ((2, width, m), BF16)
        vm["ry_" + name] = ((width, m), BF16)
        vm["zb_" + name] = ((dp, width // dp, m), BF16)
        for k in range(zsteps):
            vm[f"zr{k}_{name}"] = ((dp >> (k + 1), width // dp, m), BF16)
    copies = 140 + 8 * zsteps
    sems = dict(send=pltpu.SemaphoreType.DMA((copies,)), recv=pltpu.SemaphoreType.DMA((copies,)), local=pltpu.SemaphoreType.DMA((8,)))
    in_hbm = {"wa_h", "wo_h", "w1_h", "w2_h", "cx_h"}
    results = pl.pallas_call(
        functools.partial(layers, list(ins) + list(outs) + list(vm) + list(sems)),
        name="layers",
        out_shape=[jax.ShapeDtypeStruct(*o) for o in outs.values()],
        in_specs=[pl.BlockSpec(memory_space=pl.ANY if n in in_hbm else pltpu.VMEM) for n in ins],
        out_specs=[pl.BlockSpec(memory_space=pltpu.VMEM)] * len(outs),
        scratch_shapes=[pltpu.VMEM(*s) for s in vm.values()] + list(sems.values()),
        compiler_params=pltpu.CompilerParams(vmem_limit_bytes=VMEM_LIMIT, collective_id=0, has_side_effects=True),
    )(*ins.values())
    sec, gx, dgain, da, dwo, dc, dw1, dw2 = results
    share = width // dp
    dgain = lax.dynamic_slice(dgain, (0, lax.axis_index("dp") * share), (3, share))
    return (
        sec.reshape(1, rows, own, width), gx.reshape(1, rows, own, width), dgain[None], da.reshape(1, -1, 3, hw),
        dwo.T[None], dc.reshape(1, -1, 2, hw), dw1[None], dw2.T[None],
    )


def solution(mesh):
    return jax.shard_map(
        body,
        mesh=mesh,
        in_specs=(
            P("pipe", "dp", "tensor", None),
            P(None, "dp", None),
            P("dp", "tensor", None),
            P("pipe", None, None),
            P("pipe", None, None, "tensor"),
            P("pipe", "tensor", None),
            P("pipe", None, None, "tensor"),
            P("pipe", None, "tensor"),
            P("pipe", "tensor", None),
        ),
        out_specs=(
            P("pipe", "dp", "tensor", None),
            P("pipe", "dp", "tensor", None),
            P("pipe", None, "dp"),
            P("pipe", "dp", None, "tensor"),
            P("pipe", "tensor", "dp"),
            P("pipe", "dp", None, "tensor"),
            P("pipe", "dp", "tensor"),
            P("pipe", "tensor", "dp"),
        ),
        check_vma=False,
    )
```

```python
import functools

import jax
import jax.numpy as jnp
from jax import lax
from jax.experimental import pallas as pl
from jax.experimental.pallas import tpu as pltpu
from jax.sharding import PartitionSpec as P

EPS = 1e-05
MASKED = -1000000000.0
DH = 64
HALO = 64
F32 = jnp.float32
BF16 = jnp.bfloat16
GELU_C = 0.7978845608028654
GELU_A = 0.044715
MESH = pl.DeviceIdType.MESH
VMEM_LIMIT = 63 << 20


def mm(a, b):
    return lax.dot_general(a, b, (((1,), (0,)), ((), ())), preferred_element_type=F32)


def mm_nt(a, b):
    return lax.dot_general(a, b, (((1,), (1,)), ((), ())), preferred_element_type=F32)


def mm_tn(a, b):
    return lax.dot_general(a, b, (((0,), (0,)), ((), ())), preferred_element_type=F32)


def norm_parts(v):
    c = v - jnp.mean(v, axis=-1, keepdims=True)
    r = lax.rsqrt(jnp.mean(c * c, axis=-1, keepdims=True) + EPS)
    return c * r, r


def norm(v, gain):
    xhat, _ = norm_parts(v)
    return xhat * gain


def norm_back(v, gain, dn):
    xhat, r = norm_parts(v)
    dxh = dn * gain
    m1 = jnp.mean(dxh, axis=-1, keepdims=True)
    m2 = jnp.mean(dxh * xhat, axis=-1, keepdims=True)
    return r * (dxh - m1 - xhat * m2), jnp.sum(dn * xhat, axis=0, keepdims=True)


def lane_low(shape):
    return lax.broadcasted_iota(jnp.int32, shape, 1) < DH


def pair_join(a, b):
    return jnp.where(lane_low(a.shape), a, b)


def swap_halves(v):
    return pltpu.roll(v, DH, 1)


def attend(q2, k2, v2, mask, keep):
    low, lowq = lane_low(v2.shape), lane_low(q2.shape)
    one, zero = jnp.ones_like(v2), jnp.zeros_like(q2)
    outs = []
    for h in range(2):
        qh = jnp.where(lowq, q2, zero) if h == 0 else jnp.where(lowq, zero, q2)
        s = mask(mm_nt(qh, k2))
        e = jnp.exp(s - jnp.max(s, axis=-1, keepdims=True)).astype(BF16)
        keep(h, e)
        outs.append(mm(e, jnp.where(low, v2, one) if h == 0 else jnp.where(low, one, v2)))
    inv = 1.0 / swap_halves(pair_join(outs[1], outs[0]))
    return pair_join(*outs) * inv, inv


def attend_back(q2, k2, v2, do2, o2, inv, kept):
    low, lowq = lane_low(v2.shape), lane_low(q2.shape)
    one = jnp.ones_like(v2)
    scaled = do2.astype(F32) * inv.astype(F32)
    dob = scaled.astype(BF16)
    minus = (-swap_halves(dob.astype(F32) * o2.astype(F32))).astype(BF16)
    q_t, do_t = q2.T, dob.T
    dq, dk, dv = [], [], []
    for h in range(2):
        e = kept(h)
        rows = slice(h * DH, (h + 1) * DH)
        lhs = jnp.where(lowq, dob, minus) if h == 0 else jnp.where(lowq, minus, dob)
        dp = mm_nt(lhs, jnp.where(low, v2, one) if h == 0 else jnp.where(low, one, v2))
        ds = (dp * e.astype(F32)).astype(BF16)
        dq.append(mm(ds, k2))
        dv.append(mm(do_t[rows], e).astype(BF16))
        dk.append(mm(q_t[rows], ds).astype(BF16))
    return (pair_join(*dq) * (DH**-0.5)).astype(BF16), jnp.concatenate(dk, 0).T, jnp.concatenate(dv, 0).T


def gelu_parts(h):
    h2 = h * h
    half = 0.5 + 0.5 * jnp.tanh(h * (GELU_C + (GELU_C * GELU_A) * h2))
    u = h * half
    slope = half + u * ((1.0 - half) * (2.0 * GELU_C + (6.0 * GELU_C * GELU_A) * h2))
    return u, slope


def flip(i, bit):
    return i + bit - 2 * bit * lax.rem(lax.div(i, bit), 2)


def bit_of(i, bit):
    return lax.rem(lax.div(i, bit), 2)


def reversed_bits(i, count):
    out, bit = 0, 1
    while bit < count:
        out = 2 * out + (i // bit) % 2
        bit *= 2
    return out


class Links:
    def __init__(self, send, recv, local):
        self.send, self.recv, self.local = send, recv, local
        self.n = self.m = 0
        self.sent = []

    def take(self, count=1):
        self.n += count
        return self.n - count

    def remote(self, src, dst, device, at=None):
        at = self.take() if at is None else at
        return pltpu.make_async_remote_copy(
            src_ref=src, dst_ref=dst, send_sem=self.send.at[at], recv_sem=self.recv.at[at],
            device_id=device, device_id_type=MESH,
        )

    def here(self, src, dst):
        self.m += 1
        return pltpu.make_async_copy(src, dst, self.local.at[self.m - 1])


class Gather:
    def __init__(self, links, src, slot, at, planes=None):
        t, t2 = at["t"], at["t2"]
        depth = slot(t, None).shape[0]
        half = depth // 2
        whole = pl.ds(0, depth)
        mine = pl.ds(pl.multiple_of(at["b"] * half, half), half)
        other = pl.ds(pl.multiple_of((1 - at["b"]) * half, half), half)
        if src is None:
            self.own = []
        elif planes is None:
            self.own = [links.here(src, slot(t, whole))]
        else:
            self.own = [links.here(src.at[i], slot(t, whole, i)) for i in range(planes)]
        self.inner = src is None or planes is not None
        src = slot(t, whole) if self.inner else src
        self.core = links.remote(src, slot(t, whole), at["C"])
        self.over_y = links.remote(src.at[mine], slot(t, mine), at["Y"])
        self.over_z = links.remote(slot(t2, mine), slot(t2, mine), at["Z"][0])
        self.core_a = links.remote(slot(t2, mine), slot(t2, mine), at["C"])
        self.core_b = links.remote(slot(t2, other), slot(t2, other), at["C"])

    def start(self):
        for c in self.own:
            c.start()
        if self.inner:
            for c in self.own:
                c.wait()
        self.over_y.start()
        self.core.start()

    def step1(self):
        self.over_y.wait_recv()
        self.over_z.start()
        self.core_a.start()

    def step2(self):
        self.over_z.wait_recv()
        self.core_b.start()

    def ready(self, i):
        if i == 0 and not self.inner:
            for c in self.own:
                c.wait()
        if i == 1:
            self.core.wait_recv()
        if i == 3:
            self.core_a.wait_recv()
            self.core_b.wait_recv()

    def finish(self):
        for c in (self.core, self.over_y, self.over_z, self.core_a, self.core_b):
            c.wait_send()


class Reduce:
    def __init__(self, links, part, rc, ry, zb, zr, at):
        self.part, self.at = part, at
        self.rc, self.ry, self.zb, self.zr = rc, ry, zb, zr
        self.dp = zb.shape[0]
        self.core = [links.remote(part(at[f]), rc.at[j], at["C"]) for j, f in enumerate(("t1", "t3"))]
        self.over_y = links.remote(part(at["t2"]), ry, at["Y"])
        self.over_z = []
        off, m, bit, k = 0, self.dp, 1, 0
        self.kept = []
        while m > 1:
            m //= 2
            b = bit_of(at["d"], bit)
            keep, give = off + b * m, off + (1 - b) * m
            self.over_z.append(links.remote(zb.at[pl.ds(give, m)], zr[k], at["Z"][k]))
            self.kept.append((keep, m))
            off, bit, k = keep, 2 * bit, k + 1

    def core_send(self, j):
        self.core[j].start()

    def core_done(self):
        self.core[0].wait_recv()
        self.core[1].wait_recv()
        far, near = self.part(self.at["t2"]), self.part(self.at["t"])
        far[...] = (far[...].astype(F32) + self.rc[1].astype(F32)).astype(BF16)
        self.over_y.start()
        near[...] = (near[...].astype(F32) + self.rc[0].astype(F32)).astype(BF16)

    def y_done(self):
        self.over_y.wait_recv()
        near = self.part(self.at["t"])
        rows = self.zb.shape[1]
        for i in range(self.dp):
            where = pl.ds(i * rows, rows)
            total = near[where].astype(F32) + self.ry[where].astype(F32)
            self.zb[reversed_bits(i, self.dp)] = total.astype(BF16)
        self.over_z[0].start()

    def z_done(self, k, out=None):
        self.over_z[k].wait_recv()
        keep, m = self.kept[k]
        if k == len(self.over_z) - 1:
            out[...] = self.zb[keep].astype(F32) + self.zr[k][0].astype(F32)
        else:
            live = self.zb.at[pl.ds(keep, m)]
            live[...] = (live[...].astype(F32) + self.zr[k][...].astype(F32)).astype(BF16)
            self.over_z[k + 1].start()

    def rest_z(self, k, out):
        for j in range(k, len(self.over_z)):
            self.z_done(j, out)

    def finish(self):
        for c in self.core + [self.over_y] + self.over_z:
            c.wait_send()


class ReduceZ:
    def __init__(self, links, part, rc, ry, zb, zr, at):
        self.part, self.at = part, at
        self.rc, self.ry, self.zb, self.zr = rc, ry, zb, zr
        self.dp = zb.shape[1]
        self.core = [links.remote(part(at[f]), rc.at[j], at["C"]) for j, f in enumerate(("t1", "t3"))]
        self.over_z, self.kept = [], []
        off, m, bit, k = 0, self.dp, 1, 0
        while m > 1:
            m //= 2
            b = bit_of(at["d"], bit)
            keep, give = off + b * m, off + (1 - b) * m
            self.over_z.append(links.remote(zb.at[:, pl.ds(give, m)], zr[k], at["Z"][k]))
            self.kept.append((keep, m))
            off, bit, k = keep, 2 * bit, k + 1
        self.off = off
        self.over_y = links.remote(zb.at[0, off], ry, at["Y"])

    def core_send(self, j):
        self.core[j].start()

    def core_done(self):
        self.core[0].wait_recv()
        self.core[1].wait_recv()
        rows = self.zb.shape[2]
        for j, f in enumerate(("t2", "t")):
            part = self.part(self.at[f])
            for i in range(self.dp):
                where = pl.ds(i * rows, rows)
                total = part[where, :].astype(F32) + self.rc[1 - j, where, :].astype(F32)
                self.zb[j, reversed_bits(i, self.dp)] = total.astype(BF16)
        self.over_z[0].start()

    def z_done(self, k):
        self.over_z[k].wait_recv()
        keep, m = self.kept[k]
        for j in range(2):
            live = self.zb.at[j, pl.ds(keep, m)]
            live[...] = (live[...].astype(F32) + self.zr[k][j].astype(F32)).astype(BF16)
        (self.over_z[k + 1] if k + 1 < len(self.over_z) else self.over_y).start()

    def y_done(self, out):
        self.over_y.wait_recv()
        out[...] = self.zb[1, self.off].astype(F32) + self.ry[...].astype(F32)

    def finish(self):
        for c in self.core + [self.over_y] + self.over_z:
            c.wait_send()


def layers(names, *refs):
    ref = dict(zip(names, refs))
    R = lambda name: ref[name]
    p, d, t = lax.axis_index("pipe"), lax.axis_index("dp"), lax.axis_index("tensor")
    is_enc, is_dec = p == 0, p == 1
    dp = lax.axis_size("dp")
    t1, t2, t3 = flip(t, 1), flip(t, 2), 3 - t
    zbits = []
    while 2 ** len(zbits) < dp:
        zbits.append((p, flip(d, 2 ** len(zbits)), t))
    at = dict(t=t, t1=t1, t2=t2, t3=t3, d=d, b=bit_of(d, 1), C=(p, d, t1), Y=(p, d, t2), T=(p, d, t3), X=(1 - p, d, t), Z=zbits)
    rows, own, width = R("x").shape
    win, cwin = own + 2 * HALO, 2 * own + 2 * HALO
    slots = 4 * own
    tokens = rows * own
    hw = R("wa").shape[2] // 3
    fw = R("w1").shape[2]
    inner = t % 3 != 0
    scale = jnp.asarray(DH**-0.5, BF16)
    gain_ref, x_ref = R("gains"), R("x")
    side = 3 * own // 4
    copies_out = []

    def rowsl(r, n=own):
        return pl.ds(pl.multiple_of(r * n, n), n)

    def lanes(s, n=hw):
        return pl.ds(pl.multiple_of(s * n, n), n)

    def far_lanes(s):
        return pl.ds(pl.multiple_of(s * 2 * hw + hw, hw), hw)

    def in_row(r, span):
        return pl.ds(pl.multiple_of(r * slots + span.start, HALO), span.size)

    def near_first(i):
        return 2 * lax.rem(lax.div(t, 2) + lax.div(i, 2), 2) + lax.rem(lax.rem(t, 2) + lax.rem(i, 2), 2)

    def far_first(i):
        return 2 * lax.rem(lax.div(t, 2) + lax.rem(lax.div(i + 1, 2), 2), 2) + lax.rem(lax.rem(t, 2) + 1 - lax.div(i, 2), 2)

    def seg_row(side_, r, start):
        row = jnp.broadcast_to(R("segs")[side_, pl.ds(r, 1), :].astype(F32), (8, slots))
        return pltpu.roll(row, lax.rem(2 * slots - start, slots), 1)

    def seg_column(side_, r):
        row = seg_row(side_, r, t * own)[:1, :own]
        return jnp.broadcast_to(row, (128, own)).T

    def spread(column, n):
        return jnp.concatenate([column] * (n // 128), axis=1)

    links = Links(R("send"), R("recv"), R("local"))

    def by_shard(name, n=None):
        def slot(s, span, i=None):
            full = R(name).at[s] if span is None else R(name).at[s, span]
            return full if i is None else full.at[:, pl.ds(i * n, n)]

        return slot

    def by_columns(name, n):
        def slot(s, span):
            return R(name).at[:, lanes(s, n)] if span is None else R(name).at[span, lanes(s, n)]

        return slot

    g_wa = Gather(links, R("wa_h"), by_shard("wa", hw), at, 3)
    g_wo = Gather(links, R("wo_h"), by_shard("wo"), at)
    g_w1 = Gather(links, R("w1_h"), by_shard("w1"), at)
    g_w2 = Gather(links, R("w2_h"), by_shard("w2"), at)
    g_cq = Gather(links, R("cx_h").at[:, pl.ds(0, hw)], by_columns("cqw", hw), at)
    g_co = Gather(links, R("cx_h").at[:, pl.ds(hw, hw)], by_columns("cow", hw), at)
    c0_x = links.remote(R("cx_h"), R("c0").at[:, lanes(t, 2 * hw)], at["X"])
    g_c0 = Gather(links, None, by_columns("c0", 2 * hw), at)
    x_right = links.remote(x_ref.at[:, pl.ds(own - HALO, HALO)], R("xh").at[0], (p, d, lax.rem(t + 1, 4)))
    x_left = links.remote(x_ref.at[:, pl.ds(0, HALO)], R("xh").at[1], (p, d, lax.rem(t + 3, 4)))
    base_mem, base_memc, base_memt = links.take(rows), links.take(rows), links.take(rows)
    base_dmc, base_dmt, base_dmx = links.take(rows), links.take(rows), links.take(rows)
    block = pl.ds(pl.multiple_of(t * own, own), own)
    block1 = pl.ds(pl.multiple_of(t1 * own, own), own)
    edge_out = pl.ds(pl.multiple_of(lax.rem(own // 2 + side * t, slots), HALO), side)
    edge_in = pl.ds(pl.multiple_of(lax.rem(own // 2 + side * t3, slots), HALO), side)

    def mem_x(r):
        return links.remote(R("secs").at[rowsl(r)], R("memf").at[in_row(r, block)], at["X"], base_mem + r)

    def mem_c(r):
        return links.remote(R("memf").at[in_row(r, block)], R("memf").at[in_row(r, block)], at["C"], base_memc + r)

    def mem_t(r):
        return links.remote(R("memf").at[in_row(r, edge_out)], R("memf").at[in_row(r, edge_out)], at["T"], base_memt + r)

    def dm_rows(r, span):
        return R("dmf").at[in_row(r, span)]

    def dm_c(r):
        return links.remote(dm_rows(r, block1), R("rcc").at[r], at["C"], base_dmc + r)

    def dm_t(r):
        return links.remote(dm_rows(r, edge_in), R("rct").at[r], at["T"], base_dmt + r)

    def dm_x(r):
        return links.remote(R("dm").at[r], R("dm").at[r], at["X"], base_dmx + r)

    def by_rows(name, m):
        return lambda s: R(name).at[pl.ds(pl.multiple_of(s * width, width), width), pl.ds(0, m)]

    def by_lanes(name, m, row=0):
        return lambda s: R(name).at[pl.ds(row, width), lanes(s, m)]

    def reduce_of(name, part, kind=Reduce):
        zr = [R(f"zr{k}_{name}") for k in range(len(zbits))]
        return kind(links, part, R("rc_" + name), R("ry_" + name), R("zb_" + name), zr, at)

    r_w2 = reduce_of("w2", by_rows("memf", fw))
    r_w1 = reduce_of("w1", by_rows("dmf", fw), ReduceZ)
    r_wo = reduce_of("wo", by_lanes("dwo", hw))
    r_wa = reduce_of("wa", by_rows("cp", 3 * hw))
    r_c0 = reduce_of("c0", by_lanes("kv", 2 * hw))
    r_c1 = reduce_of("c1", by_lanes("kv", 2 * hw, width))
    c0_back = links.remote(R("dc0"), R("dc0r"), at["X"])
    dn_right = links.remote(R("dhs").at[1], R("dhr").at[0], (p, d, lax.rem(t + 1, 4)))
    dn_left = links.remote(R("dhs").at[0], R("dhr").at[1], (p, d, lax.rem(t + 3, 4)))
    gain_links = [links.remote(R("dgs").at[k], R("dgr").at[k], dev) for k, dev in enumerate([at["C"], at["Y"]] + zbits)]

    @pl.when(is_dec)
    def _():
        for at_t, start in ((0, 2 * own), (1, 2 * own + side), (3, 2 * own - 2 * HALO)):
            @pl.when(t == at_t)
            def _():
                for r in range(rows):
                    R("memf")[pl.ds(r * slots + start, 2 * HALO), :] = jnp.zeros((2 * HALO, width), BF16)

    barrier = pltpu.get_barrier_semaphore()
    partners = [at["C"], at["Y"], at["T"], at["X"]] + zbits
    for dev in partners:
        pl.semaphore_signal(barrier, inc=1, device_id=dev, device_id_type=MESH)
    pl.semaphore_wait(barrier, len(partners))

    pl.when(t < 3)(x_right.start)
    pl.when(t > 0)(x_left.start)
    g_wa.start()
    g_wo.start()

    @pl.when(is_enc)
    def _():
        g_w1.start()
        g_w2.start()
        c0_x.start()

    @pl.when(is_dec)
    def _():
        g_cq.start()
        g_co.start()
        g_w2.start()
        g_w1.start()

    nw_ref, bias_ref = R("nw"), R("bias")
    gain0, gain1, gain2 = gain_ref[0], gain_ref[1], gain_ref[2]
    for r in range(rows):
        nw_ref[pl.ds(r * win + HALO, own), :] = norm(x_ref[r].astype(F32), gain0).astype(BF16)
        keys = seg_row(p, r, lax.rem(t * own + slots - HALO, slots))[:1, :win]
        same = spread(seg_column(p, r), win) == keys
        qpos = lax.broadcasted_iota(jnp.int32, (own, win), 0)
        kpos = lax.broadcasted_iota(jnp.int32, (own, win), 1) - HALO
        before = kpos - qpos <= jnp.where(is_enc, 4 * win, 0)
        bias_ref[r] = jnp.where(same & before, 0.0, MASKED)

    @pl.when(t == 0)
    def _():
        R("xh")[0] = jnp.zeros((rows, HALO, width), BF16)

    @pl.when(t == 3)
    def _():
        R("xh")[1] = jnp.zeros((rows, HALO, width), BF16)

    pl.when(t > 0)(x_right.wait_recv)
    pl.when(t < 3)(x_left.wait_recv)
    for r in range(rows):
        nw_ref[pl.ds(r * win, HALO), :] = norm(R("xh")[0, r].astype(F32), gain0).astype(BF16)
        nw_ref[pl.ds(r * win + HALO + own, HALO), :] = norm(R("xh")[1, r].astype(F32), gain0).astype(BF16)

    def after_pair(i):
        @pl.when(i == 1)
        def _():
            g_wa.step1()
            g_wo.step1()

            @pl.when(is_dec)
            def _():
                c0_x.wait_recv()
                g_c0.start()

            g_wa.step2()

        @pl.when(i == 2)
        def _():
            pl.when(is_enc)(g_w1.step1)

            @pl.when(is_dec)
            def _():
                g_cq.step1()
                g_co.step1()

            g_wo.step2()

        @pl.when(i == 3)
        def _():
            pl.when(is_enc)(g_w2.step1)
            pl.when(is_dec)(g_w2.step1)

    def wait_ready(i, *weights):
        for k in range(4):
            @pl.when(i == k)
            def _():
                for w in weights:
                    w.ready(k)

    q_ref, k_ref, v_ref, p_ref, o_ref, inv_ref = R("q"), R("k"), R("v"), R("p"), R("o"), R("inv")

    def self_pair(i, _):
        s = near_first(i)
        wait_ready(i, g_wa)
        packed = mm(nw_ref[...], R("wa")[s])
        for r in range(rows):
            q_ref[s, r] = packed[r * win + HALO : r * win + HALO + own, :hw].astype(BF16) * scale
            k_ref[s, r] = packed[r * win : (r + 1) * win, hw : 2 * hw].astype(BF16)
            v_ref[s, r] = packed[r * win : (r + 1) * win, 2 * hw :].astype(BF16)
        for r in range(rows):
            def keep(h, e):
                p_ref[s, r, h] = e

            o2, inv = attend(q_ref[s, r], k_ref[s, r], v_ref[s, r], lambda scores: scores + bias_ref[r], keep)
            o_ref[pl.ds(r * own, own), lanes(s)] = o2.astype(BF16)
            inv_ref[pl.ds(r * own, own), lanes(s)] = inv.astype(BF16)
        after_pair(i)
        return 0

    lax.fori_loop(0, 4, self_pair, 0)
    for k in range(4):
        g_wo.ready(k)
    r1_ref, r2_ref, n2_ref, n3_ref = R("r1"), R("r2"), R("n2"), R("n3")
    u_ref, gp_ref, sec_ref = R("u"), R("gp"), R("secs")
    acc_ref, g_ref, gb_ref, do_ref = R("acc"), R("g"), R("gb"), R("do")
    first = mm(o_ref[...], R("wo")[...].reshape(4 * hw, width))
    for r in range(rows):
        r1_ref[pl.ds(r * own, own), :] = x_ref[r].astype(F32) + first[r * own : (r + 1) * own]
    n2_ref[...] = norm(r1_ref[...], gain1).astype(BF16)

    @pl.when(is_enc)
    def _():
        r2_ref[...] = r1_ref[...]

        def feed(i, rs):
            s = near_first(i)
            u, gp = gelu_parts(mm(n2_ref[rs, :], R("w1")[s]))
            u = u.astype(BF16)
            u_ref[s, rs, :] = u
            gp_ref[s, rs, :] = gp.astype(BF16)
            r2_ref[rs, :] += mm(u, R("w2")[s])

        def near(i, _):
            wait_ready(i, g_w1, g_w2)
            feed(i, pl.ds(0, tokens))
            pl.when(i == 0)(g_w1.step2)
            pl.when(i == 1)(g_w2.step2)
            return 0

        lax.fori_loop(0, 2, near, 0)

        def row(r, _):
            rs = rowsl(r)

            def far(i, _):
                pl.when(r == 0)(lambda: wait_ready(i, g_w1, g_w2))
                feed(i, rs)
                return 0

            lax.fori_loop(2, 4, far, 0)
            sec_ref[rs, :] = norm(r2_ref[rs, :], gain2).astype(BF16)
            mem_x(r).start()
            return 0

        lax.fori_loop(0, rows, row, 0)

    cstart = pl.multiple_of(jnp.minimum(t * (own - HALO), slots - cwin), HALO)
    cwindow = pl.ds(cstart, cwin)
    kv_ref, cq_ref, cp_ref, dkv_ref, cinv_ref = R("kv"), R("cq"), R("cp"), R("dkv"), R("cinv")
    c0_ref, cqw_ref, cow_ref, oc_ref, cot_ref = R("c0"), R("cqw"), R("cow"), R("oc"), R("cot")
    cols, keys_ref = R("cols"), R("keys")
    half = 4 * hw

    @pl.when(is_dec)
    def _():
        g_cq.step2()
        g_co.step2()
        g_c0.step1()
        g_w1.step1()
        kv_ref[...] = jnp.zeros_like(kv_ref)
        R("dmf")[...] = jnp.zeros_like(R("dmf"))
        for r in range(rows):
            cols[r] = seg_column(1, r)
            keys_ref[r] = seg_row(0, r, cstart)[:, :cwin]
        g_w2.step2()
        for k in range(4):
            g_cq.ready(k)
        cq_ref[...] = mm(n2_ref[...], cqw_ref[...]).astype(BF16) * scale
        g_c0.step2()
        g_w1.step2()
        for k in range(4):
            g_w2.ready(k)

        def early(s, _):
            gp_ref[s] = mm_nt(cot_ref[...], R("w2")[s]).astype(BF16)
            return 0

        lax.fori_loop(0, 4, early, 0)
        for k in range(4):
            g_w1.ready(k)
            g_co.ready(k)
            g_c0.ready(k)

        def row(r, _):
            rs = rowsl(r)

            def project(span):
                for j in range(2):
                    kv = mm(R("memf")[in_row(r, span), :], c0_ref[:, j * half : (j + 1) * half])
                    kv_ref[span, j * half : (j + 1) * half] = kv.astype(BF16)

            mem_x(r).wait_recv()
            mem_c(r).start()
            pl.when(inner)(mem_t(r).start)
            project(block)
            mem_c(r).wait_recv()
            project(block1)

            @pl.when(inner)
            def _():
                mem_t(r).wait_recv()
                project(edge_in)

            def cross(i, _):
                for s in (2 * i, 2 * i + 1):
                    def keep(h, e):
                        cp_ref[rowsl(2 * s + h), :] = e

                    def mask(scores):
                        same = spread(cols[r], cwin) == keys_ref[r, pl.ds(0, 1), :]
                        return jnp.where(same, scores, MASKED)

                    o2, inv = attend(cq_ref[rs, lanes(s)], kv_ref[cwindow, lanes(2 * s)], kv_ref[cwindow, lanes(2 * s + 1)], mask, keep)
                    oc_ref[rs, lanes(s)] = o2.astype(BF16)
                    cinv_ref[:, lanes(s)] = inv.astype(BF16)
                return 0

            lax.fori_loop(0, 2, cross, 0)
            r2_ref[rs, :] = r1_ref[rs, :] + mm_nt(oc_ref[rs, :], cow_ref[...])
            n3_ref[rs, :] = norm(r2_ref[rs, :], gain2).astype(BF16)
            dn = pl.ds(0, own)
            acc_ref[dn, :] = jnp.zeros((own, width), F32)
            g_ref[rs, :] = r2_ref[rs, :]

            def feed(s, _):
                u, gp = gelu_parts(mm(n3_ref[rs, :], R("w1")[s]))
                u = u.astype(BF16)
                u_ref[s, rs, :] = u
                g_ref[rs, :] += mm(u, R("w2")[s])
                dh = (gp_ref[s, rs, :].astype(F32) * gp).astype(BF16)
                gp_ref[s, rs, :] = dh
                acc_ref[dn, :] += mm_nt(dh, R("w1")[s])
                return 0

            lax.fori_loop(0, 4, feed, 0)
            sec_ref[rs, :] = g_ref[rs, :].astype(BF16)
            dx, dg = norm_back(r2_ref[rs, :], gain2, acc_ref[dn, :])
            R("dg")[r, pl.ds(2, 1), :] = dg
            g2 = cot_ref[rs, :].astype(F32) + dx
            g_ref[rs, :] = g2
            gb_ref[rs, :] = g2.astype(BF16)
            do_ref[rs, :] = mm(gb_ref[rs, :], cow_ref[...]).astype(BF16)
            ws = pl.ds(pl.multiple_of(r * cwin, HALO), cwin)

            def back(i, _):
                for s in (2 * i, 2 * i + 1):
                    dq, dk, dv = attend_back(
                        cq_ref[rs, lanes(s)], kv_ref[cwindow, lanes(2 * s)], kv_ref[cwindow, lanes(2 * s + 1)],
                        do_ref[rs, lanes(s)], oc_ref[rs, lanes(s)], cinv_ref[:, lanes(s)], lambda h: cp_ref[rowsl(2 * s + h), :],
                    )
                    cq_ref[rs, lanes(s)] = dq
                    dkv_ref[ws, lanes(2 * s)] = dk
                    dkv_ref[ws, lanes(2 * s + 1)] = dv
                return 0

            lax.fori_loop(0, 2, back, 0)
            R("dmf")[in_row(r, cwindow), :] = mm_nt(dkv_ref[ws, :], c0_ref[...]).astype(BF16)
            dm_c(r).start()
            pl.when(inner)(dm_t(r).start)
            dx, dg = norm_back(r1_ref[rs, :], gain1, mm_nt(cq_ref[rs, :], cqw_ref[...]))
            R("dg")[r, pl.ds(1, 1), :] = dg
            g_ref[rs, :] += dx
            dm_c(r).wait_recv()
            acc_ref[dn, :] = R("dmf")[in_row(r, block), :].astype(F32) + R("rcc")[r].astype(F32)

            @pl.when(inner)
            def _():
                dm_t(r).wait_recv()
                place = pl.ds(pl.multiple_of((2 - t) * (own - side), HALO), side)
                acc_ref[place, :] += R("rct")[r].astype(F32)

            R("dm")[r] = acc_ref[dn, :].astype(BF16)
            dm_x(r).start()
            return 0

        lax.fori_loop(0, rows, row, 0)
        for r in range(rows):
            dm_c(r).wait_send()
            pl.when(inner)(dm_t(r).wait_send)

        def sends(reduction, i):
            pl.when(i == 0)(lambda: reduction.core_send(0))
            pl.when(i == 1)(lambda: reduction.core_send(1))

        def c0_grad(i, _):
            s = far_first(i)
            total = mm_tn(R("memf")[in_row(0, cwindow), :], dkv_ref[pl.ds(0, cwin), lanes(s, 2 * hw)])
            for r in range(1, rows):
                total += mm_tn(R("memf")[in_row(r, cwindow), :], dkv_ref[pl.ds(r * cwin, cwin), lanes(s, 2 * hw)])
            r_c0.part(s)[...] = total.astype(BF16)
            sends(r_c0, i)
            return 0

        lax.fori_loop(0, 4, c0_grad, 0)
        dcq = mm_tn(n2_ref[...], cq_ref[...]).astype(BF16)
        dco = mm_tn(gb_ref[...], oc_ref[...]).astype(BF16)
        for s in range(4):
            r_c1.part(s)[:, :hw] = dcq[:, s * hw : (s + 1) * hw]
            r_c1.part(s)[:, hw:] = dco[:, s * hw : (s + 1) * hw]
        r_c1.core_send(0)
        r_c1.core_send(1)
        r_c0.core_done()

        for r in range(rows):
            mem_c(r).wait_send()
            pl.when(inner)(mem_t(r).wait_send)

        def w2_grad(i, _):
            s = far_first(i)
            r_w2.part(s)[...] = mm_tn(cot_ref[...], u_ref[s]).astype(BF16)
            sends(r_w2, i)
            return 0

        lax.fori_loop(0, 4, w2_grad, 0)
        r_c1.core_done()

        def w1_grad(i, _):
            s = far_first(i)
            r_w1.part(s)[...] = mm_tn(n3_ref[...], gp_ref[s]).astype(BF16)
            sends(r_w1, i)
            pl.when(i == 0)(r_w2.core_done)
            return 0

        lax.fori_loop(0, 4, w1_grad, 0)

    @pl.when(is_enc)
    def _():
        def row(r, _):
            rs = rowsl(r)
            dm_x(r).wait_recv()
            dx, dg = norm_back(r2_ref[rs, :], gain2, R("dm")[r].astype(F32))
            R("dg")[r, pl.ds(2, 1), :] = dg
            g_ref[rs, :] = dx
            gb_ref[rs, :] = dx.astype(BF16)
            return 0

        lax.fori_loop(0, rows, row, 0)

        def sends(reduction, i):
            pl.when(i == 0)(lambda: reduction.core_send(0))
            pl.when(i == 1)(lambda: reduction.core_send(1))

        def w2_grad(i, _):
            s = far_first(i)
            r_w2.part(s)[...] = mm_tn(gb_ref[...], u_ref[s]).astype(BF16)
            sends(r_w2, i)
            return 0

        lax.fori_loop(0, 4, w2_grad, 0)
        dn = pl.ds(0, tokens)
        acc_ref[dn, :] = jnp.zeros((tokens, width), F32)

        def w1_grad(i, _):
            s = far_first(i)
            dh = (mm_nt(gb_ref[...], R("w2")[s]) * gp_ref[s].astype(F32)).astype(BF16)
            r_w1.part(s)[...] = mm_tn(n2_ref[...], dh).astype(BF16)
            sends(r_w1, i)
            acc_ref[dn, :] += mm_nt(dh, R("w1")[s])
            pl.when(i == 0)(r_w2.core_done)
            return 0

        lax.fori_loop(0, 4, w1_grad, 0)
        dx, dg = norm_back(r1_ref[...], gain1, acc_ref[dn, :])
        R("dg")[0, pl.ds(1, 1), :] = dg
        for r in range(1, rows):
            R("dg")[r, pl.ds(1, 1), :] = jnp.zeros_like(dg)
        g_ref[...] += dx

    sec_out = links.here(sec_ref, R("sec"))
    sec_out.start()
    r_w1.core_done()
    gb_ref[...] = g_ref[...].astype(BF16)
    R("dwo")[...] = mm_tn(gb_ref[...], o_ref[...]).astype(BF16)
    r_wo.core_send(0)
    r_wo.core_send(1)
    do_ref[...] = mm_nt(gb_ref[...], R("wo")[...].reshape(4 * hw, width)).astype(BF16)
    acc_ref[...] = jnp.zeros_like(acc_ref)
    dqkv_ref = R("dqkv")
    for r in range(rows):
        dqkv_ref[pl.ds(r * win, HALO), :hw] = jnp.zeros((HALO, hw), BF16)
        dqkv_ref[pl.ds(r * win + HALO + own, HALO), :hw] = jnp.zeros((HALO, hw), BF16)

    def self_back(i, _):
        s = far_first(i)
        for r in range(rows):
            rs = pl.ds(r * own, own)
            dq, dk, dv = attend_back(
                q_ref[s, r], k_ref[s, r], v_ref[s, r], do_ref[rs, lanes(s)], o_ref[rs, lanes(s)], inv_ref[rs, lanes(s)],
                lambda h: p_ref[s, r, h],
            )
            dqkv_ref[pl.ds(r * win + HALO, own), :hw] = dq
            dqkv_ref[pl.ds(r * win, win), hw : 2 * hw] = dk
            dqkv_ref[pl.ds(r * win, win), 2 * hw :] = dv
        r_wa.part(s)[...] = mm_tn(nw_ref[...], dqkv_ref[...]).astype(BF16)
        acc_ref[...] += mm_nt(dqkv_ref[...], R("wa")[s])

        @pl.when(i == 0)
        def _():
            r_wa.core_send(0)
            r_wo.core_done()

        @pl.when(i == 1)
        def _():
            r_wa.core_send(1)
            pl.when(is_dec)(r_c0.y_done)

        @pl.when(i == 2)
        def _():
            pl.when(is_enc)(r_w2.y_done)

        @pl.when(i == 3)
        def _():
            @pl.when(is_dec)
            def _():
                r_c1.y_done()
                r_c0.z_done(0, R("dc0"))

        return 0

    lax.fori_loop(0, 4, self_back, 0)
    for r in range(rows):
        R("dhs")[0, r] = acc_ref[pl.ds(r * win, HALO), :].astype(BF16)
        R("dhs")[1, r] = acc_ref[pl.ds(r * win + HALO + own, HALO), :].astype(BF16)
    pl.when(t < 3)(dn_right.start)
    pl.when(t > 0)(dn_left.start)
    r_wa.core_done()
    r_w1.z_done(0)

    @pl.when(t == 0)
    def _():
        R("dhr")[0] = jnp.zeros((rows, HALO, width), BF16)

    @pl.when(t == 3)
    def _():
        R("dhr")[1] = jnp.zeros((rows, HALO, width), BF16)

    pl.when(t > 0)(dn_right.wait_recv)
    pl.when(t < 3)(dn_left.wait_recv)
    for r in range(rows):
        lo, hi = pl.ds(r * win + HALO, HALO), pl.ds(r * win + own, HALO)
        acc_ref[lo, :] += R("dhr")[0, r].astype(F32)
        acc_ref[hi, :] += R("dhr")[1, r].astype(F32)
    total = jnp.zeros((1, width), F32)
    for r in range(rows):
        rs = pl.ds(r * own, own)
        dx, dg = norm_back(x_ref[r].astype(F32), gain0, acc_ref[pl.ds(r * win + HALO, own), :])
        gb_ref[rs, :] = (g_ref[rs, :] + dx).astype(BF16)
        total += dg
    gx_out = links.here(gb_ref, R("gx"))
    gx_out.start()
    R("dgs")[0] = jnp.zeros((8, width), F32)
    R("dgs")[0, pl.ds(0, 1), :] = total
    R("dgs")[0, pl.ds(1, 2), :] = sum(R("dg")[r, pl.ds(1, 2), :] for r in range(rows))
    gain_links[0].start()

    def gain_step(k):
        gain_links[k].wait_recv()
        if k + 1 < len(gain_links):
            R("dgs")[k + 1] = R("dgs")[k] + R("dgr")[k]
            gain_links[k + 1].start()
        else:
            R("dgain")[...] = pltpu.roll(R("dgs")[k] + R("dgr")[k], lax.rem(width - d * (width // dp), width), 1)

    pl.when(is_dec)(r_w2.y_done)
    r_wo.y_done()
    r_w2.z_done(0, R("dw2_o"))
    gain_step(0)

    @pl.when(is_dec)
    def _():
        r_c0.rest_z(1, R("dc0"))
        c0_back.start()
        r_c1.z_done(0, R("dc"))

    for k in range(1, len(zbits)):
        r_w1.z_done(k)
    r_wo.z_done(0, R("dwo_o"))
    gain_step(1)
    r_w2.rest_z(1, R("dw2_o"))
    r_wa.y_done()
    gain_step(2)
    pl.when(is_dec)(lambda: r_c1.rest_z(1, R("dc")))
    r_wo.rest_z(1, R("dwo_o"))
    r_w1.y_done(R("dw1_o"))
    r_wa.z_done(0, R("da_o"))
    for k in range(3, len(gain_links)):
        gain_step(k)
    r_wa.rest_z(1, R("da_o"))

    sec_out.wait()
    gx_out.wait()
    for g in (g_wa, g_wo, g_w1, g_w2):
        g.finish()
    for g in (r_w2, r_w1, r_wo, r_wa):
        g.finish()
    for c in gain_links:
        c.wait_send()
    pl.when(t < 3)(x_right.wait_send)
    pl.when(t > 0)(x_left.wait_send)
    pl.when(t < 3)(dn_right.wait_send)
    pl.when(t > 0)(dn_left.wait_send)

    @pl.when(is_enc)
    def _():
        c0_x.wait_send()
        for r in range(rows):
            mem_x(r).wait_send()
        c0_back.wait_recv()
        R("dc")[...] = R("dc0r")[...]

    @pl.when(is_dec)
    def _():
        for g in (g_cq, g_co, g_c0, r_c0, r_c1):
            g.finish()
        for r in range(rows):
            dm_x(r).wait_send()
        c0_back.wait_send()


def arrange(aligned, sec, gx, dgain, da, dwo, dc, dw1, dw2, sec_o, gx_o, dgain_o, da_o, dwo_o, dc_o, dw1_o, dw2_o):
    share, hw = dwo.shape
    sec_o[...] = sec[...]
    gx_o[...] = gx[...]
    for i in range(3):
        dgain_o[i] = dgain[pl.ds(i, 1), pl.ds(0, share)]
        da_o[i] = da[:, pl.ds(i * hw, hw)]
    for i in range(2):
        dc_o[:, i, :] = dc[:, pl.ds(i * hw, hw)]
    dw1_o[...] = dw1[...]
    dwo_o[...] = dwo[...].T if aligned else dwo[...]
    dw2_o[...] = dw2[...].T if aligned else dw2[...]


def body(embeds, segments, cotangent, norm_gains, attn_in, attn_out, cross_proj, ffn_in, ffn_out):
    dp = lax.axis_size("dp")
    rows, own, width = embeds.shape[1:]
    slots = segments.shape[2]
    hw = attn_in.shape[3]
    fw = ffn_in.shape[2]
    win = own + 2 * HALO
    cwin = 2 * own + 2 * HALO
    tokens = rows * own
    side = 3 * own // 4
    share = width // dp
    zsteps = (dp - 1).bit_length()

    ins = dict(
        x=embeds[0], segs=segments, gains=norm_gains.transpose(1, 0, 2), cot=cotangent.reshape(tokens, width),
        wa_h=attn_in[0].transpose(1, 0, 2), wo_h=attn_out[0], w1_h=ffn_in[0], w2_h=ffn_out[0],
        cx_h=cross_proj[0].reshape(width, 2 * hw),
    )
    outs = dict(
        sec=((tokens, width), BF16), gx=((tokens, width), BF16), dgain=((8, width), F32),
        da_o=((share, 3 * hw), F32), dwo_o=((share, hw), F32), dc=((share, 2 * hw), F32),
        dw1_o=((share, fw), F32), dw2_o=((share, fw), F32),
    )
    vm = dict(
        wa=((4, width, 3 * hw), BF16), wo=((4, hw, width), BF16), w1=((4, width, fw), BF16), w2=((4, fw, width), BF16),
        c0=((width, 8 * hw), BF16), cqw=((width, 4 * hw), BF16), cow=((width, 4 * hw), BF16),
        xh=((2, rows, HALO, width), BF16), nw=((rows * win, width), BF16),
        q=((4, rows, own, hw), BF16), k=((4, rows, win, hw), BF16), v=((4, rows, win, hw), BF16),
        p=((4, rows, 2, own, win), BF16), o=((tokens, width), BF16), inv=((tokens, width), BF16), bias=((rows, own, win), F32),
        r1=((tokens, width), F32), r2=((tokens, width), F32), n2=((tokens, width), BF16), n3=((tokens, width), BF16),
        u=((4, tokens, fw), BF16), gp=((4, tokens, fw), BF16), secs=((tokens, width), BF16),
        acc=((rows * win, width), F32), g=((tokens, width), F32), gb=((tokens, width), BF16), do=((tokens, width), BF16),
        memf=((max(rows * slots, 4 * width), max(width, fw)), BF16), kv=((slots, 8 * hw), BF16), cq=((tokens, width), BF16),
        cp=((max(8 * own, 4 * width), cwin), BF16), cinv=((own, width), BF16), oc=((tokens, width), BF16),
        cols=((rows, own, 128), F32), keys=((rows, 8, cwin), F32),
        dkv=((rows * cwin, 8 * hw), BF16), dmf=((max(rows * slots, 4 * width), max(width, fw)), BF16),
        rcc=((rows, own, width), BF16), rct=((rows, side, width), BF16), dm=((rows, own, width), BF16),
        dg=((rows, 8, width), F32),
        dqkv=((rows * win, 3 * hw), BF16), dhs=((2, rows, HALO, width), BF16), dhr=((2, rows, HALO, width), BF16),
        dgs=((2 + zsteps, 8, width), F32), dgr=((2 + zsteps, 8, width), F32),
        dwo=((width, 4 * hw), BF16),
        dc0=((share, 2 * hw), F32), dc0r=((share, 2 * hw), F32),
    )
    for name, m in dict(w2=fw, w1=fw, wo=hw, wa=3 * hw, c0=2 * hw, c1=2 * hw).items():
        both = (2,) if name == "w1" else ()
        vm["rc_" + name] = ((2, width, m), BF16)
        vm["ry_" + name] = ((share if both else width, m), BF16)
        vm["zb_" + name] = (both + (dp, share, m), BF16)
        for k in range(zsteps):
            vm[f"zr{k}_{name}"] = (both + (dp >> (k + 1), share, m), BF16)
    copies = 140 + 8 * zsteps
    sems = dict(send=pltpu.SemaphoreType.DMA((copies,)), recv=pltpu.SemaphoreType.DMA((copies,)), local=pltpu.SemaphoreType.DMA((12,)))
    in_hbm = {"wa_h", "wo_h", "w1_h", "w2_h", "cx_h"}
    out_hbm = {"sec", "gx"}
    results = pl.pallas_call(
        functools.partial(layers, list(ins) + list(outs) + list(vm) + list(sems)),
        name="layers",
        out_shape=[jax.ShapeDtypeStruct(*o) for o in outs.values()],
        in_specs=[pl.BlockSpec(memory_space=pl.ANY if n in in_hbm else pltpu.VMEM) for n in ins],
        out_specs=[pl.BlockSpec(memory_space=pl.ANY if n in out_hbm else pltpu.VMEM) for n in outs],
        scratch_shapes=[pltpu.VMEM(*s) for s in vm.values()] + list(sems.values()),
        compiler_params=pltpu.CompilerParams(vmem_limit_bytes=VMEM_LIMIT, collective_id=0, has_side_effects=True),
    )(*ins.values())
    aligned = share % 128 == 0
    flat, turned = (share, hw), (hw, share)
    sec, gx, dgain, da, dwo, dc, dw1, dw2 = pl.pallas_call(
        functools.partial(arrange, aligned),
        name="arrange",
        out_shape=[
            jax.ShapeDtypeStruct((tokens, width), BF16),
            jax.ShapeDtypeStruct((tokens, width), BF16),
            jax.ShapeDtypeStruct((3, 1, share), F32),
            jax.ShapeDtypeStruct((3, share, hw), F32),
            jax.ShapeDtypeStruct((hw, share) if aligned else (share, hw), F32),
            jax.ShapeDtypeStruct((share, 2, hw), F32),
            jax.ShapeDtypeStruct((share, fw), F32),
            jax.ShapeDtypeStruct((fw, share) if aligned else (share, fw), F32),
        ],
        in_specs=[pl.BlockSpec(memory_space=pltpu.VMEM)] * 8,
        out_specs=[pl.BlockSpec(memory_space=pltpu.VMEM)] * 8,
    )(*results)
    if not aligned:
        dwo, dw2 = dwo.T, dw2.T
    return (
        sec.reshape(1, rows, own, width), gx.reshape(1, rows, own, width), dgain.transpose(1, 0, 2),
        da.transpose(1, 0, 2)[None], dwo[None], dc[None], dw1[None], dw2[None],
    )


def solution(mesh):
    return jax.shard_map(
        body,
        mesh=mesh,
        in_specs=(
            P("pipe", "dp", "tensor", None),
            P(None, "dp", None),
            P("dp", "tensor", None),
            P("pipe", None, None),
            P("pipe", None, None, "tensor"),
            P("pipe", "tensor", None),
            P("pipe", None, None, "tensor"),
            P("pipe", None, "tensor"),
            P("pipe", "tensor", None),
        ),
        out_specs=(
            P("pipe", "dp", "tensor", None),
            P("pipe", "dp", "tensor", None),
            P("pipe", None, "dp"),
            P("pipe", "dp", None, "tensor"),
            P("pipe", "tensor", "dp"),
            P("pipe", "dp", None, "tensor"),
            P("pipe", "dp", "tensor"),
            P("pipe", "tensor", "dp"),
        ),
        check_vma=False,
    )
```

```python
import functools

import jax
import jax.numpy as jnp
from jax import lax
from jax.experimental import pallas as pl
from jax.experimental.pallas import tpu as pltpu
from jax.sharding import PartitionSpec as P

EPS = 1e-05
MASKED = -1000000000.0
DH = 64
HALO = 64
F32 = jnp.float32
BF16 = jnp.bfloat16
GELU_C = 0.7978845608028654
GELU_A = 0.044715
MESH = pl.DeviceIdType.MESH
VMEM_LIMIT = 63 << 20


def mm(a, b):
    return lax.dot_general(a, b, (((1,), (0,)), ((), ())), preferred_element_type=F32)


def mm_nt(a, b):
    return lax.dot_general(a, b, (((1,), (1,)), ((), ())), preferred_element_type=F32)


def mm_tn(a, b):
    return lax.dot_general(a, b, (((0,), (0,)), ((), ())), preferred_element_type=F32)


def norm_parts(v):
    c = v - jnp.mean(v, axis=-1, keepdims=True)
    r = lax.rsqrt(jnp.mean(c * c, axis=-1, keepdims=True) + EPS)
    return c * r, r


def norm(v, gain):
    xhat, _ = norm_parts(v)
    return xhat * gain


def norm_back(v, gain, dn):
    xhat, r = norm_parts(v)
    dxh = dn * gain
    m1 = jnp.mean(dxh, axis=-1, keepdims=True)
    m2 = jnp.mean(dxh * xhat, axis=-1, keepdims=True)
    return r * (dxh - m1 - xhat * m2), jnp.sum(dn * xhat, axis=0, keepdims=True)


def lane_low(shape):
    return lax.broadcasted_iota(jnp.int32, shape, 1) < DH


def pair_join(a, b):
    return jnp.where(lane_low(a.shape), a, b)


def swap_halves(v):
    return pltpu.roll(v, DH, 1)


def attend(q2, k2, v2, mask, keep):
    low, lowq = lane_low(v2.shape), lane_low(q2.shape)
    one, zero = jnp.ones_like(v2), jnp.zeros_like(q2)
    outs = []
    for h in range(2):
        qh = jnp.where(lowq, q2, zero) if h == 0 else jnp.where(lowq, zero, q2)
        s = mask(mm_nt(qh, k2))
        e = jnp.exp(s - jnp.max(s, axis=-1, keepdims=True)).astype(BF16)
        keep(h, e)
        outs.append(mm(e, jnp.where(low, v2, one) if h == 0 else jnp.where(low, one, v2)))
    inv = 1.0 / swap_halves(pair_join(outs[1], outs[0]))
    return pair_join(*outs) * inv, inv


def attend_back(q2, k2, v2, do2, o2, inv, kept):
    low, lowq = lane_low(v2.shape), lane_low(q2.shape)
    one = jnp.ones_like(v2)
    scaled = do2.astype(F32) * inv.astype(F32)
    dob = scaled.astype(BF16)
    minus = (-swap_halves(dob.astype(F32) * o2.astype(F32))).astype(BF16)
    q_t, do_t = q2.T, dob.T
    dq, dk, dv = [], [], []
    for h in range(2):
        e = kept(h)
        rows = slice(h * DH, (h + 1) * DH)
        lhs = jnp.where(lowq, dob, minus) if h == 0 else jnp.where(lowq, minus, dob)
        dp = mm_nt(lhs, jnp.where(low, v2, one) if h == 0 else jnp.where(low, one, v2))
        ds = (dp * e.astype(F32)).astype(BF16)
        dq.append(mm(ds, k2))
        dv.append(mm(do_t[rows], e).astype(BF16))
        dk.append(mm(q_t[rows], ds).astype(BF16))
    return (pair_join(*dq) * (DH**-0.5)).astype(BF16), jnp.concatenate(dk, 0).T, jnp.concatenate(dv, 0).T


def gelu_parts(h):
    h2 = h * h
    half = 0.5 + 0.5 * jnp.tanh(h * (GELU_C + (GELU_C * GELU_A) * h2))
    u = h * half
    slope = half + u * ((1.0 - half) * (2.0 * GELU_C + (6.0 * GELU_C * GELU_A) * h2))
    return u, slope


def flip(i, bit):
    return i + bit - 2 * bit * lax.rem(lax.div(i, bit), 2)


def bit_of(i, bit):
    return lax.rem(lax.div(i, bit), 2)


def reversed_bits(i, count):
    out, bit = 0, 1
    while bit < count:
        out = 2 * out + (i // bit) % 2
        bit *= 2
    return out


class Links:
    def __init__(self, send, recv, local):
        self.send, self.recv, self.local = send, recv, local
        self.n = self.m = 0
        self.sent = []

    def take(self, count=1):
        self.n += count
        return self.n - count

    def remote(self, src, dst, device, at=None):
        at = self.take() if at is None else at
        return pltpu.make_async_remote_copy(
            src_ref=src, dst_ref=dst, send_sem=self.send.at[at], recv_sem=self.recv.at[at],
            device_id=device, device_id_type=MESH,
        )

    def here(self, src, dst):
        self.m += 1
        return pltpu.make_async_copy(src, dst, self.local.at[self.m - 1])


class Gather:
    def __init__(self, links, src, slot, depth, at, pieces=1, planes=None):
        t, t2 = at["t"], at["t2"]
        half = depth // 2
        n = half // pieces
        whole = pl.ds(0, depth)
        if src is None:
            self.own = []
        elif planes is None:
            self.own = [links.here(src, slot(t, whole))]
        else:
            self.own = [links.here(src.at[i], slot(t, whole, i)) for i in range(planes)]
        self.inner = src is None or planes is not None
        src = slot(t, whole) if self.inner else src
        self.core = links.remote(src, slot(t, whole), at["C"])
        self.over_y, self.over_z, self.core_a, self.core_b = [], [], [], []
        for i in range(pieces):
            mine = pl.ds(pl.multiple_of(at["b"] * half + i * n, n), n)
            other = pl.ds(pl.multiple_of((1 - at["b"]) * half + i * n, n), n)
            self.over_y.append(links.remote(src.at[mine], slot(t, mine), at["Y"]))
            self.over_z.append(links.remote(slot(t2, mine), slot(t2, mine), at["Z"][0]))
            self.core_a.append(links.remote(slot(t2, mine), slot(t2, mine), at["C"]))
            self.core_b.append(links.remote(slot(t2, other), slot(t2, other), at["C"]))

    def start(self):
        for c in self.own:
            c.start()
        if self.inner:
            for c in self.own:
                c.wait()
        for c in self.over_y:
            c.start()
        self.core.start()

    def step1(self, i=0):
        self.over_y[i].wait_recv()
        self.over_z[i].start()
        self.core_a[i].start()

    def step2(self, i=0):
        self.over_z[i].wait_recv()
        self.core_b[i].start()

    def ready(self, i):
        if i == 0 and not self.inner:
            for c in self.own:
                c.wait()
        if i == 1:
            self.core.wait_recv()
        if i == 3:
            for c in self.core_a + self.core_b:
                c.wait_recv()

    def finish(self):
        for c in [self.core] + self.over_y + self.over_z + self.core_a + self.core_b:
            c.wait_send()


class Reduce:
    def __init__(self, links, part, rc, ry, zb, zr, at, y_first):
        self.part, self.at, self.y_first = part, at, y_first
        self.rc, self.ry, self.zb, self.zr = rc, ry, zb, zr
        self.n = zb.shape[0]
        self.dp, self.rows = zb.shape[1:3]
        self.core = [links.remote(part(at[f]), rc.at[j], at["C"]) for j, f in enumerate(("t1", "t3"))]
        self.over_z, self.kept = [], []
        off, m, bit, k = 0, self.dp, 1, 0
        while m > 1:
            m //= 2
            b = bit_of(at["d"], bit)
            keep, give = off + b * m, off + (1 - b) * m
            self.over_z.append(links.remote(zb.at[:, pl.ds(give, m)], zr[k], at["Z"][k]))
            self.kept.append((keep, m))
            off, bit, k = keep, 2 * bit, k + 1
        self.off = off
        self.over_y = links.remote(part(at["t2"]) if y_first else zb.at[1, off], ry, at["Y"])

    def core_send(self, j):
        self.core[j].start()

    def into_zb(self, j, mine, theirs):
        for i in range(self.dp):
            where = pl.ds(i * self.rows, self.rows)
            self.zb[j, reversed_bits(i, self.dp)] = (mine[where, :].astype(F32) + theirs[where, :].astype(F32)).astype(BF16)

    def core_done(self):
        self.core[0].wait_recv()
        self.core[1].wait_recv()
        far, near = self.part(self.at["t2"]), self.part(self.at["t"])
        if self.y_first:
            far[...] = (far[...].astype(F32) + self.rc[1].astype(F32)).astype(BF16)
            self.over_y.start()
            near[...] = (near[...].astype(F32) + self.rc[0].astype(F32)).astype(BF16)
        else:
            self.into_zb(0, near, self.rc.at[0])
            self.into_zb(1, far, self.rc.at[1])
            self.over_z[0].start()

    def y_done(self, out=None):
        self.over_y.wait_recv()
        if self.y_first:
            self.into_zb(0, self.part(self.at["t"]), self.ry)
            self.over_z[0].start()
        else:
            out[...] = self.zb[0, self.off].astype(F32) + self.ry[...].astype(F32)

    def z_done(self, k, out=None):
        self.over_z[k].wait_recv()
        keep, m = self.kept[k]
        last = k == len(self.over_z) - 1
        if last and self.y_first:
            out[...] = self.zb[0, keep].astype(F32) + self.zr[k][0, 0].astype(F32)
        else:
            for j in range(self.n):
                live = self.zb.at[j, pl.ds(keep, m)]
                live[...] = (live[...].astype(F32) + self.zr[k][j].astype(F32)).astype(BF16)
            (self.over_y if last else self.over_z[k + 1]).start()

    def z_rest(self, out=None):
        for k in range(1, len(self.over_z)):
            self.z_done(k, out)

    def finish(self):
        for c in self.core + [self.over_y] + self.over_z:
            c.wait_send()


def layers(names, *refs):
    ref = dict(zip(names, refs))
    R = lambda name: ref[name]
    p, d, t = lax.axis_index("pipe"), lax.axis_index("dp"), lax.axis_index("tensor")
    is_enc, is_dec = p == 0, p == 1
    dp = lax.axis_size("dp")
    t1, t2, t3 = flip(t, 1), flip(t, 2), 3 - t
    zbits = []
    while 2 ** len(zbits) < dp:
        zbits.append((p, flip(d, 2 ** len(zbits)), t))
    at = dict(t=t, t1=t1, t2=t2, t3=t3, d=d, b=bit_of(d, 1), C=(p, d, t1), Y=(p, d, t2), T=(p, d, t3), X=(1 - p, d, t), Z=zbits)
    rows, own, width = R("x").shape
    win, cwin = own + 2 * HALO, 2 * own + 2 * HALO
    slots = 4 * own
    tokens = rows * own
    hw = R("wa").shape[2] // 3
    fw = R("w1").shape[2]
    inner = t % 3 != 0
    scale = jnp.asarray(DH**-0.5, BF16)
    gain_ref, x_ref = R("gains"), R("x")
    side = 3 * own // 4

    def rowsl(r, n=own):
        return pl.ds(pl.multiple_of(r * n, n), n)

    def lanes(s, n=hw):
        return pl.ds(pl.multiple_of(s * n, n), n)

    def far_lanes(s):
        return pl.ds(pl.multiple_of(s * 2 * hw + hw, hw), hw)

    def in_row(r, span):
        return pl.ds(pl.multiple_of(r * slots + span.start, HALO), span.size)

    def near_first(i):
        return 2 * lax.rem(lax.div(t, 2) + lax.div(i, 2), 2) + lax.rem(lax.rem(t, 2) + lax.rem(i, 2), 2)

    def far_first(i):
        return 2 * lax.rem(lax.div(t, 2) + lax.rem(lax.div(i + 1, 2), 2), 2) + lax.rem(lax.rem(t, 2) + 1 - lax.div(i, 2), 2)

    def seg_row(side_, r, start):
        row = jnp.broadcast_to(R("segs")[side_, pl.ds(r, 1), :].astype(F32), (8, slots))
        return pltpu.roll(row, lax.rem(2 * slots - start, slots), 1)

    def seg_column(side_, r):
        row = seg_row(side_, r, t * own)[:1, :own]
        return jnp.broadcast_to(row, (128, own)).T

    def spread(column, n):
        return jnp.concatenate([column] * (n // 128), axis=1)

    links = Links(R("send"), R("recv"), R("local"))

    def by_shard(name, n=None):
        def slot(s, span, i=None):
            full = R(name).at[s, span]
            return full if i is None else full.at[:, pl.ds(i * n, n)]

        return slot

    def by_columns(name, n, row):
        def slot(s, span):
            return R(name).at[pl.ds(pl.multiple_of(span.start + row, HALO), span.size), lanes(s, n)]

        return slot

    g_wa = Gather(links, R("wa_h"), by_shard("wa", hw), width, at, 2, 3)
    g_wo = Gather(links, R("wo_h"), by_shard("wo"), hw, at)
    g_w1 = Gather(links, R("w1_h"), by_shard("w1"), width, at, 2)
    g_w2 = Gather(links, R("w2_h"), by_shard("w2"), fw, at, 2)
    g_c1 = Gather(links, R("cx_h"), by_columns("dmf", hw, 0), 2 * width, at)
    c0_x = links.remote(R("cx_h"), R("dmf").at[pl.ds(2 * width, 2 * width), lanes(t)], at["X"])
    g_c0 = Gather(links, None, by_columns("dmf", hw, 2 * width), 2 * width, at)
    loads = [links.here(R(n + "_h"), R(n)) for n in ("x", "cot", "segs")]
    x_right = links.remote(R("x_h").at[:, pl.ds(own - HALO, HALO)], R("xh").at[0], (p, d, lax.rem(t + 1, 4)))
    x_left = links.remote(R("x_h").at[:, pl.ds(0, HALO)], R("xh").at[1], (p, d, lax.rem(t + 3, 4)))
    base_mem, base_memc, base_memt = links.take(rows), links.take(rows), links.take(rows)
    base_dmc, base_dmt, base_dmx = links.take(rows), links.take(rows), links.take(rows)
    block = pl.ds(pl.multiple_of(t * own, own), own)
    block1 = pl.ds(pl.multiple_of(t1 * own, own), own)
    edge_out = pl.ds(pl.multiple_of(lax.rem(own // 2 + side * t, slots), HALO), side)
    edge_in = pl.ds(pl.multiple_of(lax.rem(own // 2 + side * t3, slots), HALO), side)

    def mem_x(r):
        return links.remote(R("secs").at[rowsl(r)], R("memf").at[in_row(r, block)], at["X"], base_mem + r)

    def mem_c(r):
        return links.remote(R("memf").at[in_row(r, block)], R("memf").at[in_row(r, block)], at["C"], base_memc + r)

    def mem_t(r):
        return links.remote(R("memf").at[in_row(r, edge_out)], R("memf").at[in_row(r, edge_out)], at["T"], base_memt + r)

    def dm_rows(r, span):
        return R("dmf").at[in_row(r, span)]

    def dm_c(r):
        return links.remote(dm_rows(r, block1), R("rcc").at[r], at["C"], base_dmc + r)

    def dm_t(r):
        return links.remote(dm_rows(r, edge_in), R("rct").at[r], at["T"], base_dmt + r)

    def dm_x(r):
        return links.remote(R("dm").at[r], R("dm").at[r], at["X"], base_dmx + r)

    def by_rows(name, m, col=0):
        return lambda s: R(name).at[pl.ds(pl.multiple_of(s * width, width), width), pl.ds(col, m)]

    def by_lanes(name, m, row=0):
        return lambda s: R(name).at[pl.ds(row, width), lanes(s, m)]

    def reduce_of(name, part, y_first=True):
        zr = [R(f"zr{k}_{name}") for k in range(len(zbits))]
        return Reduce(links, part, R("rc_" + name), R("ry_" + name), R("zb_" + name), zr, at, y_first)

    fh = fw // 2
    r_w2 = [reduce_of(f"w2{j}", by_rows("dw2", fh, j * fh), j > 0) for j in range(2)]
    r_w1 = [reduce_of(f"w1{j}", by_rows("dmf", fh, j * fh)) for j in range(2)]
    r_wo = reduce_of("wo", by_lanes("dwo", hw))
    r_wa = [reduce_of(f"wa{j}", by_rows("cp", hw, j * hw)) for j in range(3)]
    r_c0 = reduce_of("c0", by_lanes("kv", 2 * hw))
    r_c1 = reduce_of("c1", by_lanes("kv", 2 * hw, width))
    w2_out = [R("dw2_o").at[:, pl.ds(j * fh, fh)] for j in range(2)]
    w1_out = [R("dw1_o").at[:, pl.ds(j * fh, fh)] for j in range(2)]
    wa_out = [R("da_o").at[:, pl.ds(j * hw, hw)] for j in range(3)]
    c0_back = links.remote(R("dc0"), R("dc0r"), at["X"])
    dn_right = links.remote(R("xh").at[1], R("dhr").at[0], (p, d, lax.rem(t + 1, 4)))
    dn_left = links.remote(R("xh").at[0], R("dhr").at[1], (p, d, lax.rem(t + 3, 4)))
    gain_links = [links.remote(R("dgs").at[k], R("dgr").at[k], dev) for k, dev in enumerate([at["C"]] + zbits + [at["Y"]])]

    @pl.when(is_dec)
    def _():
        for at_t, start in ((0, 2 * own), (1, 2 * own + side), (3, 2 * own - 2 * HALO)):
            @pl.when(t == at_t)
            def _():
                for r in range(rows):
                    R("memf")[pl.ds(r * slots + start, 2 * HALO), :] = jnp.zeros((2 * HALO, width), BF16)

    for c in loads:
        c.start()
    barrier = pltpu.get_barrier_semaphore()
    partners = [at["C"], at["Y"], at["T"], at["X"]] + zbits
    for dev in partners:
        pl.semaphore_signal(barrier, inc=1, device_id=dev, device_id_type=MESH)
    pl.semaphore_wait(barrier, len(partners))

    pl.when(t < 3)(x_right.start)
    pl.when(t > 0)(x_left.start)
    g_wa.start()
    g_wo.start()

    @pl.when(is_enc)
    def _():
        c0_x.start()
        g_w1.start()
        g_w2.start()

    @pl.when(is_dec)
    def _():
        g_c1.start()

    for c in loads:
        c.wait()

    nw_ref, bias_ref = R("nw"), R("bias")
    gain0, gain1, gain2 = gain_ref[0], gain_ref[1], gain_ref[2]
    for r in range(rows):
        nw_ref[pl.ds(r * win + HALO, own), :] = norm(x_ref[r].astype(F32), gain0).astype(BF16)
        keys = seg_row(p, r, lax.rem(t * own + slots - HALO, slots))[:1, :win]
        same = spread(seg_column(p, r), win) == keys
        qpos = lax.broadcasted_iota(jnp.int32, (own, win), 0)
        kpos = lax.broadcasted_iota(jnp.int32, (own, win), 1) - HALO
        before = kpos - qpos <= jnp.where(is_enc, 4 * win, 0)
        bias_ref[r] = jnp.where(same & before, 0.0, MASKED)

    @pl.when(t == 0)
    def _():
        R("xh")[0] = jnp.zeros((rows, HALO, width), BF16)

    @pl.when(t == 3)
    def _():
        R("xh")[1] = jnp.zeros((rows, HALO, width), BF16)

    pl.when(t > 0)(x_right.wait_recv)
    pl.when(t < 3)(x_left.wait_recv)
    for r in range(rows):
        nw_ref[pl.ds(r * win, HALO), :] = norm(R("xh")[0, r].astype(F32), gain0).astype(BF16)
        nw_ref[pl.ds(r * win + HALO + own, HALO), :] = norm(R("xh")[1, r].astype(F32), gain0).astype(BF16)

    def after_pair(i):
        @pl.when(i == 0)
        def _():
            g_wa.step1(0)

        @pl.when(i == 1)
        def _():
            g_wa.step1(1)
            g_wa.step2(0)
            g_wo.step1()

            @pl.when(is_dec)
            def _():
                c0_x.wait_recv()
                g_c0.start()
                g_w2.start()
                g_w1.start()

            g_wa.step2(1)

        @pl.when(i == 2)
        def _():
            pl.when(is_enc)(lambda: g_w1.step1(0))
            pl.when(is_dec)(g_c1.step1)
            g_wo.step2()

        @pl.when(i == 3)
        def _():
            @pl.when(is_enc)
            def _():
                g_w1.step1(1)
                g_w1.step2(0)

            @pl.when(is_dec)
            def _():
                g_c0.step1()
                g_c1.step2()

    def wait_ready(i, *weights):
        for k in range(4):
            @pl.when(i == k)
            def _():
                for w in weights:
                    w.ready(k)

    q_ref, k_ref, v_ref, p_ref, o_ref, inv_ref = R("q"), R("k"), R("v"), R("p"), R("o"), R("inv")

    def self_pair(i, _):
        s = near_first(i)
        wait_ready(i, g_wa)
        packed = mm(nw_ref[...], R("wa")[s])
        for r in range(rows):
            q_ref[s, r] = packed[r * win + HALO : r * win + HALO + own, :hw].astype(BF16) * scale
            k_ref[s, r] = packed[r * win : (r + 1) * win, hw : 2 * hw].astype(BF16)
            v_ref[s, r] = packed[r * win : (r + 1) * win, 2 * hw :].astype(BF16)
        for r in range(rows):
            def keep(h, e):
                p_ref[s, r, h] = e

            o2, inv = attend(q_ref[s, r], k_ref[s, r], v_ref[s, r], lambda scores: scores + bias_ref[r], keep)
            o_ref[pl.ds(r * own, own), lanes(s)] = o2.astype(BF16)
            inv_ref[pl.ds(r * own, own), lanes(s)] = inv.astype(BF16)
        after_pair(i)
        return 0

    lax.fori_loop(0, 4, self_pair, 0)
    for k in range(4):
        g_wo.ready(k)
    r1_ref, r2_ref, n2_ref, n3_ref = R("r1"), R("r2"), R("n2"), R("n3")
    u_ref, gp_ref, sec_ref = R("u"), R("gp"), R("secs")
    acc_ref, g_ref, gb_ref, do_ref = R("acc"), R("g"), R("gb"), R("do")
    first = mm(o_ref[...], R("wo")[...].reshape(4 * hw, width))
    for r in range(rows):
        r1_ref[pl.ds(r * own, own), :] = x_ref[r].astype(F32) + first[r * own : (r + 1) * own]
    n2_ref[...] = norm(r1_ref[...], gain1).astype(BF16)

    @pl.when(is_enc)
    def _():
        r2_ref[...] = r1_ref[...]

        def up(i):
            s = near_first(i)
            u, gp = gelu_parts(mm(n2_ref[...], R("w1")[s]))
            u_ref[s] = u.astype(BF16)
            gp_ref[s] = gp.astype(BF16)
            return s

        g_w2.step1(0)

        def near(i, _):
            wait_ready(i, g_w1, g_w2)
            s = up(i)
            r2_ref[...] += mm(u_ref[s], R("w2")[s])
            pl.when(i == 0)(lambda: g_w1.step2(1))
            pl.when(i == 1)(lambda: g_w2.step1(1))
            return 0

        lax.fori_loop(0, 2, near, 0)

        def far(i, _):
            wait_ready(i, g_w1)
            up(i)
            pl.when(i == 2)(lambda: g_w2.step2(0))
            pl.when(i == 3)(lambda: g_w2.step2(1))
            return 0

        lax.fori_loop(2, 4, far, 0)
        g_w2.ready(3)
        far1, far2 = near_first(2), near_first(3)

        def row(r, _):
            rs = rowsl(r)
            total = r2_ref[rs, :] + mm(u_ref[far1, rs, :], R("w2")[far1]) + mm(u_ref[far2, rs, :], R("w2")[far2])
            r2_ref[rs, :] = total
            sec_ref[rs, :] = norm(total, gain2).astype(BF16)
            mem_x(r).start()
            return 0

        lax.fori_loop(0, rows, row, 0)

    def sends(reductions, i):
        for j in range(2):
            @pl.when(i == j)
            def _():
                for reduction in reductions:
                    reduction.core_send(j)

    cstart = pl.multiple_of(jnp.minimum(t * (own - HALO), slots - cwin), HALO)
    cwindow = pl.ds(cstart, cwin)
    kv_ref, cq_ref, cp_ref, dkv_ref, cinv_ref = R("kv"), R("cq"), R("cp"), R("dkv"), R("cinv")
    c0_ref, cqw_ref, cow_ref, oc_ref, cot_ref = R("c0"), R("cqw"), R("cow"), R("oc"), R("cot")
    cols, keys_ref = R("cols"), R("keys")
    half = 4 * hw

    @pl.when(is_dec)
    def _():
        g_c0.step2()
        g_w2.step1(0)
        for k in range(4):
            g_c1.ready(k)
        pick_shape = (width // 4, width // 2)
        twice = 2 * lax.broadcasted_iota(jnp.int32, pick_shape, 0)
        at_col = lax.broadcasted_iota(jnp.int32, pick_shape, 1)
        picks = [jnp.where(at_col == twice + j, 1.0, 0.0).astype(BF16) for j in range(2)]

        def unweave(base, m):
            return [mm(pick, R("dmf")[pl.ds(base + m * (width // 2), width // 2), :]).astype(BF16) for pick in picks]

        for m in range(4):
            span = pl.ds(m * (width // 4), width // 4)
            cqw_ref[span, :], cow_ref[span, :] = unweave(0, m)
        cq_ref[...] = mm(n2_ref[...], cqw_ref[...]).astype(BF16) * scale
        g_w2.step1(1)
        g_w2.step2(0)
        g_w1.step1(0)
        kv_ref[...] = jnp.zeros_like(kv_ref)
        for r in range(rows):
            cols[r] = seg_column(1, r)
            keys_ref[r] = seg_row(0, r, cstart)[:, :cwin]
        for k in range(4):
            g_c0.ready(k)
        for m in range(4):
            span = pl.ds(m * (width // 4), width // 4)
            ck, cv = unweave(2 * width, m)
            for s in range(4):
                c0_ref[span, 2 * s * hw : (2 * s + 1) * hw] = ck[:, s * hw : (s + 1) * hw]
                c0_ref[span, (2 * s + 1) * hw : (2 * s + 2) * hw] = cv[:, s * hw : (s + 1) * hw]
        g_w2.step2(1)
        g_w1.step1(1)
        g_w1.step2(0)
        for g in (g_c1, g_c0):
            g.finish()
        R("dmf")[...] = jnp.zeros_like(R("dmf"))
        for k in range(4):
            g_w2.ready(k)

        def early(s, _):
            gp_ref[s] = mm_nt(cot_ref[...], R("w2")[s]).astype(BF16)
            return 0

        lax.fori_loop(0, 4, early, 0)
        g_w1.step2(1)
        for k in range(4):
            g_w1.ready(k)

        def settle(r):
            span = pl.ds(0, own)
            dm_c(r).wait_recv()
            acc_ref[span, :] = R("dmf")[in_row(r, block), :].astype(F32) + R("rcc")[r].astype(F32)

            @pl.when(inner)
            def _():
                dm_t(r).wait_recv()
                place = pl.ds(pl.multiple_of((2 - t) * (own - side), HALO), side)
                acc_ref[place, :] += R("rct")[r].astype(F32)

            R("dm")[r] = acc_ref[span, :].astype(BF16)
            dm_x(r).start()

        def row(r, _):
            rs = rowsl(r)

            def project(span):
                for j in range(2):
                    kv = mm(R("memf")[in_row(r, span), :], c0_ref[:, j * half : (j + 1) * half])
                    kv_ref[span, j * half : (j + 1) * half] = kv.astype(BF16)

            mem_x(r).wait_recv()
            mem_c(r).start()
            pl.when(inner)(mem_t(r).start)
            project(block)
            mem_c(r).wait_recv()
            project(block1)

            @pl.when(inner)
            def _():
                mem_t(r).wait_recv()
                project(edge_in)

            def cross(i, _):
                for s in (2 * i, 2 * i + 1):
                    def keep(h, e):
                        cp_ref[rowsl(2 * s + h), :] = e

                    def mask(scores):
                        same = spread(cols[r], cwin) == keys_ref[r, pl.ds(0, 1), :]
                        return jnp.where(same, scores, MASKED)

                    o2, inv = attend(cq_ref[rs, lanes(s)], kv_ref[cwindow, lanes(2 * s)], kv_ref[cwindow, lanes(2 * s + 1)], mask, keep)
                    oc_ref[rs, lanes(s)] = o2.astype(BF16)
                    cinv_ref[:, lanes(s)] = inv.astype(BF16)
                return 0

            lax.fori_loop(0, 2, cross, 0)
            pl.when(r > 0)(lambda: settle(r - 1))
            r2_ref[rs, :] = r1_ref[rs, :] + mm_nt(oc_ref[rs, :], cow_ref[...])
            n3_ref[rs, :] = norm(r2_ref[rs, :], gain2).astype(BF16)
            dn = pl.ds(0, own)
            acc_ref[dn, :] = jnp.zeros((own, width), F32)
            g_ref[rs, :] = r2_ref[rs, :]

            def feed(s, _):
                u, gp = gelu_parts(mm(n3_ref[rs, :], R("w1")[s]))
                u = u.astype(BF16)
                u_ref[s, rs, :] = u
                g_ref[rs, :] += mm(u, R("w2")[s])
                dh = (gp_ref[s, rs, :].astype(F32) * gp).astype(BF16)
                gp_ref[s, rs, :] = dh
                acc_ref[dn, :] += mm_nt(dh, R("w1")[s])
                return 0

            lax.fori_loop(0, 4, feed, 0)
            sec_ref[rs, :] = g_ref[rs, :].astype(BF16)
            dx, dg = norm_back(r2_ref[rs, :], gain2, acc_ref[dn, :])
            R("dg")[r, pl.ds(2, 1), :] = dg
            g2 = cot_ref[rs, :].astype(F32) + dx
            g_ref[rs, :] = g2
            gb_ref[rs, :] = g2.astype(BF16)
            do_ref[rs, :] = mm(gb_ref[rs, :], cow_ref[...]).astype(BF16)

            @pl.when(r == rows - 1)
            def _():
                def w2_grad(i, _):
                    s = far_first(i)
                    R("dw2")[rowsl(s, width), :] = mm_tn(cot_ref[...], u_ref[s]).astype(BF16)
                    sends(r_w2, i)
                    return 0

                lax.fori_loop(0, 4, w2_grad, 0)

            ws = pl.ds(pl.multiple_of(r * cwin, HALO), cwin)

            def back(i, _):
                for s in (2 * i, 2 * i + 1):
                    dq, dk, dv = attend_back(
                        cq_ref[rs, lanes(s)], kv_ref[cwindow, lanes(2 * s)], kv_ref[cwindow, lanes(2 * s + 1)],
                        do_ref[rs, lanes(s)], oc_ref[rs, lanes(s)], cinv_ref[:, lanes(s)], lambda h: cp_ref[rowsl(2 * s + h), :],
                    )
                    cq_ref[rs, lanes(s)] = dq
                    dkv_ref[ws, lanes(2 * s)] = dk
                    dkv_ref[ws, lanes(2 * s + 1)] = dv
                return 0

            lax.fori_loop(0, 2, back, 0)
            R("dmf")[in_row(r, cwindow), :] = mm_nt(dkv_ref[ws, :], c0_ref[...]).astype(BF16)
            dm_c(r).start()
            pl.when(inner)(dm_t(r).start)
            dx, dg = norm_back(r1_ref[rs, :], gain1, mm_nt(cq_ref[rs, :], cqw_ref[...]))
            R("dg")[r, pl.ds(1, 1), :] = dg
            g_ref[rs, :] += dx

            @pl.when(r == rows - 1)
            def _():
                r_w2[0].core_done()
                r_w2[1].core_done()
                settle(r)

            return 0

        lax.fori_loop(0, rows, row, 0)
        for r in range(rows):
            dm_c(r).wait_send()
            pl.when(inner)(dm_t(r).wait_send)

        def w1_grad(i, _):
            s = far_first(i)
            R("dmf")[rowsl(s, width), :] = mm_tn(n3_ref[...], gp_ref[s]).astype(BF16)
            sends(r_w1, i)
            return 0

        lax.fori_loop(0, 4, w1_grad, 0)

        def c0_grad(i, _):
            s = far_first(i)
            total = mm_tn(R("memf")[in_row(0, cwindow), :], dkv_ref[pl.ds(0, cwin), lanes(s, 2 * hw)])
            for r in range(1, rows):
                total += mm_tn(R("memf")[in_row(r, cwindow), :], dkv_ref[pl.ds(r * cwin, cwin), lanes(s, 2 * hw)])
            r_c0.part(s)[...] = total.astype(BF16)
            sends([r_c0], i)

            @pl.when(i == 1)
            def _():
                r_w1[0].core_done()
                r_w1[1].core_done()

            return 0

        lax.fori_loop(0, 4, c0_grad, 0)
        dcq = mm_tn(n2_ref[...], cq_ref[...]).astype(BF16)
        dco = mm_tn(gb_ref[...], oc_ref[...]).astype(BF16)
        r_c0.core_done()
        for s in range(4):
            r_c1.part(s)[:, :hw] = dcq[:, s * hw : (s + 1) * hw]
            r_c1.part(s)[:, hw:] = dco[:, s * hw : (s + 1) * hw]
        sends([r_c1], 0)
        sends([r_c1], 1)

    @pl.when(is_enc)
    def _():
        def row(r, _):
            rs = rowsl(r)
            dm_x(r).wait_recv()
            dx, dg = norm_back(r2_ref[rs, :], gain2, R("dm")[r].astype(F32))
            R("dg")[r, pl.ds(2, 1), :] = dg
            g_ref[rs, :] = dx
            gb_ref[rs, :] = dx.astype(BF16)
            return 0

        lax.fori_loop(0, rows, row, 0)

        def w2_grad(i, _):
            s = far_first(i)
            R("dw2")[rowsl(s, width), :] = mm_tn(gb_ref[...], u_ref[s]).astype(BF16)
            sends(r_w2, i)
            return 0

        lax.fori_loop(0, 4, w2_grad, 0)
        dn = pl.ds(0, tokens)
        acc_ref[dn, :] = jnp.zeros((tokens, width), F32)

        def w1_grad(i, _):
            s = far_first(i)
            dh = (mm_nt(gb_ref[...], R("w2")[s]) * gp_ref[s].astype(F32)).astype(BF16)
            R("dmf")[rowsl(s, width), :] = mm_tn(n2_ref[...], dh).astype(BF16)
            sends(r_w1, i)
            acc_ref[dn, :] += mm_nt(dh, R("w1")[s])

            @pl.when(i == 0)
            def _():
                r_w2[0].core_done()
                r_w2[1].core_done()

            return 0

        lax.fori_loop(0, 4, w1_grad, 0)
        r_w1[0].core_done()
        r_w1[1].core_done()
        dx, dg = norm_back(r1_ref[...], gain1, acc_ref[dn, :])
        R("dg")[0, pl.ds(1, 1), :] = dg
        for r in range(1, rows):
            R("dg")[r, pl.ds(1, 1), :] = jnp.zeros_like(dg)
        g_ref[...] += dx

    sec_out = links.here(sec_ref, R("sec"))
    sec_out.start()
    gb_ref[...] = g_ref[...].astype(BF16)
    R("dwo")[...] = mm_tn(gb_ref[...], o_ref[...]).astype(BF16)
    r_wo.core_send(0)
    r_wo.core_send(1)
    do_ref[...] = mm_nt(gb_ref[...], R("wo")[...].reshape(4 * hw, width)).astype(BF16)
    acc_ref[...] = jnp.zeros_like(acc_ref)
    dqkv_ref = R("dqkv")
    for r in range(rows):
        dqkv_ref[pl.ds(r * win, HALO), :hw] = jnp.zeros((HALO, hw), BF16)
        dqkv_ref[pl.ds(r * win + HALO + own, HALO), :hw] = jnp.zeros((HALO, hw), BF16)

    def self_back(i, _):
        s = far_first(i)
        for r in range(rows):
            rs = pl.ds(r * own, own)
            dq, dk, dv = attend_back(
                q_ref[s, r], k_ref[s, r], v_ref[s, r], do_ref[rs, lanes(s)], o_ref[rs, lanes(s)], inv_ref[rs, lanes(s)],
                lambda h: p_ref[s, r, h],
            )
            dqkv_ref[pl.ds(r * win + HALO, own), :hw] = dq
            dqkv_ref[pl.ds(r * win, win), hw : 2 * hw] = dk
            dqkv_ref[pl.ds(r * win, win), 2 * hw :] = dv
        R("cp")[rowsl(s, width), pl.ds(0, 3 * hw)] = mm_tn(nw_ref[...], dqkv_ref[...]).astype(BF16)
        sends(r_wa, i)
        acc_ref[...] += mm_nt(dqkv_ref[...], R("wa")[s])

        @pl.when(i == 0)
        def _():
            r_wo.core_done()
            r_w2[0].z_done(0)
            r_w2[1].y_done()

        @pl.when((i == 1) & is_dec)
        def _():
            r_w1[0].y_done()
            for k in range(1, len(zbits)):
                r_w2[0].z_done(k)

        @pl.when((i == 2) & is_enc)
        def _():
            r_w1[0].y_done()
            r_w2[1].z_done(0, w2_out[1])

        @pl.when((i == 2) & is_dec)
        def _():
            r_w2[1].z_done(0, w2_out[1])
            r_w1[0].z_done(0, w1_out[0])

        @pl.when((i == 3) & is_enc)
        def _():
            for k in range(1, len(zbits)):
                r_w2[0].z_done(k)
            r_w2[1].z_rest(w2_out[1])

        @pl.when((i == 3) & is_dec)
        def _():
            r_w1[1].y_done()
            r_w2[1].z_rest(w2_out[1])

        return 0

    lax.fori_loop(0, 4, self_back, 0)
    for r in range(rows):
        R("xh")[0, r] = acc_ref[pl.ds(r * win, HALO), :].astype(BF16)
        R("xh")[1, r] = acc_ref[pl.ds(r * win + HALO + own, HALO), :].astype(BF16)
    pl.when(t < 3)(dn_right.start)
    pl.when(t > 0)(dn_left.start)
    pl.when(is_dec)(r_c1.core_done)
    for j in range(3):
        r_wa[j].core_done()

    @pl.when(t == 0)
    def _():
        R("dhr")[0] = jnp.zeros((rows, HALO, width), BF16)

    @pl.when(t == 3)
    def _():
        R("dhr")[1] = jnp.zeros((rows, HALO, width), BF16)

    @pl.when(is_enc)
    def _():
        r_w1[1].y_done()
        r_w1[0].z_done(0, w1_out[0])

    @pl.when(is_dec)
    def _():
        r_w1[0].z_rest(w1_out[0])
        r_w1[1].z_done(0, w1_out[1])
        r_c0.y_done()

    pl.when(t > 0)(dn_right.wait_recv)
    pl.when(t < 3)(dn_left.wait_recv)
    for r in range(rows):
        lo, hi = pl.ds(r * win + HALO, HALO), pl.ds(r * win + own, HALO)
        acc_ref[lo, :] += R("dhr")[0, r].astype(F32)
        acc_ref[hi, :] += R("dhr")[1, r].astype(F32)
    total = jnp.zeros((1, width), F32)
    for r in range(rows):
        rs = pl.ds(r * own, own)
        dx, dg = norm_back(x_ref[r].astype(F32), gain0, acc_ref[pl.ds(r * win + HALO, own), :])
        gb_ref[rs, :] = (g_ref[rs, :] + dx).astype(BF16)
        total += dg
    gx_out = links.here(gb_ref, R("gx"))
    gx_out.start()
    R("dgs")[0] = jnp.zeros((8, width), F32)
    R("dgs")[0, pl.ds(0, 1), :] = total
    R("dgs")[0, pl.ds(1, 2), :] = sum(R("dg")[r, pl.ds(1, 2), :] for r in range(rows))
    gain_links[0].start()

    def gain_step(k):
        gain_links[k].wait_recv()
        if k + 1 < len(gain_links):
            R("dgs")[k + 1] = R("dgs")[k] + R("dgr")[k]
            gain_links[k + 1].start()
        else:
            R("dgain")[...] = pltpu.roll(R("dgs")[k] + R("dgr")[k], lax.rem(width - d * (width // dp), width), 1)

    last_gain = len(gain_links) - 1

    @pl.when(is_enc)
    def _():
        r_w1[0].z_rest(w1_out[0])
        gain_step(0)
        r_w1[1].z_done(0, w1_out[1])
        r_wo.y_done()
        r_wa[0].y_done()
        r_w1[1].z_rest(w1_out[1])
        r_wo.z_done(0, R("dwo_o"))
        for k in range(1, last_gain):
            gain_step(k)
        r_wa[1].y_done()
        r_wa[0].z_done(0, wa_out[0])
        r_wo.z_rest(R("dwo_o"))
        r_wa[2].y_done()
        r_wa[1].z_done(0, wa_out[1])
        r_wa[0].z_rest(wa_out[0])
        r_w2[0].y_done(w2_out[0])
        r_wa[2].z_done(0, wa_out[2])
        r_wa[1].z_rest(wa_out[1])
        gain_step(last_gain)
        r_wa[2].z_rest(wa_out[2])

    @pl.when(is_dec)
    def _():
        r_w1[1].z_rest(w1_out[1])
        r_c0.z_done(0, R("dc0"))
        gain_step(0)
        r_wo.y_done()
        r_c0.z_rest(R("dc0"))
        c0_back.start()
        r_c1.y_done()
        r_wo.z_done(0, R("dwo_o"))
        for k in range(1, last_gain):
            gain_step(k)
        r_wa[0].y_done()
        r_c1.z_done(0, R("dc"))
        r_wo.z_rest(R("dwo_o"))
        r_wa[1].y_done()
        r_wa[0].z_done(0, wa_out[0])
        r_c1.z_rest(R("dc"))
        r_wa[2].y_done()
        r_wa[1].z_done(0, wa_out[1])
        r_wa[0].z_rest(wa_out[0])
        r_w2[0].y_done(w2_out[0])
        r_wa[2].z_done(0, wa_out[2])
        r_wa[1].z_rest(wa_out[1])
        gain_step(last_gain)
        r_wa[2].z_rest(wa_out[2])

    sec_out.wait()
    gx_out.wait()
    for g in (g_wa, g_wo, g_w1, g_w2):
        g.finish()
    for g in r_w2 + r_w1 + [r_wo] + r_wa:
        g.finish()
    for c in gain_links:
        c.wait_send()
    pl.when(t < 3)(x_right.wait_send)
    pl.when(t > 0)(x_left.wait_send)
    pl.when(t < 3)(dn_right.wait_send)
    pl.when(t > 0)(dn_left.wait_send)

    @pl.when(is_enc)
    def _():
        c0_x.wait_send()
        for r in range(rows):
            mem_x(r).wait_send()
        c0_back.wait_recv()
        R("dc")[...] = R("dc0r")[...]

    @pl.when(is_dec)
    def _():
        for g in (r_c0, r_c1):
            g.finish()
        for r in range(rows):
            mem_c(r).wait_send()
            pl.when(inner)(mem_t(r).wait_send)
            dm_x(r).wait_send()
        c0_back.wait_send()


def arrange(aligned, sec, gx, dgain, da, dwo, dc, dw1, dw2, sec_o, gx_o, dgain_o, da_o, dwo_o, dc_o, dw1_o, dw2_o):
    share, hw = dwo.shape
    sec_o[...] = sec[...]
    gx_o[...] = gx[...]
    for i in range(3):
        dgain_o[i] = dgain[pl.ds(i, 1), pl.ds(0, share)]
        da_o[i] = da[:, pl.ds(i * hw, hw)]
    for i in range(2):
        dc_o[:, i, :] = dc[:, pl.ds(i * hw, hw)]
    dw1_o[...] = dw1[...]
    dwo_o[...] = dwo[...].T if aligned else dwo[...]
    dw2_o[...] = dw2[...].T if aligned else dw2[...]


def body(embeds, segments, cotangent, norm_gains, attn_in, attn_out, cross_proj, ffn_in, ffn_out):
    dp = lax.axis_size("dp")
    rows, own, width = embeds.shape[1:]
    slots = segments.shape[2]
    hw = attn_in.shape[3]
    fw = ffn_in.shape[2]
    win = own + 2 * HALO
    cwin = 2 * own + 2 * HALO
    tokens = rows * own
    side = 3 * own // 4
    share = width // dp
    zsteps = (dp - 1).bit_length()

    ins = dict(
        x_h=embeds[0], segs_h=segments, gains=norm_gains.transpose(1, 0, 2), cot_h=cotangent.reshape(tokens, width),
        wa_h=attn_in[0].transpose(1, 0, 2), wo_h=attn_out[0], w1_h=ffn_in[0], w2_h=ffn_out[0],
        cx_h=cross_proj[0].reshape(2 * width, hw),
    )
    outs = dict(
        sec=((tokens, width), BF16), gx=((tokens, width), BF16), dgain=((8, width), F32),
        da_o=((share, 3 * hw), F32), dwo_o=((share, hw), F32), dc=((share, 2 * hw), F32),
        dw1_o=((share, fw), F32), dw2_o=((share, fw), F32),
    )
    vm = dict(
        x=((rows, own, width), BF16), cot=((tokens, width), BF16), segs=(segments.shape, jnp.int32),
        wa=((4, width, 3 * hw), BF16), wo=((4, hw, width), BF16), w1=((4, width, fw), BF16), w2=((4, fw, width), BF16),
        c0=((width, 8 * hw), BF16), cqw=((width, 4 * hw), BF16), cow=((width, 4 * hw), BF16),
        xh=((2, rows, HALO, width), BF16), nw=((rows * win, width), BF16),
        q=((4, rows, own, hw), BF16), k=((4, rows, win, hw), BF16), v=((4, rows, win, hw), BF16),
        p=((4, rows, 2, own, win), BF16), o=((tokens, width), BF16), inv=((tokens, width), BF16), bias=((rows, own, win), F32),
        r1=((tokens, width), F32), r2=((tokens, width), F32), n2=((tokens, width), BF16), n3=((tokens, width), BF16),
        u=((4, tokens, fw), BF16), gp=((4, tokens, fw), BF16), secs=((tokens, width), BF16),
        acc=((rows * win, width), F32), g=((tokens, width), F32), gb=((tokens, width), BF16), do=((tokens, width), BF16),
        memf=((max(rows * slots, 4 * width), max(width, fw)), BF16), kv=((slots, 8 * hw), BF16), cq=((tokens, width), BF16),
        cp=((max(8 * own, 4 * width), cwin), BF16), cinv=((own, width), BF16), oc=((tokens, width), BF16),
        cols=((rows, own, 128), F32), keys=((rows, 8, cwin), F32),
        dkv=((rows * cwin, 8 * hw), BF16), dmf=((max(rows * slots, 4 * width), max(width, fw)), BF16),
        rcc=((rows, own, width), BF16), rct=((rows, side, width), BF16), dm=((rows, own, width), BF16),
        dg=((rows, 8, width), F32),
        dqkv=((rows * win, 3 * hw), BF16), dhr=((2, rows, HALO, width), BF16),
        dgs=((2 + zsteps, 8, width), F32), dgr=((2 + zsteps, 8, width), F32),
        dw2=((4 * width, fw), BF16), dwo=((width, 4 * hw), BF16),
        dc0=((share, 2 * hw), F32), dc0r=((share, 2 * hw), F32),
    )
    sums = dict(w20=fw // 2, w21=fw // 2, w10=fw // 2, w11=fw // 2, wo=hw, wa0=hw, wa1=hw, wa2=hw, c0=2 * hw, c1=2 * hw)
    for name, m in sums.items():
        shards = 2 if name == "w20" else 1
        vm["rc_" + name] = ((2, width, m), BF16)
        vm["ry_" + name] = ((share if shards == 2 else width, m), BF16)
        vm["zb_" + name] = ((shards, dp, share, m), BF16)
        for k in range(zsteps):
            vm[f"zr{k}_{name}"] = ((shards, dp >> (k + 1), share, m), BF16)
    copies = 150 + 12 * zsteps
    sems = dict(send=pltpu.SemaphoreType.DMA((copies,)), recv=pltpu.SemaphoreType.DMA((copies,)), local=pltpu.SemaphoreType.DMA((16,)))
    in_hbm = {n for n in ins if n.endswith("_h")}
    out_hbm = {"sec", "gx"}
    results = pl.pallas_call(
        functools.partial(layers, list(ins) + list(outs) + list(vm) + list(sems)),
        name="layers",
        out_shape=[jax.ShapeDtypeStruct(*o) for o in outs.values()],
        in_specs=[pl.BlockSpec(memory_space=pl.ANY if n in in_hbm else pltpu.VMEM) for n in ins],
        out_specs=[pl.BlockSpec(memory_space=pl.ANY if n in out_hbm else pltpu.VMEM) for n in outs],
        scratch_shapes=[pltpu.VMEM(*s) for s in vm.values()] + list(sems.values()),
        compiler_params=pltpu.CompilerParams(vmem_limit_bytes=VMEM_LIMIT, collective_id=0, has_side_effects=True),
    )(*ins.values())
    aligned = share % 128 == 0
    flat, turned = (share, hw), (hw, share)
    sec, gx, dgain, da, dwo, dc, dw1, dw2 = pl.pallas_call(
        functools.partial(arrange, aligned),
        name="arrange",
        out_shape=[
            jax.ShapeDtypeStruct((tokens, width), BF16),
            jax.ShapeDtypeStruct((tokens, width), BF16),
            jax.ShapeDtypeStruct((3, 1, share), F32),
            jax.ShapeDtypeStruct((3, share, hw), F32),
            jax.ShapeDtypeStruct((hw, share) if aligned else (share, hw), F32),
            jax.ShapeDtypeStruct((share, 2, hw), F32),
            jax.ShapeDtypeStruct((share, fw), F32),
            jax.ShapeDtypeStruct((fw, share) if aligned else (share, fw), F32),
        ],
        in_specs=[pl.BlockSpec(memory_space=pltpu.VMEM)] * 8,
        out_specs=[pl.BlockSpec(memory_space=pltpu.VMEM)] * 8,
    )(*results)
    if not aligned:
        dwo, dw2 = dwo.T, dw2.T
    return (
        sec.reshape(1, rows, own, width), gx.reshape(1, rows, own, width), dgain.transpose(1, 0, 2),
        da.transpose(1, 0, 2)[None], dwo[None], dc[None], dw1[None], dw2[None],
    )


def solution(mesh):
    return jax.shard_map(
        body,
        mesh=mesh,
        in_specs=(
            P("pipe", "dp", "tensor", None),
            P(None, "dp", None),
            P("dp", "tensor", None),
            P("pipe", None, None),
            P("pipe", None, None, "tensor"),
            P("pipe", "tensor", None),
            P("pipe", None, None, "tensor"),
            P("pipe", None, "tensor"),
            P("pipe", "tensor", None),
        ),
        out_specs=(
            P("pipe", "dp", "tensor", None),
            P("pipe", "dp", "tensor", None),
            P("pipe", None, "dp"),
            P("pipe", "dp", None, "tensor"),
            P("pipe", "tensor", "dp"),
            P("pipe", "dp", None, "tensor"),
            P("pipe", "dp", "tensor"),
            P("pipe", "tensor", "dp"),
        ),
        check_vma=False,
    )
```

```python
import functools

import jax
import jax.numpy as jnp
from jax import lax
from jax.experimental import pallas as pl
from jax.experimental.pallas import tpu as pltpu
from jax.sharding import PartitionSpec as P

EPS = 1e-05
MASKED = -1000000000.0
DH = 64
HALO = 64
F32 = jnp.float32
BF16 = jnp.bfloat16
GELU_C = 0.7978845608028654
GELU_A = 0.044715
MESH = pl.DeviceIdType.MESH
VMEM_LIMIT = 63 << 20


def mm(a, b):
    return lax.dot_general(a, b, (((1,), (0,)), ((), ())), preferred_element_type=F32)


def mm_nt(a, b):
    return lax.dot_general(a, b, (((1,), (1,)), ((), ())), preferred_element_type=F32)


def mm_tn(a, b):
    return lax.dot_general(a, b, (((0,), (0,)), ((), ())), preferred_element_type=F32)


def norm_parts(v):
    c = v - jnp.mean(v, axis=-1, keepdims=True)
    r = lax.rsqrt(jnp.mean(c * c, axis=-1, keepdims=True) + EPS)
    return c * r, r


def norm(v, gain):
    xhat, _ = norm_parts(v)
    return xhat * gain


def norm_back(v, gain, dn):
    xhat, r = norm_parts(v)
    dxh = dn * gain
    m1 = jnp.mean(dxh, axis=-1, keepdims=True)
    m2 = jnp.mean(dxh * xhat, axis=-1, keepdims=True)
    return r * (dxh - m1 - xhat * m2), jnp.sum(dn * xhat, axis=0, keepdims=True)


def lane_low(shape):
    return lax.broadcasted_iota(jnp.int32, shape, 1) < DH


def pair_join(a, b):
    return jnp.where(lane_low(a.shape), a, b)


def swap_halves(v):
    return pltpu.roll(v, DH, 1)


def attend(q2, k2, v2, mask, keep):
    low, lowq = lane_low(v2.shape), lane_low(q2.shape)
    one, zero = jnp.ones_like(v2), jnp.zeros_like(q2)
    outs = []
    for h in range(2):
        qh = jnp.where(lowq, q2, zero) if h == 0 else jnp.where(lowq, zero, q2)
        s = mask(mm_nt(qh, k2))
        e = jnp.exp(s - jnp.max(s, axis=-1, keepdims=True)).astype(BF16)
        keep(h, e)
        outs.append(mm(e, jnp.where(low, v2, one) if h == 0 else jnp.where(low, one, v2)))
    inv = 1.0 / swap_halves(pair_join(outs[1], outs[0]))
    return pair_join(*outs) * inv, inv


def attend_back(q2, k2, v2, do2, o2, inv, kept):
    low, lowq = lane_low(v2.shape), lane_low(q2.shape)
    one = jnp.ones_like(v2)
    scaled = do2.astype(F32) * inv.astype(F32)
    dob = scaled.astype(BF16)
    minus = (-swap_halves(dob.astype(F32) * o2.astype(F32))).astype(BF16)
    q_t, do_t = q2.T, dob.T
    dq, dk, dv = [], [], []
    for h in range(2):
        e = kept(h)
        rows = slice(h * DH, (h + 1) * DH)
        lhs = jnp.where(lowq, dob, minus) if h == 0 else jnp.where(lowq, minus, dob)
        dp = mm_nt(lhs, jnp.where(low, v2, one) if h == 0 else jnp.where(low, one, v2))
        ds = (dp * e.astype(F32)).astype(BF16)
        dq.append(mm(ds, k2))
        dv.append(mm(do_t[rows], e).astype(BF16))
        dk.append(mm(q_t[rows], ds).astype(BF16))
    return (pair_join(*dq) * (DH**-0.5)).astype(BF16), jnp.concatenate(dk, 0).T, jnp.concatenate(dv, 0).T


def gelu_parts(h):
    h2 = h * h
    half = 0.5 + 0.5 * jnp.tanh(h * (GELU_C + (GELU_C * GELU_A) * h2))
    u = h * half
    slope = half + u * ((1.0 - half) * (2.0 * GELU_C + (6.0 * GELU_C * GELU_A) * h2))
    return u, slope


def flip(i, bit):
    return i + bit - 2 * bit * lax.rem(lax.div(i, bit), 2)


def bit_of(i, bit):
    return lax.rem(lax.div(i, bit), 2)


def reversed_bits(i, count):
    out, bit = 0, 1
    while bit < count:
        out = 2 * out + (i // bit) % 2
        bit *= 2
    return out


class Links:
    def __init__(self, send, recv, local):
        self.send, self.recv, self.local = send, recv, local
        self.n = self.m = 0
        self.sent = []

    def take(self, count=1):
        self.n += count
        return self.n - count

    def remote(self, src, dst, device, at=None):
        at = self.take() if at is None else at
        return pltpu.make_async_remote_copy(
            src_ref=src, dst_ref=dst, send_sem=self.send.at[at], recv_sem=self.recv.at[at],
            device_id=device, device_id_type=MESH,
        )

    def here(self, src, dst):
        self.m += 1
        return pltpu.make_async_copy(src, dst, self.local.at[self.m - 1])


class Gather:
    def __init__(self, links, src, slot, depth, at, pieces=1, planes=None):
        t, t2 = at["t"], at["t2"]
        half = depth // 2
        n = half // pieces
        whole = pl.ds(0, depth)
        if src is None:
            self.own = []
        elif planes is None:
            self.own = [links.here(src, slot(t, whole))]
        else:
            self.own = [links.here(src.at[i], slot(t, whole, i)) for i in range(planes)]
        self.inner = src is None or planes is not None
        src = slot(t, whole) if self.inner else src
        self.core = links.remote(src, slot(t, whole), at["C"])
        self.over_y, self.over_z, self.core_a, self.core_b = [], [], [], []
        for i in range(pieces):
            mine = pl.ds(pl.multiple_of(at["b"] * half + i * n, n), n)
            other = pl.ds(pl.multiple_of((1 - at["b"]) * half + i * n, n), n)
            self.over_y.append(links.remote(src.at[mine], slot(t, mine), at["Y"]))
            self.over_z.append(links.remote(slot(t2, mine), slot(t2, mine), at["Z"][0]))
            self.core_a.append(links.remote(slot(t2, mine), slot(t2, mine), at["C"]))
            self.core_b.append(links.remote(slot(t2, other), slot(t2, other), at["C"]))

    def start(self):
        for c in self.own:
            c.start()
        if self.inner:
            for c in self.own:
                c.wait()
        for c in self.over_y:
            c.start()
        self.core.start()

    def step1(self, i=0):
        self.over_y[i].wait_recv()
        self.over_z[i].start()
        self.core_a[i].start()

    def step2(self, i=0):
        self.over_z[i].wait_recv()
        self.core_b[i].start()

    def ready(self, i):
        if i == 0 and not self.inner:
            for c in self.own:
                c.wait()
        if i == 1:
            self.core.wait_recv()
        if i == 3:
            for c in self.core_a + self.core_b:
                c.wait_recv()

    def finish(self):
        for c in [self.core] + self.over_y + self.over_z + self.core_a + self.core_b:
            c.wait_send()


class Reduce:
    def __init__(self, links, part, rc, ry, zb, zr, at, y_first):
        self.part, self.at, self.y_first = part, at, y_first
        self.rc, self.ry, self.zb, self.zr = rc, ry, zb, zr
        self.n = zb.shape[0]
        self.dp, self.rows = zb.shape[1:3]
        self.core = [links.remote(part(at[f]), rc.at[j], at["C"]) for j, f in enumerate(("t1", "t3"))]
        self.over_z, self.kept = [], []
        off, m, bit, k = 0, self.dp, 1, 0
        while m > 1:
            m //= 2
            b = bit_of(at["d"], bit)
            keep, give = off + b * m, off + (1 - b) * m
            self.over_z.append(links.remote(zb.at[:, pl.ds(give, m)], zr[k], at["Z"][k]))
            self.kept.append((keep, m))
            off, bit, k = keep, 2 * bit, k + 1
        self.off = off
        self.over_y = links.remote(part(at["t2"]) if y_first else zb.at[1, off], ry, at["Y"])

    def core_send(self, j):
        self.core[j].start()

    def into_zb(self, j, mine, theirs):
        for i in range(self.dp):
            where = pl.ds(i * self.rows, self.rows)
            self.zb[j, reversed_bits(i, self.dp)] = (mine[where, :].astype(F32) + theirs[where, :].astype(F32)).astype(BF16)

    def core_done(self):
        self.core[0].wait_recv()
        self.core[1].wait_recv()
        far, near = self.part(self.at["t2"]), self.part(self.at["t"])
        if self.y_first:
            far[...] = (far[...].astype(F32) + self.rc[1].astype(F32)).astype(BF16)
            self.over_y.start()
            near[...] = (near[...].astype(F32) + self.rc[0].astype(F32)).astype(BF16)
        else:
            self.into_zb(0, near, self.rc.at[0])
            self.into_zb(1, far, self.rc.at[1])
            self.over_z[0].start()

    def y_done(self, out=None):
        self.over_y.wait_recv()
        if self.y_first:
            self.into_zb(0, self.part(self.at["t"]), self.ry)
            self.over_z[0].start()
        else:
            out[...] = self.zb[0, self.off].astype(F32) + self.ry[...].astype(F32)

    def z_done(self, k, out=None):
        self.over_z[k].wait_recv()
        keep, m = self.kept[k]
        last = k == len(self.over_z) - 1
        if last and self.y_first:
            out[...] = self.zb[0, keep].astype(F32) + self.zr[k][0, 0].astype(F32)
        else:
            for j in range(self.n):
                live = self.zb.at[j, pl.ds(keep, m)]
                live[...] = (live[...].astype(F32) + self.zr[k][j].astype(F32)).astype(BF16)
            (self.over_y if last else self.over_z[k + 1]).start()

    def z_rest(self, out=None):
        for k in range(1, len(self.over_z)):
            self.z_done(k, out)

    def finish(self):
        for c in self.core + [self.over_y] + self.over_z:
            c.wait_send()


def layers(names, *refs):
    ref = dict(zip(names, refs))
    R = lambda name: ref[name]
    p, d, t = lax.axis_index("pipe"), lax.axis_index("dp"), lax.axis_index("tensor")
    is_enc, is_dec = p == 0, p == 1
    dp = lax.axis_size("dp")
    t1, t2, t3 = flip(t, 1), flip(t, 2), 3 - t
    zbits = []
    while 2 ** len(zbits) < dp:
        zbits.append((p, flip(d, 2 ** len(zbits)), t))
    at = dict(t=t, t1=t1, t2=t2, t3=t3, d=d, b=bit_of(d, 1), C=(p, d, t1), Y=(p, d, t2), T=(p, d, t3), X=(1 - p, d, t), Z=zbits)
    rows, own, width = R("x").shape
    win, cwin = own + 2 * HALO, 2 * own + 2 * HALO
    slots = 4 * own
    tokens = rows * own
    hw = R("wa").shape[2] // 3
    fw = R("w1").shape[2]
    inner = t % 3 != 0
    scale = jnp.asarray(DH**-0.5, BF16)
    gain_ref, x_ref = R("gains"), R("x")
    side = 3 * own // 4

    def rowsl(r, n=own):
        return pl.ds(pl.multiple_of(r * n, n), n)

    def lanes(s, n=hw):
        return pl.ds(pl.multiple_of(s * n, n), n)

    def far_lanes(s):
        return pl.ds(pl.multiple_of(s * 2 * hw + hw, hw), hw)

    def in_row(r, span):
        return pl.ds(pl.multiple_of(r * slots + span.start, HALO), span.size)

    def near_first(i):
        return 2 * lax.rem(lax.div(t, 2) + lax.div(i, 2), 2) + lax.rem(lax.rem(t, 2) + lax.rem(i, 2), 2)

    def far_first(i):
        return 2 * lax.rem(lax.div(t, 2) + lax.rem(lax.div(i + 1, 2), 2), 2) + lax.rem(lax.rem(t, 2) + 1 - lax.div(i, 2), 2)

    def seg_row(side_, r, start):
        row = jnp.broadcast_to(R("segs")[side_, pl.ds(r, 1), :].astype(F32), (8, slots))
        return pltpu.roll(row, lax.rem(2 * slots - start, slots), 1)

    def seg_column(side_, r):
        row = seg_row(side_, r, t * own)[:1, :own]
        return jnp.broadcast_to(row, (128, own)).T

    def spread(column, n):
        return jnp.concatenate([column] * (n // 128), axis=1)

    links = Links(R("send"), R("recv"), R("local"))

    def by_shard(name, n=None):
        def slot(s, span, i=None):
            full = R(name).at[s, span]
            return full if i is None else full.at[:, pl.ds(i * n, n)]

        return slot

    def by_columns(name, n, row):
        def slot(s, span):
            return R(name).at[pl.ds(pl.multiple_of(span.start + row, HALO), span.size), lanes(s, n)]

        return slot

    g_wa = Gather(links, R("wa_h"), by_shard("wa", hw), width, at, 2, 3)
    g_wo = Gather(links, R("wo_h"), by_shard("wo"), hw, at)
    g_w1 = Gather(links, R("w1_h"), by_shard("w1"), width, at, 2)
    g_w2 = Gather(links, R("w2_h"), by_shard("w2"), fw, at, 4)
    g_c1 = Gather(links, R("cx_h"), by_columns("dmf", hw, 0), 2 * width, at)
    c0_x = links.remote(R("cx_h"), R("dmf").at[pl.ds(2 * width, 2 * width), lanes(t)], at["X"])
    g_c0 = Gather(links, None, by_columns("dmf", hw, 2 * width), 2 * width, at)
    loads = [links.here(R(n + "_h"), R(n)) for n in ("x", "cot", "segs")]
    x_right = links.remote(R("x_h").at[:, pl.ds(own - HALO, HALO)], R("xh").at[0], (p, d, lax.rem(t + 1, 4)))
    x_left = links.remote(R("x_h").at[:, pl.ds(0, HALO)], R("xh").at[1], (p, d, lax.rem(t + 3, 4)))
    base_mem, base_memc, base_memt = links.take(rows), links.take(rows), links.take(rows)
    base_dmc, base_dmt, base_dmx = links.take(rows), links.take(rows), links.take(rows)
    block = pl.ds(pl.multiple_of(t * own, own), own)
    block1 = pl.ds(pl.multiple_of(t1 * own, own), own)
    edge_out = pl.ds(pl.multiple_of(lax.rem(own // 2 + side * t, slots), HALO), side)
    edge_in = pl.ds(pl.multiple_of(lax.rem(own // 2 + side * t3, slots), HALO), side)

    def mem_x(r):
        return links.remote(R("secs").at[rowsl(r)], R("memf").at[in_row(r, block)], at["X"], base_mem + r)

    def mem_c(r):
        return links.remote(R("memf").at[in_row(r, block)], R("memf").at[in_row(r, block)], at["C"], base_memc + r)

    def mem_t(r):
        return links.remote(R("memf").at[in_row(r, edge_out)], R("memf").at[in_row(r, edge_out)], at["T"], base_memt + r)

    def dm_rows(r, span):
        return R("dmf").at[in_row(r, span)]

    def dm_c(r):
        return links.remote(dm_rows(r, block1), R("rcc").at[r], at["C"], base_dmc + r)

    def dm_t(r):
        return links.remote(dm_rows(r, edge_in), R("rct").at[r], at["T"], base_dmt + r)

    def dm_x(r):
        return links.remote(R("rcc").at[r], R("rcc").at[r], at["X"], base_dmx + r)

    def by_rows(name, m, col=0):
        return lambda s: R(name).at[pl.ds(pl.multiple_of(s * width, width), width), pl.ds(col, m)]

    def by_lanes(name, m, row=0):
        return lambda s: R(name).at[pl.ds(row, width), lanes(s, m)]

    def reduce_of(name, part, y_first=True):
        zr = [R(f"zr{k}_{name}") for k in range(len(zbits))]
        return Reduce(links, part, R("rc_" + name), R("ry_" + name), R("zb_" + name), zr, at, y_first)

    fh = fw // 2
    r_w2 = [reduce_of(f"w2{j}", by_rows("dw2", fh, j * fh), j == 1) for j in range(2)]
    r_w1 = [reduce_of(f"w1{j}", by_rows("dmf", fh, j * fh), j == 0) for j in range(2)]
    r_wo = reduce_of("wo", by_lanes("dwo", hw))
    r_wa = [reduce_of(f"wa{j}", by_rows("cp", hw, j * hw)) for j in range(3)]
    r_c0 = reduce_of("c0", by_lanes("kv", 2 * hw))
    r_c1 = reduce_of("c1", by_lanes("kv", 2 * hw, width))
    w2_out = [R("dw2_o").at[:, pl.ds(j * fh, fh)] for j in range(2)]
    w1_out = [R("dw1_o").at[:, pl.ds(j * fh, fh)] for j in range(2)]
    wa_out = [R("da_o").at[:, pl.ds(j * hw, hw)] for j in range(3)]
    c0_back = links.remote(R("dc0"), R("dc0r"), at["X"])
    dn_right = links.remote(R("xh").at[1], R("dhr").at[0], (p, d, lax.rem(t + 1, 4)))
    dn_left = links.remote(R("xh").at[0], R("dhr").at[1], (p, d, lax.rem(t + 3, 4)))
    gain_over_t = [links.remote(R("dgt").at[t], R("dgt").at[t], at[f]) for f in ("C", "Y", "T")]
    gain_over_d = []
    for k in range(1, dp):
        to = lax.rem(d + k, dp)
        gain_over_d.append(links.remote(R("dgd").at[d], R("dgd").at[d], (p, to, t)))

    @pl.when(is_dec)
    def _():
        for at_t, start in ((0, 2 * own), (1, 2 * own + side), (3, 2 * own - 2 * HALO)):
            @pl.when(t == at_t)
            def _():
                for r in range(rows):
                    R("memf")[pl.ds(r * slots + start, 2 * HALO), :] = jnp.zeros((2 * HALO, width), BF16)

    for c in loads:
        c.start()
    barrier = pltpu.get_barrier_semaphore()
    partners = [at["C"], at["Y"], at["T"], at["X"]] + [(p, lax.rem(d + k, dp), t) for k in range(1, dp)]
    for dev in partners:
        pl.semaphore_signal(barrier, inc=1, device_id=dev, device_id_type=MESH)
    pl.semaphore_wait(barrier, len(partners))

    pl.when(t < 3)(x_right.start)
    pl.when(t > 0)(x_left.start)
    g_wa.start()
    g_wo.start()

    @pl.when(is_enc)
    def _():
        c0_x.start()
        g_w1.start()
        g_w2.start()

    @pl.when(is_dec)
    def _():
        g_c1.start()

    for c in loads:
        c.wait()

    nw_ref, bias_ref = R("nw"), R("bias")
    gain0, gain1, gain2 = gain_ref[0], gain_ref[1], gain_ref[2]
    for r in range(rows):
        nw_ref[pl.ds(r * win + HALO, own), :] = norm(x_ref[r].astype(F32), gain0).astype(BF16)
        keys = seg_row(p, r, lax.rem(t * own + slots - HALO, slots))[:1, :win]
        same = spread(seg_column(p, r), win) == keys
        qpos = lax.broadcasted_iota(jnp.int32, (own, win), 0)
        kpos = lax.broadcasted_iota(jnp.int32, (own, win), 1) - HALO
        before = kpos - qpos <= jnp.where(is_enc, 4 * win, 0)
        bias_ref[r] = jnp.where(same & before, 0.0, MASKED)

    @pl.when(t == 0)
    def _():
        R("xh")[0] = jnp.zeros((rows, HALO, width), BF16)

    @pl.when(t == 3)
    def _():
        R("xh")[1] = jnp.zeros((rows, HALO, width), BF16)

    pl.when(t > 0)(x_right.wait_recv)
    pl.when(t < 3)(x_left.wait_recv)
    for r in range(rows):
        nw_ref[pl.ds(r * win, HALO), :] = norm(R("xh")[0, r].astype(F32), gain0).astype(BF16)
        nw_ref[pl.ds(r * win + HALO + own, HALO), :] = norm(R("xh")[1, r].astype(F32), gain0).astype(BF16)

    def after_pair(i):
        @pl.when(i == 0)
        def _():
            g_wa.step1(0)

        @pl.when(i == 1)
        def _():
            g_wa.step1(1)
            g_wo.step1()
            g_wa.step2(0)

            @pl.when(is_dec)
            def _():
                c0_x.wait_recv()
                g_c0.start()
                g_w2.start()
                g_w1.start()
                g_c1.step1()

            pl.when(is_enc)(lambda: g_w1.step1(0))
            g_wa.step2(1)

        @pl.when(i == 2)
        def _():
            g_wo.step2()
            pl.when(is_enc)(lambda: g_w1.step1(1))

        @pl.when(i == 3)
        def _():
            pl.when(is_dec)(g_c0.step1)

    def wait_ready(i, *weights):
        for k in range(4):
            @pl.when(i == k)
            def _():
                for w in weights:
                    w.ready(k)

    q_ref, k_ref, v_ref, p_ref, o_ref, inv_ref = R("q"), R("k"), R("v"), R("p"), R("o"), R("inv")

    def self_pair(i, _):
        s = near_first(i)
        wait_ready(i, g_wa)
        packed = mm(nw_ref[...], R("wa")[s])
        for r in range(rows):
            q_ref[s, r] = packed[r * win + HALO : r * win + HALO + own, :hw].astype(BF16) * scale
            k_ref[s, r] = packed[r * win : (r + 1) * win, hw : 2 * hw].astype(BF16)
            v_ref[s, r] = packed[r * win : (r + 1) * win, 2 * hw :].astype(BF16)
        for r in range(rows):
            def keep(h, e):
                p_ref[s, r, h] = e

            o2, inv = attend(q_ref[s, r], k_ref[s, r], v_ref[s, r], lambda scores: scores + bias_ref[r], keep)
            o_ref[pl.ds(r * own, own), lanes(s)] = o2.astype(BF16)
            inv_ref[pl.ds(r * own, own), lanes(s)] = inv.astype(BF16)
        after_pair(i)
        return 0

    lax.fori_loop(0, 4, self_pair, 0)
    for k in range(4):
        g_wo.ready(k)
    r1_ref, r2_ref, n2_ref, n3_ref = R("r1"), R("r2"), R("n2"), R("n3")
    u_ref, gp_ref, sec_ref = R("u"), R("gp"), R("secs")
    acc_ref, g_ref, gb_ref, do_ref = R("acc"), R("g"), R("gb"), R("do")
    first = mm(o_ref[...], R("wo")[...].reshape(4 * hw, width))
    for r in range(rows):
        r1_ref[pl.ds(r * own, own), :] = x_ref[r].astype(F32) + first[r * own : (r + 1) * own]
    n2_ref[...] = norm(r1_ref[...], gain1).astype(BF16)

    @pl.when(is_enc)
    def _():
        r2_ref[...] = r1_ref[...]

        def up(i):
            s = near_first(i)
            u, gp = gelu_parts(mm(n2_ref[...], R("w1")[s]))
            u_ref[s] = u.astype(BF16)
            gp_ref[s] = gp.astype(BF16)
            return s

        g_w2.step1(0)
        g_w1.step2(0)

        def near(i, _):
            wait_ready(i, g_w1, g_w2)
            s = up(i)
            r2_ref[...] += mm(u_ref[s], R("w2")[s])

            @pl.when(i == 0)
            def _():
                g_w2.step1(1)
                g_w1.step2(1)

            @pl.when(i == 1)
            def _():
                g_w2.step1(2)
                g_w2.step2(0)
                g_w2.step1(3)

            return 0

        lax.fori_loop(0, 2, near, 0)

        def far(i, _):
            wait_ready(i, g_w1)
            up(i)
            pl.when(i == 2)(lambda: g_w2.step2(1))

            @pl.when(i == 3)
            def _():
                g_w2.step2(2)
                g_w2.step2(3)

            return 0

        lax.fori_loop(2, 4, far, 0)
        g_w2.ready(3)
        far1, far2 = near_first(2), near_first(3)

        def row(r, _):
            rs = rowsl(r)
            total = r2_ref[rs, :] + mm(u_ref[far1, rs, :], R("w2")[far1]) + mm(u_ref[far2, rs, :], R("w2")[far2])
            r2_ref[rs, :] = total
            sec_ref[rs, :] = norm(total, gain2).astype(BF16)
            mem_x(r).start()
            return 0

        lax.fori_loop(0, rows, row, 0)

    def sends(reductions, i):
        for j in range(2):
            @pl.when(i == j)
            def _():
                for reduction in reductions:
                    reduction.core_send(j)

    cstart = pl.multiple_of(jnp.minimum(t * (own - HALO), slots - cwin), HALO)
    cwindow = pl.ds(cstart, cwin)
    kv_ref, cq_ref, cp_ref, dkv_ref, cinv_ref = R("kv"), R("cq"), R("cp"), R("dkv"), R("cinv")
    c0_ref, cqw_ref, cow_ref, oc_ref, cot_ref = R("c0"), R("cqw"), R("cow"), R("oc"), R("cot")
    cols, keys_ref = R("cols"), R("keys")
    half = 4 * hw

    @pl.when(is_dec)
    def _():
        g_w2.step1(0)
        g_c1.step2()
        for k in range(4):
            g_c1.ready(k)
        pick_shape = (width // 4, width // 2)
        twice = 2 * lax.broadcasted_iota(jnp.int32, pick_shape, 0)
        at_col = lax.broadcasted_iota(jnp.int32, pick_shape, 1)
        picks = [jnp.where(at_col == twice + j, 1.0, 0.0).astype(BF16) for j in range(2)]

        def unweave(base, m):
            return [mm(pick, R("dmf")[pl.ds(base + m * (width // 2), width // 2), :]).astype(BF16) for pick in picks]

        for m in range(4):
            span = pl.ds(m * (width // 4), width // 4)
            cqw_ref[span, :], cow_ref[span, :] = unweave(0, m)
        cq_ref[...] = mm(n2_ref[...], cqw_ref[...]).astype(BF16) * scale
        g_w2.step1(1)
        g_c0.step2()
        g_w2.step1(2)
        g_w2.step1(3)
        kv_ref[...] = jnp.zeros_like(kv_ref)
        for r in range(rows):
            cols[r] = seg_column(1, r)
            keys_ref[r] = seg_row(0, r, cstart)[:, :cwin]
        for k in range(4):
            g_c0.ready(k)
        for m in range(4):
            span = pl.ds(m * (width // 4), width // 4)
            ck, cv = unweave(2 * width, m)
            for s in range(4):
                c0_ref[span, 2 * s * hw : (2 * s + 1) * hw] = ck[:, s * hw : (s + 1) * hw]
                c0_ref[span, (2 * s + 1) * hw : (2 * s + 2) * hw] = cv[:, s * hw : (s + 1) * hw]
        g_w1.step1(0)
        g_w2.step2(0)
        g_w2.step2(1)
        for g in (g_c1, g_c0):
            g.finish()
        R("dmf")[...] = jnp.zeros_like(R("dmf"))
        g_w1.step1(1)
        g_w2.step2(2)
        g_w2.step2(3)
        for k in range(4):
            g_w2.ready(k)

        def early(s, _):
            gp_ref[s] = mm_nt(cot_ref[...], R("w2")[s]).astype(BF16)
            return 0

        lax.fori_loop(0, 4, early, 0)
        g_w1.step2(0)
        g_w1.step2(1)
        for k in range(4):
            g_w1.ready(k)

        def settle(r):
            span = pl.ds(0, own)
            dm_c(r).wait_recv()
            acc_ref[span, :] = R("dmf")[in_row(r, block), :].astype(F32) + R("rcc")[r].astype(F32)

            @pl.when(inner)
            def _():
                dm_t(r).wait_recv()
                place = pl.ds(pl.multiple_of((2 - t) * (own - side), HALO), side)
                acc_ref[place, :] += R("rct")[r].astype(F32)

            R("rcc")[r] = acc_ref[span, :].astype(BF16)
            dm_x(r).start()

        def row(r, _):
            rs = rowsl(r)

            def project(span):
                for j in range(2):
                    kv = mm(R("memf")[in_row(r, span), :], c0_ref[:, j * half : (j + 1) * half])
                    kv_ref[span, j * half : (j + 1) * half] = kv.astype(BF16)

            mem_x(r).wait_recv()
            mem_c(r).start()
            pl.when(inner)(mem_t(r).start)
            project(block)
            mem_c(r).wait_recv()
            project(block1)

            @pl.when(inner)
            def _():
                mem_t(r).wait_recv()
                project(edge_in)

            def cross(i, _):
                for s in (2 * i, 2 * i + 1):
                    def keep(h, e):
                        cp_ref[rowsl(2 * s + h), :] = e

                    def mask(scores):
                        same = spread(cols[r], cwin) == keys_ref[r, pl.ds(0, 1), :]
                        return jnp.where(same, scores, MASKED)

                    o2, inv = attend(cq_ref[rs, lanes(s)], kv_ref[cwindow, lanes(2 * s)], kv_ref[cwindow, lanes(2 * s + 1)], mask, keep)
                    oc_ref[rs, lanes(s)] = o2.astype(BF16)
                    cinv_ref[:, lanes(s)] = inv.astype(BF16)
                return 0

            lax.fori_loop(0, 2, cross, 0)
            pl.when(r > 0)(lambda: settle(r - 1))
            r2_ref[rs, :] = r1_ref[rs, :] + mm_nt(oc_ref[rs, :], cow_ref[...])
            n3_ref[rs, :] = norm(r2_ref[rs, :], gain2).astype(BF16)
            dn = pl.ds(0, own)
            acc_ref[dn, :] = jnp.zeros((own, width), F32)
            g_ref[rs, :] = r2_ref[rs, :]

            def feed(s, _):
                u, gp = gelu_parts(mm(n3_ref[rs, :], R("w1")[s]))
                u = u.astype(BF16)
                u_ref[s, rs, :] = u
                g_ref[rs, :] += mm(u, R("w2")[s])
                dh = (gp_ref[s, rs, :].astype(F32) * gp).astype(BF16)
                gp_ref[s, rs, :] = dh
                acc_ref[dn, :] += mm_nt(dh, R("w1")[s])
                return 0

            lax.fori_loop(0, 4, feed, 0)
            sec_ref[rs, :] = g_ref[rs, :].astype(BF16)
            dx, dg = norm_back(r2_ref[rs, :], gain2, acc_ref[dn, :])
            R("dg")[r, pl.ds(2, 1), :] = dg
            g2 = cot_ref[rs, :].astype(F32) + dx
            g_ref[rs, :] = g2
            gb_ref[rs, :] = g2.astype(BF16)
            do_ref[rs, :] = mm(gb_ref[rs, :], cow_ref[...]).astype(BF16)
            ws = pl.ds(pl.multiple_of(r * cwin, HALO), cwin)

            def back(i, _):
                for s in (2 * i, 2 * i + 1):
                    dq, dk, dv = attend_back(
                        cq_ref[rs, lanes(s)], kv_ref[cwindow, lanes(2 * s)], kv_ref[cwindow, lanes(2 * s + 1)],
                        do_ref[rs, lanes(s)], oc_ref[rs, lanes(s)], cinv_ref[:, lanes(s)], lambda h: cp_ref[rowsl(2 * s + h), :],
                    )
                    cq_ref[rs, lanes(s)] = dq
                    dkv_ref[ws, lanes(2 * s)] = dk
                    dkv_ref[ws, lanes(2 * s + 1)] = dv
                return 0

            lax.fori_loop(0, 2, back, 0)
            R("dmf")[in_row(r, cwindow), :] = mm_nt(dkv_ref[ws, :], c0_ref[...]).astype(BF16)
            dm_c(r).start()
            pl.when(inner)(dm_t(r).start)

            @pl.when(r == rows - 1)
            def _():
                def w2_grad(i, _):
                    s = far_first(i)
                    R("dw2")[rowsl(s, width), :] = mm_tn(cot_ref[...], u_ref[s]).astype(BF16)
                    sends(r_w2, i)
                    return 0

                lax.fori_loop(0, 4, w2_grad, 0)
                settle(r)

            dx, dg = norm_back(r1_ref[rs, :], gain1, mm_nt(cq_ref[rs, :], cqw_ref[...]))
            R("dg")[r, pl.ds(1, 1), :] = dg
            g_ref[rs, :] += dx
            return 0

        lax.fori_loop(0, rows, row, 0)
        for r in range(rows):
            dm_c(r).wait_send()
            pl.when(inner)(dm_t(r).wait_send)

        def w1_grad(i, _):
            s = far_first(i)
            R("dmf")[rowsl(s, width), :] = mm_tn(n3_ref[...], gp_ref[s]).astype(BF16)
            sends(r_w1, i)

            @pl.when(i == 0)
            def _():
                r_w2[0].core_done()
                r_w2[1].core_done()

            return 0

        lax.fori_loop(0, 4, w1_grad, 0)

        def c0_grad(i, _):
            s = far_first(i)
            total = mm_tn(R("memf")[in_row(0, cwindow), :], dkv_ref[pl.ds(0, cwin), lanes(s, 2 * hw)])
            for r in range(1, rows):
                total += mm_tn(R("memf")[in_row(r, cwindow), :], dkv_ref[pl.ds(r * cwin, cwin), lanes(s, 2 * hw)])
            r_c0.part(s)[...] = total.astype(BF16)
            sends([r_c0], i)

            @pl.when(i == 1)
            def _():
                r_w1[0].core_done()
                r_w1[1].core_done()

            return 0

        lax.fori_loop(0, 4, c0_grad, 0)
        dcq = mm_tn(n2_ref[...], cq_ref[...]).astype(BF16)
        dco = mm_tn(gb_ref[...], oc_ref[...]).astype(BF16)
        r_c0.core_done()
        for s in range(4):
            r_c1.part(s)[:, :hw] = dcq[:, s * hw : (s + 1) * hw]
            r_c1.part(s)[:, hw:] = dco[:, s * hw : (s + 1) * hw]
        sends([r_c1], 0)
        sends([r_c1], 1)

    @pl.when(is_enc)
    def _():
        def row(r, _):
            rs = rowsl(r)
            dm_x(r).wait_recv()
            dx, dg = norm_back(r2_ref[rs, :], gain2, R("rcc")[r].astype(F32))
            R("dg")[r, pl.ds(2, 1), :] = dg
            g_ref[rs, :] = dx
            gb_ref[rs, :] = dx.astype(BF16)
            return 0

        lax.fori_loop(0, rows, row, 0)

        def w2_grad(i, _):
            s = far_first(i)
            R("dw2")[rowsl(s, width), :] = mm_tn(gb_ref[...], u_ref[s]).astype(BF16)
            sends(r_w2, i)
            return 0

        lax.fori_loop(0, 4, w2_grad, 0)
        dn = pl.ds(0, tokens)
        acc_ref[dn, :] = jnp.zeros((tokens, width), F32)

        def w1_grad(i, _):
            s = far_first(i)
            dh = (mm_nt(gb_ref[...], R("w2")[s]) * gp_ref[s].astype(F32)).astype(BF16)
            R("dmf")[rowsl(s, width), :] = mm_tn(n2_ref[...], dh).astype(BF16)
            sends(r_w1, i)
            acc_ref[dn, :] += mm_nt(dh, R("w1")[s])

            @pl.when(i == 0)
            def _():
                r_w2[0].core_done()
                r_w2[1].core_done()

            return 0

        lax.fori_loop(0, 4, w1_grad, 0)
        r_w1[0].core_done()
        r_w1[1].core_done()
        dx, dg = norm_back(r1_ref[...], gain1, acc_ref[dn, :])
        R("dg")[0, pl.ds(1, 1), :] = dg
        for r in range(1, rows):
            R("dg")[r, pl.ds(1, 1), :] = jnp.zeros_like(dg)
        g_ref[...] += dx

    sec_out = links.here(sec_ref, R("sec"))
    sec_out.start()
    gb_ref[...] = g_ref[...].astype(BF16)
    R("dwo")[...] = mm_tn(gb_ref[...], o_ref[...]).astype(BF16)
    r_wo.core_send(0)
    r_wo.core_send(1)
    do_ref[...] = mm_nt(gb_ref[...], R("wo")[...].reshape(4 * hw, width)).astype(BF16)
    acc_ref[...] = jnp.zeros_like(acc_ref)
    dqkv_ref = R("dqkv")
    for r in range(rows):
        dqkv_ref[pl.ds(r * win, HALO), :hw] = jnp.zeros((HALO, hw), BF16)
        dqkv_ref[pl.ds(r * win + HALO + own, HALO), :hw] = jnp.zeros((HALO, hw), BF16)

    def self_back(i, _):
        s = far_first(i)
        for r in range(rows):
            rs = pl.ds(r * own, own)
            dq, dk, dv = attend_back(
                q_ref[s, r], k_ref[s, r], v_ref[s, r], do_ref[rs, lanes(s)], o_ref[rs, lanes(s)], inv_ref[rs, lanes(s)],
                lambda h: p_ref[s, r, h],
            )
            dqkv_ref[pl.ds(r * win + HALO, own), :hw] = dq
            dqkv_ref[pl.ds(r * win, win), hw : 2 * hw] = dk
            dqkv_ref[pl.ds(r * win, win), 2 * hw :] = dv
        R("cp")[rowsl(s, width), pl.ds(0, 3 * hw)] = mm_tn(nw_ref[...], dqkv_ref[...]).astype(BF16)
        sends(r_wa, i)
        acc_ref[...] += mm_nt(dqkv_ref[...], R("wa")[s])

        @pl.when(i == 0)
        def _():
            r_w2[0].z_done(0)
            pl.when(is_dec)(r_c1.core_done)
            r_wo.core_done()
            r_w2[1].y_done()

        @pl.when(i == 2)
        def _():
            r_w1[1].z_done(0)
            r_w1[0].y_done()

        @pl.when(i == 3)
        def _():
            pl.when(is_enc)(r_wo.y_done)
            r_w2[1].z_done(0, w2_out[1])
            r_w2[0].z_rest()
            pl.when(is_dec)(r_c0.y_done)

        return 0

    lax.fori_loop(0, 4, self_back, 0)
    for r in range(rows):
        R("xh")[0, r] = acc_ref[pl.ds(r * win, HALO), :].astype(BF16)
        R("xh")[1, r] = acc_ref[pl.ds(r * win + HALO + own, HALO), :].astype(BF16)
    pl.when(t < 3)(dn_right.start)
    pl.when(t > 0)(dn_left.start)
    for j in range(3):
        r_wa[j].core_done()

    @pl.when(t == 0)
    def _():
        R("dhr")[0] = jnp.zeros((rows, HALO, width), BF16)

    @pl.when(t == 3)
    def _():
        R("dhr")[1] = jnp.zeros((rows, HALO, width), BF16)

    @pl.when(is_dec)
    def _():
        r_w1[0].z_done(0, w1_out[0])
        r_w1[1].z_rest()
        r_c1.y_done()
        r_w2[1].z_rest(w2_out[1])
        r_wo.y_done()
        r_c0.z_done(0, R("dc0"))

    pl.when(t > 0)(dn_right.wait_recv)
    pl.when(t < 3)(dn_left.wait_recv)
    for r in range(rows):
        lo, hi = pl.ds(r * win + HALO, HALO), pl.ds(r * win + own, HALO)
        acc_ref[lo, :] += R("dhr")[0, r].astype(F32)
        acc_ref[hi, :] += R("dhr")[1, r].astype(F32)
    total = jnp.zeros((1, width), F32)
    for r in range(rows):
        rs = pl.ds(r * own, own)
        dx, dg = norm_back(x_ref[r].astype(F32), gain0, acc_ref[pl.ds(r * win + HALO, own), :])
        gb_ref[rs, :] = (g_ref[rs, :] + dx).astype(BF16)
        total += dg
    dgt, dgd = R("dgt"), R("dgd")
    dgt[t] = jnp.zeros((8, width), F32)
    dgt[t, pl.ds(0, 1), :] = total
    dgt[t, pl.ds(1, 2), :] = sum(R("dg")[r, pl.ds(1, 2), :] for r in range(rows))
    for c in gain_over_t:
        c.start()
    gx_out = links.here(gb_ref, R("gx"))
    gx_out.start()

    def gains_over_t():
        for c in gain_over_t:
            c.wait_recv()
        dgd[d] = dgt[0] + dgt[1] + dgt[2] + dgt[3]
        for c in gain_over_d:
            c.start()

    def gains_over_d():
        total = jnp.zeros((8, width), F32)
        for c in gain_over_d:
            c.wait_recv()
        for k in range(dp):
            total += dgd[k]
        R("dgain")[...] = pltpu.roll(total, lax.rem(width - d * (width // dp), width), 1)

    @pl.when(is_enc)
    def _():
        r_w2[0].y_done(w2_out[0])
        r_w1[0].z_done(0, w1_out[0])
        r_w1[1].z_rest()
        r_wa[0].y_done()
        r_wo.z_done(0, R("dwo_o"))
        r_wa[1].y_done()
        gains_over_t()
        r_w2[1].z_rest(w2_out[1])
        r_wa[0].z_done(0, wa_out[0])
        r_wa[2].y_done()
        r_w1[0].z_rest(w1_out[0])
        r_wa[1].z_done(0, wa_out[1])
        r_w1[1].y_done(w1_out[1])
        gains_over_d()
        r_wo.z_rest(R("dwo_o"))

    @pl.when(is_dec)
    def _():
        r_w2[0].y_done(w2_out[0])
        r_w1[0].z_rest(w1_out[0])
        r_c1.z_done(0, R("dc"))
        r_wa[0].y_done()
        r_wo.z_done(0, R("dwo_o"))
        r_wa[1].y_done()
        r_c0.z_rest(R("dc0"))
        c0_back.start()
        r_wa[0].z_done(0, wa_out[0])
        r_wa[2].y_done()
        r_c1.z_rest(R("dc"))
        r_wa[1].z_done(0, wa_out[1])
        r_w1[1].y_done(w1_out[1])
        gains_over_t()
        r_wo.z_rest(R("dwo_o"))
        gains_over_d()

    r_wa[2].z_done(0, wa_out[2])
    for j in range(3):
        r_wa[j].z_rest(wa_out[j])

    sec_out.wait()
    gx_out.wait()
    for g in (g_wa, g_wo, g_w1, g_w2):
        g.finish()
    for g in r_w2 + r_w1 + [r_wo] + r_wa:
        g.finish()
    for c in gain_over_t + gain_over_d:
        c.wait_send()
    pl.when(t < 3)(x_right.wait_send)
    pl.when(t > 0)(x_left.wait_send)
    pl.when(t < 3)(dn_right.wait_send)
    pl.when(t > 0)(dn_left.wait_send)

    @pl.when(is_enc)
    def _():
        c0_x.wait_send()
        for r in range(rows):
            mem_x(r).wait_send()
        c0_back.wait_recv()
        R("dc")[...] = R("dc0r")[...]

    @pl.when(is_dec)
    def _():
        for g in (r_c0, r_c1):
            g.finish()
        for r in range(rows):
            mem_c(r).wait_send()
            pl.when(inner)(mem_t(r).wait_send)
            dm_x(r).wait_send()
        c0_back.wait_send()


def arrange(aligned, sec, gx, dgain, da, dwo, dc, dw1, dw2, sec_o, gx_o, dgain_o, da_o, dwo_o, dc_o, dw1_o, dw2_o):
    share, hw = dwo.shape
    sec_o[...] = sec[...]
    gx_o[...] = gx[...]
    for i in range(3):
        dgain_o[i] = dgain[pl.ds(i, 1), pl.ds(0, share)]
        da_o[i] = da[:, pl.ds(i * hw, hw)]
    for i in range(2):
        dc_o[:, i, :] = dc[:, pl.ds(i * hw, hw)]
    dw1_o[...] = dw1[...]
    dwo_o[...] = dwo[...].T if aligned else dwo[...]
    dw2_o[...] = dw2[...].T if aligned else dw2[...]


def body(embeds, segments, cotangent, norm_gains, attn_in, attn_out, cross_proj, ffn_in, ffn_out):
    dp = lax.axis_size("dp")
    rows, own, width = embeds.shape[1:]
    slots = segments.shape[2]
    hw = attn_in.shape[3]
    fw = ffn_in.shape[2]
    win = own + 2 * HALO
    cwin = 2 * own + 2 * HALO
    tokens = rows * own
    side = 3 * own // 4
    share = width // dp
    zsteps = (dp - 1).bit_length()

    ins = dict(
        x_h=embeds[0], segs_h=segments, gains=norm_gains.transpose(1, 0, 2), cot_h=cotangent.reshape(tokens, width),
        wa_h=attn_in[0].transpose(1, 0, 2), wo_h=attn_out[0], w1_h=ffn_in[0], w2_h=ffn_out[0],
        cx_h=cross_proj[0].reshape(2 * width, hw),
    )
    outs = dict(
        sec=((tokens, width), BF16), gx=((tokens, width), BF16), dgain=((8, width), F32),
        da_o=((share, 3 * hw), F32), dwo_o=((share, hw), F32), dc=((share, 2 * hw), F32),
        dw1_o=((share, fw), F32), dw2_o=((share, fw), F32),
    )
    vm = dict(
        x=((rows, own, width), BF16), cot=((tokens, width), BF16), segs=(segments.shape, jnp.int32),
        wa=((4, width, 3 * hw), BF16), wo=((4, hw, width), BF16), w1=((4, width, fw), BF16), w2=((4, fw, width), BF16),
        c0=((width, 8 * hw), BF16), cqw=((width, 4 * hw), BF16), cow=((width, 4 * hw), BF16),
        xh=((2, rows, HALO, width), BF16), nw=((rows * win, width), BF16),
        q=((4, rows, own, hw), BF16), k=((4, rows, win, hw), BF16), v=((4, rows, win, hw), BF16),
        p=((4, rows, 2, own, win), BF16), o=((tokens, width), BF16), inv=((tokens, width), BF16), bias=((rows, own, win), F32),
        r1=((tokens, width), F32), r2=((tokens, width), F32), n2=((tokens, width), BF16), n3=((tokens, width), BF16),
        u=((4, tokens, fw), BF16), gp=((4, tokens, fw), BF16), secs=((tokens, width), BF16),
        acc=((rows * win, width), F32), g=((tokens, width), F32), gb=((tokens, width), BF16), do=((tokens, width), BF16),
        memf=((max(rows * slots, 4 * width), max(width, fw)), BF16), kv=((slots, 8 * hw), BF16), cq=((tokens, width), BF16),
        cp=((max(8 * own, 4 * width), cwin), BF16), cinv=((own, width), BF16), oc=((tokens, width), BF16),
        cols=((rows, own, 128), F32), keys=((rows, 8, cwin), F32),
        dkv=((rows * cwin, 8 * hw), BF16), dmf=((max(rows * slots, 4 * width), max(width, fw)), BF16),
        rcc=((rows, own, width), BF16), rct=((rows, side, width), BF16),
        dg=((rows, 8, width), F32),
        dqkv=((rows * win, 3 * hw), BF16), dhr=((2, rows, HALO, width), BF16),
        dgt=((4, 8, width), F32), dgd=((dp, 8, width), F32),
        dw2=((4 * width, fw), BF16), dwo=((width, 4 * hw), BF16),
        dc0=((share, 2 * hw), F32), dc0r=((share, 2 * hw), F32),
    )
    sums = dict(w20=fw // 2, w21=fw // 2, w10=fw // 2, w11=fw // 2, wo=hw, wa0=hw, wa1=hw, wa2=hw, c0=2 * hw, c1=2 * hw)
    for name, m in sums.items():
        shards = 2 if name in ("w20", "w11") else 1
        vm["rc_" + name] = ((2, width, m), BF16)
        vm["ry_" + name] = ((share if shards == 2 else width, m), BF16)
        vm["zb_" + name] = ((shards, dp, share, m), BF16)
        for k in range(zsteps):
            vm[f"zr{k}_{name}"] = ((shards, dp >> (k + 1), share, m), BF16)
    copies = 140 + 12 * zsteps + dp
    sems = dict(send=pltpu.SemaphoreType.DMA((copies,)), recv=pltpu.SemaphoreType.DMA((copies,)), local=pltpu.SemaphoreType.DMA((16,)))
    in_hbm = {n for n in ins if n.endswith("_h")}
    out_hbm = {"sec", "gx"}
    results = pl.pallas_call(
        functools.partial(layers, list(ins) + list(outs) + list(vm) + list(sems)),
        name="layers",
        out_shape=[jax.ShapeDtypeStruct(*o) for o in outs.values()],
        in_specs=[pl.BlockSpec(memory_space=pl.ANY if n in in_hbm else pltpu.VMEM) for n in ins],
        out_specs=[pl.BlockSpec(memory_space=pl.ANY if n in out_hbm else pltpu.VMEM) for n in outs],
        scratch_shapes=[pltpu.VMEM(*s) for s in vm.values()] + list(sems.values()),
        compiler_params=pltpu.CompilerParams(vmem_limit_bytes=VMEM_LIMIT, collective_id=0, has_side_effects=True),
    )(*ins.values())
    aligned = share % 128 == 0
    sec, gx, dgain, da, dwo, dc, dw1, dw2 = pl.pallas_call(
        functools.partial(arrange, aligned),
        name="arrange",
        out_shape=[
            jax.ShapeDtypeStruct((tokens, width), BF16),
            jax.ShapeDtypeStruct((tokens, width), BF16),
            jax.ShapeDtypeStruct((3, 1, share), F32),
            jax.ShapeDtypeStruct((3, share, hw), F32),
            jax.ShapeDtypeStruct((hw, share) if aligned else (share, hw), F32),
            jax.ShapeDtypeStruct((share, 2, hw), F32),
            jax.ShapeDtypeStruct((share, fw), F32),
            jax.ShapeDtypeStruct((fw, share) if aligned else (share, fw), F32),
        ],
        in_specs=[pl.BlockSpec(memory_space=pltpu.VMEM)] * 8,
        out_specs=[pl.BlockSpec(memory_space=pltpu.VMEM)] * 8,
    )(*results)
    if not aligned:
        dwo, dw2 = dwo.T, dw2.T
    return (
        sec.reshape(1, rows, own, width), gx.reshape(1, rows, own, width), dgain.transpose(1, 0, 2),
        da.transpose(1, 0, 2)[None], dwo[None], dc[None], dw1[None], dw2[None],
    )


def solution(mesh):
    return jax.shard_map(
        body,
        mesh=mesh,
        in_specs=(
            P("pipe", "dp", "tensor", None),
            P(None, "dp", None),
            P("dp", "tensor", None),
            P("pipe", None, None),
            P("pipe", None, None, "tensor"),
            P("pipe", "tensor", None),
            P("pipe", None, None, "tensor"),
            P("pipe", None, "tensor"),
            P("pipe", "tensor", None),
        ),
        out_specs=(
            P("pipe", "dp", "tensor", None),
            P("pipe", "dp", "tensor", None),
            P("pipe", None, "dp"),
            P("pipe", "dp", None, "tensor"),
            P("pipe", "tensor", "dp"),
            P("pipe", "dp", None, "tensor"),
            P("pipe", "dp", "tensor"),
            P("pipe", "tensor", "dp"),
        ),
        check_vma=False,
    )
```

```python
import functools

import jax
import jax.numpy as jnp
from jax import lax
from jax.experimental import pallas as pl
from jax.experimental.pallas import tpu as pltpu
from jax.sharding import PartitionSpec as P

EPS = 1e-05
MASKED = -1000000000.0
DH = 64
HALO = 64
F32 = jnp.float32
BF16 = jnp.bfloat16
GELU_C = 0.7978845608028654
GELU_A = 0.044715
MESH = pl.DeviceIdType.MESH
VMEM_LIMIT = 63 << 20


def mm(a, b):
    return lax.dot_general(a, b, (((1,), (0,)), ((), ())), preferred_element_type=F32)


def mm_nt(a, b):
    return lax.dot_general(a, b, (((1,), (1,)), ((), ())), preferred_element_type=F32)


def mm_tn(a, b):
    return lax.dot_general(a, b, (((0,), (0,)), ((), ())), preferred_element_type=F32)


def norm_parts(v):
    c = v - jnp.mean(v, axis=-1, keepdims=True)
    r = lax.rsqrt(jnp.mean(c * c, axis=-1, keepdims=True) + EPS)
    return c * r, r


def norm(v, gain):
    xhat, _ = norm_parts(v)
    return xhat * gain


def norm_back(v, gain, dn):
    xhat, r = norm_parts(v)
    dxh = dn * gain
    m1 = jnp.mean(dxh, axis=-1, keepdims=True)
    m2 = jnp.mean(dxh * xhat, axis=-1, keepdims=True)
    return r * (dxh - m1 - xhat * m2), jnp.sum(dn * xhat, axis=0, keepdims=True)


def lane_low(shape):
    return lax.broadcasted_iota(jnp.int32, shape, 1) < DH


def pair_join(a, b):
    return jnp.where(lane_low(a.shape), a, b)


def swap_halves(v):
    return pltpu.roll(v, DH, 1)


def attend(q2, k2, v2, mask, keep):
    low, lowq = lane_low(v2.shape), lane_low(q2.shape)
    one, zero = jnp.ones_like(v2), jnp.zeros_like(q2)
    outs = []
    for h in range(2):
        qh = jnp.where(lowq, q2, zero) if h == 0 else jnp.where(lowq, zero, q2)
        s = mask(mm_nt(qh, k2))
        e = jnp.exp(s - jnp.max(s, axis=-1, keepdims=True)).astype(BF16)
        keep(h, e)
        outs.append(mm(e, jnp.where(low, v2, one) if h == 0 else jnp.where(low, one, v2)))
    inv = 1.0 / swap_halves(pair_join(outs[1], outs[0]))
    return pair_join(*outs) * inv, inv


def attend_back(q2, k2, v2, do2, o2, inv, kept):
    low, lowq = lane_low(v2.shape), lane_low(q2.shape)
    one = jnp.ones_like(v2)
    scaled = do2.astype(F32) * inv.astype(F32)
    dob = scaled.astype(BF16)
    minus = (-swap_halves(dob.astype(F32) * o2.astype(F32))).astype(BF16)
    q_t, do_t = q2.T, dob.T
    dq, dk, dv = [], [], []
    for h in range(2):
        e = kept(h)
        rows = slice(h * DH, (h + 1) * DH)
        lhs = jnp.where(lowq, dob, minus) if h == 0 else jnp.where(lowq, minus, dob)
        dp = mm_nt(lhs, jnp.where(low, v2, one) if h == 0 else jnp.where(low, one, v2))
        ds = (dp * e.astype(F32)).astype(BF16)
        dq.append(mm(ds, k2))
        dv.append(mm(do_t[rows], e).astype(BF16))
        dk.append(mm(q_t[rows], ds).astype(BF16))
    return (pair_join(*dq) * (DH**-0.5)).astype(BF16), jnp.concatenate(dk, 0).T, jnp.concatenate(dv, 0).T


def gelu_parts(h):
    h2 = h * h
    half = 0.5 + 0.5 * jnp.tanh(h * (GELU_C + (GELU_C * GELU_A) * h2))
    u = h * half
    slope = half + u * ((1.0 - half) * (2.0 * GELU_C + (6.0 * GELU_C * GELU_A) * h2))
    return u, slope


def flip(i, bit):
    return i + bit - 2 * bit * lax.rem(lax.div(i, bit), 2)


def bit_of(i, bit):
    return lax.rem(lax.div(i, bit), 2)


def reversed_bits(i, count):
    out, bit = 0, 1
    while bit < count:
        out = 2 * out + (i // bit) % 2
        bit *= 2
    return out


class Links:
    def __init__(self, send, recv, local):
        self.send, self.recv, self.local = send, recv, local
        self.n = self.m = 0
        self.sent = []

    def take(self, count=1):
        self.n += count
        return self.n - count

    def remote(self, src, dst, device, at=None):
        at = self.take() if at is None else at
        return pltpu.make_async_remote_copy(
            src_ref=src, dst_ref=dst, send_sem=self.send.at[at], recv_sem=self.recv.at[at],
            device_id=device, device_id_type=MESH,
        )

    def here(self, src, dst):
        self.m += 1
        return pltpu.make_async_copy(src, dst, self.local.at[self.m - 1])


class Gather:
    def __init__(self, links, src, slot, depth, at, pieces=1, planes=None):
        t, t2 = at["t"], at["t2"]
        half = depth // 2
        n = half // pieces
        whole = pl.ds(0, depth)
        if src is None:
            self.own = []
        elif planes is None:
            self.own = [links.here(src, slot(t, whole))]
        else:
            self.own = [links.here(src.at[i], slot(t, whole, i)) for i in range(planes)]
        self.inner = src is None or planes is not None
        src = slot(t, whole) if self.inner else src
        self.core = links.remote(src, slot(t, whole), at["C"])
        self.over_y, self.over_z, self.core_a, self.core_b = [], [], [], []
        for i in range(pieces):
            mine = pl.ds(pl.multiple_of(at["b"] * half + i * n, n), n)
            other = pl.ds(pl.multiple_of((1 - at["b"]) * half + i * n, n), n)
            self.over_y.append(links.remote(src.at[mine], slot(t, mine), at["Y"]))
            self.over_z.append(links.remote(slot(t2, mine), slot(t2, mine), at["Z"][0]))
            self.core_a.append(links.remote(slot(t2, mine), slot(t2, mine), at["C"]))
            self.core_b.append(links.remote(slot(t2, other), slot(t2, other), at["C"]))

    def start(self):
        for c in self.own:
            c.start()
        if self.inner:
            for c in self.own:
                c.wait()
        for c in self.over_y:
            c.start()
        self.core.start()

    def step1(self, i=0):
        self.over_y[i].wait_recv()
        self.over_z[i].start()
        self.core_a[i].start()

    def step2(self, i=0):
        self.over_z[i].wait_recv()
        self.core_b[i].start()

    def ready(self, i):
        if i == 0 and not self.inner:
            for c in self.own:
                c.wait()
        if i == 1:
            self.core.wait_recv()
        if i == 3:
            for c in self.core_a + self.core_b:
                c.wait_recv()

    def finish(self):
        for c in [self.core] + self.over_y + self.over_z + self.core_a + self.core_b:
            c.wait_send()


class Reduce:
    def __init__(self, links, part, rc, ry, zb, zr, at, y_first):
        self.part, self.at, self.y_first = part, at, y_first
        self.rc, self.ry, self.zb, self.zr = rc, ry, zb, zr
        self.n = zb.shape[0]
        self.dp, self.rows = zb.shape[1:3]
        self.core = [links.remote(part(at[f]), rc.at[j], at["C"]) for j, f in enumerate(("t1", "t3"))]
        self.over_z, self.kept = [], []
        off, m, bit, k = 0, self.dp, 1, 0
        while m > 1:
            m //= 2
            b = bit_of(at["d"], bit)
            keep, give = off + b * m, off + (1 - b) * m
            self.over_z.append(links.remote(zb.at[:, pl.ds(give, m)], zr[k], at["Z"][k]))
            self.kept.append((keep, m))
            off, bit, k = keep, 2 * bit, k + 1
        self.off = off
        self.over_y = links.remote(part(at["t2"]) if y_first else zb.at[1, off], ry, at["Y"])

    def core_send(self, j):
        self.core[j].start()

    def into_zb(self, j, mine, theirs):
        for i in range(self.dp):
            where = pl.ds(i * self.rows, self.rows)
            self.zb[j, reversed_bits(i, self.dp)] = (mine[where, :].astype(F32) + theirs[where, :].astype(F32)).astype(BF16)

    def core_done(self):
        self.core[0].wait_recv()
        self.core[1].wait_recv()
        far, near = self.part(self.at["t2"]), self.part(self.at["t"])
        if self.y_first:
            far[...] = (far[...].astype(F32) + self.rc[1].astype(F32)).astype(BF16)
            self.over_y.start()
            near[...] = (near[...].astype(F32) + self.rc[0].astype(F32)).astype(BF16)
        else:
            self.into_zb(0, near, self.rc.at[0])
            self.into_zb(1, far, self.rc.at[1])
            self.over_z[0].start()

    def y_done(self, out=None):
        self.over_y.wait_recv()
        if self.y_first:
            self.into_zb(0, self.part(self.at["t"]), self.ry)
            self.over_z[0].start()
        else:
            out[...] = self.zb[0, self.off].astype(F32) + self.ry[...].astype(F32)

    def z_done(self, k, out=None):
        self.over_z[k].wait_recv()
        keep, m = self.kept[k]
        last = k == len(self.over_z) - 1
        if last and self.y_first:
            out[...] = self.zb[0, keep].astype(F32) + self.zr[k][0, 0].astype(F32)
        else:
            for j in range(self.n):
                live = self.zb.at[j, pl.ds(keep, m)]
                live[...] = (live[...].astype(F32) + self.zr[k][j].astype(F32)).astype(BF16)
            (self.over_y if last else self.over_z[k + 1]).start()

    def z_rest(self, out=None):
        for k in range(1, len(self.over_z)):
            self.z_done(k, out)

    def finish(self):
        for c in self.core + [self.over_y] + self.over_z:
            c.wait_send()


def layers(names, *refs):
    ref = dict(zip(names, refs))
    R = lambda name: ref[name]
    p, d, t = lax.axis_index("pipe"), lax.axis_index("dp"), lax.axis_index("tensor")
    is_enc, is_dec = p == 0, p == 1
    dp = lax.axis_size("dp")
    t1, t2, t3 = flip(t, 1), flip(t, 2), 3 - t
    zbits = []
    while 2 ** len(zbits) < dp:
        zbits.append((p, flip(d, 2 ** len(zbits)), t))
    at = dict(t=t, t1=t1, t2=t2, t3=t3, d=d, b=bit_of(d, 1), C=(p, d, t1), Y=(p, d, t2), T=(p, d, t3), X=(1 - p, d, t), Z=zbits)
    rows, own, width = R("x").shape
    win, cwin = own + 2 * HALO, 2 * own + 2 * HALO
    slots = 4 * own
    tokens = rows * own
    hw = R("wa").shape[2] // 3
    fw = R("w1").shape[2]
    inner = t % 3 != 0
    scale = jnp.asarray(DH**-0.5, BF16)
    gain_ref, x_ref = R("gains"), R("x")
    side = 3 * own // 4

    def rowsl(r, n=own):
        return pl.ds(pl.multiple_of(r * n, n), n)

    def lanes(s, n=hw):
        return pl.ds(pl.multiple_of(s * n, n), n)

    def far_lanes(s):
        return pl.ds(pl.multiple_of(s * 2 * hw + hw, hw), hw)

    def in_row(r, span):
        return pl.ds(pl.multiple_of(r * slots + span.start, HALO), span.size)

    def near_first(i):
        return 2 * lax.rem(lax.div(t, 2) + lax.div(i, 2), 2) + lax.rem(lax.rem(t, 2) + lax.rem(i, 2), 2)

    def far_first(i):
        return 2 * lax.rem(lax.div(t, 2) + lax.rem(lax.div(i + 1, 2), 2), 2) + lax.rem(lax.rem(t, 2) + 1 - lax.div(i, 2), 2)

    def seg_row(side_, r, start):
        row = jnp.broadcast_to(R("segs")[side_, pl.ds(r, 1), :].astype(F32), (8, slots))
        return pltpu.roll(row, lax.rem(2 * slots - start, slots), 1)

    def seg_column(side_, r):
        row = seg_row(side_, r, t * own)[:1, :own]
        return jnp.broadcast_to(row, (128, own)).T

    def spread(column, n):
        return jnp.concatenate([column] * (n // 128), axis=1)

    links = Links(R("send"), R("recv"), R("local"))

    def by_shard(name, n=None):
        def slot(s, span, i=None):
            full = R(name).at[s, span]
            return full if i is None else full.at[:, pl.ds(i * n, n)]

        return slot

    def by_columns(name, n, row):
        def slot(s, span):
            return R(name).at[pl.ds(pl.multiple_of(span.start + row, HALO), span.size), lanes(s, n)]

        return slot

    g_wa = Gather(links, R("wa_h"), by_shard("wa", hw), width, at, 2, 3)
    g_wo = Gather(links, R("wo_h"), by_shard("wo"), hw, at)
    g_w1 = Gather(links, R("w1_h"), by_shard("w1"), width, at, 2)
    g_w2 = Gather(links, R("w2_h"), by_shard("w2"), fw, at, 4)
    g_c1 = Gather(links, R("cx_h"), by_columns("dmf", hw, 0), 2 * width, at)
    c0_x = links.remote(R("cx_h"), R("dmf").at[pl.ds(2 * width, 2 * width), lanes(t)], at["X"])
    g_c0 = Gather(links, None, by_columns("dmf", hw, 2 * width), 2 * width, at)
    loads = [links.here(R(n + "_h"), R(n)) for n in ("x", "cot", "segs")]
    x_right = links.remote(R("x_h").at[:, pl.ds(own - HALO, HALO)], R("xh").at[0], (p, d, lax.rem(t + 1, 4)))
    x_left = links.remote(R("x_h").at[:, pl.ds(0, HALO)], R("xh").at[1], (p, d, lax.rem(t + 3, 4)))
    base_mem, base_memc, base_memt = links.take(rows), links.take(rows), links.take(rows)
    base_dmc, base_dmt, base_dmx = links.take(rows), links.take(rows), links.take(rows)
    block = pl.ds(pl.multiple_of(t * own, own), own)
    block1 = pl.ds(pl.multiple_of(t1 * own, own), own)
    edge_out = pl.ds(pl.multiple_of(lax.rem(own // 2 + side * t, slots), HALO), side)
    edge_in = pl.ds(pl.multiple_of(lax.rem(own // 2 + side * t3, slots), HALO), side)

    def mem_x(r):
        return links.remote(R("secs").at[rowsl(r)], R("memf").at[in_row(r, block)], at["X"], base_mem + r)

    def mem_c(r):
        return links.remote(R("memf").at[in_row(r, block)], R("memf").at[in_row(r, block)], at["C"], base_memc + r)

    def mem_t(r):
        return links.remote(R("memf").at[in_row(r, edge_out)], R("memf").at[in_row(r, edge_out)], at["T"], base_memt + r)

    def dm_rows(r, span):
        return R("dmf").at[in_row(r, span)]

    def dm_c(r):
        return links.remote(dm_rows(r, block1), R("rcc").at[r], at["C"], base_dmc + r)

    def dm_t(r):
        return links.remote(dm_rows(r, edge_in), R("rct").at[r], at["T"], base_dmt + r)

    def dm_x(r):
        return links.remote(R("rcc").at[r], R("rcc").at[r], at["X"], base_dmx + r)

    def by_rows(name, m, col=0):
        return lambda s: R(name).at[pl.ds(pl.multiple_of(s * width, width), width), pl.ds(col, m)]

    def by_lanes(name, m, row=0):
        return lambda s: R(name).at[pl.ds(row, width), lanes(s, m)]

    def reduce_of(name, part, y_first=True):
        zr = [R(f"zr{k}_{name}") for k in range(len(zbits))]
        return Reduce(links, part, R("rc_" + name), R("ry_" + name), R("zb_" + name), zr, at, y_first)

    fh = fw // 2
    r_w2 = [reduce_of(f"w2{j}", by_rows("dw2", fh, j * fh), j == 1) for j in range(2)]
    r_w1 = [reduce_of(f"w1{j}", by_rows("dmf", fh, j * fh), j == 0) for j in range(2)]
    r_wo = reduce_of("wo", by_lanes("dwo", hw))
    r_wa = [reduce_of(f"wa{j}", by_rows("cp", hw, j * hw)) for j in range(3)]
    r_c0 = reduce_of("c0", by_lanes("kv", 2 * hw))
    r_c1 = reduce_of("c1", by_lanes("kv", 2 * hw, width))
    w2_out = [R("dw2_o").at[:, pl.ds(j * fh, fh)] for j in range(2)]
    w1_out = [R("dw1_o").at[:, pl.ds(j * fh, fh)] for j in range(2)]
    wa_out = [R("da_o").at[:, pl.ds(j * hw, hw)] for j in range(3)]
    c0_back = links.remote(R("dc0"), R("dc0r"), at["X"])
    dn_right = links.remote(R("xh").at[1], R("dhr").at[0], (p, d, lax.rem(t + 1, 4)))
    dn_left = links.remote(R("xh").at[0], R("dhr").at[1], (p, d, lax.rem(t + 3, 4)))
    gain_over_t = [links.remote(R("dgt").at[t], R("dgt").at[t], at[f]) for f in ("C", "Y", "T")]
    gain_over_d = []
    for k in range(1, dp):
        to = lax.rem(d + k, dp)
        gain_over_d.append(links.remote(R("dgd").at[d], R("dgd").at[d], (p, to, t)))

    @pl.when(is_dec)
    def _():
        for at_t, start in ((0, 2 * own), (1, 2 * own + side), (3, 2 * own - 2 * HALO)):
            @pl.when(t == at_t)
            def _():
                for r in range(rows):
                    R("memf")[pl.ds(r * slots + start, 2 * HALO), :] = jnp.zeros((2 * HALO, width), BF16)

    for c in loads:
        c.start()
    barrier = pltpu.get_barrier_semaphore()
    partners = [at["C"], at["Y"], at["T"], at["X"]] + [(p, lax.rem(d + k, dp), t) for k in range(1, dp)]
    for dev in partners:
        pl.semaphore_signal(barrier, inc=1, device_id=dev, device_id_type=MESH)
    pl.semaphore_wait(barrier, len(partners))

    pl.when(t < 3)(x_right.start)
    pl.when(t > 0)(x_left.start)
    g_wa.start()
    g_wo.start()

    @pl.when(is_enc)
    def _():
        c0_x.start()
        g_w1.start()
        g_w2.start()

    @pl.when(is_dec)
    def _():
        g_c1.start()

    for c in loads:
        c.wait()

    nw_ref, bias_ref = R("nw"), R("bias")
    gain0, gain1, gain2 = gain_ref[0], gain_ref[1], gain_ref[2]
    for r in range(rows):
        nw_ref[pl.ds(r * win + HALO, own), :] = norm(x_ref[r].astype(F32), gain0).astype(BF16)
        keys = seg_row(p, r, lax.rem(t * own + slots - HALO, slots))[:1, :win]
        same = spread(seg_column(p, r), win) == keys
        qpos = lax.broadcasted_iota(jnp.int32, (own, win), 0)
        kpos = lax.broadcasted_iota(jnp.int32, (own, win), 1) - HALO
        before = kpos - qpos <= jnp.where(is_enc, 4 * win, 0)
        bias_ref[r] = jnp.where(same & before, 0.0, MASKED)

    @pl.when(t == 0)
    def _():
        R("xh")[0] = jnp.zeros((rows, HALO, width), BF16)

    @pl.when(t == 3)
    def _():
        R("xh")[1] = jnp.zeros((rows, HALO, width), BF16)

    pl.when(t > 0)(x_right.wait_recv)
    pl.when(t < 3)(x_left.wait_recv)
    for r in range(rows):
        nw_ref[pl.ds(r * win, HALO), :] = norm(R("xh")[0, r].astype(F32), gain0).astype(BF16)
        nw_ref[pl.ds(r * win + HALO + own, HALO), :] = norm(R("xh")[1, r].astype(F32), gain0).astype(BF16)

    def after_pair(i):
        @pl.when(i == 0)
        def _():
            g_wa.step1(0)

        @pl.when(i == 1)
        def _():
            g_wa.step1(1)
            g_wo.step1()
            g_wa.step2(0)

            @pl.when(is_dec)
            def _():
                c0_x.wait_recv()
                g_c0.start()
                g_w2.start()
                g_w1.start()
                g_c1.step1()

            pl.when(is_enc)(lambda: g_w1.step1(0))
            g_wa.step2(1)

        @pl.when(i == 2)
        def _():
            g_wo.step2()
            pl.when(is_enc)(lambda: g_w1.step1(1))

        @pl.when(i == 3)
        def _():
            pl.when(is_dec)(g_c0.step1)

    def wait_ready(i, *weights):
        for k in range(4):
            @pl.when(i == k)
            def _():
                for w in weights:
                    w.ready(k)

    q_ref, k_ref, v_ref, p_ref, o_ref, inv_ref = R("q"), R("k"), R("v"), R("p"), R("o"), R("inv")

    def self_pair(i, _):
        s = near_first(i)
        wait_ready(i, g_wa)
        packed = mm(nw_ref[...], R("wa")[s])
        for r in range(rows):
            q_ref[s, r] = packed[r * win + HALO : r * win + HALO + own, :hw].astype(BF16) * scale
            k_ref[s, r] = packed[r * win : (r + 1) * win, hw : 2 * hw].astype(BF16)
            v_ref[s, r] = packed[r * win : (r + 1) * win, 2 * hw :].astype(BF16)
        for r in range(rows):
            def keep(h, e):
                p_ref[s, r, h] = e

            o2, inv = attend(q_ref[s, r], k_ref[s, r], v_ref[s, r], lambda scores: scores + bias_ref[r], keep)
            o_ref[pl.ds(r * own, own), lanes(s)] = o2.astype(BF16)
            inv_ref[pl.ds(r * own, own), lanes(s)] = inv.astype(BF16)
        after_pair(i)
        return 0

    lax.fori_loop(0, 4, self_pair, 0)
    for k in range(4):
        g_wo.ready(k)
    r1_ref, r2_ref, n2_ref, n3_ref = R("r1"), R("r2"), R("n2"), R("n3")
    u_ref, gp_ref, sec_ref = R("u"), R("gp"), R("secs")
    acc_ref, g_ref, gb_ref, do_ref = R("acc"), R("g"), R("gb"), R("do")
    first = mm(o_ref[...], R("wo")[...].reshape(4 * hw, width))
    for r in range(rows):
        r1_ref[pl.ds(r * own, own), :] = x_ref[r].astype(F32) + first[r * own : (r + 1) * own]
    n2_ref[...] = norm(r1_ref[...], gain1).astype(BF16)

    @pl.when(is_enc)
    def _():
        r2_ref[...] = r1_ref[...]

        def up(i):
            s = near_first(i)
            u, gp = gelu_parts(mm(n2_ref[...], R("w1")[s]))
            u_ref[s] = u.astype(BF16)
            gp_ref[s] = gp.astype(BF16)
            return s

        g_w2.step1(0)
        g_w1.step2(0)

        def near(i, _):
            wait_ready(i, g_w1, g_w2)
            s = up(i)
            r2_ref[...] += mm(u_ref[s], R("w2")[s])

            @pl.when(i == 0)
            def _():
                g_w2.step1(1)
                g_w1.step2(1)

            @pl.when(i == 1)
            def _():
                g_w2.step1(2)
                g_w2.step2(0)
                g_w2.step1(3)

            return 0

        lax.fori_loop(0, 2, near, 0)

        def far(i, _):
            wait_ready(i, g_w1)
            up(i)
            pl.when(i == 2)(lambda: g_w2.step2(1))

            @pl.when(i == 3)
            def _():
                g_w2.step2(2)
                g_w2.step2(3)

            return 0

        lax.fori_loop(2, 4, far, 0)
        g_w2.ready(3)
        far1, far2 = near_first(2), near_first(3)

        def row(r, _):
            rs = rowsl(r)
            total = r2_ref[rs, :] + mm(u_ref[far1, rs, :], R("w2")[far1]) + mm(u_ref[far2, rs, :], R("w2")[far2])
            r2_ref[rs, :] = total
            sec_ref[rs, :] = norm(total, gain2).astype(BF16)
            mem_x(r).start()
            return 0

        lax.fori_loop(0, rows, row, 0)

    def sends(reductions, i):
        for j in range(2):
            @pl.when(i == j)
            def _():
                for reduction in reductions:
                    reduction.core_send(j)

    cstart = pl.multiple_of(jnp.minimum(t * (own - HALO), slots - cwin), HALO)
    cwindow = pl.ds(cstart, cwin)
    kv_ref, cq_ref, cp_ref, dkv_ref, cinv_ref = R("kv"), R("cq"), R("cp"), R("dkv"), R("cinv")
    c0_ref, cqw_ref, cow_ref, oc_ref, cot_ref = R("c0"), R("cqw"), R("cow"), R("oc"), R("cot")
    cols, keys_ref = R("cols"), R("keys")

    @pl.when(is_dec)
    def _():
        g_w2.step1(0)
        g_c1.step2()
        for k in range(4):
            g_c1.ready(k)
        pick_shape = (width // 4, width // 2)
        twice = 2 * lax.broadcasted_iota(jnp.int32, pick_shape, 0)
        at_col = lax.broadcasted_iota(jnp.int32, pick_shape, 1)
        picks = [jnp.where(at_col == twice + j, 1.0, 0.0).astype(BF16) for j in range(2)]

        def unweave(base, m):
            return [mm(pick, R("dmf")[pl.ds(base + m * (width // 2), width // 2), :]).astype(BF16) for pick in picks]

        for m in range(4):
            span = pl.ds(m * (width // 4), width // 4)
            cqw_ref[span, :], cow_ref[span, :] = unweave(0, m)
        cq_ref[...] = mm(n2_ref[...], cqw_ref[...]).astype(BF16) * scale
        g_w2.step1(1)
        g_c0.step2()
        g_w2.step1(2)
        g_w2.step1(3)
        kv_ref[...] = jnp.zeros_like(kv_ref)
        for r in range(rows):
            cols[r] = seg_column(1, r)
            keys_ref[r] = seg_row(0, r, cstart)[:, :cwin]
        for k in range(4):
            g_c0.ready(k)
        for m in range(4):
            span = pl.ds(m * (width // 4), width // 4)
            ck, cv = unweave(2 * width, m)
            for s in range(4):
                c0_ref[span, 2 * s * hw : (2 * s + 1) * hw] = ck[:, s * hw : (s + 1) * hw]
                c0_ref[span, (2 * s + 1) * hw : (2 * s + 2) * hw] = cv[:, s * hw : (s + 1) * hw]
        g_w1.step1(0)
        g_w2.step2(0)
        g_w2.step2(1)
        g_w1.step1(1)
        for g in (g_c1, g_c0):
            g.finish()
        R("dmf")[...] = jnp.zeros_like(R("dmf"))
        g_w2.step2(2)
        g_w2.step2(3)
        g_w1.step2(0)
        for k in range(4):
            g_w2.ready(k)

        def early(s, _):
            gp_ref[s] = mm_nt(cot_ref[...], R("w2")[s]).astype(BF16)
            return 0

        lax.fori_loop(0, 4, early, 0)

        def pass_memory_on(r):
            mem_x(r).wait_recv()
            mem_c(r).start()
            pl.when(inner)(mem_t(r).start)

        def settle(r):
            span = pl.ds(0, own)
            dm_c(r).wait_recv()
            acc_ref[span, :] = R("dmf")[in_row(r, block), :].astype(F32) + R("rcc")[r].astype(F32)

            @pl.when(inner)
            def _():
                dm_t(r).wait_recv()
                place = pl.ds(pl.multiple_of((2 - t) * (own - side), HALO), side)
                acc_ref[place, :] += R("rct")[r].astype(F32)

            R("rcc")[r] = acc_ref[span, :].astype(BF16)
            dm_x(r).start()

        def row(r, _):
            rs = rowsl(r)

            def project(span):
                kv_ref[span, :] = mm(R("memf")[in_row(r, span), :], c0_ref[...]).astype(BF16)

            @pl.when(r == 0)
            def _():
                g_w1.step2(1)
                pass_memory_on(0)

            project(block)
            pl.when(r > 0)(lambda: settle(r - 1))
            mem_c(r).wait_recv()
            project(block1)

            @pl.when(inner)
            def _():
                mem_t(r).wait_recv()
                project(edge_in)

            def cross(i, _):
                for s in (2 * i, 2 * i + 1):
                    def keep(h, e):
                        cp_ref[rowsl(2 * s + h), :] = e

                    def mask(scores):
                        same = spread(cols[r], cwin) == keys_ref[r, pl.ds(0, 1), :]
                        return jnp.where(same, scores, MASKED)

                    o2, inv = attend(cq_ref[rs, lanes(s)], kv_ref[cwindow, lanes(2 * s)], kv_ref[cwindow, lanes(2 * s + 1)], mask, keep)
                    oc_ref[rs, lanes(s)] = o2.astype(BF16)
                    cinv_ref[:, lanes(s)] = inv.astype(BF16)
                return 0

            lax.fori_loop(0, 2, cross, 0)
            pl.when(r < rows - 1)(lambda: pass_memory_on(r + 1))
            r2_ref[rs, :] = r1_ref[rs, :] + mm_nt(oc_ref[rs, :], cow_ref[...])
            n3_ref[rs, :] = norm(r2_ref[rs, :], gain2).astype(BF16)

            @pl.when(r == 0)
            def _():
                for k in range(4):
                    g_w1.ready(k)

            dn = pl.ds(0, own)
            acc_ref[dn, :] = jnp.zeros((own, width), F32)

            def feed(i, _):
                back = acc_ref[dn, :]
                for s in (2 * i, 2 * i + 1):
                    u, gp = gelu_parts(mm(n3_ref[rs, :], R("w1")[s]))
                    u = u.astype(BF16)
                    u_ref[s, rs, :] = u
                    dh = (gp_ref[s, rs, :].astype(F32) * gp).astype(BF16)
                    gp_ref[s, rs, :] = dh
                    back += mm_nt(dh, R("w1")[s])
                acc_ref[dn, :] = back
                return 0

            lax.fori_loop(0, 2, feed, 0)
            dx, dg = norm_back(r2_ref[rs, :], gain2, acc_ref[dn, :])
            R("dg")[r, pl.ds(2, 1), :] = dg
            g2 = cot_ref[rs, :].astype(F32) + dx
            g_ref[rs, :] = g2
            gb_ref[rs, :] = g2.astype(BF16)
            do_ref[rs, :] = mm(gb_ref[rs, :], cow_ref[...]).astype(BF16)
            ws = pl.ds(pl.multiple_of(r * cwin, HALO), cwin)

            def back(i, _):
                for s in (2 * i, 2 * i + 1):
                    dq, dk, dv = attend_back(
                        cq_ref[rs, lanes(s)], kv_ref[cwindow, lanes(2 * s)], kv_ref[cwindow, lanes(2 * s + 1)],
                        do_ref[rs, lanes(s)], oc_ref[rs, lanes(s)], cinv_ref[:, lanes(s)], lambda h: cp_ref[rowsl(2 * s + h), :],
                    )
                    cq_ref[rs, lanes(s)] = dq
                    dkv_ref[ws, lanes(2 * s)] = dk
                    dkv_ref[ws, lanes(2 * s + 1)] = dv
                return 0

            lax.fori_loop(0, 2, back, 0)
            R("dmf")[in_row(r, cwindow), :] = mm_nt(dkv_ref[ws, :], c0_ref[...]).astype(BF16)
            dm_c(r).start()
            pl.when(inner)(dm_t(r).start)

            @pl.when(r == rows - 1)
            def _():
                def w2_grad(i, _):
                    s = far_first(i)
                    R("dw2")[rowsl(s, width), :] = mm_tn(cot_ref[...], u_ref[s]).astype(BF16)
                    sends(r_w2, i)
                    return 0

                lax.fori_loop(0, 4, w2_grad, 0)
                settle(r)

            return 0

        lax.fori_loop(0, rows, row, 0)
        for r in range(rows):
            dm_c(r).wait_send()
            pl.when(inner)(dm_t(r).wait_send)

        def w1_grad(i, _):
            s = far_first(i)
            R("dmf")[rowsl(s, width), :] = mm_tn(n3_ref[...], gp_ref[s]).astype(BF16)
            sends(r_w1, i)

            @pl.when(i == 0)
            def _():
                r_w2[0].core_done()
                r_w2[1].core_done()

            return 0

        lax.fori_loop(0, 4, w1_grad, 0)

        def c0_grad(i, _):
            s = far_first(i)
            total = mm_tn(R("memf")[in_row(0, cwindow), :], dkv_ref[pl.ds(0, cwin), lanes(s, 2 * hw)])
            for r in range(1, rows):
                total += mm_tn(R("memf")[in_row(r, cwindow), :], dkv_ref[pl.ds(r * cwin, cwin), lanes(s, 2 * hw)])
            r_c0.part(s)[...] = total.astype(BF16)
            sends([r_c0], i)

            @pl.when(i == 1)
            def _():
                r_w1[0].core_done()
                r_w1[1].core_done()

            return 0

        lax.fori_loop(0, 4, c0_grad, 0)
        def query_norm(r, _):
            rs = rowsl(r)
            dx, dg = norm_back(r1_ref[rs, :], gain1, mm_nt(cq_ref[rs, :], cqw_ref[...]))
            R("dg")[r, pl.ds(1, 1), :] = dg
            g_ref[rs, :] += dx
            return 0

        lax.fori_loop(0, rows, query_norm, 0)
        dcq = mm_tn(n2_ref[...], cq_ref[...]).astype(BF16)
        dco = mm_tn(gb_ref[...], oc_ref[...]).astype(BF16)
        r_c0.core_done()
        for s in range(4):
            r_c1.part(s)[:, :hw] = dcq[:, s * hw : (s + 1) * hw]
            r_c1.part(s)[:, hw:] = dco[:, s * hw : (s + 1) * hw]
        sends([r_c1], 0)
        sends([r_c1], 1)

    @pl.when(is_enc)
    def _():
        def row(r, _):
            rs = rowsl(r)
            dm_x(r).wait_recv()
            dx, dg = norm_back(r2_ref[rs, :], gain2, R("rcc")[r].astype(F32))
            R("dg")[r, pl.ds(2, 1), :] = dg
            g_ref[rs, :] = dx
            gb_ref[rs, :] = dx.astype(BF16)
            return 0

        lax.fori_loop(0, rows, row, 0)

        def w2_grad(i, _):
            s = far_first(i)
            R("dw2")[rowsl(s, width), :] = mm_tn(gb_ref[...], u_ref[s]).astype(BF16)
            sends(r_w2, i)
            return 0

        lax.fori_loop(0, 4, w2_grad, 0)
        dn = pl.ds(0, tokens)
        acc_ref[dn, :] = jnp.zeros((tokens, width), F32)

        def w1_grad(i, _):
            s = far_first(i)
            dh = (mm_nt(gb_ref[...], R("w2")[s]) * gp_ref[s].astype(F32)).astype(BF16)

            @pl.when(i == 1)
            def _():
                r_w2[0].core_done()
                r_w2[1].core_done()

            R("dmf")[rowsl(s, width), :] = mm_tn(n2_ref[...], dh).astype(BF16)
            sends(r_w1, i)
            acc_ref[dn, :] += mm_nt(dh, R("w1")[s])
            return 0

        lax.fori_loop(0, 4, w1_grad, 0)
        r_w1[0].core_done()
        r_w1[1].core_done()
        dx, dg = norm_back(r1_ref[...], gain1, acc_ref[dn, :])
        R("dg")[0, pl.ds(1, 1), :] = dg
        for r in range(1, rows):
            R("dg")[r, pl.ds(1, 1), :] = jnp.zeros_like(dg)
        g_ref[...] += dx

    sec_out = links.here(sec_ref, R("sec"))
    pl.when(is_enc)(sec_out.start)
    gb_ref[...] = g_ref[...].astype(BF16)
    R("dwo")[...] = mm_tn(gb_ref[...], o_ref[...]).astype(BF16)
    r_wo.core_send(0)
    r_wo.core_send(1)
    do_ref[...] = mm_nt(gb_ref[...], R("wo")[...].reshape(4 * hw, width)).astype(BF16)
    acc_ref[...] = jnp.zeros_like(acc_ref)
    dqkv_ref = R("dqkv")
    for r in range(rows):
        dqkv_ref[pl.ds(r * win, HALO), :hw] = jnp.zeros((HALO, hw), BF16)
        dqkv_ref[pl.ds(r * win + HALO + own, HALO), :hw] = jnp.zeros((HALO, hw), BF16)

    def self_back(i, _):
        s = far_first(i)
        for r in range(rows):
            rs = pl.ds(r * own, own)
            dq, dk, dv = attend_back(
                q_ref[s, r], k_ref[s, r], v_ref[s, r], do_ref[rs, lanes(s)], o_ref[rs, lanes(s)], inv_ref[rs, lanes(s)],
                lambda h: p_ref[s, r, h],
            )
            dqkv_ref[pl.ds(r * win + HALO, own), :hw] = dq
            dqkv_ref[pl.ds(r * win, win), hw : 2 * hw] = dk
            dqkv_ref[pl.ds(r * win, win), 2 * hw :] = dv
        R("cp")[rowsl(s, width), pl.ds(0, 3 * hw)] = mm_tn(nw_ref[...], dqkv_ref[...]).astype(BF16)
        sends(r_wa, i)
        acc_ref[...] += mm_nt(dqkv_ref[...], R("wa")[s])

        @pl.when(i == 0)
        def _():
            r_w2[0].z_done(0)
            pl.when(is_dec)(r_c1.core_done)
            r_wo.core_done()
            r_w2[1].y_done()

        @pl.when(i == 2)
        def _():
            r_w1[1].z_done(0)
            r_w1[0].y_done()

        @pl.when(i == 3)
        def _():
            pl.when(is_enc)(r_wo.y_done)
            r_w2[1].z_done(0, w2_out[1])
            r_w2[0].z_rest()
            pl.when(is_dec)(r_c0.y_done)

        return 0

    lax.fori_loop(0, 4, self_back, 0)
    for r in range(rows):
        R("xh")[0, r] = acc_ref[pl.ds(r * win, HALO), :].astype(BF16)
        R("xh")[1, r] = acc_ref[pl.ds(r * win + HALO + own, HALO), :].astype(BF16)
    pl.when(t < 3)(dn_right.start)
    pl.when(t > 0)(dn_left.start)
    for j in range(3):
        r_wa[j].core_done()

    @pl.when(is_dec)
    def _():
        def decoded(r, _):
            rs = rowsl(r)
            total = r2_ref[rs, :]
            for s in range(4):
                total += mm(u_ref[s, rs, :], R("w2")[s])
            sec_ref[rs, :] = total.astype(BF16)
            return 0

        lax.fori_loop(0, rows, decoded, 0)
        sec_out.start()

    @pl.when(t == 0)
    def _():
        R("dhr")[0] = jnp.zeros((rows, HALO, width), BF16)

    @pl.when(t == 3)
    def _():
        R("dhr")[1] = jnp.zeros((rows, HALO, width), BF16)

    @pl.when(is_dec)
    def _():
        r_w1[0].z_done(0, w1_out[0])
        r_w1[1].z_rest()
        r_c1.y_done()
        r_w2[1].z_rest(w2_out[1])
        r_wo.y_done()
        r_c0.z_done(0, R("dc0"))

    pl.when(t > 0)(dn_right.wait_recv)
    pl.when(t < 3)(dn_left.wait_recv)
    for r in range(rows):
        lo, hi = pl.ds(r * win + HALO, HALO), pl.ds(r * win + own, HALO)
        acc_ref[lo, :] += R("dhr")[0, r].astype(F32)
        acc_ref[hi, :] += R("dhr")[1, r].astype(F32)
    total = jnp.zeros((1, width), F32)
    for r in range(rows):
        rs = pl.ds(r * own, own)
        dx, dg = norm_back(x_ref[r].astype(F32), gain0, acc_ref[pl.ds(r * win + HALO, own), :])
        gb_ref[rs, :] = (g_ref[rs, :] + dx).astype(BF16)
        total += dg
    dgt, dgd = R("dgt"), R("dgd")
    dgt[t] = jnp.zeros((8, width), F32)
    dgt[t, pl.ds(0, 1), :] = total
    dgt[t, pl.ds(1, 2), :] = sum(R("dg")[r, pl.ds(1, 2), :] for r in range(rows))
    for c in gain_over_t:
        c.start()
    gx_out = links.here(gb_ref, R("gx"))
    gx_out.start()

    def gains_over_t():
        for c in gain_over_t:
            c.wait_recv()
        dgd[d] = dgt[0] + dgt[1] + dgt[2] + dgt[3]
        for c in gain_over_d:
            c.start()

    def gains_over_d():
        total = jnp.zeros((8, width), F32)
        for c in gain_over_d:
            c.wait_recv()
        for k in range(dp):
            total += dgd[k]
        R("dgain")[...] = pltpu.roll(total, lax.rem(width - d * (width // dp), width), 1)

    @pl.when(is_enc)
    def _():
        r_w2[0].y_done(w2_out[0])
        r_w1[0].z_done(0, w1_out[0])
        r_w1[1].z_rest()
        r_wa[0].y_done()
        r_wo.z_done(0, R("dwo_o"))
        r_wa[1].y_done()
        gains_over_t()
        r_w2[1].z_rest(w2_out[1])
        r_wa[0].z_done(0, wa_out[0])
        r_wa[2].y_done()
        r_w1[0].z_rest(w1_out[0])
        r_wa[1].z_done(0, wa_out[1])
        r_w1[1].y_done(w1_out[1])
        gains_over_d()
        r_wo.z_rest(R("dwo_o"))

    @pl.when(is_dec)
    def _():
        r_w2[0].y_done(w2_out[0])
        r_w1[0].z_rest(w1_out[0])
        r_c1.z_done(0, R("dc"))
        r_wa[0].y_done()
        r_wo.z_done(0, R("dwo_o"))
        r_wa[1].y_done()
        r_c0.z_rest(R("dc0"))
        c0_back.start()
        r_wa[0].z_done(0, wa_out[0])
        r_wa[2].y_done()
        r_c1.z_rest(R("dc"))
        r_wa[1].z_done(0, wa_out[1])
        r_w1[1].y_done(w1_out[1])
        gains_over_t()
        r_wo.z_rest(R("dwo_o"))
        gains_over_d()

    r_wa[2].z_done(0, wa_out[2])
    for j in range(3):
        r_wa[j].z_rest(wa_out[j])

    sec_out.wait()
    gx_out.wait()
    for g in (g_wa, g_wo, g_w1, g_w2):
        g.finish()
    for g in r_w2 + r_w1 + [r_wo] + r_wa:
        g.finish()
    for c in gain_over_t + gain_over_d:
        c.wait_send()
    pl.when(t < 3)(x_right.wait_send)
    pl.when(t > 0)(x_left.wait_send)
    pl.when(t < 3)(dn_right.wait_send)
    pl.when(t > 0)(dn_left.wait_send)

    @pl.when(is_enc)
    def _():
        c0_x.wait_send()
        for r in range(rows):
            mem_x(r).wait_send()
        c0_back.wait_recv()
        R("dc")[...] = R("dc0r")[...]

    @pl.when(is_dec)
    def _():
        for g in (r_c0, r_c1):
            g.finish()
        for r in range(rows):
            mem_c(r).wait_send()
            pl.when(inner)(mem_t(r).wait_send)
            dm_x(r).wait_send()
        c0_back.wait_send()


def arrange(aligned, sec, gx, dgain, da, dwo, dc, dw1, dw2, sec_o, gx_o, dgain_o, da_o, dwo_o, dc_o, dw1_o, dw2_o):
    share, hw = dwo.shape
    sec_o[...] = sec[...]
    gx_o[...] = gx[...]
    for i in range(3):
        dgain_o[i] = dgain[pl.ds(i, 1), pl.ds(0, share)]
        da_o[i] = da[:, pl.ds(i * hw, hw)]
    for i in range(2):
        dc_o[:, i, :] = dc[:, pl.ds(i * hw, hw)]
    dw1_o[...] = dw1[...]
    dwo_o[...] = dwo[...].T if aligned else dwo[...]
    dw2_o[...] = dw2[...].T if aligned else dw2[...]


def body(embeds, segments, cotangent, norm_gains, attn_in, attn_out, cross_proj, ffn_in, ffn_out):
    dp = lax.axis_size("dp")
    rows, own, width = embeds.shape[1:]
    slots = segments.shape[2]
    hw = attn_in.shape[3]
    fw = ffn_in.shape[2]
    win = own + 2 * HALO
    cwin = 2 * own + 2 * HALO
    tokens = rows * own
    side = 3 * own // 4
    share = width // dp
    zsteps = (dp - 1).bit_length()

    ins = dict(
        x_h=embeds[0], segs_h=segments, gains=norm_gains.transpose(1, 0, 2), cot_h=cotangent.reshape(tokens, width),
        wa_h=attn_in[0].transpose(1, 0, 2), wo_h=attn_out[0], w1_h=ffn_in[0], w2_h=ffn_out[0],
        cx_h=cross_proj[0].reshape(2 * width, hw),
    )
    outs = dict(
        sec=((tokens, width), BF16), gx=((tokens, width), BF16), dgain=((8, width), F32),
        da_o=((share, 3 * hw), F32), dwo_o=((share, hw), F32), dc=((share, 2 * hw), F32),
        dw1_o=((share, fw), F32), dw2_o=((share, fw), F32),
    )
    vm = dict(
        x=((rows, own, width), BF16), cot=((tokens, width), BF16), segs=(segments.shape, jnp.int32),
        wa=((4, width, 3 * hw), BF16), wo=((4, hw, width), BF16), w1=((4, width, fw), BF16), w2=((4, fw, width), BF16),
        c0=((width, 8 * hw), BF16), cqw=((width, 4 * hw), BF16), cow=((width, 4 * hw), BF16),
        xh=((2, rows, HALO, width), BF16), nw=((rows * win, width), BF16),
        q=((4, rows, own, hw), BF16), k=((4, rows, win, hw), BF16), v=((4, rows, win, hw), BF16),
        p=((4, rows, 2, own, win), BF16), o=((tokens, width), BF16), inv=((tokens, width), BF16), bias=((rows, own, win), F32),
        r1=((tokens, width), F32), r2=((tokens, width), F32), n2=((tokens, width), BF16), n3=((tokens, width), BF16),
        u=((4, tokens, fw), BF16), gp=((4, tokens, fw), BF16), secs=((tokens, width), BF16),
        acc=((rows * win, width), F32), g=((tokens, width), F32), gb=((tokens, width), BF16), do=((tokens, width), BF16),
        memf=((max(rows * slots, 4 * width), max(width, fw)), BF16), kv=((slots, 8 * hw), BF16), cq=((tokens, width), BF16),
        cp=((max(8 * own, 4 * width), cwin), BF16), cinv=((own, width), BF16), oc=((tokens, width), BF16),
        cols=((rows, own, 128), F32), keys=((rows, 8, cwin), F32),
        dkv=((rows * cwin, 8 * hw), BF16), dmf=((max(rows * slots, 4 * width), max(width, fw)), BF16),
        rcc=((rows, own, width), BF16), rct=((rows, side, width), BF16),
        dg=((rows, 8, width), F32),
        dqkv=((rows * win, 3 * hw), BF16), dhr=((2, rows, HALO, width), BF16),
        dgt=((4, 8, width), F32), dgd=((dp, 8, width), F32),
        dw2=((4 * width, fw), BF16), dwo=((width, 4 * hw), BF16),
        dc0=((share, 2 * hw), F32), dc0r=((share, 2 * hw), F32),
    )
    sums = dict(w20=fw // 2, w21=fw // 2, w10=fw // 2, w11=fw // 2, wo=hw, wa0=hw, wa1=hw, wa2=hw, c0=2 * hw, c1=2 * hw)
    for name, m in sums.items():
        shards = 2 if name in ("w20", "w11") else 1
        vm["rc_" + name] = ((2, width, m), BF16)
        vm["ry_" + name] = ((share if shards == 2 else width, m), BF16)
        vm["zb_" + name] = ((shards, dp, share, m), BF16)
        for k in range(zsteps):
            vm[f"zr{k}_{name}"] = ((shards, dp >> (k + 1), share, m), BF16)
    copies = 140 + 12 * zsteps + dp
    sems = dict(send=pltpu.SemaphoreType.DMA((copies,)), recv=pltpu.SemaphoreType.DMA((copies,)), local=pltpu.SemaphoreType.DMA((16,)))
    in_hbm = {n for n in ins if n.endswith("_h")}
    out_hbm = {"sec", "gx"}
    results = pl.pallas_call(
        functools.partial(layers, list(ins) + list(outs) + list(vm) + list(sems)),
        name="layers",
        out_shape=[jax.ShapeDtypeStruct(*o) for o in outs.values()],
        in_specs=[pl.BlockSpec(memory_space=pl.ANY if n in in_hbm else pltpu.VMEM) for n in ins],
        out_specs=[pl.BlockSpec(memory_space=pl.ANY if n in out_hbm else pltpu.VMEM) for n in outs],
        scratch_shapes=[pltpu.VMEM(*s) for s in vm.values()] + list(sems.values()),
        compiler_params=pltpu.CompilerParams(vmem_limit_bytes=VMEM_LIMIT, collective_id=0, has_side_effects=True),
    )(*ins.values())
    aligned = share % 128 == 0
    sec, gx, dgain, da, dwo, dc, dw1, dw2 = pl.pallas_call(
        functools.partial(arrange, aligned),
        name="arrange",
        out_shape=[
            jax.ShapeDtypeStruct((tokens, width), BF16),
            jax.ShapeDtypeStruct((tokens, width), BF16),
            jax.ShapeDtypeStruct((3, 1, share), F32),
            jax.ShapeDtypeStruct((3, share, hw), F32),
            jax.ShapeDtypeStruct((hw, share) if aligned else (share, hw), F32),
            jax.ShapeDtypeStruct((share, 2, hw), F32),
            jax.ShapeDtypeStruct((share, fw), F32),
            jax.ShapeDtypeStruct((fw, share) if aligned else (share, fw), F32),
        ],
        in_specs=[pl.BlockSpec(memory_space=pltpu.VMEM)] * 8,
        out_specs=[pl.BlockSpec(memory_space=pltpu.VMEM)] * 8,
    )(*results)
    if not aligned:
        dwo, dw2 = dwo.T, dw2.T
    return (
        sec.reshape(1, rows, own, width), gx.reshape(1, rows, own, width), dgain.transpose(1, 0, 2),
        da.transpose(1, 0, 2)[None], dwo[None], dc[None], dw1[None], dw2[None],
    )


def solution(mesh):
    return jax.shard_map(
        body,
        mesh=mesh,
        in_specs=(
            P("pipe", "dp", "tensor", None),
            P(None, "dp", None),
            P("dp", "tensor", None),
            P("pipe", None, None),
            P("pipe", None, None, "tensor"),
            P("pipe", "tensor", None),
            P("pipe", None, None, "tensor"),
            P("pipe", None, "tensor"),
            P("pipe", "tensor", None),
        ),
        out_specs=(
            P("pipe", "dp", "tensor", None),
            P("pipe", "dp", "tensor", None),
            P("pipe", None, "dp"),
            P("pipe", "dp", None, "tensor"),
            P("pipe", "tensor", "dp"),
            P("pipe", "dp", None, "tensor"),
            P("pipe", "dp", "tensor"),
            P("pipe", "tensor", "dp"),
        ),
        check_vma=False,
    )
```

```python
import functools

import jax
import jax.numpy as jnp
from jax import lax
from jax.experimental import pallas as pl
from jax.experimental.pallas import tpu as pltpu
from jax.sharding import PartitionSpec as P

EPS = 1e-05
MASKED = -1000000000.0
DH = 64
HALO = 64
F32 = jnp.float32
BF16 = jnp.bfloat16
GELU_C = 0.7978845608028654
GELU_A = 0.044715
MESH = pl.DeviceIdType.MESH
VMEM_LIMIT = 63 << 20


def mm(a, b):
    return lax.dot_general(a, b, (((1,), (0,)), ((), ())), preferred_element_type=F32)


def mm_nt(a, b):
    return lax.dot_general(a, b, (((1,), (1,)), ((), ())), preferred_element_type=F32)


def mm_tn(a, b):
    return lax.dot_general(a, b, (((0,), (0,)), ((), ())), preferred_element_type=F32)


def norm_parts(v):
    c = v - jnp.mean(v, axis=-1, keepdims=True)
    r = lax.rsqrt(jnp.mean(c * c, axis=-1, keepdims=True) + EPS)
    return c * r, r


def norm(v, gain):
    xhat, _ = norm_parts(v)
    return xhat * gain


def norm_back(v, gain, dn):
    xhat, r = norm_parts(v)
    dxh = dn * gain
    m1 = jnp.mean(dxh, axis=-1, keepdims=True)
    m2 = jnp.mean(dxh * xhat, axis=-1, keepdims=True)
    return r * (dxh - m1 - xhat * m2), jnp.sum(dn * xhat, axis=0, keepdims=True)


def lane_low(shape):
    return lax.broadcasted_iota(jnp.int32, shape, 1) < DH


def pair_join(a, b):
    return jnp.where(lane_low(a.shape), a, b)


def swap_halves(v):
    return pltpu.roll(v, DH, 1)


def attend(q2, k2, v2, mask, keep):
    low, lowq = lane_low(v2.shape), lane_low(q2.shape)
    one, zero = jnp.ones_like(v2), jnp.zeros_like(q2)
    outs = []
    for h in range(2):
        qh = jnp.where(lowq, q2, zero) if h == 0 else jnp.where(lowq, zero, q2)
        s = mask(mm_nt(qh, k2))
        e = jnp.exp(s - jnp.max(s, axis=-1, keepdims=True)).astype(BF16)
        keep(h, e)
        outs.append(mm(e, jnp.where(low, v2, one) if h == 0 else jnp.where(low, one, v2)))
    inv = 1.0 / swap_halves(pair_join(outs[1], outs[0]))
    return pair_join(*outs) * inv, inv


def attend_back(q2, k2, v2, do2, o2, inv, kept):
    low, lowq = lane_low(v2.shape), lane_low(q2.shape)
    one = jnp.ones_like(v2)
    scaled = do2.astype(F32) * inv.astype(F32)
    dob = scaled.astype(BF16)
    minus = (-swap_halves(dob.astype(F32) * o2.astype(F32))).astype(BF16)
    q_t, do_t = q2.T, dob.T
    dq, dk, dv = [], [], []
    for h in range(2):
        e = kept(h)
        rows = slice(h * DH, (h + 1) * DH)
        lhs = jnp.where(lowq, dob, minus) if h == 0 else jnp.where(lowq, minus, dob)
        dp = mm_nt(lhs, jnp.where(low, v2, one) if h == 0 else jnp.where(low, one, v2))
        ds = (dp * e.astype(F32)).astype(BF16)
        dq.append(mm(ds, k2))
        dv.append(mm(do_t[rows], e).astype(BF16))
        dk.append(mm(q_t[rows], ds).astype(BF16))
    return (pair_join(*dq) * (DH**-0.5)).astype(BF16), jnp.concatenate(dk, 0).T, jnp.concatenate(dv, 0).T


def gelu_parts(h):
    h2 = h * h
    half = 0.5 + 0.5 * jnp.tanh(h * (GELU_C + (GELU_C * GELU_A) * h2))
    u = h * half
    slope = half + u * ((1.0 - half) * (2.0 * GELU_C + (6.0 * GELU_C * GELU_A) * h2))
    return u, slope


def flip(i, bit):
    return i + bit - 2 * bit * lax.rem(lax.div(i, bit), 2)


def bit_of(i, bit):
    return lax.rem(lax.div(i, bit), 2)


def reversed_bits(i, count):
    out, bit = 0, 1
    while bit < count:
        out = 2 * out + (i // bit) % 2
        bit *= 2
    return out


class Links:
    def __init__(self, send, recv, local):
        self.send, self.recv, self.local = send, recv, local
        self.n = self.m = 0
        self.sent = []

    def take(self, count=1):
        self.n += count
        return self.n - count

    def remote(self, src, dst, device, at=None):
        at = self.take() if at is None else at
        return pltpu.make_async_remote_copy(
            src_ref=src, dst_ref=dst, send_sem=self.send.at[at], recv_sem=self.recv.at[at],
            device_id=device, device_id_type=MESH,
        )

    def here(self, src, dst):
        self.m += 1
        return pltpu.make_async_copy(src, dst, self.local.at[self.m - 1])


class Gather:
    def __init__(self, links, src, slot, depth, at, pieces=1, planes=None, last_straight=False):
        t, t2 = at["t"], at["t2"]
        half = depth // 2
        n = half // pieces
        whole = pl.ds(0, depth)
        if src is None:
            self.own = []
        elif planes is None:
            self.own = [links.here(src, slot(t, whole))]
        else:
            self.own = [links.here(src.at[i], slot(t, whole, i)) for i in range(planes)]
        self.inner = src is None or planes is not None
        self.straight = pieces - 1 if last_straight else None
        src = slot(t, whole) if self.inner else src
        self.core = links.remote(src, slot(t, whole), at["C"])
        self.over_y, self.over_z, self.core_a, self.core_b = [], [], [], []
        for i in range(pieces):
            mine = pl.ds(pl.multiple_of(at["b"] * half + i * n, n), n)
            other = pl.ds(pl.multiple_of((1 - at["b"]) * half + i * n, n), n)
            self.over_y.append(links.remote(src.at[mine], slot(t, mine), at["Y"]))
            if last_straight and i == pieces - 1:
                self.over_z.append(links.remote(src.at[other], slot(t, other), at["Y"]))
            else:
                self.over_z.append(links.remote(slot(t2, mine), slot(t2, mine), at["Z"][0]))
            self.core_a.append(links.remote(slot(t2, mine), slot(t2, mine), at["C"]))
            self.core_b.append(links.remote(slot(t2, other), slot(t2, other), at["C"]))

    def start(self):
        for c in self.own:
            c.start()
        if self.inner:
            for c in self.own:
                c.wait()
        for c in self.over_y:
            c.start()
        if self.straight is not None:
            self.over_z[self.straight].start()
        self.core.start()

    def step1(self, i=0):
        self.over_y[i].wait_recv()
        if i != self.straight:
            self.over_z[i].start()
        self.core_a[i].start()

    def step2(self, i=0):
        self.over_z[i].wait_recv()
        self.core_b[i].start()

    def ready(self, i):
        if i == 0 and not self.inner:
            for c in self.own:
                c.wait()
        if i == 1:
            self.core.wait_recv()
        if i == 3:
            for c in self.core_a + self.core_b:
                c.wait_recv()

    def finish(self):
        for c in [self.core] + self.over_y + self.over_z + self.core_a + self.core_b:
            c.wait_send()


class Reduce:
    def __init__(self, links, part, rc, ry, zb, zr, at, y_first):
        self.part, self.at, self.y_first = part, at, y_first
        self.rc, self.ry, self.zb, self.zr = rc, ry, zb, zr
        self.n = zb.shape[0]
        self.dp, self.rows = zb.shape[1:3]
        self.core = [links.remote(part(at[f]), rc.at[j], at["C"]) for j, f in enumerate(("t1", "t3"))]
        self.over_z, self.kept = [], []
        off, m, bit, k = 0, self.dp, 1, 0
        while m > 1:
            m //= 2
            b = bit_of(at["d"], bit)
            keep, give = off + b * m, off + (1 - b) * m
            self.over_z.append(links.remote(zb.at[:, pl.ds(give, m)], zr[k], at["Z"][k]))
            self.kept.append((keep, m))
            off, bit, k = keep, 2 * bit, k + 1
        self.off = off
        self.over_y = links.remote(part(at["t2"]) if y_first else zb.at[1, off], ry, at["Y"])

    def core_send(self, j):
        self.core[j].start()

    def into_zb(self, j, mine, theirs):
        for i in range(self.dp):
            where = pl.ds(i * self.rows, self.rows)
            self.zb[j, reversed_bits(i, self.dp)] = (mine[where, :].astype(F32) + theirs[where, :].astype(F32)).astype(BF16)

    def core_done(self):
        self.core[0].wait_recv()
        self.core[1].wait_recv()
        far, near = self.part(self.at["t2"]), self.part(self.at["t"])
        if self.y_first:
            far[...] = (far[...].astype(F32) + self.rc[1].astype(F32)).astype(BF16)
            self.over_y.start()
            near[...] = (near[...].astype(F32) + self.rc[0].astype(F32)).astype(BF16)
        else:
            self.into_zb(0, near, self.rc.at[0])
            self.into_zb(1, far, self.rc.at[1])
            self.over_z[0].start()

    def y_done(self, out=None):
        self.over_y.wait_recv()
        if self.y_first:
            self.into_zb(0, self.part(self.at["t"]), self.ry)
            self.over_z[0].start()
        else:
            out[...] = self.zb[0, self.off].astype(F32) + self.ry[...].astype(F32)

    def z_done(self, k, out=None):
        self.over_z[k].wait_recv()
        keep, m = self.kept[k]
        last = k == len(self.over_z) - 1
        if last and self.y_first:
            out[...] = self.zb[0, keep].astype(F32) + self.zr[k][0, 0].astype(F32)
        else:
            for j in range(self.n):
                live = self.zb.at[j, pl.ds(keep, m)]
                live[...] = (live[...].astype(F32) + self.zr[k][j].astype(F32)).astype(BF16)
            (self.over_y if last else self.over_z[k + 1]).start()

    def z_rest(self, out=None):
        for k in range(1, len(self.over_z)):
            self.z_done(k, out)

    def finish(self):
        for c in self.core + [self.over_y] + self.over_z:
            c.wait_send()


def layers(names, *refs):
    ref = dict(zip(names, refs))
    R = lambda name: ref[name]
    p, d, t = lax.axis_index("pipe"), lax.axis_index("dp"), lax.axis_index("tensor")
    is_enc, is_dec = p == 0, p == 1
    dp = lax.axis_size("dp")
    t1, t2, t3 = flip(t, 1), flip(t, 2), 3 - t
    zbits = []
    while 2 ** len(zbits) < dp:
        zbits.append((p, flip(d, 2 ** len(zbits)), t))
    at = dict(t=t, t1=t1, t2=t2, t3=t3, d=d, b=bit_of(d, 1), C=(p, d, t1), Y=(p, d, t2), T=(p, d, t3), X=(1 - p, d, t), Z=zbits)
    rows, own, width = R("x").shape
    win, cwin = own + 2 * HALO, 2 * own + 2 * HALO
    slots = 4 * own
    tokens = rows * own
    hw = R("wa").shape[2] // 3
    fw = R("w1").shape[2]
    inner = t % 3 != 0
    scale = jnp.asarray(DH**-0.5, BF16)
    gain_ref, x_ref = R("gains"), R("x")
    side = 3 * own // 4

    def rowsl(r, n=own):
        return pl.ds(pl.multiple_of(r * n, n), n)

    def lanes(s, n=hw):
        return pl.ds(pl.multiple_of(s * n, n), n)

    def far_lanes(s):
        return pl.ds(pl.multiple_of(s * 2 * hw + hw, hw), hw)

    def in_row(r, span):
        return pl.ds(pl.multiple_of(r * slots + span.start, HALO), span.size)

    def near_first(i):
        return 2 * lax.rem(lax.div(t, 2) + lax.div(i, 2), 2) + lax.rem(lax.rem(t, 2) + lax.rem(i, 2), 2)

    def far_first(i):
        return 2 * lax.rem(lax.div(t, 2) + lax.rem(lax.div(i + 1, 2), 2), 2) + lax.rem(lax.rem(t, 2) + 1 - lax.div(i, 2), 2)

    def seg_row(side_, r, start):
        row = jnp.broadcast_to(R("segs")[side_, pl.ds(r, 1), :].astype(F32), (8, slots))
        return pltpu.roll(row, lax.rem(2 * slots - start, slots), 1)

    def seg_column(side_, r):
        row = seg_row(side_, r, t * own)[:1, :own]
        return jnp.broadcast_to(row, (128, own)).T

    def spread(column, n):
        return jnp.concatenate([column] * (n // 128), axis=1)

    links = Links(R("send"), R("recv"), R("local"))

    def by_shard(name, n=None):
        def slot(s, span, i=None):
            full = R(name).at[s, span]
            return full if i is None else full.at[:, pl.ds(i * n, n)]

        return slot

    def by_columns(name, n, row):
        def slot(s, span):
            return R(name).at[pl.ds(pl.multiple_of(span.start + row, HALO), span.size), lanes(s, n)]

        return slot

    g_wa = Gather(links, R("wa_h"), by_shard("wa", hw), width, at, 2, 3)
    g_wo = Gather(links, R("wo_h"), by_shard("wo"), hw, at)
    g_w1 = Gather(links, R("w1_h"), by_shard("w1"), width, at, 2)
    g_w2 = Gather(links, R("w2_h"), by_shard("w2"), fw, at, 4, None, True)
    g_c1 = Gather(links, R("cx_h"), by_columns("dmf", hw, 0), 2 * width, at)
    c0_x = links.remote(R("cx_h"), R("dmf").at[pl.ds(2 * width, 2 * width), lanes(t)], at["X"])
    g_c0 = Gather(links, None, by_columns("dmf", hw, 2 * width), 2 * width, at)
    loads = [links.here(R(n + "_h"), R(n)) for n in ("x", "cot", "segs")]
    x_right = links.remote(R("x_h").at[:, pl.ds(own - HALO, HALO)], R("xh").at[0], (p, d, lax.rem(t + 1, 4)))
    x_left = links.remote(R("x_h").at[:, pl.ds(0, HALO)], R("xh").at[1], (p, d, lax.rem(t + 3, 4)))
    base_mem, base_memc, base_memt = links.take(rows), links.take(rows), links.take(rows)
    base_dmc, base_dmt, base_dmx = links.take(rows), links.take(rows), links.take(rows)
    block = pl.ds(pl.multiple_of(t * own, own), own)
    block1 = pl.ds(pl.multiple_of(t1 * own, own), own)
    edge_out = pl.ds(pl.multiple_of(lax.rem(own // 2 + side * t, slots), HALO), side)
    edge_in = pl.ds(pl.multiple_of(lax.rem(own // 2 + side * t3, slots), HALO), side)

    def mem_x(r):
        return links.remote(R("secs").at[rowsl(r)], R("memf").at[in_row(r, block)], at["X"], base_mem + r)

    def mem_c(r):
        return links.remote(R("memf").at[in_row(r, block)], R("memf").at[in_row(r, block)], at["C"], base_memc + r)

    def mem_t(r):
        return links.remote(R("memf").at[in_row(r, edge_out)], R("memf").at[in_row(r, edge_out)], at["T"], base_memt + r)

    def dm_rows(r, span):
        return R("dmf").at[in_row(r, span)]

    def dm_c(r):
        return links.remote(dm_rows(r, block1), R("rcc").at[r], at["C"], base_dmc + r)

    def dm_t(r):
        return links.remote(dm_rows(r, edge_in), R("rct").at[r], at["T"], base_dmt + r)

    def dm_x(r):
        return links.remote(R("rcc").at[r], R("rcc").at[r], at["X"], base_dmx + r)

    def by_rows(name, m, col=0):
        return lambda s: R(name).at[pl.ds(pl.multiple_of(s * width, width), width), pl.ds(col, m)]

    def by_lanes(name, m, row=0):
        return lambda s: R(name).at[pl.ds(row, width), lanes(s, m)]

    def reduce_of(name, part, y_first=True):
        zr = [R(f"zr{k}_{name}") for k in range(len(zbits))]
        return Reduce(links, part, R("rc_" + name), R("ry_" + name), R("zb_" + name), zr, at, y_first)

    fh = fw // 2
    r_w2 = [reduce_of(f"w2{j}", by_rows("dw2", fh, j * fh), j == 1) for j in range(2)]
    r_w1 = [reduce_of(f"w1{j}", by_rows("dmf", fh, j * fh), j == 0) for j in range(2)]
    r_wo = reduce_of("wo", by_lanes("dwo", hw))
    r_wa = [reduce_of(f"wa{j}", by_rows("cp", hw, j * hw)) for j in range(3)]
    r_c0 = reduce_of("c0", by_lanes("kv", 2 * hw))
    r_c1 = reduce_of("c1", by_lanes("kv", 2 * hw, width))
    w2_out = [R("dw2_o").at[:, pl.ds(j * fh, fh)] for j in range(2)]
    w1_out = [R("dw1_o").at[:, pl.ds(j * fh, fh)] for j in range(2)]
    wa_out = [R("da_o").at[:, pl.ds(j * hw, hw)] for j in range(3)]
    c0_back = links.remote(R("dc0"), R("dc0r"), at["X"])
    dn_right = links.remote(R("xh").at[1], R("dhr").at[0], (p, d, lax.rem(t + 1, 4)))
    dn_left = links.remote(R("xh").at[0], R("dhr").at[1], (p, d, lax.rem(t + 3, 4)))
    gain_over_t = [links.remote(R("dgt").at[t], R("dgt").at[t], at[f]) for f in ("C", "Y", "T")]
    gain_over_d = []
    for k in range(1, dp):
        to = lax.rem(d + k, dp)
        gain_over_d.append(links.remote(R("dgd").at[d], R("dgd").at[d], (p, to, t)))

    @pl.when(is_dec)
    def _():
        for at_t, start in ((0, 2 * own), (1, 2 * own + side), (3, 2 * own - 2 * HALO)):
            @pl.when(t == at_t)
            def _():
                for r in range(rows):
                    R("memf")[pl.ds(r * slots + start, 2 * HALO), :] = jnp.zeros((2 * HALO, width), BF16)

    for c in loads:
        c.start()
    barrier = pltpu.get_barrier_semaphore()
    partners = [at["C"], at["Y"], at["T"], at["X"]] + [(p, lax.rem(d + k, dp), t) for k in range(1, dp)]
    for dev in partners:
        pl.semaphore_signal(barrier, inc=1, device_id=dev, device_id_type=MESH)
    pl.semaphore_wait(barrier, len(partners))

    pl.when(t < 3)(x_right.start)
    pl.when(t > 0)(x_left.start)
    g_wa.start()
    g_wo.start()

    @pl.when(is_enc)
    def _():
        c0_x.start()
        g_w1.start()
        g_w2.start()

    @pl.when(is_dec)
    def _():
        g_c1.start()

    for c in loads:
        c.wait()

    nw_ref, bias_ref = R("nw"), R("bias")
    gain0, gain1, gain2 = gain_ref[0], gain_ref[1], gain_ref[2]
    for r in range(rows):
        nw_ref[pl.ds(r * win + HALO, own), :] = norm(x_ref[r].astype(F32), gain0).astype(BF16)
        keys = seg_row(p, r, lax.rem(t * own + slots - HALO, slots))[:1, :win]
        same = spread(seg_column(p, r), win) == keys
        qpos = lax.broadcasted_iota(jnp.int32, (own, win), 0)
        kpos = lax.broadcasted_iota(jnp.int32, (own, win), 1) - HALO
        before = kpos - qpos <= jnp.where(is_enc, 4 * win, 0)
        bias_ref[r] = jnp.where(same & before, 0.0, MASKED)

    @pl.when(t == 0)
    def _():
        R("xh")[0] = jnp.zeros((rows, HALO, width), BF16)

    @pl.when(t == 3)
    def _():
        R("xh")[1] = jnp.zeros((rows, HALO, width), BF16)

    pl.when(t > 0)(x_right.wait_recv)
    pl.when(t < 3)(x_left.wait_recv)
    for r in range(rows):
        nw_ref[pl.ds(r * win, HALO), :] = norm(R("xh")[0, r].astype(F32), gain0).astype(BF16)
        nw_ref[pl.ds(r * win + HALO + own, HALO), :] = norm(R("xh")[1, r].astype(F32), gain0).astype(BF16)

    def after_pair(i):
        @pl.when(i == 0)
        def _():
            g_wa.step1(0)

        @pl.when(i == 1)
        def _():
            g_wa.step1(1)
            g_wo.step1()
            g_wa.step2(0)

            @pl.when(is_dec)
            def _():
                c0_x.wait_recv()
                g_c0.start()
                g_w2.start()
                g_w1.start()
                g_c1.step1()

            pl.when(is_enc)(lambda: g_w1.step1(0))
            g_wa.step2(1)

        @pl.when(i == 2)
        def _():
            g_wo.step2()
            pl.when(is_enc)(lambda: g_w1.step1(1))

        @pl.when(i == 3)
        def _():
            pl.when(is_dec)(g_c0.step1)

    def wait_ready(i, *weights):
        for k in range(4):
            @pl.when(i == k)
            def _():
                for w in weights:
                    w.ready(k)

    q_ref, k_ref, v_ref, p_ref, o_ref, inv_ref = R("q"), R("k"), R("v"), R("p"), R("o"), R("inv")

    def self_pair(i, _):
        s = near_first(i)
        wait_ready(i, g_wa)
        packed = mm(nw_ref[...], R("wa")[s])
        for r in range(rows):
            q_ref[s, r] = packed[r * win + HALO : r * win + HALO + own, :hw].astype(BF16) * scale
            k_ref[s, r] = packed[r * win : (r + 1) * win, hw : 2 * hw].astype(BF16)
            v_ref[s, r] = packed[r * win : (r + 1) * win, 2 * hw :].astype(BF16)
        for r in range(rows):
            def keep(h, e):
                p_ref[s, r, h] = e

            o2, inv = attend(q_ref[s, r], k_ref[s, r], v_ref[s, r], lambda scores: scores + bias_ref[r], keep)
            o_ref[pl.ds(r * own, own), lanes(s)] = o2.astype(BF16)
            inv_ref[pl.ds(r * own, own), lanes(s)] = inv.astype(BF16)
        after_pair(i)
        return 0

    lax.fori_loop(0, 4, self_pair, 0)
    for k in range(4):
        g_wo.ready(k)
    r1_ref, r2_ref, n2_ref, n3_ref = R("r1"), R("r2"), R("n2"), R("n3")
    u_ref, gp_ref, sec_ref = R("u"), R("gp"), R("secs")
    acc_ref, g_ref, gb_ref, do_ref = R("acc"), R("g"), R("gb"), R("do")
    first = mm(o_ref[...], R("wo")[...].reshape(4 * hw, width))
    for r in range(rows):
        r1_ref[pl.ds(r * own, own), :] = x_ref[r].astype(F32) + first[r * own : (r + 1) * own]
    n2_ref[...] = norm(r1_ref[...], gain1).astype(BF16)

    @pl.when(is_enc)
    def _():
        r2_ref[...] = r1_ref[...]

        def up(i):
            s = near_first(i)
            u, gp = gelu_parts(mm(n2_ref[...], R("w1")[s]))
            u_ref[s] = u.astype(BF16)
            gp_ref[s] = gp.astype(BF16)
            return s

        g_w2.step1(0)
        g_w1.step2(0)

        def near(i, _):
            wait_ready(i, g_w1, g_w2)
            s = up(i)
            r2_ref[...] += mm(u_ref[s], R("w2")[s])

            @pl.when(i == 0)
            def _():
                g_w2.step1(1)
                g_w1.step2(1)

            @pl.when(i == 1)
            def _():
                g_w2.step1(2)
                g_w2.step2(0)
                g_w2.step1(3)

            return 0

        lax.fori_loop(0, 2, near, 0)

        def far(i, _):
            wait_ready(i, g_w1)
            up(i)
            pl.when(i == 2)(lambda: g_w2.step2(1))

            @pl.when(i == 3)
            def _():
                g_w2.step2(2)
                g_w2.step2(3)

            return 0

        lax.fori_loop(2, 4, far, 0)
        g_w2.ready(3)
        far1, far2 = near_first(2), near_first(3)

        def row(r, _):
            rs = rowsl(r)
            total = r2_ref[rs, :] + mm(u_ref[far1, rs, :], R("w2")[far1]) + mm(u_ref[far2, rs, :], R("w2")[far2])
            r2_ref[rs, :] = total
            sec_ref[rs, :] = norm(total, gain2).astype(BF16)
            mem_x(r).start()
            return 0

        lax.fori_loop(0, rows, row, 0)

    def sends(reductions, i):
        for j in range(2):
            @pl.when(i == j)
            def _():
                for reduction in reductions:
                    reduction.core_send(j)

    cstart = pl.multiple_of(jnp.minimum(t * (own - HALO), slots - cwin), HALO)
    cwindow = pl.ds(cstart, cwin)
    kv_ref, cq_ref, cp_ref, dkv_ref, cinv_ref = R("kv"), R("cq"), R("cp"), R("dkv"), R("cinv")
    c0_ref, cqw_ref, cow_ref, oc_ref, cot_ref = R("c0"), R("cqw"), R("cow"), R("oc"), R("cot")
    cols, keys_ref = R("cols"), R("keys")

    @pl.when(is_dec)
    def _():
        g_w2.step1(0)
        g_c1.step2()
        for k in range(4):
            g_c1.ready(k)
        pick_shape = (width // 4, width // 2)
        twice = 2 * lax.broadcasted_iota(jnp.int32, pick_shape, 0)
        at_col = lax.broadcasted_iota(jnp.int32, pick_shape, 1)
        picks = [jnp.where(at_col == twice + j, 1.0, 0.0).astype(BF16) for j in range(2)]

        def unweave(base, m):
            return [mm(pick, R("dmf")[pl.ds(base + m * (width // 2), width // 2), :]).astype(BF16) for pick in picks]

        for m in range(4):
            span = pl.ds(m * (width // 4), width // 4)
            cqw_ref[span, :], cow_ref[span, :] = unweave(0, m)
        cq_ref[...] = mm(n2_ref[...], cqw_ref[...]).astype(BF16) * scale
        g_w2.step1(1)
        g_c0.step2()
        g_w2.step1(2)
        g_w2.step1(3)
        kv_ref[...] = jnp.zeros_like(kv_ref)
        for r in range(rows):
            cols[r] = seg_column(1, r)
            keys_ref[r] = seg_row(0, r, cstart)[:, :cwin]
        for k in range(4):
            g_c0.ready(k)
        for m in range(4):
            span = pl.ds(m * (width // 4), width // 4)
            ck, cv = unweave(2 * width, m)
            for s in range(4):
                c0_ref[span, 2 * s * hw : (2 * s + 1) * hw] = ck[:, s * hw : (s + 1) * hw]
                c0_ref[span, (2 * s + 1) * hw : (2 * s + 2) * hw] = cv[:, s * hw : (s + 1) * hw]
        g_w1.step1(0)
        g_w2.step2(0)
        g_w2.step2(1)
        g_w1.step1(1)
        for g in (g_c1, g_c0):
            g.finish()
        R("dmf")[...] = jnp.zeros_like(R("dmf"))
        g_w2.step2(2)
        g_w2.step2(3)
        g_w1.step2(0)
        for k in range(4):
            g_w2.ready(k)

        def early(s, _):
            gp_ref[s] = mm_nt(cot_ref[...], R("w2")[s]).astype(BF16)
            return 0

        lax.fori_loop(0, 4, early, 0)

        def pass_memory_on(r):
            mem_x(r).wait_recv()
            mem_c(r).start()
            pl.when(inner)(mem_t(r).start)

        def settle(r):
            span = pl.ds(0, own)
            dm_c(r).wait_recv()
            acc_ref[span, :] = R("dmf")[in_row(r, block), :].astype(F32) + R("rcc")[r].astype(F32)

            @pl.when(inner)
            def _():
                dm_t(r).wait_recv()
                place = pl.ds(pl.multiple_of((2 - t) * (own - side), HALO), side)
                acc_ref[place, :] += R("rct")[r].astype(F32)

            R("rcc")[r] = acc_ref[span, :].astype(BF16)
            dm_x(r).start()

        def row(r, _):
            rs = rowsl(r)

            def project(span):
                kv_ref[span, :] = mm(R("memf")[in_row(r, span), :], c0_ref[...]).astype(BF16)

            @pl.when(r == 0)
            def _():
                g_w1.step2(1)
                pass_memory_on(0)

            project(block)
            pl.when(r > 0)(lambda: settle(r - 1))
            mem_c(r).wait_recv()
            project(block1)

            @pl.when(inner)
            def _():
                mem_t(r).wait_recv()
                project(edge_in)

            def cross(i, _):
                for s in range(4):
                    def keep(h, e):
                        cp_ref[rowsl(2 * s + h), :] = e

                    def mask(scores):
                        same = spread(cols[r], cwin) == keys_ref[r, pl.ds(0, 1), :]
                        return jnp.where(same, scores, MASKED)

                    o2, inv = attend(cq_ref[rs, lanes(s)], kv_ref[cwindow, lanes(2 * s)], kv_ref[cwindow, lanes(2 * s + 1)], mask, keep)
                    oc_ref[rs, lanes(s)] = o2.astype(BF16)
                    cinv_ref[:, lanes(s)] = inv.astype(BF16)
                return 0

            cross(0, 0)
            pl.when(r < rows - 1)(lambda: pass_memory_on(r + 1))
            r2_ref[rs, :] = r1_ref[rs, :] + mm_nt(oc_ref[rs, :], cow_ref[...])
            n3_ref[rs, :] = norm(r2_ref[rs, :], gain2).astype(BF16)

            @pl.when(r == 0)
            def _():
                for k in range(4):
                    g_w1.ready(k)

            dn = pl.ds(0, own)
            acc_ref[dn, :] = jnp.zeros((own, width), F32)

            def feed(i, _):
                back = acc_ref[dn, :]
                for s in range(4):
                    u, gp = gelu_parts(mm(n3_ref[rs, :], R("w1")[s]))
                    u = u.astype(BF16)
                    u_ref[s, rs, :] = u
                    dh = (gp_ref[s, rs, :].astype(F32) * gp).astype(BF16)
                    gp_ref[s, rs, :] = dh
                    back += mm_nt(dh, R("w1")[s])
                acc_ref[dn, :] = back
                return 0

            feed(0, 0)
            dx, dg = norm_back(r2_ref[rs, :], gain2, acc_ref[dn, :])
            R("dg")[r, pl.ds(2, 1), :] = dg
            g2 = cot_ref[rs, :].astype(F32) + dx
            g_ref[rs, :] = g2
            gb_ref[rs, :] = g2.astype(BF16)
            do_ref[rs, :] = mm(gb_ref[rs, :], cow_ref[...]).astype(BF16)
            ws = pl.ds(pl.multiple_of(r * cwin, HALO), cwin)

            def back(i, _):
                for s in range(4):
                    dq, dk, dv = attend_back(
                        cq_ref[rs, lanes(s)], kv_ref[cwindow, lanes(2 * s)], kv_ref[cwindow, lanes(2 * s + 1)],
                        do_ref[rs, lanes(s)], oc_ref[rs, lanes(s)], cinv_ref[:, lanes(s)], lambda h: cp_ref[rowsl(2 * s + h), :],
                    )
                    cq_ref[rs, lanes(s)] = dq
                    dkv_ref[ws, lanes(2 * s)] = dk
                    dkv_ref[ws, lanes(2 * s + 1)] = dv
                return 0

            back(0, 0)
            R("dmf")[in_row(r, cwindow), :] = mm_nt(dkv_ref[ws, :], c0_ref[...]).astype(BF16)
            dm_c(r).start()
            pl.when(inner)(dm_t(r).start)

            @pl.when(r == rows - 1)
            def _():
                def w2_grad(i, _):
                    s = far_first(i)
                    R("dw2")[rowsl(s, width), :] = mm_tn(cot_ref[...], u_ref[s]).astype(BF16)
                    sends(r_w2, i)
                    return 0

                lax.fori_loop(0, 4, w2_grad, 0)
                settle(r)

            return 0

        lax.fori_loop(0, rows, row, 0)
        for r in range(rows):
            dm_c(r).wait_send()
            pl.when(inner)(dm_t(r).wait_send)

        def w1_grad(i, _):
            s = far_first(i)
            R("dmf")[rowsl(s, width), :] = mm_tn(n3_ref[...], gp_ref[s]).astype(BF16)
            sends(r_w1, i)

            @pl.when(i == 0)
            def _():
                r_w2[0].core_done()
                r_w2[1].core_done()

            return 0

        lax.fori_loop(0, 4, w1_grad, 0)

        def c0_grad(i, _):
            s = far_first(i)
            total = mm_tn(R("memf")[in_row(0, cwindow), :], dkv_ref[pl.ds(0, cwin), lanes(s, 2 * hw)])
            for r in range(1, rows):
                total += mm_tn(R("memf")[in_row(r, cwindow), :], dkv_ref[pl.ds(r * cwin, cwin), lanes(s, 2 * hw)])
            r_c0.part(s)[...] = total.astype(BF16)
            sends([r_c0], i)

            @pl.when(i == 1)
            def _():
                r_w1[0].core_done()
                r_w1[1].core_done()

            return 0

        lax.fori_loop(0, 4, c0_grad, 0)
        def query_norm(r, _):
            rs = rowsl(r)
            dx, dg = norm_back(r1_ref[rs, :], gain1, mm_nt(cq_ref[rs, :], cqw_ref[...]))
            R("dg")[r, pl.ds(1, 1), :] = dg
            g_ref[rs, :] += dx
            return 0

        lax.fori_loop(0, rows, query_norm, 0)
        dcq = mm_tn(n2_ref[...], cq_ref[...]).astype(BF16)
        dco = mm_tn(gb_ref[...], oc_ref[...]).astype(BF16)
        r_c0.core_done()
        for s in range(4):
            r_c1.part(s)[:, :hw] = dcq[:, s * hw : (s + 1) * hw]
            r_c1.part(s)[:, hw:] = dco[:, s * hw : (s + 1) * hw]
        sends([r_c1], 0)
        sends([r_c1], 1)

    @pl.when(is_enc)
    def _():
        def receive(r):
            rs = rowsl(r)
            dm_x(r).wait_recv()
            dx, dg = norm_back(r2_ref[rs, :], gain2, R("rcc")[r].astype(F32))
            R("dg")[r, pl.ds(2, 1), :] = dg
            g_ref[rs, :] = dx
            gb_ref[rs, :] = dx.astype(BF16)

        def hidden_back(s, rs):
            dh = (mm_nt(gb_ref[rs, :], R("w2")[s]) * gp_ref[s, rs, :].astype(F32)).astype(BF16)
            gp_ref[s, rs, :] = dh
            acc_ref[rs, :] += mm_nt(dh, R("w1")[s])

        head, last = pl.ds(0, (rows - 1) * own), pl.ds((rows - 1) * own, own)
        acc_ref[pl.ds(0, tokens), :] = jnp.zeros((tokens, width), F32)
        for r in range(rows - 1):
            receive(r)

        def head_grads(s, _):
            R("dw2")[rowsl(s, width), :] = mm_tn(gb_ref[head, :], u_ref[s, head, :]).astype(BF16)
            hidden_back(s, head)
            return 0

        lax.fori_loop(0, 4, head_grads, 0)
        receive(rows - 1)

        def w2_grad(i, _):
            s = far_first(i)
            part = R("dw2").at[rowsl(s, width)]
            part[...] = (part[...].astype(F32) + mm_tn(gb_ref[last, :], u_ref[s, last, :])).astype(BF16)
            sends(r_w2, i)
            return 0

        lax.fori_loop(0, 4, w2_grad, 0)

        def w1_grad(i, _):
            s = far_first(i)
            hidden_back(s, last)

            @pl.when(i == 1)
            def _():
                r_w2[0].core_done()
                r_w2[1].core_done()

            R("dmf")[rowsl(s, width), :] = mm_tn(n2_ref[...], gp_ref[s]).astype(BF16)
            sends(r_w1, i)
            return 0

        lax.fori_loop(0, 4, w1_grad, 0)
        r_w1[0].core_done()
        r_w1[1].core_done()
        dx, dg = norm_back(r1_ref[...], gain1, acc_ref[pl.ds(0, tokens), :])
        R("dg")[0, pl.ds(1, 1), :] = dg
        for r in range(1, rows):
            R("dg")[r, pl.ds(1, 1), :] = jnp.zeros_like(dg)
        g_ref[...] += dx

    sec_out = links.here(sec_ref, R("sec"))
    pl.when(is_enc)(sec_out.start)
    gb_ref[...] = g_ref[...].astype(BF16)
    R("dwo")[...] = mm_tn(gb_ref[...], o_ref[...]).astype(BF16)
    r_wo.core_send(0)
    r_wo.core_send(1)
    do_ref[...] = mm_nt(gb_ref[...], R("wo")[...].reshape(4 * hw, width)).astype(BF16)
    acc_ref[...] = jnp.zeros_like(acc_ref)
    dqkv_ref = R("dqkv")
    for r in range(rows):
        dqkv_ref[pl.ds(r * win, HALO), :hw] = jnp.zeros((HALO, hw), BF16)
        dqkv_ref[pl.ds(r * win + HALO + own, HALO), :hw] = jnp.zeros((HALO, hw), BF16)

    def self_back(i, _):
        s = far_first(i)
        for r in range(rows):
            rs = pl.ds(r * own, own)
            dq, dk, dv = attend_back(
                q_ref[s, r], k_ref[s, r], v_ref[s, r], do_ref[rs, lanes(s)], o_ref[rs, lanes(s)], inv_ref[rs, lanes(s)],
                lambda h: p_ref[s, r, h],
            )
            dqkv_ref[pl.ds(r * win + HALO, own), :hw] = dq
            dqkv_ref[pl.ds(r * win, win), hw : 2 * hw] = dk
            dqkv_ref[pl.ds(r * win, win), 2 * hw :] = dv
        R("cp")[rowsl(s, width), pl.ds(0, 3 * hw)] = mm_tn(nw_ref[...], dqkv_ref[...]).astype(BF16)
        sends(r_wa, i)
        acc_ref[...] += mm_nt(dqkv_ref[...], R("wa")[s])

        @pl.when(i == 0)
        def _():
            r_w2[0].z_done(0)
            pl.when(is_dec)(r_c1.core_done)
            r_wo.core_done()
            r_w2[1].y_done()

        @pl.when(i == 2)
        def _():
            r_w1[1].z_done(0)
            r_w1[0].y_done()

        @pl.when(i == 3)
        def _():
            pl.when(is_enc)(r_wo.y_done)
            r_w2[1].z_done(0, w2_out[1])
            r_w2[0].z_rest()
            pl.when(is_dec)(r_c0.y_done)

        return 0

    lax.fori_loop(0, 4, self_back, 0)
    for r in range(rows):
        R("xh")[0, r] = acc_ref[pl.ds(r * win, HALO), :].astype(BF16)
        R("xh")[1, r] = acc_ref[pl.ds(r * win + HALO + own, HALO), :].astype(BF16)
    pl.when(t < 3)(dn_right.start)
    pl.when(t > 0)(dn_left.start)
    for j in range(3):
        r_wa[j].core_done()

    @pl.when(is_dec)
    def _():
        def decoded(r, _):
            rs = rowsl(r)
            total = r2_ref[rs, :]
            for s in range(4):
                total += mm(u_ref[s, rs, :], R("w2")[s])
            sec_ref[rs, :] = total.astype(BF16)
            return 0

        lax.fori_loop(0, rows, decoded, 0)
        sec_out.start()

    @pl.when(t == 0)
    def _():
        R("dhr")[0] = jnp.zeros((rows, HALO, width), BF16)

    @pl.when(t == 3)
    def _():
        R("dhr")[1] = jnp.zeros((rows, HALO, width), BF16)

    @pl.when(is_dec)
    def _():
        r_w1[0].z_done(0, w1_out[0])
        r_w1[1].z_rest()
        r_c1.y_done()
        r_w2[1].z_rest(w2_out[1])
        r_wo.y_done()
        r_c0.z_done(0, R("dc0"))

    pl.when(t > 0)(dn_right.wait_recv)
    pl.when(t < 3)(dn_left.wait_recv)
    for r in range(rows):
        lo, hi = pl.ds(r * win + HALO, HALO), pl.ds(r * win + own, HALO)
        acc_ref[lo, :] += R("dhr")[0, r].astype(F32)
        acc_ref[hi, :] += R("dhr")[1, r].astype(F32)
    total = jnp.zeros((1, width), F32)
    for r in range(rows):
        rs = pl.ds(r * own, own)
        dx, dg = norm_back(x_ref[r].astype(F32), gain0, acc_ref[pl.ds(r * win + HALO, own), :])
        gb_ref[rs, :] = (g_ref[rs, :] + dx).astype(BF16)
        total += dg
    dgt, dgd = R("dgt"), R("dgd")
    dgt[t] = jnp.zeros((8, width), F32)
    dgt[t, pl.ds(0, 1), :] = total
    dgt[t, pl.ds(1, 2), :] = sum(R("dg")[r, pl.ds(1, 2), :] for r in range(rows))
    for c in gain_over_t:
        c.start()
    gx_out = links.here(gb_ref, R("gx"))
    gx_out.start()

    def gains_over_t():
        for c in gain_over_t:
            c.wait_recv()
        dgd[d] = dgt[0] + dgt[1] + dgt[2] + dgt[3]
        for c in gain_over_d:
            c.start()

    def gains_over_d():
        total = jnp.zeros((8, width), F32)
        for c in gain_over_d:
            c.wait_recv()
        for k in range(dp):
            total += dgd[k]
        R("dgain")[...] = pltpu.roll(total, lax.rem(width - d * (width // dp), width), 1)

    @pl.when(is_enc)
    def _():
        r_w2[0].y_done(w2_out[0])
        r_w1[0].z_done(0, w1_out[0])
        r_w1[1].z_rest()
        r_wa[0].y_done()
        r_wo.z_done(0, R("dwo_o"))
        r_wa[1].y_done()
        gains_over_t()
        r_w2[1].z_rest(w2_out[1])
        r_wa[0].z_done(0, wa_out[0])
        r_wa[2].y_done()
        r_w1[0].z_rest(w1_out[0])
        r_wa[1].z_done(0, wa_out[1])
        r_w1[1].y_done(w1_out[1])
        gains_over_d()
        r_wo.z_rest(R("dwo_o"))

    @pl.when(is_dec)
    def _():
        r_w2[0].y_done(w2_out[0])
        r_w1[0].z_rest(w1_out[0])
        r_c1.z_done(0, R("dc"))
        r_wa[0].y_done()
        r_wo.z_done(0, R("dwo_o"))
        r_wa[1].y_done()
        r_c0.z_rest(R("dc0"))
        c0_back.start()
        r_wa[0].z_done(0, wa_out[0])
        r_wa[2].y_done()
        r_c1.z_rest(R("dc"))
        r_wa[1].z_done(0, wa_out[1])
        r_w1[1].y_done(w1_out[1])
        gains_over_t()
        r_wo.z_rest(R("dwo_o"))
        gains_over_d()

    r_wa[2].z_done(0, wa_out[2])
    for j in range(3):
        r_wa[j].z_rest(wa_out[j])

    sec_out.wait()
    gx_out.wait()
    for g in (g_wa, g_wo, g_w1, g_w2):
        g.finish()
    for g in r_w2 + r_w1 + [r_wo] + r_wa:
        g.finish()
    for c in gain_over_t + gain_over_d:
        c.wait_send()
    pl.when(t < 3)(x_right.wait_send)
    pl.when(t > 0)(x_left.wait_send)
    pl.when(t < 3)(dn_right.wait_send)
    pl.when(t > 0)(dn_left.wait_send)

    @pl.when(is_enc)
    def _():
        c0_x.wait_send()
        for r in range(rows):
            mem_x(r).wait_send()
        c0_back.wait_recv()
        R("dc")[...] = R("dc0r")[...]

    @pl.when(is_dec)
    def _():
        for g in (r_c0, r_c1):
            g.finish()
        for r in range(rows):
            mem_c(r).wait_send()
            pl.when(inner)(mem_t(r).wait_send)
            dm_x(r).wait_send()
        c0_back.wait_send()


def arrange(aligned, sec, gx, dgain, da, dwo, dc, dw1, dw2, sec_o, gx_o, dgain_o, da_o, dwo_o, dc_o, dw1_o, dw2_o):
    share, hw = dwo.shape
    sec_o[...] = sec[...]
    gx_o[...] = gx[...]
    for i in range(3):
        dgain_o[i] = dgain[pl.ds(i, 1), pl.ds(0, share)]
        da_o[i] = da[:, pl.ds(i * hw, hw)]
    for i in range(2):
        dc_o[:, i, :] = dc[:, pl.ds(i * hw, hw)]
    dw1_o[...] = dw1[...]
    dwo_o[...] = dwo[...].T if aligned else dwo[...]
    dw2_o[...] = dw2[...].T if aligned else dw2[...]


def body(embeds, segments, cotangent, norm_gains, attn_in, attn_out, cross_proj, ffn_in, ffn_out):
    dp = lax.axis_size("dp")
    rows, own, width = embeds.shape[1:]
    slots = segments.shape[2]
    hw = attn_in.shape[3]
    fw = ffn_in.shape[2]
    win = own + 2 * HALO
    cwin = 2 * own + 2 * HALO
    tokens = rows * own
    side = 3 * own // 4
    share = width // dp
    zsteps = (dp - 1).bit_length()

    ins = dict(
        x_h=embeds[0], segs_h=segments, gains=norm_gains.transpose(1, 0, 2), cot_h=cotangent.reshape(tokens, width),
        wa_h=attn_in[0].transpose(1, 0, 2), wo_h=attn_out[0], w1_h=ffn_in[0], w2_h=ffn_out[0],
        cx_h=cross_proj[0].reshape(2 * width, hw),
    )
    outs = dict(
        sec=((tokens, width), BF16), gx=((tokens, width), BF16), dgain=((8, width), F32),
        da_o=((share, 3 * hw), F32), dwo_o=((share, hw), F32), dc=((share, 2 * hw), F32),
        dw1_o=((share, fw), F32), dw2_o=((share, fw), F32),
    )
    vm = dict(
        x=((rows, own, width), BF16), cot=((tokens, width), BF16), segs=(segments.shape, jnp.int32),
        wa=((4, width, 3 * hw), BF16), wo=((4, hw, width), BF16), w1=((4, width, fw), BF16), w2=((4, fw, width), BF16),
        c0=((width, 8 * hw), BF16), cqw=((width, 4 * hw), BF16), cow=((width, 4 * hw), BF16),
        xh=((2, rows, HALO, width), BF16), nw=((rows * win, width), BF16),
        q=((4, rows, own, hw), BF16), k=((4, rows, win, hw), BF16), v=((4, rows, win, hw), BF16),
        p=((4, rows, 2, own, win), BF16), o=((tokens, width), BF16), inv=((tokens, width), BF16), bias=((rows, own, win), F32),
        r1=((tokens, width), F32), r2=((tokens, width), F32), n2=((tokens, width), BF16), n3=((tokens, width), BF16),
        u=((4, tokens, fw), BF16), gp=((4, tokens, fw), BF16), secs=((tokens, width), BF16),
        acc=((rows * win, width), F32), g=((tokens, width), F32), gb=((tokens, width), BF16), do=((tokens, width), BF16),
        memf=((max(rows * slots, 4 * width), max(width, fw)), BF16), kv=((slots, 8 * hw), BF16), cq=((tokens, width), BF16),
        cp=((max(8 * own, 4 * width), cwin), BF16), cinv=((own, width), BF16), oc=((tokens, width), BF16),
        cols=((rows, own, 128), F32), keys=((rows, 8, cwin), F32),
        dkv=((rows * cwin, 8 * hw), BF16), dmf=((max(rows * slots, 4 * width), max(width, fw)), BF16),
        rcc=((rows, own, width), BF16), rct=((rows, side, width), BF16),
        dg=((rows, 8, width), F32),
        dqkv=((rows * win, 3 * hw), BF16), dhr=((2, rows, HALO, width), BF16),
        dgt=((4, 8, width), F32), dgd=((dp, 8, width), F32),
        dw2=((4 * width, fw), BF16), dwo=((width, 4 * hw), BF16),
        dc0=((share, 2 * hw), F32), dc0r=((share, 2 * hw), F32),
    )
    sums = dict(w20=fw // 2, w21=fw // 2, w10=fw // 2, w11=fw // 2, wo=hw, wa0=hw, wa1=hw, wa2=hw, c0=2 * hw, c1=2 * hw)
    for name, m in sums.items():
        shards = 2 if name in ("w20", "w11") else 1
        vm["rc_" + name] = ((2, width, m), BF16)
        vm["ry_" + name] = ((share if shards == 2 else width, m), BF16)
        vm["zb_" + name] = ((shards, dp, share, m), BF16)
        for k in range(zsteps):
            vm[f"zr{k}_{name}"] = ((shards, dp >> (k + 1), share, m), BF16)
    copies = 140 + 12 * zsteps + dp
    sems = dict(send=pltpu.SemaphoreType.DMA((copies,)), recv=pltpu.SemaphoreType.DMA((copies,)), local=pltpu.SemaphoreType.DMA((16,)))
    in_hbm = {n for n in ins if n.endswith("_h")}
    out_hbm = {"sec", "gx"}
    results = pl.pallas_call(
        functools.partial(layers, list(ins) + list(outs) + list(vm) + list(sems)),
        name="layers",
        out_shape=[jax.ShapeDtypeStruct(*o) for o in outs.values()],
        in_specs=[pl.BlockSpec(memory_space=pl.ANY if n in in_hbm else pltpu.VMEM) for n in ins],
        out_specs=[pl.BlockSpec(memory_space=pl.ANY if n in out_hbm else pltpu.VMEM) for n in outs],
        scratch_shapes=[pltpu.VMEM(*s) for s in vm.values()] + list(sems.values()),
        compiler_params=pltpu.CompilerParams(vmem_limit_bytes=VMEM_LIMIT, collective_id=0, has_side_effects=True),
    )(*ins.values())
    aligned = share % 128 == 0
    sec, gx, dgain, da, dwo, dc, dw1, dw2 = pl.pallas_call(
        functools.partial(arrange, aligned),
        name="arrange",
        out_shape=[
            jax.ShapeDtypeStruct((tokens, width), BF16),
            jax.ShapeDtypeStruct((tokens, width), BF16),
            jax.ShapeDtypeStruct((3, 1, share), F32),
            jax.ShapeDtypeStruct((3, share, hw), F32),
            jax.ShapeDtypeStruct((hw, share) if aligned else (share, hw), F32),
            jax.ShapeDtypeStruct((share, 2, hw), F32),
            jax.ShapeDtypeStruct((share, fw), F32),
            jax.ShapeDtypeStruct((fw, share) if aligned else (share, fw), F32),
        ],
        in_specs=[pl.BlockSpec(memory_space=pltpu.VMEM)] * 8,
        out_specs=[pl.BlockSpec(memory_space=pltpu.VMEM)] * 8,
    )(*results)
    if not aligned:
        dwo, dw2 = dwo.T, dw2.T
    return (
        sec.reshape(1, rows, own, width), gx.reshape(1, rows, own, width), dgain.transpose(1, 0, 2),
        da.transpose(1, 0, 2)[None], dwo[None], dc[None], dw1[None], dw2[None],
    )


def solution(mesh):
    return jax.shard_map(
        body,
        mesh=mesh,
        in_specs=(
            P("pipe", "dp", "tensor", None),
            P(None, "dp", None),
            P("dp", "tensor", None),
            P("pipe", None, None),
            P("pipe", None, None, "tensor"),
            P("pipe", "tensor", None),
            P("pipe", None, None, "tensor"),
            P("pipe", None, "tensor"),
            P("pipe", "tensor", None),
        ),
        out_specs=(
            P("pipe", "dp", "tensor", None),
            P("pipe", "dp", "tensor", None),
            P("pipe", None, "dp"),
            P("pipe", "dp", None, "tensor"),
            P("pipe", "tensor", "dp"),
            P("pipe", "dp", None, "tensor"),
            P("pipe", "dp", "tensor"),
            P("pipe", "tensor", "dp"),
        ),
        check_vma=False,
    )
```

```python
import functools

import jax
import jax.numpy as jnp
from jax import lax
from jax.experimental import pallas as pl
from jax.experimental.pallas import tpu as pltpu
from jax.sharding import PartitionSpec as P

EPS = 1e-05
MASKED = -1000000000.0
DH = 64
HALO = 64
F32 = jnp.float32
BF16 = jnp.bfloat16
GELU_C = 0.7978845608028654
GELU_A = 0.044715
MESH = pl.DeviceIdType.MESH
VMEM_LIMIT = 63 << 20


def mm(a, b):
    return lax.dot_general(a, b, (((1,), (0,)), ((), ())), preferred_element_type=F32)


def mm_nt(a, b):
    return lax.dot_general(a, b, (((1,), (1,)), ((), ())), preferred_element_type=F32)


def mm_tn(a, b):
    return lax.dot_general(a, b, (((0,), (0,)), ((), ())), preferred_element_type=F32)


def norm_parts(v):
    c = v - jnp.mean(v, axis=-1, keepdims=True)
    r = lax.rsqrt(jnp.mean(c * c, axis=-1, keepdims=True) + EPS)
    return c * r, r


def norm(v, gain):
    xhat, _ = norm_parts(v)
    return xhat * gain


def norm_back(v, gain, dn):
    xhat, r = norm_parts(v)
    dxh = dn * gain
    m1 = jnp.mean(dxh, axis=-1, keepdims=True)
    m2 = jnp.mean(dxh * xhat, axis=-1, keepdims=True)
    return r * (dxh - m1 - xhat * m2), jnp.sum(dn * xhat, axis=0, keepdims=True)


def lane_low(shape):
    return lax.broadcasted_iota(jnp.int32, shape, 1) < DH


def pair_join(a, b):
    return jnp.where(lane_low(a.shape), a, b)


def swap_halves(v):
    return pltpu.roll(v, DH, 1)


def attend(q2, k2, v2, mask, keep):
    n, width = q2.shape
    lowq, zero = lane_low(q2.shape), jnp.zeros_like(q2)
    s = mm_nt(jnp.concatenate([jnp.where(lowq, q2, zero), jnp.where(lowq, zero, q2)], axis=0), k2)
    s = jnp.concatenate([mask(s[:n]), mask(s[n:])], axis=0)
    e = jnp.exp(s - jnp.max(s, axis=-1, keepdims=True)).astype(BF16)
    keep(e)
    out = mm(e, jnp.concatenate([v2, jnp.ones_like(v2)], axis=1))
    inv = 1.0 / pair_join(out[:n, width:], out[n:, width:])
    return pair_join(out[:n, :width], out[n:, :width]) * inv, inv


def attend_back(q2, k2, v2, do2, o2, inv, kept):
    low, lowq = lane_low(v2.shape), lane_low(q2.shape)
    one = jnp.ones_like(v2)
    scaled = do2.astype(F32) * inv.astype(F32)
    dob = scaled.astype(BF16)
    minus = (-swap_halves(dob.astype(F32) * o2.astype(F32))).astype(BF16)
    q_t, do_t = q2.T, dob.T
    dq, dk, dv = [], [], []
    for h in range(2):
        e = kept(h)
        rows = slice(h * DH, (h + 1) * DH)
        lhs = jnp.where(lowq, dob, minus) if h == 0 else jnp.where(lowq, minus, dob)
        dp = mm_nt(lhs, jnp.where(low, v2, one) if h == 0 else jnp.where(low, one, v2))
        ds = (dp * e.astype(F32)).astype(BF16)
        dq.append(mm(ds, k2))
        dv.append(mm(do_t[rows], e).astype(BF16))
        dk.append(mm(q_t[rows], ds).astype(BF16))
    return (pair_join(*dq) * (DH**-0.5)).astype(BF16), jnp.concatenate(dk, 0).T, jnp.concatenate(dv, 0).T


def gelu_parts(h):
    h2 = h * h
    half = 0.5 + 0.5 * jnp.tanh(h * (GELU_C + (GELU_C * GELU_A) * h2))
    u = h * half
    slope = half + u * ((1.0 - half) * (2.0 * GELU_C + (6.0 * GELU_C * GELU_A) * h2))
    return u, slope


def flip(i, bit):
    return i + bit - 2 * bit * lax.rem(lax.div(i, bit), 2)


def bit_of(i, bit):
    return lax.rem(lax.div(i, bit), 2)


def reversed_bits(i, count):
    out, bit = 0, 1
    while bit < count:
        out = 2 * out + (i // bit) % 2
        bit *= 2
    return out


class Links:
    def __init__(self, send, recv, local):
        self.send, self.recv, self.local = send, recv, local
        self.n = self.m = 0
        self.sent = []

    def take(self, count=1):
        self.n += count
        return self.n - count

    def remote(self, src, dst, device, at=None):
        at = self.take() if at is None else at
        return pltpu.make_async_remote_copy(
            src_ref=src, dst_ref=dst, send_sem=self.send.at[at], recv_sem=self.recv.at[at],
            device_id=device, device_id_type=MESH,
        )

    def here(self, src, dst):
        self.m += 1
        return pltpu.make_async_copy(src, dst, self.local.at[self.m - 1])


class Gather:
    def __init__(self, links, src, slot, depth, at, pieces=1, planes=None, last_straight=False):
        t, t2 = at["t"], at["t2"]
        half = depth // 2
        n = half // pieces
        whole = pl.ds(0, depth)
        if src is None:
            self.own = []
        elif planes is None:
            self.own = [links.here(src, slot(t, whole))]
        else:
            self.own = [links.here(src.at[i], slot(t, whole, i)) for i in range(planes)]
        self.inner = src is None or planes is not None
        self.straight = pieces - 1 if last_straight else None
        src = slot(t, whole) if self.inner else src
        self.core = links.remote(src, slot(t, whole), at["C"])
        self.over_y, self.over_z, self.core_a, self.core_b = [], [], [], []
        for i in range(pieces):
            mine = pl.ds(pl.multiple_of(at["b"] * half + i * n, n), n)
            other = pl.ds(pl.multiple_of((1 - at["b"]) * half + i * n, n), n)
            self.over_y.append(links.remote(src.at[mine], slot(t, mine), at["Y"]))
            if last_straight and i == pieces - 1:
                self.over_z.append(links.remote(src.at[other], slot(t, other), at["Y"]))
            else:
                self.over_z.append(links.remote(slot(t2, mine), slot(t2, mine), at["Z"][0]))
            self.core_a.append(links.remote(slot(t2, mine), slot(t2, mine), at["C"]))
            self.core_b.append(links.remote(slot(t2, other), slot(t2, other), at["C"]))

    def start(self):
        for c in self.own:
            c.start()
        if self.inner:
            for c in self.own:
                c.wait()
        for c in self.over_y:
            c.start()
        if self.straight is not None:
            self.over_z[self.straight].start()
        self.core.start()

    def step1(self, i=0):
        self.over_y[i].wait_recv()
        if i != self.straight:
            self.over_z[i].start()
        self.core_a[i].start()

    def step2(self, i=0):
        self.over_z[i].wait_recv()
        self.core_b[i].start()

    def ready(self, i):
        if i == 0 and not self.inner:
            for c in self.own:
                c.wait()
        if i == 1:
            self.core.wait_recv()
        if i == 3:
            for c in self.core_a + self.core_b:
                c.wait_recv()

    def finish(self):
        for c in [self.core] + self.over_y + self.over_z + self.core_a + self.core_b:
            c.wait_send()


class Reduce:
    def __init__(self, links, part, rc, ry, zb, zr, at, y_first):
        self.part, self.at, self.y_first = part, at, y_first
        self.rc, self.ry, self.zb, self.zr = rc, ry, zb, zr
        self.n = zb.shape[0]
        self.dp, self.rows = zb.shape[1:3]
        self.core = [links.remote(part(at[f]), rc.at[j], at["C"]) for j, f in enumerate(("t1", "t3"))]
        self.over_z, self.kept = [], []
        off, m, bit, k = 0, self.dp, 1, 0
        while m > 1:
            m //= 2
            b = bit_of(at["d"], bit)
            keep, give = off + b * m, off + (1 - b) * m
            self.over_z.append(links.remote(zb.at[:, pl.ds(give, m)], zr[k], at["Z"][k]))
            self.kept.append((keep, m))
            off, bit, k = keep, 2 * bit, k + 1
        self.off = off
        self.over_y = links.remote(part(at["t2"]) if y_first else zb.at[1, off], ry, at["Y"])

    def core_send(self, j):
        self.core[j].start()

    def into_zb(self, j, mine, theirs):
        for i in range(self.dp):
            where = pl.ds(i * self.rows, self.rows)
            self.zb[j, reversed_bits(i, self.dp)] = (mine[where, :].astype(F32) + theirs[where, :].astype(F32)).astype(BF16)

    def core_done(self):
        self.core[0].wait_recv()
        self.core[1].wait_recv()
        far, near = self.part(self.at["t2"]), self.part(self.at["t"])
        if self.y_first:
            far[...] = (far[...].astype(F32) + self.rc[1].astype(F32)).astype(BF16)
            self.over_y.start()
            near[...] = (near[...].astype(F32) + self.rc[0].astype(F32)).astype(BF16)
        else:
            self.into_zb(0, near, self.rc.at[0])
            self.into_zb(1, far, self.rc.at[1])
            self.over_z[0].start()

    def y_done(self, out=None):
        self.over_y.wait_recv()
        if self.y_first:
            self.into_zb(0, self.part(self.at["t"]), self.ry)
            self.over_z[0].start()
        else:
            out[...] = self.zb[0, self.off].astype(F32) + self.ry[...].astype(F32)

    def z_done(self, k, out=None):
        self.over_z[k].wait_recv()
        keep, m = self.kept[k]
        last = k == len(self.over_z) - 1
        if last and self.y_first:
            out[...] = self.zb[0, keep].astype(F32) + self.zr[k][0, 0].astype(F32)
        else:
            for j in range(self.n):
                live = self.zb.at[j, pl.ds(keep, m)]
                live[...] = (live[...].astype(F32) + self.zr[k][j].astype(F32)).astype(BF16)
            (self.over_y if last else self.over_z[k + 1]).start()

    def z_rest(self, out=None):
        for k in range(1, len(self.over_z)):
            self.z_done(k, out)

    def finish(self):
        for c in self.core + [self.over_y] + self.over_z:
            c.wait_send()


def layers(names, *refs):
    ref = dict(zip(names, refs))
    R = lambda name: ref[name]
    p, d, t = lax.axis_index("pipe"), lax.axis_index("dp"), lax.axis_index("tensor")
    is_enc, is_dec = p == 0, p == 1
    dp = lax.axis_size("dp")
    t1, t2, t3 = flip(t, 1), flip(t, 2), 3 - t
    zbits = []
    while 2 ** len(zbits) < dp:
        zbits.append((p, flip(d, 2 ** len(zbits)), t))
    at = dict(t=t, t1=t1, t2=t2, t3=t3, d=d, b=bit_of(d, 1), C=(p, d, t1), Y=(p, d, t2), T=(p, d, t3), X=(1 - p, d, t), Z=zbits)
    rows, own, width = R("x").shape
    win, cwin = own + 2 * HALO, 2 * own + 2 * HALO
    slots = 4 * own
    tokens = rows * own
    hw = R("wa").shape[2] // 3
    fw = R("w1").shape[2]
    inner = t % 3 != 0
    scale = jnp.asarray(DH**-0.5, BF16)
    gain_ref, x_ref = R("gains"), R("x")
    side = 3 * own // 4

    def rowsl(r, n=own):
        return pl.ds(pl.multiple_of(r * n, n), n)

    def lanes(s, n=hw):
        return pl.ds(pl.multiple_of(s * n, n), n)

    def far_lanes(s):
        return pl.ds(pl.multiple_of(s * 2 * hw + hw, hw), hw)

    def in_row(r, span):
        return pl.ds(pl.multiple_of(r * slots + span.start, HALO), span.size)

    def near_first(i):
        return 2 * lax.rem(lax.div(t, 2) + lax.div(i, 2), 2) + lax.rem(lax.rem(t, 2) + lax.rem(i, 2), 2)

    def far_first(i):
        return 2 * lax.rem(lax.div(t, 2) + lax.rem(lax.div(i + 1, 2), 2), 2) + lax.rem(lax.rem(t, 2) + 1 - lax.div(i, 2), 2)

    def seg_row(side_, r, start):
        row = jnp.broadcast_to(R("segs")[side_, pl.ds(r, 1), :].astype(F32), (8, slots))
        return pltpu.roll(row, lax.rem(2 * slots - start, slots), 1)

    def seg_column(side_, r):
        row = seg_row(side_, r, t * own)[:1, :own]
        return jnp.broadcast_to(row, (128, own)).T

    def spread(column, n):
        return jnp.concatenate([column] * (n // 128), axis=1)

    links = Links(R("send"), R("recv"), R("local"))

    def by_shard(name, n=None):
        def slot(s, span, i=None):
            full = R(name).at[s, span]
            return full if i is None else full.at[:, pl.ds(i * n, n)]

        return slot

    def by_columns(name, n, row):
        def slot(s, span):
            return R(name).at[pl.ds(pl.multiple_of(span.start + row, HALO), span.size), lanes(s, n)]

        return slot

    g_wa = Gather(links, R("wa_h"), by_shard("wa", hw), width, at, 2, 3)
    g_wo = Gather(links, R("wo_h"), by_shard("wo"), hw, at)
    g_w1 = Gather(links, R("w1_h"), by_shard("w1"), width, at, 2)
    g_w2 = Gather(links, R("w2_h"), by_shard("w2"), fw, at, 4, None, True)
    g_c1 = Gather(links, R("cx_h"), by_columns("dmf", hw, 0), 2 * width, at)
    c0_x = links.remote(R("cx_h"), R("dmf").at[pl.ds(2 * width, 2 * width), lanes(t)], at["X"])
    g_c0 = Gather(links, None, by_columns("dmf", hw, 2 * width), 2 * width, at)
    loads = [links.here(R(n + "_h"), R(n)) for n in ("x", "cot", "segs")]
    x_right = links.remote(R("x_h").at[:, pl.ds(own - HALO, HALO)], R("xh").at[0], (p, d, lax.rem(t + 1, 4)))
    x_left = links.remote(R("x_h").at[:, pl.ds(0, HALO)], R("xh").at[1], (p, d, lax.rem(t + 3, 4)))
    base_mem, base_memc, base_memt = links.take(rows), links.take(rows), links.take(rows)
    base_dmc, base_dmt, base_dmx = links.take(rows), links.take(rows), links.take(rows)
    block = pl.ds(pl.multiple_of(t * own, own), own)
    block1 = pl.ds(pl.multiple_of(t1 * own, own), own)
    edge_out = pl.ds(pl.multiple_of(lax.rem(own // 2 + side * t, slots), HALO), side)
    edge_in = pl.ds(pl.multiple_of(lax.rem(own // 2 + side * t3, slots), HALO), side)

    def mem_x(r):
        return links.remote(R("secs").at[rowsl(r)], R("memf").at[in_row(r, block)], at["X"], base_mem + r)

    def mem_c(r):
        return links.remote(R("memf").at[in_row(r, block)], R("memf").at[in_row(r, block)], at["C"], base_memc + r)

    def mem_t(r):
        return links.remote(R("memf").at[in_row(r, edge_out)], R("memf").at[in_row(r, edge_out)], at["T"], base_memt + r)

    def dm_rows(r, span):
        return R("dmf").at[in_row(r, span)]

    def dm_c(r):
        return links.remote(dm_rows(r, block1), R("rcc").at[r], at["C"], base_dmc + r)

    def dm_t(r):
        return links.remote(dm_rows(r, edge_in), R("rct").at[r], at["T"], base_dmt + r)

    def dm_x(r):
        return links.remote(R("rcc").at[r], R("rcc").at[r], at["X"], base_dmx + r)

    def by_rows(name, m, col=0):
        return lambda s: R(name).at[pl.ds(pl.multiple_of(s * width, width), width), pl.ds(col, m)]

    def by_lanes(name, m, row=0):
        return lambda s: R(name).at[pl.ds(row, width), lanes(s, m)]

    def reduce_of(name, part, y_first=True):
        zr = [R(f"zr{k}_{name}") for k in range(len(zbits))]
        return Reduce(links, part, R("rc_" + name), R("ry_" + name), R("zb_" + name), zr, at, y_first)

    fh = fw // 2
    r_w2 = [reduce_of(f"w2{j}", by_rows("dw2", fh, j * fh), j == 1) for j in range(2)]
    r_w1 = [reduce_of(f"w1{j}", by_rows("dmf", fh, j * fh), j == 0) for j in range(2)]
    r_wo = reduce_of("wo", by_lanes("dwo", hw))
    r_wa = [reduce_of(f"wa{j}", by_rows("cp", hw, j * hw)) for j in range(3)]
    r_c0 = reduce_of("c0", by_lanes("kv", 2 * hw))
    r_c1 = reduce_of("c1", by_lanes("kv", 2 * hw, width))
    w2_out = [R("dw2_o").at[:, pl.ds(j * fh, fh)] for j in range(2)]
    w1_out = [R("dw1_o").at[:, pl.ds(j * fh, fh)] for j in range(2)]
    wa_out = [R("da_o").at[:, pl.ds(j * hw, hw)] for j in range(3)]
    c0_back = links.remote(R("dc0"), R("dc0r"), at["X"])
    dn_right = links.remote(R("xh").at[1], R("dhr").at[0], (p, d, lax.rem(t + 1, 4)))
    dn_left = links.remote(R("xh").at[0], R("dhr").at[1], (p, d, lax.rem(t + 3, 4)))
    gain_over_t = [links.remote(R("dgt").at[t], R("dgt").at[t], at[f]) for f in ("C", "Y", "T")]
    gain_over_d = []
    for k in range(1, dp):
        to = lax.rem(d + k, dp)
        gain_over_d.append(links.remote(R("dgd").at[d], R("dgd").at[d], (p, to, t)))

    @pl.when(is_dec)
    def _():
        for at_t, start in ((0, 2 * own), (1, 2 * own + side), (3, 2 * own - 2 * HALO)):
            @pl.when(t == at_t)
            def _():
                for r in range(rows):
                    R("memf")[pl.ds(r * slots + start, 2 * HALO), :] = jnp.zeros((2 * HALO, width), BF16)

    for c in loads:
        c.start()
    barrier = pltpu.get_barrier_semaphore()
    partners = [at["C"], at["Y"], at["T"], at["X"]] + [(p, lax.rem(d + k, dp), t) for k in range(1, dp)]
    for dev in partners:
        pl.semaphore_signal(barrier, inc=1, device_id=dev, device_id_type=MESH)
    pl.semaphore_wait(barrier, len(partners))

    pl.when(t < 3)(x_right.start)
    pl.when(t > 0)(x_left.start)
    g_wa.start()
    g_wo.start()

    @pl.when(is_enc)
    def _():
        c0_x.start()
        g_w1.start()
        g_w2.start()

    @pl.when(is_dec)
    def _():
        g_c1.start()

    for c in loads:
        c.wait()

    nw_ref, bias_ref = R("nw"), R("bias")
    gain0, gain1, gain2 = gain_ref[0], gain_ref[1], gain_ref[2]
    for r in range(rows):
        nw_ref[pl.ds(r * win + HALO, own), :] = norm(x_ref[r].astype(F32), gain0).astype(BF16)
        keys = seg_row(p, r, lax.rem(t * own + slots - HALO, slots))[:1, :win]
        same = spread(seg_column(p, r), win) == keys
        qpos = lax.broadcasted_iota(jnp.int32, (own, win), 0)
        kpos = lax.broadcasted_iota(jnp.int32, (own, win), 1) - HALO
        before = kpos - qpos <= jnp.where(is_enc, 4 * win, 0)
        bias_ref[r] = jnp.where(same & before, 0.0, MASKED)

    @pl.when(t == 0)
    def _():
        R("xh")[0] = jnp.zeros((rows, HALO, width), BF16)

    @pl.when(t == 3)
    def _():
        R("xh")[1] = jnp.zeros((rows, HALO, width), BF16)

    pl.when(t > 0)(x_right.wait_recv)
    pl.when(t < 3)(x_left.wait_recv)
    for r in range(rows):
        nw_ref[pl.ds(r * win, HALO), :] = norm(R("xh")[0, r].astype(F32), gain0).astype(BF16)
        nw_ref[pl.ds(r * win + HALO + own, HALO), :] = norm(R("xh")[1, r].astype(F32), gain0).astype(BF16)

    def after_pair(i):
        @pl.when(i == 0)
        def _():
            g_wa.step1(0)

        @pl.when(i == 1)
        def _():
            g_wa.step1(1)
            g_wo.step1()
            g_wa.step2(0)

            @pl.when(is_dec)
            def _():
                c0_x.wait_recv()
                g_c0.start()
                g_w2.start()
                g_w1.start()
                g_c1.step1()

            pl.when(is_enc)(lambda: g_w1.step1(0))
            g_wa.step2(1)

        @pl.when(i == 2)
        def _():
            g_wo.step2()
            pl.when(is_enc)(lambda: g_w1.step1(1))

        @pl.when(i == 3)
        def _():
            pl.when(is_dec)(g_c0.step1)

    def wait_ready(i, *weights):
        for k in range(4):
            @pl.when(i == k)
            def _():
                for w in weights:
                    w.ready(k)

    q_ref, k_ref, v_ref, p_ref, o_ref, inv_ref = R("q"), R("k"), R("v"), R("p"), R("o"), R("inv")

    def self_pair(i, _):
        s = near_first(i)
        wait_ready(i, g_wa)
        packed = mm(nw_ref[...], R("wa")[s])
        for r in range(rows):
            q_ref[s, r] = packed[r * win + HALO : r * win + HALO + own, :hw].astype(BF16) * scale
            k_ref[s, r] = packed[r * win : (r + 1) * win, hw : 2 * hw].astype(BF16)
            v_ref[s, r] = packed[r * win : (r + 1) * win, 2 * hw :].astype(BF16)
        for r in range(rows):
            def keep(e):
                p_ref[s, r] = e

            o2, inv = attend(q_ref[s, r], k_ref[s, r], v_ref[s, r], lambda scores: scores + bias_ref[r], keep)
            o_ref[pl.ds(r * own, own), lanes(s)] = o2.astype(BF16)
            inv_ref[pl.ds(r * own, own), lanes(s)] = inv.astype(BF16)
        after_pair(i)
        return 0

    lax.fori_loop(0, 4, self_pair, 0)
    for k in range(4):
        g_wo.ready(k)
    r1_ref, r2_ref, n2_ref, n3_ref = R("r1"), R("r2"), R("n2"), R("n3")
    u_ref, gp_ref, sec_ref = R("u"), R("gp"), R("secs")
    acc_ref, g_ref, gb_ref, do_ref = R("acc"), R("g"), R("gb"), R("do")
    first = mm(o_ref[...], R("wo")[...].reshape(4 * hw, width))
    for r in range(rows):
        r1_ref[pl.ds(r * own, own), :] = x_ref[r].astype(F32) + first[r * own : (r + 1) * own]
    n2_ref[...] = norm(r1_ref[...], gain1).astype(BF16)

    @pl.when(is_enc)
    def _():
        r2_ref[...] = r1_ref[...]

        def up(i):
            s = near_first(i)
            u, gp = gelu_parts(mm(n2_ref[...], R("w1")[s]))
            u_ref[s] = u.astype(BF16)
            gp_ref[s] = gp.astype(BF16)
            return s

        g_w2.step1(0)
        g_w1.step2(0)

        def near(i, _):
            wait_ready(i, g_w1, g_w2)
            s = up(i)
            r2_ref[...] += mm(u_ref[s], R("w2")[s])

            @pl.when(i == 0)
            def _():
                g_w2.step1(1)
                g_w1.step2(1)

            @pl.when(i == 1)
            def _():
                g_w2.step1(2)
                g_w2.step2(0)
                g_w2.step1(3)

            return 0

        lax.fori_loop(0, 2, near, 0)

        def far(i, _):
            wait_ready(i, g_w1)
            up(i)
            pl.when(i == 2)(lambda: g_w2.step2(1))

            @pl.when(i == 3)
            def _():
                g_w2.step2(2)
                g_w2.step2(3)

            return 0

        lax.fori_loop(2, 4, far, 0)
        g_w2.ready(3)
        far1, far2 = near_first(2), near_first(3)

        def row(r, _):
            rs = rowsl(r)
            total = r2_ref[rs, :] + mm(u_ref[far1, rs, :], R("w2")[far1]) + mm(u_ref[far2, rs, :], R("w2")[far2])
            r2_ref[rs, :] = total
            sec_ref[rs, :] = norm(total, gain2).astype(BF16)
            mem_x(r).start()
            return 0

        lax.fori_loop(0, rows, row, 0)

    def sends(reductions, i):
        for j in range(2):
            @pl.when(i == j)
            def _():
                for reduction in reductions:
                    reduction.core_send(j)

    cstart = pl.multiple_of(jnp.minimum(t * (own - HALO), slots - cwin), HALO)
    cwindow = pl.ds(cstart, cwin)
    kv_ref, cq_ref, cp_ref, dkv_ref, cinv_ref = R("kv"), R("cq"), R("cp"), R("dkv"), R("cinv")
    c0_ref, cqw_ref, cow_ref, oc_ref, cot_ref = R("c0"), R("cqw"), R("cow"), R("oc"), R("cot")
    cols, keys_ref = R("cols"), R("keys")

    @pl.when(is_dec)
    def _():
        g_w2.step1(0)
        g_c1.step2()
        for k in range(4):
            g_c1.ready(k)
        pick_shape = (width // 4, width // 2)
        twice = 2 * lax.broadcasted_iota(jnp.int32, pick_shape, 0)
        at_col = lax.broadcasted_iota(jnp.int32, pick_shape, 1)
        picks = [jnp.where(at_col == twice + j, 1.0, 0.0).astype(BF16) for j in range(2)]

        def unweave(base, m):
            return [mm(pick, R("dmf")[pl.ds(base + m * (width // 2), width // 2), :]).astype(BF16) for pick in picks]

        for m in range(4):
            span = pl.ds(m * (width // 4), width // 4)
            cqw_ref[span, :], cow_ref[span, :] = unweave(0, m)
        cq_ref[...] = mm(n2_ref[...], cqw_ref[...]).astype(BF16) * scale
        g_w2.step1(1)
        g_c0.step2()
        g_w2.step1(2)
        g_w2.step1(3)
        kv_ref[...] = jnp.zeros_like(kv_ref)
        for r in range(rows):
            cols[r] = seg_column(1, r)
            keys_ref[r] = seg_row(0, r, cstart)[:, :cwin]
        for k in range(4):
            g_c0.ready(k)
        for m in range(4):
            span = pl.ds(m * (width // 4), width // 4)
            ck, cv = unweave(2 * width, m)
            for s in range(4):
                c0_ref[span, 2 * s * hw : (2 * s + 1) * hw] = ck[:, s * hw : (s + 1) * hw]
                c0_ref[span, (2 * s + 1) * hw : (2 * s + 2) * hw] = cv[:, s * hw : (s + 1) * hw]
        g_w1.step1(0)
        g_w2.step2(0)
        g_w2.step2(1)
        g_w1.step1(1)
        for g in (g_c1, g_c0):
            g.finish()
        R("dmf")[...] = jnp.zeros_like(R("dmf"))
        g_w2.step2(2)
        g_w2.step2(3)
        g_w1.step2(0)
        for k in range(4):
            g_w2.ready(k)

        def early(s, _):
            gp_ref[s] = mm_nt(cot_ref[...], R("w2")[s]).astype(BF16)
            return 0

        lax.fori_loop(0, 4, early, 0)

        def pass_memory_on(r):
            mem_x(r).wait_recv()
            mem_c(r).start()
            pl.when(inner)(mem_t(r).start)

        def settle(r):
            span = pl.ds(0, own)
            dm_c(r).wait_recv()
            acc_ref[span, :] = R("dmf")[in_row(r, block), :].astype(F32) + R("rcc")[r].astype(F32)

            @pl.when(inner)
            def _():
                dm_t(r).wait_recv()
                place = pl.ds(pl.multiple_of((2 - t) * (own - side), HALO), side)
                acc_ref[place, :] += R("rct")[r].astype(F32)

            R("rcc")[r] = acc_ref[span, :].astype(BF16)
            dm_x(r).start()

        def row(r, _):
            rs = rowsl(r)

            def project(span):
                kv_ref[span, :] = mm(R("memf")[in_row(r, span), :], c0_ref[...]).astype(BF16)

            @pl.when(r == 0)
            def _():
                g_w1.step2(1)
                pass_memory_on(0)

            project(block)
            pl.when(r > 0)(lambda: settle(r - 1))
            mem_c(r).wait_recv()
            project(block1)

            @pl.when(inner)
            def _():
                mem_t(r).wait_recv()
                project(edge_in)

            def cross(i, _):
                for s in range(4):
                    def keep(e):
                        cp_ref[rowsl(s, 2 * own), :] = e

                    def mask(scores):
                        same = spread(cols[r], cwin) == keys_ref[r, pl.ds(0, 1), :]
                        return jnp.where(same, scores, MASKED)

                    o2, inv = attend(cq_ref[rs, lanes(s)], kv_ref[cwindow, lanes(2 * s)], kv_ref[cwindow, lanes(2 * s + 1)], mask, keep)
                    oc_ref[rs, lanes(s)] = o2.astype(BF16)
                    cinv_ref[:, lanes(s)] = inv.astype(BF16)
                return 0

            cross(0, 0)
            pl.when(r < rows - 1)(lambda: pass_memory_on(r + 1))
            r2_ref[rs, :] = r1_ref[rs, :] + mm_nt(oc_ref[rs, :], cow_ref[...])
            n3_ref[rs, :] = norm(r2_ref[rs, :], gain2).astype(BF16)

            @pl.when(r == 0)
            def _():
                for k in range(4):
                    g_w1.ready(k)

            dn = pl.ds(0, own)
            acc_ref[dn, :] = jnp.zeros((own, width), F32)

            def feed(i, _):
                back = acc_ref[dn, :]
                for s in range(4):
                    u, gp = gelu_parts(mm(n3_ref[rs, :], R("w1")[s]))
                    u = u.astype(BF16)
                    u_ref[s, rs, :] = u
                    dh = (gp_ref[s, rs, :].astype(F32) * gp).astype(BF16)
                    gp_ref[s, rs, :] = dh
                    back += mm_nt(dh, R("w1")[s])
                acc_ref[dn, :] = back
                return 0

            feed(0, 0)
            dx, dg = norm_back(r2_ref[rs, :], gain2, acc_ref[dn, :])
            R("dg")[r, pl.ds(2, 1), :] = dg
            g2 = cot_ref[rs, :].astype(F32) + dx
            g_ref[rs, :] = g2
            gb_ref[rs, :] = g2.astype(BF16)
            do_ref[rs, :] = mm(gb_ref[rs, :], cow_ref[...]).astype(BF16)
            ws = pl.ds(pl.multiple_of(r * cwin, HALO), cwin)

            def back(i, _):
                for s in range(4):
                    dq, dk, dv = attend_back(
                        cq_ref[rs, lanes(s)], kv_ref[cwindow, lanes(2 * s)], kv_ref[cwindow, lanes(2 * s + 1)],
                        do_ref[rs, lanes(s)], oc_ref[rs, lanes(s)], cinv_ref[:, lanes(s)], lambda h: cp_ref[rowsl(2 * s + h), :],
                    )
                    cq_ref[rs, lanes(s)] = dq
                    dkv_ref[ws, lanes(2 * s)] = dk
                    dkv_ref[ws, lanes(2 * s + 1)] = dv
                return 0

            back(0, 0)
            R("dmf")[in_row(r, cwindow), :] = mm_nt(dkv_ref[ws, :], c0_ref[...]).astype(BF16)
            dm_c(r).start()
            pl.when(inner)(dm_t(r).start)

            @pl.when(r == rows - 1)
            def _():
                def w2_grad(i, _):
                    s = far_first(i)
                    R("dw2")[rowsl(s, width), :] = mm_tn(cot_ref[...], u_ref[s]).astype(BF16)
                    sends(r_w2, i)
                    return 0

                lax.fori_loop(0, 4, w2_grad, 0)
                settle(r)

            return 0

        lax.fori_loop(0, rows, row, 0)
        for r in range(rows):
            dm_c(r).wait_send()
            pl.when(inner)(dm_t(r).wait_send)

        def w1_grad(i, _):
            s = far_first(i)
            R("dmf")[rowsl(s, width), :] = mm_tn(n3_ref[...], gp_ref[s]).astype(BF16)
            sends(r_w1, i)

            @pl.when(i == 0)
            def _():
                r_w2[0].core_done()
                r_w2[1].core_done()

            return 0

        lax.fori_loop(0, 4, w1_grad, 0)

        def c0_grad(i, _):
            s = far_first(i)
            total = mm_tn(R("memf")[in_row(0, cwindow), :], dkv_ref[pl.ds(0, cwin), lanes(s, 2 * hw)])
            for r in range(1, rows):
                total += mm_tn(R("memf")[in_row(r, cwindow), :], dkv_ref[pl.ds(r * cwin, cwin), lanes(s, 2 * hw)])
            r_c0.part(s)[...] = total.astype(BF16)
            sends([r_c0], i)

            @pl.when(i == 1)
            def _():
                r_w1[0].core_done()
                r_w1[1].core_done()

            return 0

        lax.fori_loop(0, 4, c0_grad, 0)
        def query_norm(r, _):
            rs = rowsl(r)
            dx, dg = norm_back(r1_ref[rs, :], gain1, mm_nt(cq_ref[rs, :], cqw_ref[...]))
            R("dg")[r, pl.ds(1, 1), :] = dg
            g_ref[rs, :] += dx
            return 0

        lax.fori_loop(0, rows, query_norm, 0)
        dcq = mm_tn(n2_ref[...], cq_ref[...]).astype(BF16)
        dco = mm_tn(gb_ref[...], oc_ref[...]).astype(BF16)
        r_c0.core_done()
        for s in range(4):
            r_c1.part(s)[:, :hw] = dcq[:, s * hw : (s + 1) * hw]
            r_c1.part(s)[:, hw:] = dco[:, s * hw : (s + 1) * hw]
        sends([r_c1], 0)
        sends([r_c1], 1)

    @pl.when(is_enc)
    def _():
        def receive(r):
            rs = rowsl(r)
            dm_x(r).wait_recv()
            dx, dg = norm_back(r2_ref[rs, :], gain2, R("rcc")[r].astype(F32))
            R("dg")[r, pl.ds(2, 1), :] = dg
            g_ref[rs, :] = dx
            gb_ref[rs, :] = dx.astype(BF16)

        def hidden_back(s, rs):
            dh = (mm_nt(gb_ref[rs, :], R("w2")[s]) * gp_ref[s, rs, :].astype(F32)).astype(BF16)
            gp_ref[s, rs, :] = dh
            acc_ref[rs, :] += mm_nt(dh, R("w1")[s])

        head, last = pl.ds(0, (rows - 1) * own), pl.ds((rows - 1) * own, own)
        acc_ref[pl.ds(0, tokens), :] = jnp.zeros((tokens, width), F32)
        for r in range(rows - 1):
            receive(r)

        def head_grads(s, _):
            R("dw2")[rowsl(s, width), :] = mm_tn(gb_ref[head, :], u_ref[s, head, :]).astype(BF16)
            hidden_back(s, head)
            return 0

        lax.fori_loop(0, 4, head_grads, 0)
        receive(rows - 1)

        for i in range(4):
            s = far_first(i)
            part = R("dw2").at[rowsl(s, width)]
            part[...] = (part[...].astype(F32) + mm_tn(gb_ref[last, :], u_ref[s, last, :])).astype(BF16)
            if i < 2:
                for reduction in r_w2:
                    reduction.core_send(i)
        for i in range(4):
            s = far_first(i)
            hidden_back(s, last)
            if i == 1:
                r_w2[0].core_done()
                r_w2[1].core_done()
            R("dmf")[rowsl(s, width), :] = mm_tn(n2_ref[...], gp_ref[s]).astype(BF16)
            if i < 2:
                for reduction in r_w1:
                    reduction.core_send(i)
        r_w1[0].core_done()
        r_w1[1].core_done()
        dx, dg = norm_back(r1_ref[...], gain1, acc_ref[pl.ds(0, tokens), :])
        R("dg")[0, pl.ds(1, 1), :] = dg
        for r in range(1, rows):
            R("dg")[r, pl.ds(1, 1), :] = jnp.zeros_like(dg)
        g_ref[...] += dx

    sec_out = links.here(sec_ref, R("sec"))
    pl.when(is_enc)(sec_out.start)
    gb_ref[...] = g_ref[...].astype(BF16)
    R("dwo")[...] = mm_tn(gb_ref[...], o_ref[...]).astype(BF16)
    r_wo.core_send(0)
    r_wo.core_send(1)
    do_ref[...] = mm_nt(gb_ref[...], R("wo")[...].reshape(4 * hw, width)).astype(BF16)
    acc_ref[...] = jnp.zeros_like(acc_ref)
    dqkv_ref = R("dqkv")
    for r in range(rows):
        dqkv_ref[pl.ds(r * win, HALO), :hw] = jnp.zeros((HALO, hw), BF16)
        dqkv_ref[pl.ds(r * win + HALO + own, HALO), :hw] = jnp.zeros((HALO, hw), BF16)

    def self_back(i, _):
        s = far_first(i)
        for r in range(rows):
            rs = pl.ds(r * own, own)
            dq, dk, dv = attend_back(
                q_ref[s, r], k_ref[s, r], v_ref[s, r], do_ref[rs, lanes(s)], o_ref[rs, lanes(s)], inv_ref[rs, lanes(s)],
                lambda h: p_ref[s, r, pl.ds(h * own, own), :],
            )
            dqkv_ref[pl.ds(r * win + HALO, own), :hw] = dq
            dqkv_ref[pl.ds(r * win, win), hw : 2 * hw] = dk
            dqkv_ref[pl.ds(r * win, win), 2 * hw :] = dv
        R("cp")[rowsl(s, width), pl.ds(0, 3 * hw)] = mm_tn(nw_ref[...], dqkv_ref[...]).astype(BF16)
        sends(r_wa, i)
        acc_ref[...] += mm_nt(dqkv_ref[...], R("wa")[s])

        @pl.when(i == 0)
        def _():
            r_w2[0].z_done(0)
            pl.when(is_dec)(r_c1.core_done)
            r_wo.core_done()
            r_w2[1].y_done()

        @pl.when(i == 2)
        def _():
            r_w1[1].z_done(0)
            r_w1[0].y_done()

        @pl.when(i == 3)
        def _():
            pl.when(is_enc)(r_wo.y_done)
            r_w2[1].z_done(0, w2_out[1])
            r_w2[0].z_rest()
            pl.when(is_dec)(r_c0.y_done)

        return 0

    lax.fori_loop(0, 4, self_back, 0)
    for r in range(rows):
        R("xh")[0, r] = acc_ref[pl.ds(r * win, HALO), :].astype(BF16)
        R("xh")[1, r] = acc_ref[pl.ds(r * win + HALO + own, HALO), :].astype(BF16)
    pl.when(t == 1)(dn_left.start)
    pl.when(t < 3)(dn_right.start)
    pl.when(t > 1)(dn_left.start)
    for j in range(3):
        r_wa[j].core_done()

    @pl.when(is_dec)
    def _():
        def decoded(r, _):
            rs = rowsl(r)
            total = r2_ref[rs, :]
            for s in range(4):
                total += mm(u_ref[s, rs, :], R("w2")[s])
            sec_ref[rs, :] = total.astype(BF16)
            return 0

        lax.fori_loop(0, rows, decoded, 0)
        sec_out.start()

    @pl.when(t == 0)
    def _():
        R("dhr")[0] = jnp.zeros((rows, HALO, width), BF16)

    @pl.when(t == 3)
    def _():
        R("dhr")[1] = jnp.zeros((rows, HALO, width), BF16)

    @pl.when(is_dec)
    def _():
        r_w1[0].z_done(0, w1_out[0])
        r_w1[1].z_rest()
        r_c1.y_done()
        r_w2[1].z_rest(w2_out[1])
        r_wo.y_done()
        r_c0.z_done(0, R("dc0"))

    pl.when(t > 0)(dn_right.wait_recv)
    pl.when(t < 3)(dn_left.wait_recv)
    for r in range(rows):
        lo, hi = pl.ds(r * win + HALO, HALO), pl.ds(r * win + own, HALO)
        acc_ref[lo, :] += R("dhr")[0, r].astype(F32)
        acc_ref[hi, :] += R("dhr")[1, r].astype(F32)
    total = jnp.zeros((1, width), F32)
    for r in range(rows):
        rs = pl.ds(r * own, own)
        dx, dg = norm_back(x_ref[r].astype(F32), gain0, acc_ref[pl.ds(r * win + HALO, own), :])
        gb_ref[rs, :] = (g_ref[rs, :] + dx).astype(BF16)
        total += dg
    dgt, dgd = R("dgt"), R("dgd")
    dgt[t] = jnp.zeros((8, width), F32)
    dgt[t, pl.ds(0, 1), :] = total
    dgt[t, pl.ds(1, 2), :] = sum(R("dg")[r, pl.ds(1, 2), :] for r in range(rows))
    for c in gain_over_t:
        c.start()
    gx_out = links.here(gb_ref, R("gx"))
    gx_out.start()

    def gains_over_t():
        for c in gain_over_t:
            c.wait_recv()
        dgd[d] = dgt[0] + dgt[1] + dgt[2] + dgt[3]
        for c in gain_over_d:
            c.start()

    def gains_over_d():
        total = jnp.zeros((8, width), F32)
        for c in gain_over_d:
            c.wait_recv()
        for k in range(dp):
            total += dgd[k]
        R("dgain")[...] = pltpu.roll(total, lax.rem(width - d * (width // dp), width), 1)

    @pl.when(is_enc)
    def _():
        r_w2[0].y_done(w2_out[0])
        r_w1[0].z_done(0, w1_out[0])
        r_w1[1].z_rest()
        r_wa[0].y_done()
        r_wo.z_done(0, R("dwo_o"))
        r_wa[1].y_done()
        r_w2[1].z_rest(w2_out[1])
        r_wa[0].z_done(0, wa_out[0])
        r_wa[2].y_done()
        gains_over_t()
        r_w1[0].z_rest(w1_out[0])
        r_wa[1].z_done(0, wa_out[1])
        r_w1[1].y_done(w1_out[1])
        r_wo.z_rest(R("dwo_o"))

    @pl.when(is_dec)
    def _():
        r_w2[0].y_done(w2_out[0])
        r_w1[0].z_rest(w1_out[0])
        r_c1.z_done(0, R("dc"))
        r_wa[0].y_done()
        r_wo.z_done(0, R("dwo_o"))
        r_wa[1].y_done()
        r_c0.z_rest(R("dc0"))
        c0_back.start()
        r_wa[0].z_done(0, wa_out[0])
        r_wa[2].y_done()
        r_c1.z_rest(R("dc"))
        r_wa[1].z_done(0, wa_out[1])
        r_w1[1].y_done(w1_out[1])
        gains_over_t()
        r_wo.z_rest(R("dwo_o"))

    r_wa[2].z_done(0, wa_out[2])
    for j in range(3):
        r_wa[j].z_rest(wa_out[j])
    gains_over_d()

    sec_out.wait()
    gx_out.wait()
    for g in (g_wa, g_wo, g_w1, g_w2):
        g.finish()
    for g in r_w2 + r_w1 + [r_wo] + r_wa:
        g.finish()
    for c in gain_over_t + gain_over_d:
        c.wait_send()
    pl.when(t < 3)(x_right.wait_send)
    pl.when(t > 0)(x_left.wait_send)
    pl.when(t < 3)(dn_right.wait_send)
    pl.when(t > 0)(dn_left.wait_send)

    @pl.when(is_enc)
    def _():
        c0_x.wait_send()
        for r in range(rows):
            mem_x(r).wait_send()
        c0_back.wait_recv()
        R("dc")[...] = R("dc0r")[...]

    @pl.when(is_dec)
    def _():
        for g in (r_c0, r_c1):
            g.finish()
        for r in range(rows):
            mem_c(r).wait_send()
            pl.when(inner)(mem_t(r).wait_send)
            dm_x(r).wait_send()
        c0_back.wait_send()


def arrange(aligned, sec, gx, dgain, da, dwo, dc, dw1, dw2, sec_o, gx_o, dgain_o, da_o, dwo_o, dc_o, dw1_o, dw2_o):
    share, hw = dwo.shape
    sec_o[...] = sec[...]
    gx_o[...] = gx[...]
    for i in range(3):
        dgain_o[i] = dgain[pl.ds(i, 1), pl.ds(0, share)]
        da_o[i] = da[:, pl.ds(i * hw, hw)]
    for i in range(2):
        dc_o[:, i, :] = dc[:, pl.ds(i * hw, hw)]
    dw1_o[...] = dw1[...]
    dwo_o[...] = dwo[...].T if aligned else dwo[...]
    dw2_o[...] = dw2[...].T if aligned else dw2[...]


def body(embeds, segments, cotangent, norm_gains, attn_in, attn_out, cross_proj, ffn_in, ffn_out):
    dp = lax.axis_size("dp")
    rows, own, width = embeds.shape[1:]
    slots = segments.shape[2]
    hw = attn_in.shape[3]
    fw = ffn_in.shape[2]
    win = own + 2 * HALO
    cwin = 2 * own + 2 * HALO
    tokens = rows * own
    side = 3 * own // 4
    share = width // dp
    zsteps = (dp - 1).bit_length()

    ins = dict(
        x_h=embeds[0], segs_h=segments, gains=norm_gains.transpose(1, 0, 2), cot_h=cotangent.reshape(tokens, width),
        wa_h=attn_in[0].transpose(1, 0, 2), wo_h=attn_out[0], w1_h=ffn_in[0], w2_h=ffn_out[0],
        cx_h=cross_proj[0].reshape(2 * width, hw),
    )
    outs = dict(
        sec=((tokens, width), BF16), gx=((tokens, width), BF16), dgain=((8, width), F32),
        da_o=((share, 3 * hw), F32), dwo_o=((share, hw), F32), dc=((share, 2 * hw), F32),
        dw1_o=((share, fw), F32), dw2_o=((share, fw), F32),
    )
    vm = dict(
        x=((rows, own, width), BF16), cot=((tokens, width), BF16), segs=(segments.shape, jnp.int32),
        wa=((4, width, 3 * hw), BF16), wo=((4, hw, width), BF16), w1=((4, width, fw), BF16), w2=((4, fw, width), BF16),
        c0=((width, 8 * hw), BF16), cqw=((width, 4 * hw), BF16), cow=((width, 4 * hw), BF16),
        xh=((2, rows, HALO, width), BF16), nw=((rows * win, width), BF16),
        q=((4, rows, own, hw), BF16), k=((4, rows, win, hw), BF16), v=((4, rows, win, hw), BF16),
        p=((4, rows, 2 * own, win), BF16), o=((tokens, width), BF16), inv=((tokens, width), BF16), bias=((rows, own, win), F32),
        r1=((tokens, width), F32), r2=((tokens, width), F32), n2=((tokens, width), BF16), n3=((tokens, width), BF16),
        u=((4, tokens, fw), BF16), gp=((4, tokens, fw), BF16), secs=((tokens, width), BF16),
        acc=((rows * win, width), F32), g=((tokens, width), F32), gb=((tokens, width), BF16), do=((tokens, width), BF16),
        memf=((max(rows * slots, 4 * width), max(width, fw)), BF16), kv=((slots, 8 * hw), BF16), cq=((tokens, width), BF16),
        cp=((max(8 * own, 4 * width), cwin), BF16), cinv=((own, width), BF16), oc=((tokens, width), BF16),
        cols=((rows, own, 128), F32), keys=((rows, 8, cwin), F32),
        dkv=((rows * cwin, 8 * hw), BF16), dmf=((max(rows * slots, 4 * width), max(width, fw)), BF16),
        rcc=((rows, own, width), BF16), rct=((rows, side, width), BF16),
        dg=((rows, 8, width), F32),
        dqkv=((rows * win, 3 * hw), BF16), dhr=((2, rows, HALO, width), BF16),
        dgt=((4, 8, width), F32), dgd=((dp, 8, width), F32),
        dw2=((4 * width, fw), BF16), dwo=((width, 4 * hw), BF16),
        dc0=((share, 2 * hw), F32), dc0r=((share, 2 * hw), F32),
    )
    sums = dict(w20=fw // 2, w21=fw // 2, w10=fw // 2, w11=fw // 2, wo=hw, wa0=hw, wa1=hw, wa2=hw, c0=2 * hw, c1=2 * hw)
    for name, m in sums.items():
        shards = 2 if name in ("w20", "w11") else 1
        vm["rc_" + name] = ((2, width, m), BF16)
        vm["ry_" + name] = ((share if shards == 2 else width, m), BF16)
        vm["zb_" + name] = ((shards, dp, share, m), BF16)
        for k in range(zsteps):
            vm[f"zr{k}_{name}"] = ((shards, dp >> (k + 1), share, m), BF16)
    copies = 140 + 12 * zsteps + dp
    sems = dict(send=pltpu.SemaphoreType.DMA((copies,)), recv=pltpu.SemaphoreType.DMA((copies,)), local=pltpu.SemaphoreType.DMA((16,)))
    in_hbm = {n for n in ins if n.endswith("_h")}
    out_hbm = {"sec", "gx"}
    results = pl.pallas_call(
        functools.partial(layers, list(ins) + list(outs) + list(vm) + list(sems)),
        name="layers",
        out_shape=[jax.ShapeDtypeStruct(*o) for o in outs.values()],
        in_specs=[pl.BlockSpec(memory_space=pl.ANY if n in in_hbm else pltpu.VMEM) for n in ins],
        out_specs=[pl.BlockSpec(memory_space=pl.ANY if n in out_hbm else pltpu.VMEM) for n in outs],
        scratch_shapes=[pltpu.VMEM(*s) for s in vm.values()] + list(sems.values()),
        compiler_params=pltpu.CompilerParams(vmem_limit_bytes=VMEM_LIMIT, collective_id=0, has_side_effects=True),
    )(*ins.values())
    aligned = share % 128 == 0
    sec, gx, dgain, da, dwo, dc, dw1, dw2 = pl.pallas_call(
        functools.partial(arrange, aligned),
        name="arrange",
        out_shape=[
            jax.ShapeDtypeStruct((tokens, width), BF16),
            jax.ShapeDtypeStruct((tokens, width), BF16),
            jax.ShapeDtypeStruct((3, 1, share), F32),
            jax.ShapeDtypeStruct((3, share, hw), F32),
            jax.ShapeDtypeStruct((hw, share) if aligned else (share, hw), F32),
            jax.ShapeDtypeStruct((share, 2, hw), F32),
            jax.ShapeDtypeStruct((share, fw), F32),
            jax.ShapeDtypeStruct((fw, share) if aligned else (share, fw), F32),
        ],
        in_specs=[pl.BlockSpec(memory_space=pltpu.VMEM)] * 8,
        out_specs=[pl.BlockSpec(memory_space=pltpu.VMEM)] * 8,
    )(*results)
    if not aligned:
        dwo, dw2 = dwo.T, dw2.T
    return (
        sec.reshape(1, rows, own, width), gx.reshape(1, rows, own, width), dgain.transpose(1, 0, 2),
        da.transpose(1, 0, 2)[None], dwo[None], dc[None], dw1[None], dw2[None],
    )


def solution(mesh):
    return jax.shard_map(
        body,
        mesh=mesh,
        in_specs=(
            P("pipe", "dp", "tensor", None),
            P(None, "dp", None),
            P("dp", "tensor", None),
            P("pipe", None, None),
            P("pipe", None, None, "tensor"),
            P("pipe", "tensor", None),
            P("pipe", None, None, "tensor"),
            P("pipe", None, "tensor"),
            P("pipe", "tensor", None),
        ),
        out_specs=(
            P("pipe", "dp", "tensor", None),
            P("pipe", "dp", "tensor", None),
            P("pipe", None, "dp"),
            P("pipe", "dp", None, "tensor"),
            P("pipe", "tensor", "dp"),
            P("pipe", "dp", None, "tensor"),
            P("pipe", "dp", "tensor"),
            P("pipe", "tensor", "dp"),
        ),
        check_vma=False,
    )
```

```python
import functools

import jax
import jax.numpy as jnp
from jax import lax
from jax.experimental import pallas as pl
from jax.experimental.pallas import tpu as pltpu
from jax.sharding import PartitionSpec as P

EPS = 1e-05
MASKED = -1000000000.0
DH = 64
HALO = 64
F32 = jnp.float32
BF16 = jnp.bfloat16
GELU_C = 0.7978845608028654
GELU_A = 0.044715
MESH = pl.DeviceIdType.MESH
VMEM_LIMIT = 63 << 20


def mm(a, b):
    return lax.dot_general(a, b, (((1,), (0,)), ((), ())), preferred_element_type=F32)


def mm_nt(a, b):
    return lax.dot_general(a, b, (((1,), (1,)), ((), ())), preferred_element_type=F32)


def mm_tn(a, b):
    return lax.dot_general(a, b, (((0,), (0,)), ((), ())), preferred_element_type=F32)


def norm_parts(v):
    c = v - jnp.mean(v, axis=-1, keepdims=True)
    r = lax.rsqrt(jnp.mean(c * c, axis=-1, keepdims=True) + EPS)
    return c * r, r


def norm(v, gain):
    xhat, _ = norm_parts(v)
    return xhat * gain


def norm_back(v, gain, dn):
    xhat, r = norm_parts(v)
    dxh = dn * gain
    m1 = jnp.mean(dxh, axis=-1, keepdims=True)
    m2 = jnp.mean(dxh * xhat, axis=-1, keepdims=True)
    return r * (dxh - m1 - xhat * m2), jnp.sum(dn * xhat, axis=0, keepdims=True)


def lane_low(shape):
    return lax.broadcasted_iota(jnp.int32, shape, 1) < DH


def pair_join(a, b):
    return jnp.where(lane_low(a.shape), a, b)


def swap_halves(v):
    return pltpu.roll(v, DH, 1)


def attend(q2, k2, v2, mask, keep):
    n, width = q2.shape
    lowq, zero = lane_low(q2.shape), jnp.zeros_like(q2)
    s = mm_nt(jnp.concatenate([jnp.where(lowq, q2, zero), jnp.where(lowq, zero, q2)], axis=0), k2)
    s = jnp.concatenate([mask(s[:n]), mask(s[n:])], axis=0)
    e = jnp.exp(s - jnp.max(s, axis=-1, keepdims=True)).astype(BF16)
    keep(e)
    out = mm(e, jnp.concatenate([v2, jnp.ones_like(v2)], axis=1))
    inv = 1.0 / pair_join(out[:n, width:], out[n:, width:])
    return pair_join(out[:n, :width], out[n:, :width]) * inv, inv


def attend_back(q2, k2, v2, do2, o2, inv, kept):
    low, lowq = lane_low(v2.shape), lane_low(q2.shape)
    one = jnp.ones_like(v2)
    scaled = do2.astype(F32) * inv.astype(F32)
    dob = scaled.astype(BF16)
    minus = (-swap_halves(dob.astype(F32) * o2.astype(F32))).astype(BF16)
    q_t, do_t = q2.T, dob.T
    dq, dk, dv = [], [], []
    for h in range(2):
        e = kept(h)
        rows = slice(h * DH, (h + 1) * DH)
        lhs = jnp.where(lowq, dob, minus) if h == 0 else jnp.where(lowq, minus, dob)
        dp = mm_nt(lhs, jnp.where(low, v2, one) if h == 0 else jnp.where(low, one, v2))
        ds = (dp * e.astype(F32)).astype(BF16)
        dq.append(mm(ds, k2))
        dv.append(mm(do_t[rows], e).astype(BF16))
        dk.append(mm(q_t[rows], ds).astype(BF16))
    return (pair_join(*dq) * (DH**-0.5)).astype(BF16), jnp.concatenate(dk, 0).T, jnp.concatenate(dv, 0).T


def gelu_parts(h):
    h2 = h * h
    half = 0.5 + 0.5 * jnp.tanh(h * (GELU_C + (GELU_C * GELU_A) * h2))
    u = h * half
    slope = half + u * ((1.0 - half) * (2.0 * GELU_C + (6.0 * GELU_C * GELU_A) * h2))
    return u, slope


def flip(i, bit):
    return i + bit - 2 * bit * lax.rem(lax.div(i, bit), 2)


def bit_of(i, bit):
    return lax.rem(lax.div(i, bit), 2)


def reversed_bits(i, count):
    out, bit = 0, 1
    while bit < count:
        out = 2 * out + (i // bit) % 2
        bit *= 2
    return out


class Links:
    def __init__(self, send, recv, local):
        self.send, self.recv, self.local = send, recv, local
        self.n = self.m = 0
        self.sent = []

    def take(self, count=1):
        self.n += count
        return self.n - count

    def remote(self, src, dst, device, at=None):
        at = self.take() if at is None else at
        return pltpu.make_async_remote_copy(
            src_ref=src, dst_ref=dst, send_sem=self.send.at[at], recv_sem=self.recv.at[at],
            device_id=device, device_id_type=MESH,
        )

    def here(self, src, dst):
        self.m += 1
        return pltpu.make_async_copy(src, dst, self.local.at[self.m - 1])


class Gather:
    def __init__(self, links, src, slot, depth, at, pieces=1, planes=None, last_straight=False):
        t, t2 = at["t"], at["t2"]
        half = depth // 2
        n = half // pieces
        whole = pl.ds(0, depth)
        if src is None:
            self.own = []
        elif planes is None:
            self.own = [links.here(src, slot(t, whole))]
        else:
            self.own = [links.here(src.at[i], slot(t, whole, i)) for i in range(planes)]
        self.inner = src is None or planes is not None
        self.straight = pieces - 1 if last_straight else None
        src = slot(t, whole) if self.inner else src
        self.core = links.remote(src, slot(t, whole), at["C"])
        self.over_y, self.over_z, self.core_a, self.core_b = [], [], [], []
        for i in range(pieces):
            mine = pl.ds(pl.multiple_of(at["b"] * half + i * n, n), n)
            other = pl.ds(pl.multiple_of((1 - at["b"]) * half + i * n, n), n)
            self.over_y.append(links.remote(src.at[mine], slot(t, mine), at["Y"]))
            if last_straight and i == pieces - 1:
                self.over_z.append(links.remote(src.at[other], slot(t, other), at["Y"]))
            else:
                self.over_z.append(links.remote(slot(t2, mine), slot(t2, mine), at["Z"][0]))
            self.core_a.append(links.remote(slot(t2, mine), slot(t2, mine), at["C"]))
            self.core_b.append(links.remote(slot(t2, other), slot(t2, other), at["C"]))

    def start(self):
        for c in self.own:
            c.start()
        if self.inner:
            for c in self.own:
                c.wait()
        for c in self.over_y:
            c.start()
        if self.straight is not None:
            self.over_z[self.straight].start()
        self.core.start()

    def step1(self, i=0):
        self.over_y[i].wait_recv()
        if i != self.straight:
            self.over_z[i].start()
        self.core_a[i].start()

    def step2(self, i=0):
        self.over_z[i].wait_recv()
        self.core_b[i].start()

    def ready(self, i):
        if i == 0 and not self.inner:
            for c in self.own:
                c.wait()
        if i == 1:
            self.core.wait_recv()
        if i == 3:
            for c in self.core_a + self.core_b:
                c.wait_recv()

    def finish(self):
        for c in [self.core] + self.over_y + self.over_z + self.core_a + self.core_b:
            c.wait_send()


class Reduce:
    def __init__(self, links, part, rc, ry, zb, zr, at, y_first):
        self.part, self.at, self.y_first = part, at, y_first
        self.rc, self.ry, self.zb, self.zr = rc, ry, zb, zr
        self.n = zb.shape[0]
        self.dp, self.rows = zb.shape[1:3]
        self.core = [links.remote(part(at[f]), rc.at[j], at["C"]) for j, f in enumerate(("t1", "t3"))]
        self.over_z, self.kept = [], []
        off, m, bit, k = 0, self.dp, 1, 0
        while m > 1:
            m //= 2
            b = bit_of(at["d"], bit)
            keep, give = off + b * m, off + (1 - b) * m
            self.over_z.append(links.remote(zb.at[:, pl.ds(give, m)], zr[k], at["Z"][k]))
            self.kept.append((keep, m))
            off, bit, k = keep, 2 * bit, k + 1
        self.off = off
        self.over_y = links.remote(part(at["t2"]) if y_first else zb.at[1, off], ry, at["Y"])

    def core_send(self, j):
        self.core[j].start()

    def into_zb(self, j, mine, theirs):
        for i in range(self.dp):
            where = pl.ds(i * self.rows, self.rows)
            self.zb[j, reversed_bits(i, self.dp)] = (mine[where, :].astype(F32) + theirs[where, :].astype(F32)).astype(BF16)

    def core_done(self):
        self.core[0].wait_recv()
        self.core[1].wait_recv()
        far, near = self.part(self.at["t2"]), self.part(self.at["t"])
        if self.y_first:
            far[...] = (far[...].astype(F32) + self.rc[1].astype(F32)).astype(BF16)
            self.over_y.start()
            near[...] = (near[...].astype(F32) + self.rc[0].astype(F32)).astype(BF16)
        else:
            self.into_zb(0, near, self.rc.at[0])
            self.into_zb(1, far, self.rc.at[1])
            self.over_z[0].start()

    def y_done(self, out=None):
        self.over_y.wait_recv()
        if self.y_first:
            self.into_zb(0, self.part(self.at["t"]), self.ry)
            self.over_z[0].start()
        else:
            out[...] = self.zb[0, self.off].astype(F32) + self.ry[...].astype(F32)

    def z_done(self, k, out=None):
        self.over_z[k].wait_recv()
        keep, m = self.kept[k]
        last = k == len(self.over_z) - 1
        if last and self.y_first:
            out[...] = self.zb[0, keep].astype(F32) + self.zr[k][0, 0].astype(F32)
        else:
            for j in range(self.n):
                live = self.zb.at[j, pl.ds(keep, m)]
                live[...] = (live[...].astype(F32) + self.zr[k][j].astype(F32)).astype(BF16)
            (self.over_y if last else self.over_z[k + 1]).start()

    def z_rest(self, out=None):
        for k in range(1, len(self.over_z)):
            self.z_done(k, out)

    def finish(self):
        for c in self.core + [self.over_y] + self.over_z:
            c.wait_send()


def layers(names, *refs):
    ref = dict(zip(names, refs))
    R = lambda name: ref[name]
    p, d, t = lax.axis_index("pipe"), lax.axis_index("dp"), lax.axis_index("tensor")
    is_enc, is_dec = p == 0, p == 1
    dp = lax.axis_size("dp")
    t1, t2, t3 = flip(t, 1), flip(t, 2), 3 - t
    zbits = []
    while 2 ** len(zbits) < dp:
        zbits.append((p, flip(d, 2 ** len(zbits)), t))
    at = dict(t=t, t1=t1, t2=t2, t3=t3, d=d, b=bit_of(d, 1), C=(p, d, t1), Y=(p, d, t2), T=(p, d, t3), X=(1 - p, d, t), Z=zbits)
    rows, own, width = R("x").shape
    win, cwin = own + 2 * HALO, 2 * own + 2 * HALO
    slots = 4 * own
    tokens = rows * own
    hw = R("wa").shape[2] // 3
    fw = R("w1").shape[2]
    inner = t % 3 != 0
    scale = jnp.asarray(DH**-0.5, BF16)
    gain_ref, x_ref = R("gains"), R("x")
    side = 3 * own // 4

    def rowsl(r, n=own):
        return pl.ds(pl.multiple_of(r * n, n), n)

    def lanes(s, n=hw):
        return pl.ds(pl.multiple_of(s * n, n), n)

    def far_lanes(s):
        return pl.ds(pl.multiple_of(s * 2 * hw + hw, hw), hw)

    def in_row(r, span):
        return pl.ds(pl.multiple_of(r * slots + span.start, HALO), span.size)

    def near_first(i):
        return 2 * lax.rem(lax.div(t, 2) + lax.div(i, 2), 2) + lax.rem(lax.rem(t, 2) + lax.rem(i, 2), 2)

    def far_first(i):
        return 2 * lax.rem(lax.div(t, 2) + lax.rem(lax.div(i + 1, 2), 2), 2) + lax.rem(lax.rem(t, 2) + 1 - lax.div(i, 2), 2)

    def seg_row(side_, r, start):
        row = jnp.broadcast_to(R("segs")[side_, pl.ds(r, 1), :].astype(F32), (8, slots))
        return pltpu.roll(row, lax.rem(2 * slots - start, slots), 1)

    def seg_column(side_, r):
        row = seg_row(side_, r, t * own)[:1, :own]
        return jnp.broadcast_to(row, (128, own)).T

    def spread(column, n):
        return jnp.concatenate([column] * (n // 128), axis=1)

    links = Links(R("send"), R("recv"), R("local"))

    def by_shard(name, n=None):
        def slot(s, span, i=None):
            full = R(name).at[s, span]
            return full if i is None else full.at[:, pl.ds(i * n, n)]

        return slot

    def by_columns(name, n, row):
        def slot(s, span):
            return R(name).at[pl.ds(pl.multiple_of(span.start + row, HALO), span.size), lanes(s, n)]

        return slot

    g_wa = Gather(links, R("wa_h"), by_shard("wa", hw), width, at, 2, 3)
    g_wo = Gather(links, R("wo_h"), by_shard("wo"), hw, at)
    g_w1 = Gather(links, R("w1_h"), by_shard("w1"), width, at, 2)
    g_w2 = Gather(links, R("w2_h"), by_shard("w2"), fw, at, 4, None, True)
    g_c1 = Gather(links, R("cx_h"), by_columns("dmf", hw, 0), 2 * width, at)
    c0_x = links.remote(R("cx_h"), R("dmf").at[pl.ds(2 * width, 2 * width), lanes(t)], at["X"])
    g_c0 = Gather(links, None, by_columns("dmf", hw, 2 * width), 2 * width, at)
    loads = [links.here(R(n + "_h"), R(n)) for n in ("x", "cot", "segs")]
    x_right = links.remote(R("x_h").at[:, pl.ds(own - HALO, HALO)], R("xh").at[0], (p, d, lax.rem(t + 1, 4)))
    x_left = links.remote(R("x_h").at[:, pl.ds(0, HALO)], R("xh").at[1], (p, d, lax.rem(t + 3, 4)))
    base_mem, base_memc, base_memt = links.take(2 * rows), links.take(2 * rows), links.take(rows)
    base_dmc, base_dmt, base_dmx = links.take(rows), links.take(rows), links.take(rows)
    block = pl.ds(pl.multiple_of(t * own, own), own)
    block1 = pl.ds(pl.multiple_of(t1 * own, own), own)
    edge_out = pl.ds(pl.multiple_of(lax.rem(own // 2 + side * t, slots), HALO), side)
    edge_in = pl.ds(pl.multiple_of(lax.rem(own // 2 + side * t3, slots), HALO), side)

    def half_block(h):
        return pl.ds(pl.multiple_of(t * own + h * (own // 2), own // 2), own // 2)

    def mem_x(r, h):
        half = pl.ds(pl.multiple_of(r * own + h * (own // 2), own // 2), own // 2)
        return links.remote(R("secs").at[half], R("memf").at[in_row(r, half_block(h))], at["X"], base_mem + 2 * r + h)

    def mem_c(r, h):
        rows_ = R("memf").at[in_row(r, half_block(h))]
        return links.remote(rows_, rows_, at["C"], base_memc + 2 * r + h)

    def mem_t(r):
        return links.remote(R("memf").at[in_row(r, edge_out)], R("memf").at[in_row(r, edge_out)], at["T"], base_memt + r)

    def dm_rows(r, span):
        return R("dmf").at[in_row(r, span)]

    def dm_c(r):
        return links.remote(dm_rows(r, block1), R("rcc").at[r], at["C"], base_dmc + r)

    def dm_t(r):
        return links.remote(dm_rows(r, edge_in), R("rct").at[r], at["T"], base_dmt + r)

    def dm_x(r):
        return links.remote(R("rcc").at[r], R("rcc").at[r], at["X"], base_dmx + r)

    def by_rows(name, m, col=0):
        return lambda s: R(name).at[pl.ds(pl.multiple_of(s * width, width), width), pl.ds(col, m)]

    def by_lanes(name, m, row=0):
        return lambda s: R(name).at[pl.ds(row, width), lanes(s, m)]

    def reduce_of(name, part, y_first=True):
        zr = [R(f"zr{k}_{name}") for k in range(len(zbits))]
        return Reduce(links, part, R("rc_" + name), R("ry_" + name), R("zb_" + name), zr, at, y_first)

    fh = fw // 2
    r_w2 = [reduce_of(f"w2{j}", by_rows("dw2", fh, j * fh), j == 1) for j in range(2)]
    r_w1 = [reduce_of(f"w1{j}", by_rows("dmf", fh, j * fh), j == 0) for j in range(2)]
    r_wo = reduce_of("wo", by_lanes("dwo", hw))
    r_wa = [reduce_of(f"wa{j}", by_rows("cp", hw, j * hw)) for j in range(3)]
    r_c0 = reduce_of("c0", by_lanes("kv", 2 * hw))
    r_c1 = reduce_of("c1", by_lanes("kv", 2 * hw, width))
    w2_out = [R("dw2_o").at[:, pl.ds(j * fh, fh)] for j in range(2)]
    w1_out = [R("dw1_o").at[:, pl.ds(j * fh, fh)] for j in range(2)]
    wa_out = [R("da_o").at[:, pl.ds(j * hw, hw)] for j in range(3)]
    c0_back = links.remote(R("dc0"), R("dc0r"), at["X"])
    dn_right = links.remote(R("xh").at[1], R("dhr").at[0], (p, d, lax.rem(t + 1, 4)))
    dn_left = links.remote(R("xh").at[0], R("dhr").at[1], (p, d, lax.rem(t + 3, 4)))
    gain_over_t = [links.remote(R("dgt").at[t], R("dgt").at[t], at[f]) for f in ("C", "Y", "T")]
    gain_over_d = []
    for k in range(1, dp):
        to = lax.rem(d + k, dp)
        gain_over_d.append(links.remote(R("dgd").at[d], R("dgd").at[d], (p, to, t)))

    @pl.when(is_dec)
    def _():
        for at_t, start in ((0, 2 * own), (1, 2 * own + side), (3, 2 * own - 2 * HALO)):
            @pl.when(t == at_t)
            def _():
                for r in range(rows):
                    R("memf")[pl.ds(r * slots + start, 2 * HALO), :] = jnp.zeros((2 * HALO, width), BF16)

    barrier = pltpu.get_barrier_semaphore()
    partners = [at["C"], at["Y"], at["T"], at["X"]] + [(p, lax.rem(d + k, dp), t) for k in range(1, dp)]
    for dev in partners:
        pl.semaphore_signal(barrier, inc=1, device_id=dev, device_id_type=MESH)
    pl.semaphore_wait(barrier, len(partners))

    pl.when(t < 3)(x_right.start)
    pl.when(t > 0)(x_left.start)
    loads[0].start()
    g_wa.start()
    g_wo.start()
    for c in loads[1:]:
        c.start()

    @pl.when(is_enc)
    def _():
        c0_x.start()
        g_w1.start()
        g_w2.start()

    @pl.when(is_dec)
    def _():
        g_c1.start()

    for c in loads:
        c.wait()

    nw_ref, bias_ref = R("nw"), R("bias")
    gain0, gain1, gain2 = gain_ref[0], gain_ref[1], gain_ref[2]
    for r in range(rows):
        nw_ref[pl.ds(r * win + HALO, own), :] = norm(x_ref[r].astype(F32), gain0).astype(BF16)
        keys = seg_row(p, r, lax.rem(t * own + slots - HALO, slots))[:1, :win]
        same = spread(seg_column(p, r), win) == keys
        qpos = lax.broadcasted_iota(jnp.int32, (own, win), 0)
        kpos = lax.broadcasted_iota(jnp.int32, (own, win), 1) - HALO
        before = kpos - qpos <= jnp.where(is_enc, 4 * win, 0)
        bias_ref[:, pl.ds(r * win, win)] = jnp.where(same & before, 0.0, MASKED)

    @pl.when(t == 0)
    def _():
        R("xh")[0] = jnp.zeros((rows, HALO, width), BF16)

    @pl.when(t == 3)
    def _():
        R("xh")[1] = jnp.zeros((rows, HALO, width), BF16)

    pl.when(t > 0)(x_right.wait_recv)
    pl.when(t < 3)(x_left.wait_recv)
    for r in range(rows):
        nw_ref[pl.ds(r * win, HALO), :] = norm(R("xh")[0, r].astype(F32), gain0).astype(BF16)
        nw_ref[pl.ds(r * win + HALO + own, HALO), :] = norm(R("xh")[1, r].astype(F32), gain0).astype(BF16)

    def after_pair(i):
        @pl.when(i == 0)
        def _():
            g_wa.step1(0)

        @pl.when(i == 1)
        def _():
            g_wa.step1(1)
            g_wo.step1()
            g_wa.step2(0)

            @pl.when(is_dec)
            def _():
                c0_x.wait_recv()
                g_c0.start()
                g_w2.start()
                g_w1.start()
                g_c1.step1()

            pl.when(is_enc)(lambda: g_w1.step1(0))
            g_wa.step2(1)

        @pl.when(i == 2)
        def _():
            g_wo.step2()
            pl.when(is_enc)(lambda: g_w1.step1(1))

        @pl.when(i == 3)
        def _():
            pl.when(is_dec)(g_c0.step1)

    def wait_ready(i, *weights):
        for k in range(4):
            @pl.when(i == k)
            def _():
                for w in weights:
                    w.ready(k)

    q_ref, k_ref, v_ref, p_ref, o_ref, inv_ref = R("q"), R("k"), R("v"), R("p"), R("o"), R("inv")

    def self_pair(i, _):
        s = near_first(i)
        wait_ready(i, g_wa)
        packed = mm(nw_ref[...], R("wa")[s])
        for r in range(rows):
            q_ref[s, r] = packed[r * win + HALO : r * win + HALO + own, :hw].astype(BF16) * scale
            k_ref[s, r] = packed[r * win : (r + 1) * win, hw : 2 * hw].astype(BF16)
            v_ref[s, r] = packed[r * win : (r + 1) * win, 2 * hw :].astype(BF16)
        for r in range(rows):
            def keep(e):
                p_ref[s, r] = e

            o2, inv = attend(q_ref[s, r], k_ref[s, r], v_ref[s, r], lambda scores: scores + bias_ref[:, pl.ds(r * win, win)], keep)
            o_ref[pl.ds(r * own, own), lanes(s)] = o2.astype(BF16)
            inv_ref[pl.ds(r * own, own), lanes(s)] = inv.astype(BF16)
        after_pair(i)
        return 0

    lax.fori_loop(0, 4, self_pair, 0)
    for k in range(4):
        g_wo.ready(k)
    r1_ref, r2_ref, n2_ref, n3_ref = R("r1"), R("r2"), R("n2"), R("n3")
    u_ref, gp_ref, sec_ref = R("u"), R("gp"), R("secs")
    acc_ref, g_ref, gb_ref, do_ref = R("acc"), R("g"), R("gb"), R("do")
    first = mm(o_ref[...], R("wo")[...].reshape(4 * hw, width))
    for r in range(rows):
        r1_ref[pl.ds(r * own, own), :] = x_ref[r].astype(F32) + first[r * own : (r + 1) * own]
    n2_ref[...] = norm(r1_ref[...], gain1).astype(BF16)

    @pl.when(is_enc)
    def _():
        r2_ref[...] = r1_ref[...]

        def up(i):
            s = near_first(i)
            u, gp = gelu_parts(mm(n2_ref[...], R("w1")[s]))
            u_ref[s] = u.astype(BF16)
            gp_ref[s] = gp.astype(BF16)
            return s

        g_w2.step1(0)
        g_w1.step2(0)

        def near(i, _):
            wait_ready(i, g_w1, g_w2)
            s = up(i)
            r2_ref[...] += mm(u_ref[s], R("w2")[s])

            @pl.when(i == 0)
            def _():
                g_w2.step1(1)
                g_w1.step2(1)

            @pl.when(i == 1)
            def _():
                g_w2.step1(2)
                g_w2.step2(0)
                g_w2.step1(3)

            return 0

        lax.fori_loop(0, 2, near, 0)

        def far(i, _):
            wait_ready(i, g_w1)
            up(i)
            pl.when(i == 2)(lambda: g_w2.step2(1))

            @pl.when(i == 3)
            def _():
                g_w2.step2(2)
                g_w2.step2(3)

            return 0

        lax.fori_loop(2, 4, far, 0)
        g_w2.ready(3)
        far1, far2 = near_first(2), near_first(3)

        def row(r, _):
            rs = rowsl(r)
            total = r2_ref[rs, :] + mm(u_ref[far1, rs, :], R("w2")[far1]) + mm(u_ref[far2, rs, :], R("w2")[far2])
            r2_ref[rs, :] = total
            sec_ref[rs, :] = norm(total, gain2).astype(BF16)
            for h in range(2):
                mem_x(r, h).start()
            return 0

        lax.fori_loop(0, rows, row, 0)

    def sends(reductions, i):
        for j in range(2):
            @pl.when(i == j)
            def _():
                for reduction in reductions:
                    reduction.core_send(j)

    cstart = pl.multiple_of(jnp.minimum(t * (own - HALO), slots - cwin), HALO)
    cwindow = pl.ds(cstart, cwin)
    kv_ref, cq_ref, cp_ref, dkv_ref, cinv_ref = R("kv"), R("cq"), R("cp"), R("dkv"), R("cinv")
    c0_ref, cqw_ref, cow_ref, oc_ref, cot_ref = R("c0"), R("cqw"), R("cow"), R("oc"), R("cot")
    cols, keys_ref = R("cols"), R("keys")

    @pl.when(is_dec)
    def _():
        g_w2.step1(0)
        g_c1.step2()
        for k in range(4):
            g_c1.ready(k)
        pick_shape = (width // 4, width // 2)
        twice = 2 * lax.broadcasted_iota(jnp.int32, pick_shape, 0)
        at_col = lax.broadcasted_iota(jnp.int32, pick_shape, 1)
        picks = [jnp.where(at_col == twice + j, 1.0, 0.0).astype(BF16) for j in range(2)]

        def unweave(base, m):
            return [mm(pick, R("dmf")[pl.ds(base + m * (width // 2), width // 2), :]).astype(BF16) for pick in picks]

        for m in range(4):
            span = pl.ds(m * (width // 4), width // 4)
            cqw_ref[span, :], cow_ref[span, :] = unweave(0, m)
        cq_ref[...] = mm(n2_ref[...], cqw_ref[...]).astype(BF16) * scale
        g_w2.step1(1)
        g_c0.step2()
        g_w2.step1(2)
        g_w2.step1(3)
        kv_ref[...] = jnp.zeros_like(kv_ref)
        for r in range(rows):
            cols[r] = seg_column(1, r)
            keys_ref[r] = seg_row(0, r, cstart)[:, :cwin]
        for k in range(4):
            g_c0.ready(k)
        for m in range(4):
            span = pl.ds(m * (width // 4), width // 4)
            ck, cv = unweave(2 * width, m)
            for s in range(4):
                c0_ref[span, 2 * s * hw : (2 * s + 1) * hw] = ck[:, s * hw : (s + 1) * hw]
                c0_ref[span, (2 * s + 1) * hw : (2 * s + 2) * hw] = cv[:, s * hw : (s + 1) * hw]
        g_w1.step1(0)
        g_w2.step2(0)
        g_w2.step2(1)
        g_w1.step1(1)
        for g in (g_c1, g_c0):
            g.finish()
        R("dmf")[...] = jnp.zeros_like(R("dmf"))
        g_w2.step2(2)
        g_w2.step2(3)
        g_w1.step2(0)
        for k in range(4):
            g_w2.ready(k)

        def early(s, _):
            gp_ref[s] = mm_nt(cot_ref[...], R("w2")[s]).astype(BF16)
            return 0

        lax.fori_loop(0, 4, early, 0)

        def pass_memory_on(r):
            for h in range(2):
                mem_x(r, h).wait_recv()
                mem_c(r, h).start()
            pl.when(inner)(mem_t(r).start)

        def settle(r):
            span = pl.ds(0, own)
            dm_c(r).wait_recv()
            acc_ref[span, :] = R("dmf")[in_row(r, block), :].astype(F32) + R("rcc")[r].astype(F32)

            @pl.when(inner)
            def _():
                dm_t(r).wait_recv()
                place = pl.ds(pl.multiple_of((2 - t) * (own - side), HALO), side)
                acc_ref[place, :] += R("rct")[r].astype(F32)

            R("rcc")[r] = acc_ref[span, :].astype(BF16)
            dm_x(r).start()

        def row(r, _):
            rs = rowsl(r)

            def project(span):
                kv_ref[span, :] = mm(R("memf")[in_row(r, span), :], c0_ref[...]).astype(BF16)

            @pl.when(r == 0)
            def _():
                g_w1.step2(1)
                pass_memory_on(0)

            bias_ref[:, pl.ds(0, cwin)] = jnp.where(spread(cols[r], cwin) == keys_ref[r, pl.ds(0, 1), :], 0.0, MASKED)
            project(block)
            pl.when(r > 0)(lambda: settle(r - 1))
            for h in range(2):
                mem_c(r, h).wait_recv()
            project(block1)

            @pl.when(inner)
            def _():
                mem_t(r).wait_recv()
                project(edge_in)

            def cross(i, _):
                for s in range(4):
                    def keep(e):
                        cp_ref[rowsl(s, 2 * own), :] = e

                    o2, inv = attend(cq_ref[rs, lanes(s)], kv_ref[cwindow, lanes(2 * s)], kv_ref[cwindow, lanes(2 * s + 1)], lambda scores: scores + bias_ref[:, pl.ds(0, cwin)], keep)
                    oc_ref[rs, lanes(s)] = o2.astype(BF16)
                    cinv_ref[:, lanes(s)] = inv.astype(BF16)
                return 0

            cross(0, 0)
            pl.when(r < rows - 1)(lambda: pass_memory_on(r + 1))
            r2_ref[rs, :] = r1_ref[rs, :] + mm_nt(oc_ref[rs, :], cow_ref[...])
            n3_ref[rs, :] = norm(r2_ref[rs, :], gain2).astype(BF16)

            @pl.when(r == 0)
            def _():
                for k in range(4):
                    g_w1.ready(k)

            dn = pl.ds(0, own)
            acc_ref[dn, :] = jnp.zeros((own, width), F32)

            def feed(i, _):
                back = acc_ref[dn, :]
                for s in range(4):
                    u, gp = gelu_parts(mm(n3_ref[rs, :], R("w1")[s]))
                    u = u.astype(BF16)
                    u_ref[s, rs, :] = u
                    dh = (gp_ref[s, rs, :].astype(F32) * gp).astype(BF16)
                    gp_ref[s, rs, :] = dh
                    back += mm_nt(dh, R("w1")[s])
                acc_ref[dn, :] = back
                return 0

            feed(0, 0)
            dx, dg = norm_back(r2_ref[rs, :], gain2, acc_ref[dn, :])
            R("dg")[r, pl.ds(2, 1), :] = dg
            g2 = cot_ref[rs, :].astype(F32) + dx
            g_ref[rs, :] = g2
            gb_ref[rs, :] = g2.astype(BF16)
            do_ref[rs, :] = mm(gb_ref[rs, :], cow_ref[...]).astype(BF16)
            ws = pl.ds(pl.multiple_of(r * cwin, HALO), cwin)

            def back(i, _):
                for s in range(4):
                    dq, dk, dv = attend_back(
                        cq_ref[rs, lanes(s)], kv_ref[cwindow, lanes(2 * s)], kv_ref[cwindow, lanes(2 * s + 1)],
                        do_ref[rs, lanes(s)], oc_ref[rs, lanes(s)], cinv_ref[:, lanes(s)], lambda h: cp_ref[rowsl(2 * s + h), :],
                    )
                    cq_ref[rs, lanes(s)] = dq
                    dkv_ref[ws, lanes(2 * s)] = dk
                    dkv_ref[ws, lanes(2 * s + 1)] = dv
                return 0

            back(0, 0)
            R("dmf")[in_row(r, cwindow), :] = mm_nt(dkv_ref[ws, :], c0_ref[...]).astype(BF16)
            dm_c(r).start()
            pl.when(inner)(dm_t(r).start)

            @pl.when(r == rows - 1)
            def _():
                def w2_grad(i, _):
                    s = far_first(i)
                    R("dw2")[rowsl(s, width), :] = mm_tn(cot_ref[...], u_ref[s]).astype(BF16)
                    sends(r_w2, i)
                    return 0

                lax.fori_loop(0, 4, w2_grad, 0)
                settle(r)

            return 0

        lax.fori_loop(0, rows, row, 0)
        for r in range(rows):
            dm_c(r).wait_send()
            pl.when(inner)(dm_t(r).wait_send)

        def w1_grad(i, _):
            s = far_first(i)
            R("dmf")[rowsl(s, width), :] = mm_tn(n3_ref[...], gp_ref[s]).astype(BF16)
            sends(r_w1, i)

            @pl.when(i == 0)
            def _():
                r_w2[0].core_done()
                r_w2[1].core_done()

            return 0

        lax.fori_loop(0, 4, w1_grad, 0)

        def c0_grad(i, _):
            s = far_first(i)
            total = mm_tn(R("memf")[in_row(0, cwindow), :], dkv_ref[pl.ds(0, cwin), lanes(s, 2 * hw)])
            for r in range(1, rows):
                total += mm_tn(R("memf")[in_row(r, cwindow), :], dkv_ref[pl.ds(r * cwin, cwin), lanes(s, 2 * hw)])
            r_c0.part(s)[...] = total.astype(BF16)
            sends([r_c0], i)

            @pl.when(i == 1)
            def _():
                r_w1[0].core_done()
                r_w1[1].core_done()

            return 0

        lax.fori_loop(0, 4, c0_grad, 0)
        def query_norm(r, _):
            rs = rowsl(r)
            dx, dg = norm_back(r1_ref[rs, :], gain1, mm_nt(cq_ref[rs, :], cqw_ref[...]))
            R("dg")[r, pl.ds(1, 1), :] = dg
            g_ref[rs, :] += dx
            return 0

        lax.fori_loop(0, rows, query_norm, 0)
        dcq = mm_tn(n2_ref[...], cq_ref[...]).astype(BF16)
        dco = mm_tn(gb_ref[...], oc_ref[...]).astype(BF16)
        r_c0.core_done()
        for s in range(4):
            r_c1.part(s)[:, :hw] = dcq[:, s * hw : (s + 1) * hw]
            r_c1.part(s)[:, hw:] = dco[:, s * hw : (s + 1) * hw]
        sends([r_c1], 0)
        sends([r_c1], 1)

    @pl.when(is_enc)
    def _():
        def receive(r):
            rs = rowsl(r)
            dm_x(r).wait_recv()
            dx, dg = norm_back(r2_ref[rs, :], gain2, R("rcc")[r].astype(F32))
            R("dg")[r, pl.ds(2, 1), :] = dg
            g_ref[rs, :] = dx
            gb_ref[rs, :] = dx.astype(BF16)

        def hidden_back(s, rs):
            dh = (mm_nt(gb_ref[rs, :], R("w2")[s]) * gp_ref[s, rs, :].astype(F32)).astype(BF16)
            gp_ref[s, rs, :] = dh
            acc_ref[rs, :] += mm_nt(dh, R("w1")[s])

        head, last = pl.ds(0, (rows - 1) * own), pl.ds((rows - 1) * own, own)
        acc_ref[pl.ds(0, tokens), :] = jnp.zeros((tokens, width), F32)
        for r in range(rows - 1):
            receive(r)

        def head_grads(s, _):
            R("dw2")[rowsl(s, width), :] = mm_tn(gb_ref[head, :], u_ref[s, head, :]).astype(BF16)
            hidden_back(s, head)
            return 0

        lax.fori_loop(0, 4, head_grads, 0)
        receive(rows - 1)

        for i in range(4):
            s = far_first(i)
            part = R("dw2").at[rowsl(s, width)]
            part[...] = (part[...].astype(F32) + mm_tn(gb_ref[last, :], u_ref[s, last, :])).astype(BF16)
            if i < 2:
                for reduction in r_w2:
                    reduction.core_send(i)
        for i in range(4):
            s = far_first(i)
            hidden_back(s, last)
            if i == 1:
                r_w2[0].core_done()
                r_w2[1].core_done()
            R("dmf")[rowsl(s, width), :] = mm_tn(n2_ref[...], gp_ref[s]).astype(BF16)
            if i < 2:
                for reduction in r_w1:
                    reduction.core_send(i)
        r_w1[0].core_done()
        r_w1[1].core_done()
        dx, dg = norm_back(r1_ref[...], gain1, acc_ref[pl.ds(0, tokens), :])
        R("dg")[0, pl.ds(1, 1), :] = dg
        for r in range(1, rows):
            R("dg")[r, pl.ds(1, 1), :] = jnp.zeros_like(dg)
        g_ref[...] += dx

    sec_out = links.here(sec_ref, R("sec"))
    pl.when(is_enc)(sec_out.start)
    gb_ref[...] = g_ref[...].astype(BF16)
    R("dwo")[...] = mm_tn(gb_ref[...], o_ref[...]).astype(BF16)
    r_wo.core_send(0)
    r_wo.core_send(1)
    do_ref[...] = mm_nt(gb_ref[...], R("wo")[...].reshape(4 * hw, width)).astype(BF16)
    acc_ref[...] = jnp.zeros_like(acc_ref)
    dqkv_ref = R("dqkv")
    for r in range(rows):
        dqkv_ref[pl.ds(r * win, HALO), :hw] = jnp.zeros((HALO, hw), BF16)
        dqkv_ref[pl.ds(r * win + HALO + own, HALO), :hw] = jnp.zeros((HALO, hw), BF16)

    def self_back(i, _):
        s = far_first(i)
        for r in range(rows):
            rs = pl.ds(r * own, own)
            dq, dk, dv = attend_back(
                q_ref[s, r], k_ref[s, r], v_ref[s, r], do_ref[rs, lanes(s)], o_ref[rs, lanes(s)], inv_ref[rs, lanes(s)],
                lambda h: p_ref[s, r, pl.ds(h * own, own), :],
            )
            dqkv_ref[pl.ds(r * win + HALO, own), :hw] = dq
            dqkv_ref[pl.ds(r * win, win), hw : 2 * hw] = dk
            dqkv_ref[pl.ds(r * win, win), 2 * hw :] = dv
        R("cp")[rowsl(s, width), pl.ds(0, 3 * hw)] = mm_tn(nw_ref[...], dqkv_ref[...]).astype(BF16)
        sends(r_wa, i)
        acc_ref[...] += mm_nt(dqkv_ref[...], R("wa")[s])

        @pl.when(i == 0)
        def _():
            r_w2[0].z_done(0)
            pl.when(is_dec)(r_c1.core_done)
            r_wo.core_done()
            r_w2[1].y_done()

        @pl.when(i == 2)
        def _():
            r_w1[1].z_done(0)
            r_w1[0].y_done()

        @pl.when(i == 3)
        def _():
            pl.when(is_enc)(r_wo.y_done)
            r_w2[1].z_done(0, w2_out[1])
            r_w2[0].z_rest()
            pl.when(is_dec)(r_c0.y_done)

        return 0

    lax.fori_loop(0, 4, self_back, 0)
    for r in range(rows):
        R("xh")[0, r] = acc_ref[pl.ds(r * win, HALO), :].astype(BF16)
        R("xh")[1, r] = acc_ref[pl.ds(r * win + HALO + own, HALO), :].astype(BF16)
    pl.when(t == 1)(dn_left.start)
    pl.when(t < 3)(dn_right.start)
    pl.when(t > 1)(dn_left.start)
    for j in range(3):
        r_wa[j].core_done()

    @pl.when(is_dec)
    def _():
        def decoded(r, _):
            rs = rowsl(r)
            total = r2_ref[rs, :]
            for s in range(4):
                total += mm(u_ref[s, rs, :], R("w2")[s])
            sec_ref[rs, :] = total.astype(BF16)
            return 0

        lax.fori_loop(0, rows, decoded, 0)
        sec_out.start()

    @pl.when(t == 0)
    def _():
        R("dhr")[0] = jnp.zeros((rows, HALO, width), BF16)

    @pl.when(t == 3)
    def _():
        R("dhr")[1] = jnp.zeros((rows, HALO, width), BF16)

    @pl.when(is_dec)
    def _():
        r_w1[0].z_done(0, w1_out[0])
        r_w1[1].z_rest()
        r_c1.y_done()
        r_w2[1].z_rest(w2_out[1])
        r_wo.y_done()
        r_c0.z_done(0, R("dc0"))

    pl.when(t > 0)(dn_right.wait_recv)
    pl.when(t < 3)(dn_left.wait_recv)
    for r in range(rows):
        lo, hi = pl.ds(r * win + HALO, HALO), pl.ds(r * win + own, HALO)
        acc_ref[lo, :] += R("dhr")[0, r].astype(F32)
        acc_ref[hi, :] += R("dhr")[1, r].astype(F32)
    total = jnp.zeros((1, width), F32)
    for r in range(rows):
        rs = pl.ds(r * own, own)
        dx, dg = norm_back(x_ref[r].astype(F32), gain0, acc_ref[pl.ds(r * win + HALO, own), :])
        gb_ref[rs, :] = (g_ref[rs, :] + dx).astype(BF16)
        total += dg
    dgt, dgd = R("dgt"), R("dgd")
    dgt[t] = jnp.zeros((8, width), F32)
    dgt[t, pl.ds(0, 1), :] = total
    dgt[t, pl.ds(1, 2), :] = sum(R("dg")[r, pl.ds(1, 2), :] for r in range(rows))
    for c in gain_over_t:
        c.start()
    gx_out = links.here(gb_ref, R("gx"))
    gx_out.start()

    def gains_over_t():
        for c in gain_over_t:
            c.wait_recv()
        dgd[d] = dgt[0] + dgt[1] + dgt[2] + dgt[3]
        for c in gain_over_d:
            c.start()

    def gains_over_d():
        total = jnp.zeros((8, width), F32)
        for c in gain_over_d:
            c.wait_recv()
        for k in range(dp):
            total += dgd[k]
        R("dgain")[...] = pltpu.roll(total, lax.rem(width - d * (width // dp), width), 1)

    @pl.when(is_enc)
    def _():
        r_w2[0].y_done(w2_out[0])
        r_w1[0].z_done(0, w1_out[0])
        r_w1[1].z_rest()
        r_wa[0].y_done()
        r_wo.z_done(0, R("dwo_o"))
        r_wa[1].y_done()
        r_w2[1].z_rest(w2_out[1])
        r_wa[0].z_done(0, wa_out[0])
        r_wa[2].y_done()
        gains_over_t()
        r_w1[0].z_rest(w1_out[0])
        r_wa[1].z_done(0, wa_out[1])
        r_w1[1].y_done(w1_out[1])
        r_wo.z_rest(R("dwo_o"))

    @pl.when(is_dec)
    def _():
        r_w2[0].y_done(w2_out[0])
        r_w1[0].z_rest(w1_out[0])
        r_c1.z_done(0, R("dc"))
        r_wa[0].y_done()
        r_wo.z_done(0, R("dwo_o"))
        r_wa[1].y_done()
        r_c0.z_rest(R("dc0"))
        c0_back.start()
        r_wa[0].z_done(0, wa_out[0])
        r_wa[2].y_done()
        r_c1.z_rest(R("dc"))
        r_wa[1].z_done(0, wa_out[1])
        r_w1[1].y_done(w1_out[1])
        gains_over_t()
        r_wo.z_rest(R("dwo_o"))

    r_wa[2].z_done(0, wa_out[2])
    for j in range(3):
        r_wa[j].z_rest(wa_out[j])
    gains_over_d()

    sec_out.wait()
    gx_out.wait()
    for g in (g_wa, g_wo, g_w1, g_w2):
        g.finish()
    for g in r_w2 + r_w1 + [r_wo] + r_wa:
        g.finish()
    for c in gain_over_t + gain_over_d:
        c.wait_send()
    pl.when(t < 3)(x_right.wait_send)
    pl.when(t > 0)(x_left.wait_send)
    pl.when(t < 3)(dn_right.wait_send)
    pl.when(t > 0)(dn_left.wait_send)

    @pl.when(is_enc)
    def _():
        c0_x.wait_send()
        for r in range(rows):
            for h in range(2):
                mem_x(r, h).wait_send()
        c0_back.wait_recv()
        R("dc")[...] = R("dc0r")[...]

    @pl.when(is_dec)
    def _():
        for g in (r_c0, r_c1):
            g.finish()
        for r in range(rows):
            for h in range(2):
                mem_c(r, h).wait_send()
            pl.when(inner)(mem_t(r).wait_send)
            dm_x(r).wait_send()
        c0_back.wait_send()


def arrange(aligned, sec, gx, dgain, da, dwo, dc, dw1, dw2, sec_o, gx_o, dgain_o, da_o, dwo_o, dc_o, dw1_o, dw2_o):
    share, hw = dwo.shape
    sec_o[...] = sec[...]
    gx_o[...] = gx[...]
    for i in range(3):
        dgain_o[i] = dgain[pl.ds(i, 1), pl.ds(0, share)]
        da_o[i] = da[:, pl.ds(i * hw, hw)]
    for i in range(2):
        dc_o[:, i, :] = dc[:, pl.ds(i * hw, hw)]
    dw1_o[...] = dw1[...]
    dwo_o[...] = dwo[...].T if aligned else dwo[...]
    dw2_o[...] = dw2[...].T if aligned else dw2[...]


def body(embeds, segments, cotangent, norm_gains, attn_in, attn_out, cross_proj, ffn_in, ffn_out):
    dp = lax.axis_size("dp")
    rows, own, width = embeds.shape[1:]
    slots = segments.shape[2]
    hw = attn_in.shape[3]
    fw = ffn_in.shape[2]
    win = own + 2 * HALO
    cwin = 2 * own + 2 * HALO
    tokens = rows * own
    side = 3 * own // 4
    share = width // dp
    zsteps = (dp - 1).bit_length()

    ins = dict(
        x_h=embeds[0], segs_h=segments, gains=norm_gains.transpose(1, 0, 2), cot_h=cotangent.reshape(tokens, width),
        wa_h=attn_in[0].transpose(1, 0, 2), wo_h=attn_out[0], w1_h=ffn_in[0], w2_h=ffn_out[0],
        cx_h=cross_proj[0].reshape(2 * width, hw),
    )
    outs = dict(
        sec=((tokens, width), BF16), gx=((tokens, width), BF16), dgain=((8, width), F32),
        da_o=((share, 3 * hw), F32), dwo_o=((share, hw), F32), dc=((share, 2 * hw), F32),
        dw1_o=((share, fw), F32), dw2_o=((share, fw), F32),
    )
    vm = dict(
        x=((rows, own, width), BF16), cot=((tokens, width), BF16), segs=(segments.shape, jnp.int32),
        wa=((4, width, 3 * hw), BF16), wo=((4, hw, width), BF16), w1=((4, width, fw), BF16), w2=((4, fw, width), BF16),
        c0=((width, 8 * hw), BF16), cqw=((width, 4 * hw), BF16), cow=((width, 4 * hw), BF16),
        xh=((2, rows, HALO, width), BF16), nw=((rows * win, width), BF16),
        q=((4, rows, own, hw), BF16), k=((4, rows, win, hw), BF16), v=((4, rows, win, hw), BF16),
        p=((4, rows, 2 * own, win), BF16), o=((tokens, width), BF16), inv=((tokens, width), BF16), bias=((own, max(rows * win, cwin)), F32),
        r1=((tokens, width), F32), r2=((tokens, width), F32), n2=((tokens, width), BF16), n3=((tokens, width), BF16),
        u=((4, tokens, fw), BF16), gp=((4, tokens, fw), BF16), secs=((tokens, width), BF16),
        acc=((rows * win, width), F32), g=((tokens, width), F32), gb=((tokens, width), BF16), do=((tokens, width), BF16),
        memf=((max(rows * slots, 4 * width), max(width, fw)), BF16), kv=((slots, 8 * hw), BF16), cq=((tokens, width), BF16),
        cp=((max(8 * own, 4 * width), cwin), BF16), cinv=((own, width), BF16), oc=((tokens, width), BF16),
        cols=((rows, own, 128), F32), keys=((rows, 8, cwin), F32),
        dkv=((rows * cwin, 8 * hw), BF16), dmf=((max(rows * slots, 4 * width), max(width, fw)), BF16),
        rcc=((rows, own, width), BF16), rct=((rows, side, width), BF16),
        dg=((rows, 8, width), F32),
        dqkv=((rows * win, 3 * hw), BF16), dhr=((2, rows, HALO, width), BF16),
        dgt=((4, 8, width), F32), dgd=((dp, 8, width), F32),
        dw2=((4 * width, fw), BF16), dwo=((width, 4 * hw), BF16),
        dc0=((share, 2 * hw), F32), dc0r=((share, 2 * hw), F32),
    )
    sums = dict(w20=fw // 2, w21=fw // 2, w10=fw // 2, w11=fw // 2, wo=hw, wa0=hw, wa1=hw, wa2=hw, c0=2 * hw, c1=2 * hw)
    for name, m in sums.items():
        shards = 2 if name in ("w20", "w11") else 1
        vm["rc_" + name] = ((2, width, m), BF16)
        vm["ry_" + name] = ((share if shards == 2 else width, m), BF16)
        vm["zb_" + name] = ((shards, dp, share, m), BF16)
        for k in range(zsteps):
            vm[f"zr{k}_{name}"] = ((shards, dp >> (k + 1), share, m), BF16)
    copies = 140 + 12 * zsteps + dp
    sems = dict(send=pltpu.SemaphoreType.DMA((copies,)), recv=pltpu.SemaphoreType.DMA((copies,)), local=pltpu.SemaphoreType.DMA((16,)))
    in_hbm = {n for n in ins if n.endswith("_h")}
    out_hbm = {"sec", "gx"}
    results = pl.pallas_call(
        functools.partial(layers, list(ins) + list(outs) + list(vm) + list(sems)),
        name="layers",
        out_shape=[jax.ShapeDtypeStruct(*o) for o in outs.values()],
        in_specs=[pl.BlockSpec(memory_space=pl.ANY if n in in_hbm else pltpu.VMEM) for n in ins],
        out_specs=[pl.BlockSpec(memory_space=pl.ANY if n in out_hbm else pltpu.VMEM) for n in outs],
        scratch_shapes=[pltpu.VMEM(*s) for s in vm.values()] + list(sems.values()),
        compiler_params=pltpu.CompilerParams(vmem_limit_bytes=VMEM_LIMIT, collective_id=0, has_side_effects=True),
    )(*ins.values())
    aligned = share % 128 == 0
    sec, gx, dgain, da, dwo, dc, dw1, dw2 = pl.pallas_call(
        functools.partial(arrange, aligned),
        name="arrange",
        out_shape=[
            jax.ShapeDtypeStruct((tokens, width), BF16),
            jax.ShapeDtypeStruct((tokens, width), BF16),
            jax.ShapeDtypeStruct((3, 1, share), F32),
            jax.ShapeDtypeStruct((3, share, hw), F32),
            jax.ShapeDtypeStruct((hw, share) if aligned else (share, hw), F32),
            jax.ShapeDtypeStruct((share, 2, hw), F32),
            jax.ShapeDtypeStruct((share, fw), F32),
            jax.ShapeDtypeStruct((fw, share) if aligned else (share, fw), F32),
        ],
        in_specs=[pl.BlockSpec(memory_space=pltpu.VMEM)] * 8,
        out_specs=[pl.BlockSpec(memory_space=pltpu.VMEM)] * 8,
    )(*results)
    if not aligned:
        dwo, dw2 = dwo.T, dw2.T
    return (
        sec.reshape(1, rows, own, width), gx.reshape(1, rows, own, width), dgain.transpose(1, 0, 2),
        da.transpose(1, 0, 2)[None], dwo[None], dc[None], dw1[None], dw2[None],
    )


def solution(mesh):
    return jax.shard_map(
        body,
        mesh=mesh,
        in_specs=(
            P("pipe", "dp", "tensor", None),
            P(None, "dp", None),
            P("dp", "tensor", None),
            P("pipe", None, None),
            P("pipe", None, None, "tensor"),
            P("pipe", "tensor", None),
            P("pipe", None, None, "tensor"),
            P("pipe", None, "tensor"),
            P("pipe", "tensor", None),
        ),
        out_specs=(
            P("pipe", "dp", "tensor", None),
            P("pipe", "dp", "tensor", None),
            P("pipe", None, "dp"),
            P("pipe", "dp", None, "tensor"),
            P("pipe", "tensor", "dp"),
            P("pipe", "dp", None, "tensor"),
            P("pipe", "dp", "tensor"),
            P("pipe", "tensor", "dp"),
        ),
        check_vma=False,
    )
```

```python
import functools

import jax
import jax.numpy as jnp
from jax import lax
from jax.experimental import pallas as pl
from jax.experimental.pallas import tpu as pltpu
from jax.sharding import PartitionSpec as P

EPS = 1e-05
MASKED = -1000000000.0
DH = 64
HALO = 64
F32 = jnp.float32
BF16 = jnp.bfloat16
GELU_C = 0.7978845608028654
GELU_A = 0.044715
MESH = pl.DeviceIdType.MESH
VMEM_LIMIT = 63 << 20


def mm(a, b):
    return lax.dot_general(a, b, (((1,), (0,)), ((), ())), preferred_element_type=F32)


def mm_nt(a, b):
    return lax.dot_general(a, b, (((1,), (1,)), ((), ())), preferred_element_type=F32)


def mm_tn(a, b):
    return lax.dot_general(a, b, (((0,), (0,)), ((), ())), preferred_element_type=F32)


def norm_parts(v):
    c = v - jnp.mean(v, axis=-1, keepdims=True)
    r = lax.rsqrt(jnp.mean(c * c, axis=-1, keepdims=True) + EPS)
    return c * r, r


def norm(v, gain):
    xhat, _ = norm_parts(v)
    return xhat * gain


def norm_back(v, gain, dn):
    xhat, r = norm_parts(v)
    dxh = dn * gain
    m1 = jnp.mean(dxh, axis=-1, keepdims=True)
    m2 = jnp.mean(dxh * xhat, axis=-1, keepdims=True)
    return r * (dxh - m1 - xhat * m2), jnp.sum(dn * xhat, axis=0, keepdims=True)


def lane_low(shape):
    return lax.broadcasted_iota(jnp.int32, shape, 1) < DH


def pair_join(a, b):
    return jnp.where(lane_low(a.shape), a, b)


def swap_halves(v):
    return pltpu.roll(v, DH, 1)


def attend(q2, k2, v2, mask, keep):
    n, width = q2.shape
    lowq, zero = lane_low(q2.shape), jnp.zeros_like(q2)
    s = mm_nt(jnp.concatenate([jnp.where(lowq, q2, zero), jnp.where(lowq, zero, q2)], axis=0), k2)
    s = jnp.concatenate([mask(s[:n]), mask(s[n:])], axis=0)
    e = jnp.exp(s - jnp.max(s, axis=-1, keepdims=True)).astype(BF16)
    keep(e)
    out = mm(e, jnp.concatenate([v2, jnp.ones_like(v2)], axis=1))
    inv = 1.0 / pair_join(out[:n, width:], out[n:, width:])
    return pair_join(out[:n, :width], out[n:, :width]) * inv, inv


def attend_back(q2, k2, v2, do2, o2, inv, kept):
    low, lowq = lane_low(v2.shape), lane_low(q2.shape)
    one = jnp.ones_like(v2)
    scaled = do2.astype(F32) * inv.astype(F32)
    dob = scaled.astype(BF16)
    minus = (-swap_halves(dob.astype(F32) * o2.astype(F32))).astype(BF16)
    q_t, do_t = q2.T, dob.T
    dq, dk, dv = [], [], []
    for h in range(2):
        e = kept(h)
        rows = slice(h * DH, (h + 1) * DH)
        lhs = jnp.where(lowq, dob, minus) if h == 0 else jnp.where(lowq, minus, dob)
        dp = mm_nt(lhs, jnp.where(low, v2, one) if h == 0 else jnp.where(low, one, v2))
        ds = (dp * e.astype(F32)).astype(BF16)
        dq.append(mm(ds, k2))
        dv.append(mm(do_t[rows], e).astype(BF16))
        dk.append(mm(q_t[rows], ds).astype(BF16))
    return (pair_join(*dq) * (DH**-0.5)).astype(BF16), jnp.concatenate(dk, 0).T, jnp.concatenate(dv, 0).T


def gelu_parts(h):
    h2 = h * h
    half = 0.5 + 0.5 * jnp.tanh(h * (GELU_C + (GELU_C * GELU_A) * h2))
    u = h * half
    slope = half + u * ((1.0 - half) * (2.0 * GELU_C + (6.0 * GELU_C * GELU_A) * h2))
    return u, slope


def flip(i, bit):
    return i + bit - 2 * bit * lax.rem(lax.div(i, bit), 2)


def bit_of(i, bit):
    return lax.rem(lax.div(i, bit), 2)


def reversed_bits(i, count):
    out, bit = 0, 1
    while bit < count:
        out = 2 * out + (i // bit) % 2
        bit *= 2
    return out


class Links:
    def __init__(self, send, recv, local):
        self.send, self.recv, self.local = send, recv, local
        self.n = self.m = 0
        self.sent = []

    def take(self, count=1):
        self.n += count
        return self.n - count

    def remote(self, src, dst, device, at=None):
        at = self.take() if at is None else at
        return pltpu.make_async_remote_copy(
            src_ref=src, dst_ref=dst, send_sem=self.send.at[at], recv_sem=self.recv.at[at],
            device_id=device, device_id_type=MESH,
        )

    def here(self, src, dst):
        self.m += 1
        return pltpu.make_async_copy(src, dst, self.local.at[self.m - 1])


class Gather:
    def __init__(self, links, src, slot, depth, at, pieces=1, planes=None, last_straight=False):
        t, t2 = at["t"], at["t2"]
        half = depth // 2
        n = half // pieces
        whole = pl.ds(0, depth)
        if src is None:
            self.own = []
        elif planes is None:
            self.own = [links.here(src, slot(t, whole))]
        else:
            self.own = [links.here(src.at[i], slot(t, whole, i)) for i in range(planes)]
        self.inner = src is None or planes is not None
        self.straight = pieces - 1 if last_straight else None
        src = slot(t, whole) if self.inner else src
        self.core = links.remote(src, slot(t, whole), at["C"])
        self.over_y, self.over_z, self.core_a, self.core_b = [], [], [], []
        for i in range(pieces):
            mine = pl.ds(pl.multiple_of(at["b"] * half + i * n, n), n)
            other = pl.ds(pl.multiple_of((1 - at["b"]) * half + i * n, n), n)
            self.over_y.append(links.remote(src.at[mine], slot(t, mine), at["Y"]))
            if last_straight and i == pieces - 1:
                self.over_z.append(links.remote(src.at[other], slot(t, other), at["Y"]))
            else:
                self.over_z.append(links.remote(slot(t2, mine), slot(t2, mine), at["Z"][0]))
            self.core_a.append(links.remote(slot(t2, mine), slot(t2, mine), at["C"]))
            self.core_b.append(links.remote(slot(t2, other), slot(t2, other), at["C"]))

    def start(self):
        for c in self.own:
            c.start()
        if self.inner:
            for c in self.own:
                c.wait()
        for c in self.over_y:
            c.start()
        if self.straight is not None:
            self.over_z[self.straight].start()
        self.core.start()

    def step1(self, i=0):
        self.over_y[i].wait_recv()
        if i != self.straight:
            self.over_z[i].start()
        self.core_a[i].start()

    def step2(self, i=0):
        self.over_z[i].wait_recv()
        self.core_b[i].start()

    def ready(self, i):
        if i == 0 and not self.inner:
            for c in self.own:
                c.wait()
        if i == 1:
            self.core.wait_recv()
        if i == 3:
            for c in self.core_a + self.core_b:
                c.wait_recv()

    def finish(self):
        for c in [self.core] + self.over_y + self.over_z + self.core_a + self.core_b:
            c.wait_send()


class Reduce:
    def __init__(self, links, part, rc, ry, zb, zr, at, y_first):
        self.part, self.at, self.y_first = part, at, y_first
        self.rc, self.ry, self.zb, self.zr = rc, ry, zb, zr
        self.n = zb.shape[0]
        self.dp, self.rows = zb.shape[1:3]
        self.core = [links.remote(part(at[f]), rc.at[j], at["C"]) for j, f in enumerate(("t1", "t3"))]
        self.over_z, self.kept = [], []
        off, m, bit, k = 0, self.dp, 1, 0
        while m > 1:
            m //= 2
            b = bit_of(at["d"], bit)
            keep, give = off + b * m, off + (1 - b) * m
            self.over_z.append(links.remote(zb.at[:, pl.ds(give, m)], zr[k], at["Z"][k]))
            self.kept.append((keep, m))
            off, bit, k = keep, 2 * bit, k + 1
        self.off = off
        self.over_y = links.remote(part(at["t2"]) if y_first else zb.at[1, off], ry, at["Y"])

    def core_send(self, j):
        self.core[j].start()

    def into_zb(self, j, mine, theirs):
        for i in range(self.dp):
            where = pl.ds(i * self.rows, self.rows)
            self.zb[j, reversed_bits(i, self.dp)] = (mine[where, :].astype(F32) + theirs[where, :].astype(F32)).astype(BF16)

    def core_done(self):
        self.core[0].wait_recv()
        self.core[1].wait_recv()
        far, near = self.part(self.at["t2"]), self.part(self.at["t"])
        if self.y_first:
            far[...] = (far[...].astype(F32) + self.rc[1].astype(F32)).astype(BF16)
            self.over_y.start()
            near[...] = (near[...].astype(F32) + self.rc[0].astype(F32)).astype(BF16)
        else:
            self.into_zb(0, near, self.rc.at[0])
            self.into_zb(1, far, self.rc.at[1])
            self.over_z[0].start()

    def y_done(self, out=None):
        self.over_y.wait_recv()
        if self.y_first:
            self.into_zb(0, self.part(self.at["t"]), self.ry)
            self.over_z[0].start()
        else:
            out[...] = self.zb[0, self.off].astype(F32) + self.ry[...].astype(F32)

    def z_done(self, k, out=None):
        self.over_z[k].wait_recv()
        keep, m = self.kept[k]
        last = k == len(self.over_z) - 1
        if last and self.y_first:
            out[...] = self.zb[0, keep].astype(F32) + self.zr[k][0, 0].astype(F32)
        else:
            for j in range(self.n):
                live = self.zb.at[j, pl.ds(keep, m)]
                live[...] = (live[...].astype(F32) + self.zr[k][j].astype(F32)).astype(BF16)
            (self.over_y if last else self.over_z[k + 1]).start()

    def z_rest(self, out=None):
        for k in range(1, len(self.over_z)):
            self.z_done(k, out)

    def finish(self):
        for c in self.core + [self.over_y] + self.over_z:
            c.wait_send()


def layers(names, *refs):
    ref = dict(zip(names, refs))
    R = lambda name: ref[name]
    p, d, t = lax.axis_index("pipe"), lax.axis_index("dp"), lax.axis_index("tensor")
    is_enc, is_dec = p == 0, p == 1
    dp = lax.axis_size("dp")
    t1, t2, t3 = flip(t, 1), flip(t, 2), 3 - t
    zbits = []
    while 2 ** len(zbits) < dp:
        zbits.append((p, flip(d, 2 ** len(zbits)), t))
    at = dict(t=t, t1=t1, t2=t2, t3=t3, d=d, b=bit_of(d, 1), C=(p, d, t1), Y=(p, d, t2), T=(p, d, t3), X=(1 - p, d, t), Z=zbits)
    rows, own, width = R("x").shape
    win, cwin = own + 2 * HALO, 2 * own + 2 * HALO
    slots = 4 * own
    tokens = rows * own
    hw = R("wa").shape[2] // 3
    fw = R("w1").shape[2]
    inner = t % 3 != 0
    scale = jnp.asarray(DH**-0.5, BF16)
    gain_ref, x_ref = R("gains"), R("x")
    side = 3 * own // 4

    def rowsl(r, n=own):
        return pl.ds(pl.multiple_of(r * n, n), n)

    def lanes(s, n=hw):
        return pl.ds(pl.multiple_of(s * n, n), n)

    def far_lanes(s):
        return pl.ds(pl.multiple_of(s * 2 * hw + hw, hw), hw)

    def in_row(r, span):
        return pl.ds(pl.multiple_of(r * slots + span.start, HALO), span.size)

    def near_first(i):
        return 2 * lax.rem(lax.div(t, 2) + lax.div(i, 2), 2) + lax.rem(lax.rem(t, 2) + lax.rem(i, 2), 2)

    def far_first(i):
        return 2 * lax.rem(lax.div(t, 2) + lax.rem(lax.div(i + 1, 2), 2), 2) + lax.rem(lax.rem(t, 2) + 1 - lax.div(i, 2), 2)

    def seg_row(side_, r, start):
        row = jnp.broadcast_to(R("segs")[side_, pl.ds(r, 1), :].astype(F32), (8, slots))
        return pltpu.roll(row, lax.rem(2 * slots - start, slots), 1)

    def seg_column(side_, r):
        row = seg_row(side_, r, t * own)[:1, :own]
        return jnp.broadcast_to(row, (128, own)).T

    def spread(column, n):
        return jnp.concatenate([column] * (n // 128), axis=1)

    links = Links(R("send"), R("recv"), R("local"))

    def by_shard(name, n=None):
        def slot(s, span, i=None):
            full = R(name).at[s, span]
            return full if i is None else full.at[:, pl.ds(i * n, n)]

        return slot

    def by_columns(name, n, row):
        def slot(s, span):
            return R(name).at[pl.ds(pl.multiple_of(span.start + row, HALO), span.size), lanes(s, n)]

        return slot

    g_wa = Gather(links, R("wa_h"), by_shard("wa", hw), width, at, 2, 3)
    g_wo = Gather(links, R("wo_h"), by_shard("wo"), hw, at)
    g_w1 = Gather(links, R("w1_h"), by_shard("w1"), width, at, 2)
    g_w2 = Gather(links, R("w2_h"), by_shard("w2"), fw, at, 4, None, True)
    g_c1 = Gather(links, R("cx_h"), by_columns("dmf", hw, 0), 2 * width, at)
    c0_x = links.remote(R("cx_h"), R("dmf").at[pl.ds(2 * width, 2 * width), lanes(t)], at["X"])
    g_c0 = Gather(links, None, by_columns("dmf", hw, 2 * width), 2 * width, at)
    loads = [links.here(R(n + "_h"), R(n)) for n in ("x", "cot", "segs")]
    x_right = links.remote(R("x_h").at[:, pl.ds(own - HALO, HALO)], R("xh").at[0], (p, d, lax.rem(t + 1, 4)))
    x_left = links.remote(R("x_h").at[:, pl.ds(0, HALO)], R("xh").at[1], (p, d, lax.rem(t + 3, 4)))
    base_mem, base_memc, base_memt = links.take(2 * rows), links.take(2 * rows), links.take(rows)
    base_dmc, base_dmt, base_dmx = links.take(rows), links.take(rows), links.take(rows)
    block = pl.ds(pl.multiple_of(t * own, own), own)
    block1 = pl.ds(pl.multiple_of(t1 * own, own), own)
    edge_out = pl.ds(pl.multiple_of(lax.rem(own // 2 + side * t, slots), HALO), side)
    edge_in = pl.ds(pl.multiple_of(lax.rem(own // 2 + side * t3, slots), HALO), side)

    def half_block(h):
        return pl.ds(pl.multiple_of(t * own + h * (own // 2), own // 2), own // 2)

    def mem_x(r, h):
        half = pl.ds(pl.multiple_of(r * own + h * (own // 2), own // 2), own // 2)
        return links.remote(R("secs").at[half], R("memf").at[in_row(r, half_block(h))], at["X"], base_mem + 2 * r + h)

    def mem_c(r, h):
        rows_ = R("memf").at[in_row(r, half_block(h))]
        return links.remote(rows_, rows_, at["C"], base_memc + 2 * r + h)

    def mem_t(r):
        return links.remote(R("memf").at[in_row(r, edge_out)], R("memf").at[in_row(r, edge_out)], at["T"], base_memt + r)

    def dm_rows(r, span):
        return R("dmf").at[in_row(r, span)]

    def dm_c(r):
        return links.remote(dm_rows(r, block1), R("rcc").at[r], at["C"], base_dmc + r)

    def dm_t(r):
        return links.remote(dm_rows(r, edge_in), R("rct").at[r], at["T"], base_dmt + r)

    def dm_x(r):
        return links.remote(R("rcc").at[r], R("rcc").at[r], at["X"], base_dmx + r)

    def by_rows(name, m, col=0):
        return lambda s: R(name).at[pl.ds(pl.multiple_of(s * width, width), width), pl.ds(col, m)]

    def by_lanes(name, m, row=0):
        return lambda s: R(name).at[pl.ds(row, width), lanes(s, m)]

    def reduce_of(name, part, y_first=True):
        zr = [R(f"zr{k}_{name}") for k in range(len(zbits))]
        return Reduce(links, part, R("rc_" + name), R("ry_" + name), R("zb_" + name), zr, at, y_first)

    fh = fw // 2
    r_w2 = [reduce_of(f"w2{j}", by_rows("dw2", fh, j * fh), j == 1) for j in range(2)]
    r_w1 = [reduce_of(f"w1{j}", by_rows("dmf", fh, j * fh), j == 0) for j in range(2)]
    r_wo = reduce_of("wo", by_lanes("dwo", hw))
    r_wa = [reduce_of(f"wa{j}", by_rows("cp", hw, j * hw)) for j in range(3)]
    r_c0 = reduce_of("c0", by_lanes("kv", 2 * hw))
    r_c1 = reduce_of("c1", by_lanes("kv", 2 * hw, width))
    w2_out = [R("dw2_o").at[:, pl.ds(j * fh, fh)] for j in range(2)]
    w1_out = [R("dw1_o").at[:, pl.ds(j * fh, fh)] for j in range(2)]
    wa_out = [R("da_o").at[:, pl.ds(j * hw, hw)] for j in range(3)]
    c0_back = links.remote(R("dc0"), R("dc0r"), at["X"])
    dn_right = links.remote(R("xh").at[1], R("dhr").at[0], (p, d, lax.rem(t + 1, 4)))
    dn_left = links.remote(R("xh").at[0], R("dhr").at[1], (p, d, lax.rem(t + 3, 4)))
    gain_over_t = [links.remote(R("dgt").at[t], R("dgt").at[t], at[f]) for f in ("C", "Y", "T")]
    gain_over_d = []
    for k in range(1, dp):
        to = lax.rem(d + k, dp)
        gain_over_d.append(links.remote(R("dgd").at[d], R("dgd").at[d], (p, to, t)))

    @pl.when(is_dec)
    def _():
        for at_t, start in ((0, 2 * own), (1, 2 * own + side), (3, 2 * own - 2 * HALO)):
            @pl.when(t == at_t)
            def _():
                for r in range(rows):
                    R("memf")[pl.ds(r * slots + start, 2 * HALO), :] = jnp.zeros((2 * HALO, width), BF16)

    barrier = pltpu.get_barrier_semaphore()
    partners = [at["C"], at["Y"], at["T"], at["X"]] + [(p, lax.rem(d + k, dp), t) for k in range(1, dp)]
    for dev in partners:
        pl.semaphore_signal(barrier, inc=1, device_id=dev, device_id_type=MESH)
    pl.semaphore_wait(barrier, len(partners))

    pl.when(t < 3)(x_right.start)
    pl.when(t > 0)(x_left.start)
    g_wa.start()
    loads[0].start()
    g_wo.start()
    for c in loads[1:]:
        c.start()

    @pl.when(is_enc)
    def _():
        c0_x.start()
        g_w1.start()
        g_w2.start()

    @pl.when(is_dec)
    def _():
        g_c1.start()

    for c in loads:
        c.wait()

    nw_ref, bias_ref = R("nw"), R("bias")
    gain0, gain1, gain2 = gain_ref[0], gain_ref[1], gain_ref[2]
    for r in range(rows):
        nw_ref[pl.ds(r * win + HALO, own), :] = norm(x_ref[r].astype(F32), gain0).astype(BF16)
        keys = seg_row(p, r, lax.rem(t * own + slots - HALO, slots))[:1, :win]
        same = spread(seg_column(p, r), win) == keys
        qpos = lax.broadcasted_iota(jnp.int32, (own, win), 0)
        kpos = lax.broadcasted_iota(jnp.int32, (own, win), 1) - HALO
        before = kpos - qpos <= jnp.where(is_enc, 4 * win, 0)
        bias_ref[:, pl.ds(r * win, win)] = jnp.where(same & before, 0.0, MASKED)

    @pl.when(t == 0)
    def _():
        R("xh")[0] = jnp.zeros((rows, HALO, width), BF16)

    @pl.when(t == 3)
    def _():
        R("xh")[1] = jnp.zeros((rows, HALO, width), BF16)

    pl.when(t > 0)(x_right.wait_recv)
    pl.when(t < 3)(x_left.wait_recv)
    for r in range(rows):
        nw_ref[pl.ds(r * win, HALO), :] = norm(R("xh")[0, r].astype(F32), gain0).astype(BF16)
        nw_ref[pl.ds(r * win + HALO + own, HALO), :] = norm(R("xh")[1, r].astype(F32), gain0).astype(BF16)

    def after_pair(i):
        @pl.when(i == 0)
        def _():
            g_wa.step1(0)

        @pl.when(i == 1)
        def _():
            g_wa.step1(1)
            g_wo.step1()
            g_wa.step2(0)

            @pl.when(is_dec)
            def _():
                c0_x.wait_recv()
                g_c0.start()
                g_w2.start()
                g_w1.start()
                g_c1.step1()

            pl.when(is_enc)(lambda: g_w1.step1(0))
            g_wa.step2(1)

        @pl.when(i == 2)
        def _():
            g_wo.step2()
            pl.when(is_enc)(lambda: g_w1.step1(1))

        @pl.when(i == 3)
        def _():
            pl.when(is_dec)(g_c0.step1)

    def wait_ready(i, *weights):
        for k in range(4):
            @pl.when(i == k)
            def _():
                for w in weights:
                    w.ready(k)

    q_ref, k_ref, v_ref, p_ref, o_ref, inv_ref = R("q"), R("k"), R("v"), R("p"), R("o"), R("inv")

    def self_pair(i, _):
        s = near_first(i)
        wait_ready(i, g_wa)
        packed = mm(nw_ref[...], R("wa")[s])
        for r in range(rows):
            q_ref[s, r] = packed[r * win + HALO : r * win + HALO + own, :hw].astype(BF16) * scale
            k_ref[s, r] = packed[r * win : (r + 1) * win, hw : 2 * hw].astype(BF16)
            v_ref[s, r] = packed[r * win : (r + 1) * win, 2 * hw :].astype(BF16)
        for r in range(rows):
            def keep(e):
                p_ref[s, r] = e

            o2, inv = attend(q_ref[s, r], k_ref[s, r], v_ref[s, r], lambda scores: scores + bias_ref[:, pl.ds(r * win, win)], keep)
            o_ref[pl.ds(r * own, own), lanes(s)] = o2.astype(BF16)
            inv_ref[pl.ds(r * own, own), lanes(s)] = inv.astype(BF16)
        after_pair(i)
        return 0

    lax.fori_loop(0, 4, self_pair, 0)
    for k in range(4):
        g_wo.ready(k)
    r1_ref, r2_ref, n2_ref, n3_ref = R("r1"), R("r2"), R("n2"), R("n3")
    u_ref, gp_ref, sec_ref = R("u"), R("gp"), R("secs")
    acc_ref, g_ref, gb_ref, do_ref = R("acc"), R("g"), R("gb"), R("do")
    first = mm(o_ref[...], R("wo")[...].reshape(4 * hw, width))
    for r in range(rows):
        r1_ref[pl.ds(r * own, own), :] = x_ref[r].astype(F32) + first[r * own : (r + 1) * own]
    n2_ref[...] = norm(r1_ref[...], gain1).astype(BF16)

    @pl.when(is_enc)
    def _():
        r2_ref[...] = r1_ref[...]

        def up(i):
            s = near_first(i)
            u, gp = gelu_parts(mm(n2_ref[...], R("w1")[s]))
            u_ref[s] = u.astype(BF16)
            gp_ref[s] = gp.astype(BF16)
            return s

        g_w2.step1(0)
        g_w1.step2(0)

        def near(i, _):
            wait_ready(i, g_w1, g_w2)
            s = up(i)
            r2_ref[...] += mm(u_ref[s], R("w2")[s])

            @pl.when(i == 0)
            def _():
                g_w2.step1(1)
                g_w1.step2(1)

            @pl.when(i == 1)
            def _():
                g_w2.step1(2)
                g_w2.step2(0)
                g_w2.step1(3)

            return 0

        lax.fori_loop(0, 2, near, 0)

        def far(i, _):
            wait_ready(i, g_w1)
            up(i)
            pl.when(i == 2)(lambda: g_w2.step2(1))

            @pl.when(i == 3)
            def _():
                g_w2.step2(2)
                g_w2.step2(3)

            return 0

        lax.fori_loop(2, 4, far, 0)
        g_w2.ready(3)
        far1, far2 = near_first(2), near_first(3)

        def row(r, _):
            rs = rowsl(r)
            total = r2_ref[rs, :] + mm(u_ref[far1, rs, :], R("w2")[far1]) + mm(u_ref[far2, rs, :], R("w2")[far2])
            r2_ref[rs, :] = total
            sec_ref[rs, :] = norm(total, gain2).astype(BF16)
            for h in range(2):
                mem_x(r, h).start()
            return 0

        lax.fori_loop(0, rows, row, 0)

    def sends(reductions, i):
        for j in range(2):
            @pl.when(i == j)
            def _():
                for reduction in reductions:
                    reduction.core_send(j)

    cstart = pl.multiple_of(jnp.minimum(t * (own - HALO), slots - cwin), HALO)
    cwindow = pl.ds(cstart, cwin)
    kv_ref, cq_ref, cp_ref, dkv_ref, cinv_ref = R("kv"), R("cq"), R("cp"), R("dkv"), R("cinv")
    c0_ref, cqw_ref, cow_ref, oc_ref, cot_ref = R("c0"), R("cqw"), R("cow"), R("oc"), R("cot")
    cols, keys_ref = R("cols"), R("keys")

    @pl.when(is_dec)
    def _():
        g_w2.step1(0)
        g_c1.step2()
        for k in range(4):
            g_c1.ready(k)
        pick_shape = (width // 4, width // 2)
        twice = 2 * lax.broadcasted_iota(jnp.int32, pick_shape, 0)
        at_col = lax.broadcasted_iota(jnp.int32, pick_shape, 1)
        picks = [jnp.where(at_col == twice + j, 1.0, 0.0).astype(BF16) for j in range(2)]

        def unweave(base, m):
            return [mm(pick, R("dmf")[pl.ds(base + m * (width // 2), width // 2), :]).astype(BF16) for pick in picks]

        for m in range(4):
            span = pl.ds(m * (width // 4), width // 4)
            cqw_ref[span, :], cow_ref[span, :] = unweave(0, m)
        cq_ref[...] = mm(n2_ref[...], cqw_ref[...]).astype(BF16) * scale
        g_w2.step1(1)
        g_c0.step2()
        g_w2.step1(2)
        g_w2.step1(3)
        kv_ref[...] = jnp.zeros_like(kv_ref)
        for r in range(rows):
            cols[r] = seg_column(1, r)
            keys_ref[r] = seg_row(0, r, cstart)[:, :cwin]
        for k in range(4):
            g_c0.ready(k)
        for m in range(4):
            span = pl.ds(m * (width // 4), width // 4)
            ck, cv = unweave(2 * width, m)
            for s in range(4):
                c0_ref[span, 2 * s * hw : (2 * s + 1) * hw] = ck[:, s * hw : (s + 1) * hw]
                c0_ref[span, (2 * s + 1) * hw : (2 * s + 2) * hw] = cv[:, s * hw : (s + 1) * hw]
        g_w1.step1(0)
        g_w2.step2(0)
        g_w2.step2(1)
        g_w1.step1(1)
        for g in (g_c1, g_c0):
            g.finish()
        R("dmf")[...] = jnp.zeros_like(R("dmf"))
        g_w2.step2(2)
        g_w2.step2(3)
        g_w1.step2(0)
        for k in range(4):
            g_w2.ready(k)

        def early(s, _):
            gp_ref[s] = mm_nt(cot_ref[...], R("w2")[s]).astype(BF16)
            return 0

        lax.fori_loop(0, 4, early, 0)

        def pass_memory_on(r):
            for h in range(2):
                mem_x(r, h).wait_recv()
                mem_c(r, h).start()
            pl.when(inner)(mem_t(r).start)

        def settle(r):
            span = pl.ds(0, own)
            dm_c(r).wait_recv()
            acc_ref[span, :] = R("dmf")[in_row(r, block), :].astype(F32) + R("rcc")[r].astype(F32)

            @pl.when(inner)
            def _():
                dm_t(r).wait_recv()
                place = pl.ds(pl.multiple_of((2 - t) * (own - side), HALO), side)
                acc_ref[place, :] += R("rct")[r].astype(F32)

            R("rcc")[r] = acc_ref[span, :].astype(BF16)
            dm_x(r).start()

        def row(r, _):
            rs = rowsl(r)

            def project(span):
                kv_ref[span, :] = mm(R("memf")[in_row(r, span), :], c0_ref[...]).astype(BF16)

            @pl.when(r == 0)
            def _():
                g_w1.step2(1)
                pass_memory_on(0)

            bias_ref[:, pl.ds(0, cwin)] = jnp.where(spread(cols[r], cwin) == keys_ref[r, pl.ds(0, 1), :], 0.0, MASKED)
            project(block)
            pl.when(r > 0)(lambda: settle(r - 1))
            for h in range(2):
                mem_c(r, h).wait_recv()
            project(block1)

            @pl.when(inner)
            def _():
                mem_t(r).wait_recv()
                project(edge_in)

            def cross(i, _):
                for s in range(4):
                    def keep(e):
                        cp_ref[rowsl(s, 2 * own), :] = e

                    o2, inv = attend(cq_ref[rs, lanes(s)], kv_ref[cwindow, lanes(2 * s)], kv_ref[cwindow, lanes(2 * s + 1)], lambda scores: scores + bias_ref[:, pl.ds(0, cwin)], keep)
                    oc_ref[rs, lanes(s)] = o2.astype(BF16)
                    cinv_ref[:, lanes(s)] = inv.astype(BF16)
                return 0

            cross(0, 0)
            pl.when(r < rows - 1)(lambda: pass_memory_on(r + 1))
            r2_ref[rs, :] = r1_ref[rs, :] + mm_nt(oc_ref[rs, :], cow_ref[...])
            n3_ref[rs, :] = norm(r2_ref[rs, :], gain2).astype(BF16)

            @pl.when(r == 0)
            def _():
                for k in range(4):
                    g_w1.ready(k)

            dn = pl.ds(0, own)
            acc_ref[dn, :] = jnp.zeros((own, width), F32)

            def feed(i, _):
                back = acc_ref[dn, :]
                for s in range(4):
                    u, gp = gelu_parts(mm(n3_ref[rs, :], R("w1")[s]))
                    u = u.astype(BF16)
                    u_ref[s, rs, :] = u
                    dh = (gp_ref[s, rs, :].astype(F32) * gp).astype(BF16)
                    gp_ref[s, rs, :] = dh
                    back += mm_nt(dh, R("w1")[s])
                acc_ref[dn, :] = back
                return 0

            feed(0, 0)
            dx, dg = norm_back(r2_ref[rs, :], gain2, acc_ref[dn, :])
            R("dg")[r, pl.ds(2, 1), :] = dg
            g2 = cot_ref[rs, :].astype(F32) + dx
            g_ref[rs, :] = g2
            gb_ref[rs, :] = g2.astype(BF16)
            do_ref[rs, :] = mm(gb_ref[rs, :], cow_ref[...]).astype(BF16)
            ws = pl.ds(pl.multiple_of(r * cwin, HALO), cwin)

            def back(i, _):
                for s in range(4):
                    dq, dk, dv = attend_back(
                        cq_ref[rs, lanes(s)], kv_ref[cwindow, lanes(2 * s)], kv_ref[cwindow, lanes(2 * s + 1)],
                        do_ref[rs, lanes(s)], oc_ref[rs, lanes(s)], cinv_ref[:, lanes(s)], lambda h: cp_ref[rowsl(2 * s + h), :],
                    )
                    cq_ref[rs, lanes(s)] = dq
                    dkv_ref[ws, lanes(2 * s)] = dk
                    dkv_ref[ws, lanes(2 * s + 1)] = dv
                return 0

            back(0, 0)
            R("dmf")[in_row(r, cwindow), :] = mm_nt(dkv_ref[ws, :], c0_ref[...]).astype(BF16)
            dm_c(r).start()
            pl.when(inner)(dm_t(r).start)

            @pl.when(r == rows - 1)
            def _():
                def w2_grad(i, _):
                    s = far_first(i)
                    R("dw2")[rowsl(s, width), :] = mm_tn(cot_ref[...], u_ref[s]).astype(BF16)
                    sends(r_w2, i)
                    return 0

                lax.fori_loop(0, 4, w2_grad, 0)
                settle(r)

            return 0

        lax.fori_loop(0, rows, row, 0)
        for r in range(rows):
            dm_c(r).wait_send()
            pl.when(inner)(dm_t(r).wait_send)

        def w1_grad(i, _):
            s = far_first(i)
            R("dmf")[rowsl(s, width), :] = mm_tn(n3_ref[...], gp_ref[s]).astype(BF16)
            sends(r_w1, i)

            @pl.when(i == 0)
            def _():
                r_w2[0].core_done()
                r_w2[1].core_done()

            return 0

        lax.fori_loop(0, 4, w1_grad, 0)

        def c0_grad(i, _):
            s = far_first(i)
            total = mm_tn(R("memf")[in_row(0, cwindow), :], dkv_ref[pl.ds(0, cwin), lanes(s, 2 * hw)])
            for r in range(1, rows):
                total += mm_tn(R("memf")[in_row(r, cwindow), :], dkv_ref[pl.ds(r * cwin, cwin), lanes(s, 2 * hw)])
            r_c0.part(s)[...] = total.astype(BF16)
            sends([r_c0], i)

            @pl.when(i == 1)
            def _():
                r_w1[0].core_done()
                r_w1[1].core_done()

            return 0

        lax.fori_loop(0, 4, c0_grad, 0)
        def query_norm(r, _):
            rs = rowsl(r)
            dx, dg = norm_back(r1_ref[rs, :], gain1, mm_nt(cq_ref[rs, :], cqw_ref[...]))
            R("dg")[r, pl.ds(1, 1), :] = dg
            g_ref[rs, :] += dx
            return 0

        lax.fori_loop(0, rows, query_norm, 0)
        dcq = mm_tn(n2_ref[...], cq_ref[...]).astype(BF16)
        dco = mm_tn(gb_ref[...], oc_ref[...]).astype(BF16)
        r_c0.core_done()
        for s in range(4):
            r_c1.part(s)[:, :hw] = dcq[:, s * hw : (s + 1) * hw]
            r_c1.part(s)[:, hw:] = dco[:, s * hw : (s + 1) * hw]
        sends([r_c1], 0)
        sends([r_c1], 1)

    @pl.when(is_enc)
    def _():
        def receive(r):
            rs = rowsl(r)
            dm_x(r).wait_recv()
            dx, dg = norm_back(r2_ref[rs, :], gain2, R("rcc")[r].astype(F32))
            R("dg")[r, pl.ds(2, 1), :] = dg
            g_ref[rs, :] = dx
            gb_ref[rs, :] = dx.astype(BF16)

        def hidden_back(s, rs):
            dh = (mm_nt(gb_ref[rs, :], R("w2")[s]) * gp_ref[s, rs, :].astype(F32)).astype(BF16)
            gp_ref[s, rs, :] = dh
            acc_ref[rs, :] += mm_nt(dh, R("w1")[s])

        head, last = pl.ds(0, (rows - 1) * own), pl.ds((rows - 1) * own, own)
        acc_ref[pl.ds(0, tokens), :] = jnp.zeros((tokens, width), F32)
        for r in range(rows - 1):
            receive(r)

        def head_grads(s, _):
            R("dw2")[rowsl(s, width), :] = mm_tn(gb_ref[head, :], u_ref[s, head, :]).astype(BF16)
            hidden_back(s, head)
            return 0

        lax.fori_loop(0, 4, head_grads, 0)
        receive(rows - 1)

        for i in range(4):
            s = far_first(i)
            part = R("dw2").at[rowsl(s, width)]
            part[...] = (part[...].astype(F32) + mm_tn(gb_ref[last, :], u_ref[s, last, :])).astype(BF16)
            if i < 2:
                for reduction in r_w2:
                    reduction.core_send(i)
        for i in range(4):
            s = far_first(i)
            hidden_back(s, last)
            if i == 1:
                r_w2[0].core_done()
                r_w2[1].core_done()
            R("dmf")[rowsl(s, width), :] = mm_tn(n2_ref[...], gp_ref[s]).astype(BF16)
            if i < 2:
                for reduction in r_w1:
                    reduction.core_send(i)
        r_w1[0].core_done()
        r_w1[1].core_done()
        dx, dg = norm_back(r1_ref[...], gain1, acc_ref[pl.ds(0, tokens), :])
        R("dg")[0, pl.ds(1, 1), :] = dg
        for r in range(1, rows):
            R("dg")[r, pl.ds(1, 1), :] = jnp.zeros_like(dg)
        g_ref[...] += dx

    sec_out = links.here(sec_ref, R("sec"))
    pl.when(is_enc)(sec_out.start)
    gb_ref[...] = g_ref[...].astype(BF16)
    R("dwo")[...] = mm_tn(gb_ref[...], o_ref[...]).astype(BF16)
    r_wo.core_send(0)
    r_wo.core_send(1)
    do_ref[...] = mm_nt(gb_ref[...], R("wo")[...].reshape(4 * hw, width)).astype(BF16)
    acc_ref[...] = jnp.zeros_like(acc_ref)
    dqkv_ref = R("dqkv")
    for r in range(rows):
        dqkv_ref[pl.ds(r * win, HALO), :hw] = jnp.zeros((HALO, hw), BF16)
        dqkv_ref[pl.ds(r * win + HALO + own, HALO), :hw] = jnp.zeros((HALO, hw), BF16)

    def self_back(i, _):
        s = far_first(i)
        for r in range(rows):
            rs = pl.ds(r * own, own)
            dq, dk, dv = attend_back(
                q_ref[s, r], k_ref[s, r], v_ref[s, r], do_ref[rs, lanes(s)], o_ref[rs, lanes(s)], inv_ref[rs, lanes(s)],
                lambda h: p_ref[s, r, pl.ds(h * own, own), :],
            )
            dqkv_ref[pl.ds(r * win + HALO, own), :hw] = dq
            dqkv_ref[pl.ds(r * win, win), hw : 2 * hw] = dk
            dqkv_ref[pl.ds(r * win, win), 2 * hw :] = dv
        R("cp")[rowsl(s, width), pl.ds(0, 3 * hw)] = mm_tn(nw_ref[...], dqkv_ref[...]).astype(BF16)
        sends(r_wa, i)
        acc_ref[...] += mm_nt(dqkv_ref[...], R("wa")[s])

        @pl.when(i == 0)
        def _():
            r_w2[0].z_done(0)
            pl.when(is_dec)(r_c1.core_done)
            r_wo.core_done()
            r_w2[1].y_done()

        @pl.when(i == 2)
        def _():
            r_w1[1].z_done(0)
            r_w1[0].y_done()

        @pl.when(i == 3)
        def _():
            pl.when(is_enc)(r_wo.y_done)
            r_w2[1].z_done(0, w2_out[1])
            r_w2[0].z_rest()
            pl.when(is_dec)(r_c0.y_done)

        return 0

    lax.fori_loop(0, 4, self_back, 0)
    for r in range(rows):
        R("xh")[0, r] = acc_ref[pl.ds(r * win, HALO), :].astype(BF16)
        R("xh")[1, r] = acc_ref[pl.ds(r * win + HALO + own, HALO), :].astype(BF16)
    pl.when(t == 1)(dn_left.start)
    pl.when(t < 3)(dn_right.start)
    pl.when(t > 1)(dn_left.start)
    for j in range(3):
        r_wa[j].core_done()

    @pl.when(is_dec)
    def _():
        def decoded(r, _):
            rs = rowsl(r)
            total = r2_ref[rs, :]
            for s in range(4):
                total += mm(u_ref[s, rs, :], R("w2")[s])
            sec_ref[rs, :] = total.astype(BF16)
            return 0

        lax.fori_loop(0, rows, decoded, 0)
        sec_out.start()

    @pl.when(t == 0)
    def _():
        R("dhr")[0] = jnp.zeros((rows, HALO, width), BF16)

    @pl.when(t == 3)
    def _():
        R("dhr")[1] = jnp.zeros((rows, HALO, width), BF16)

    @pl.when(is_dec)
    def _():
        r_w1[0].z_done(0, w1_out[0])
        r_w1[1].z_rest()
        r_c1.y_done()
        r_w2[1].z_rest(w2_out[1])
        r_wo.y_done()
        r_c0.z_done(0, R("dc0"))

    pl.when(t > 0)(dn_right.wait_recv)
    pl.when(t < 3)(dn_left.wait_recv)
    for r in range(rows):
        lo, hi = pl.ds(r * win + HALO, HALO), pl.ds(r * win + own, HALO)
        acc_ref[lo, :] += R("dhr")[0, r].astype(F32)
        acc_ref[hi, :] += R("dhr")[1, r].astype(F32)
    total = jnp.zeros((1, width), F32)
    for r in range(rows):
        rs = pl.ds(r * own, own)
        dx, dg = norm_back(x_ref[r].astype(F32), gain0, acc_ref[pl.ds(r * win + HALO, own), :])
        gb_ref[rs, :] = (g_ref[rs, :] + dx).astype(BF16)
        total += dg
    dgt, dgd = R("dgt"), R("dgd")
    dgt[t] = jnp.zeros((8, width), F32)
    dgt[t, pl.ds(0, 1), :] = total
    dgt[t, pl.ds(1, 2), :] = sum(R("dg")[r, pl.ds(1, 2), :] for r in range(rows))
    for c in gain_over_t:
        c.start()
    gx_out = links.here(gb_ref, R("gx"))
    gx_out.start()

    def gains_over_t():
        for c in gain_over_t:
            c.wait_recv()
        dgd[d] = dgt[0] + dgt[1] + dgt[2] + dgt[3]
        for c in gain_over_d:
            c.start()

    def gains_over_d():
        total = jnp.zeros((8, width), F32)
        for c in gain_over_d:
            c.wait_recv()
        for k in range(dp):
            total += dgd[k]
        R("dgain")[...] = pltpu.roll(total, lax.rem(width - d * (width // dp), width), 1)

    @pl.when(is_enc)
    def _():
        r_w2[0].y_done(w2_out[0])
        r_w1[0].z_done(0, w1_out[0])
        r_w1[1].z_rest()
        r_wa[0].y_done()
        r_wo.z_done(0, R("dwo_o"))
        r_wa[1].y_done()
        r_w2[1].z_rest(w2_out[1])
        r_wa[0].z_done(0, wa_out[0])
        r_wa[2].y_done()
        gains_over_t()
        r_w1[0].z_rest(w1_out[0])
        r_wa[1].z_done(0, wa_out[1])
        r_w1[1].y_done(w1_out[1])
        r_wo.z_rest(R("dwo_o"))

    @pl.when(is_dec)
    def _():
        r_w2[0].y_done(w2_out[0])
        r_w1[0].z_rest(w1_out[0])
        r_c1.z_done(0, R("dc"))
        r_wa[0].y_done()
        r_wo.z_done(0, R("dwo_o"))
        r_wa[1].y_done()
        r_c0.z_rest(R("dc0"))
        c0_back.start()
        r_wa[0].z_done(0, wa_out[0])
        r_wa[2].y_done()
        r_c1.z_rest(R("dc"))
        r_wa[1].z_done(0, wa_out[1])
        r_w1[1].y_done(w1_out[1])
        gains_over_t()
        r_wo.z_rest(R("dwo_o"))

    r_wa[2].z_done(0, wa_out[2])
    for j in range(3):
        r_wa[j].z_rest(wa_out[j])
    gains_over_d()

    sec_out.wait()
    gx_out.wait()
    for g in (g_wa, g_wo, g_w1, g_w2):
        g.finish()
    for g in r_w2 + r_w1 + [r_wo] + r_wa:
        g.finish()
    for c in gain_over_t + gain_over_d:
        c.wait_send()
    pl.when(t < 3)(x_right.wait_send)
    pl.when(t > 0)(x_left.wait_send)
    pl.when(t < 3)(dn_right.wait_send)
    pl.when(t > 0)(dn_left.wait_send)

    @pl.when(is_enc)
    def _():
        c0_x.wait_send()
        for r in range(rows):
            for h in range(2):
                mem_x(r, h).wait_send()
        c0_back.wait_recv()
        R("dc")[...] = R("dc0r")[...]

    @pl.when(is_dec)
    def _():
        for g in (r_c0, r_c1):
            g.finish()
        for r in range(rows):
            for h in range(2):
                mem_c(r, h).wait_send()
            pl.when(inner)(mem_t(r).wait_send)
            dm_x(r).wait_send()
        c0_back.wait_send()


def arrange(aligned, sec, gx, dgain, da, dwo, dc, dw1, dw2, sec_o, gx_o, dgain_o, da_o, dwo_o, dc_o, dw1_o, dw2_o):
    share, hw = dwo.shape
    sec_o[...] = sec[...]
    gx_o[...] = gx[...]
    for i in range(3):
        dgain_o[i] = dgain[pl.ds(i, 1), pl.ds(0, share)]
        da_o[i] = da[:, pl.ds(i * hw, hw)]
    for i in range(2):
        dc_o[:, i, :] = dc[:, pl.ds(i * hw, hw)]
    dw1_o[...] = dw1[...]
    dwo_o[...] = dwo[...].T if aligned else dwo[...]
    dw2_o[...] = dw2[...].T if aligned else dw2[...]


def body(embeds, segments, cotangent, norm_gains, attn_in, attn_out, cross_proj, ffn_in, ffn_out):
    dp = lax.axis_size("dp")
    rows, own, width = embeds.shape[1:]
    slots = segments.shape[2]
    hw = attn_in.shape[3]
    fw = ffn_in.shape[2]
    win = own + 2 * HALO
    cwin = 2 * own + 2 * HALO
    tokens = rows * own
    side = 3 * own // 4
    share = width // dp
    zsteps = (dp - 1).bit_length()

    ins = dict(
        x_h=embeds[0], segs_h=segments, gains=norm_gains.transpose(1, 0, 2), cot_h=cotangent.reshape(tokens, width),
        wa_h=attn_in[0].transpose(1, 0, 2), wo_h=attn_out[0], w1_h=ffn_in[0], w2_h=ffn_out[0],
        cx_h=cross_proj[0].reshape(2 * width, hw),
    )
    outs = dict(
        sec=((tokens, width), BF16), gx=((tokens, width), BF16), dgain=((8, width), F32),
        da_o=((share, 3 * hw), F32), dwo_o=((share, hw), F32), dc=((share, 2 * hw), F32),
        dw1_o=((share, fw), F32), dw2_o=((share, fw), F32),
    )
    vm = dict(
        x=((rows, own, width), BF16), cot=((tokens, width), BF16), segs=(segments.shape, jnp.int32),
        wa=((4, width, 3 * hw), BF16), wo=((4, hw, width), BF16), w1=((4, width, fw), BF16), w2=((4, fw, width), BF16),
        c0=((width, 8 * hw), BF16), cqw=((width, 4 * hw), BF16), cow=((width, 4 * hw), BF16),
        xh=((2, rows, HALO, width), BF16), nw=((rows * win, width), BF16),
        q=((4, rows, own, hw), BF16), k=((4, rows, win, hw), BF16), v=((4, rows, win, hw), BF16),
        p=((4, rows, 2 * own, win), BF16), o=((tokens, width), BF16), inv=((tokens, width), BF16), bias=((own, max(rows * win, cwin)), F32),
        r1=((tokens, width), F32), r2=((tokens, width), F32), n2=((tokens, width), BF16), n3=((tokens, width), BF16),
        u=((4, tokens, fw), BF16), gp=((4, tokens, fw), BF16), secs=((tokens, width), BF16),
        acc=((rows * win, width), F32), g=((tokens, width), F32), gb=((tokens, width), BF16), do=((tokens, width), BF16),
        memf=((max(rows * slots, 4 * width), max(width, fw)), BF16), kv=((slots, 8 * hw), BF16), cq=((tokens, width), BF16),
        cp=((max(8 * own, 4 * width), cwin), BF16), cinv=((own, width), BF16), oc=((tokens, width), BF16),
        cols=((rows, own, 128), F32), keys=((rows, 8, cwin), F32),
        dkv=((rows * cwin, 8 * hw), BF16), dmf=((max(rows * slots, 4 * width), max(width, fw)), BF16),
        rcc=((rows, own, width), BF16), rct=((rows, side, width), BF16),
        dg=((rows, 8, width), F32),
        dqkv=((rows * win, 3 * hw), BF16), dhr=((2, rows, HALO, width), BF16),
        dgt=((4, 8, width), F32), dgd=((dp, 8, width), F32),
        dw2=((4 * width, fw), BF16), dwo=((width, 4 * hw), BF16),
        dc0=((share, 2 * hw), F32), dc0r=((share, 2 * hw), F32),
    )
    sums = dict(w20=fw // 2, w21=fw // 2, w10=fw // 2, w11=fw // 2, wo=hw, wa0=hw, wa1=hw, wa2=hw, c0=2 * hw, c1=2 * hw)
    for name, m in sums.items():
        shards = 2 if name in ("w20", "w11") else 1
        vm["rc_" + name] = ((2, width, m), BF16)
        vm["ry_" + name] = ((share if shards == 2 else width, m), BF16)
        vm["zb_" + name] = ((shards, dp, share, m), BF16)
        for k in range(zsteps):
            vm[f"zr{k}_{name}"] = ((shards, dp >> (k + 1), share, m), BF16)
    copies = 140 + 12 * zsteps + dp
    sems = dict(send=pltpu.SemaphoreType.DMA((copies,)), recv=pltpu.SemaphoreType.DMA((copies,)), local=pltpu.SemaphoreType.DMA((16,)))
    in_hbm = {n for n in ins if n.endswith("_h")}
    out_hbm = {"sec", "gx"}
    results = pl.pallas_call(
        functools.partial(layers, list(ins) + list(outs) + list(vm) + list(sems)),
        name="layers",
        out_shape=[jax.ShapeDtypeStruct(*o) for o in outs.values()],
        in_specs=[pl.BlockSpec(memory_space=pl.ANY if n in in_hbm else pltpu.VMEM) for n in ins],
        out_specs=[pl.BlockSpec(memory_space=pl.ANY if n in out_hbm else pltpu.VMEM) for n in outs],
        scratch_shapes=[pltpu.VMEM(*s) for s in vm.values()] + list(sems.values()),
        compiler_params=pltpu.CompilerParams(vmem_limit_bytes=VMEM_LIMIT, collective_id=0, has_side_effects=True),
    )(*ins.values())
    aligned = share % 128 == 0
    sec, gx, dgain, da, dwo, dc, dw1, dw2 = pl.pallas_call(
        functools.partial(arrange, aligned),
        name="arrange",
        out_shape=[
            jax.ShapeDtypeStruct((tokens, width), BF16),
            jax.ShapeDtypeStruct((tokens, width), BF16),
            jax.ShapeDtypeStruct((3, 1, share), F32),
            jax.ShapeDtypeStruct((3, share, hw), F32),
            jax.ShapeDtypeStruct((hw, share) if aligned else (share, hw), F32),
            jax.ShapeDtypeStruct((share, 2, hw), F32),
            jax.ShapeDtypeStruct((share, fw), F32),
            jax.ShapeDtypeStruct((fw, share) if aligned else (share, fw), F32),
        ],
        in_specs=[pl.BlockSpec(memory_space=pltpu.VMEM)] * 8,
        out_specs=[pl.BlockSpec(memory_space=pltpu.VMEM)] * 8,
    )(*results)
    if not aligned:
        dwo, dw2 = dwo.T, dw2.T
    return (
        sec.reshape(1, rows, own, width), gx.reshape(1, rows, own, width), dgain.transpose(1, 0, 2),
        da.transpose(1, 0, 2)[None], dwo[None], dc[None], dw1[None], dw2[None],
    )


def solution(mesh):
    return jax.shard_map(
        body,
        mesh=mesh,
        in_specs=(
            P("pipe", "dp", "tensor", None),
            P(None, "dp", None),
            P("dp", "tensor", None),
            P("pipe", None, None),
            P("pipe", None, None, "tensor"),
            P("pipe", "tensor", None),
            P("pipe", None, None, "tensor"),
            P("pipe", None, "tensor"),
            P("pipe", "tensor", None),
        ),
        out_specs=(
            P("pipe", "dp", "tensor", None),
            P("pipe", "dp", "tensor", None),
            P("pipe", None, "dp"),
            P("pipe", "dp", None, "tensor"),
            P("pipe", "tensor", "dp"),
            P("pipe", "dp", None, "tensor"),
            P("pipe", "dp", "tensor"),
            P("pipe", "tensor", "dp"),
        ),
        check_vma=False,
    )
```
